32 devices in a mesh: dp: 16 (over z, y, x), mp: 2 (over core).
Axes of the slice: x: 2, y: 2, z: 4, core: 2. Of those that a mesh axis runs over, the one named last changes fastest.
Arguments:
- hidden_in: bfloat16 [16384, 2048], P(('dp', 'mp')), may hold values from -6 to 6
- segments: int32 [16384], P('dp'), may hold values from -1 to 16, as said below
- norm_gain: float32 [2048], replicated, may hold values from 0.25 to 1.75
- w_zx: bfloat16 [2048, 2, 4096], P('dp', None, 'mp'), may hold values from -0.125 to 0.125
- w_dt: bfloat16 [2048, 64], P('dp', 'mp'), may hold values from -0.125 to 0.125
- w_bc: bfloat16 [2048, 256], P('dp'), may hold values from -0.125 to 0.125
- conv_x: float32 [4, 4096], P(None, 'mp'), may hold values from -3 to 3
- conv_x_bias: float32 [4096], P('mp'), may hold values from -3 to 3
- conv_bc: float32 [4, 256], replicated, may hold values from -3 to 3
- conv_bc_bias: float32 [256], replicated, may hold values from -3 to 3
- dt_bias: float32 [64], P('mp'), may hold values from -6.5 to -2.5
- a_log: float32 [64], P('mp'), may hold values from 0 to 2.77
- d_skip: float32 [64], P('mp'), may hold values from 0.5 to 1.5
- gated_gain: float32 [4096], P('mp'), may hold values from 0.25 to 1.75
- w_out: bfloat16 [4096, 2048], P('mp', 'dp'), may hold values from -0.09375 to 0.09375
- cotangent: bfloat16 [16384, 2048], P(('dp', 'mp')), may hold values from -6 to 6
Outputs:
- residual_out: bfloat16 [16384, 2048], P(('dp', 'mp'))
- input_grad: float32 [16384, 2048], P(('dp', 'mp'))
- grad_norm_gain: float32 [2048], replicated
- grad_w_zx: float32 [2048, 2, 4096], P('dp', None, 'mp')
- grad_w_dt: float32 [2048, 64], P('dp', 'mp')
- grad_w_bc: float32 [2048, 256], P('dp')
- grad_conv_x: float32 [4, 4096], P(None, 'mp')
- grad_conv_x_bias: float32 [4096], P('mp')
- grad_conv_bc: float32 [4, 256], replicated
- grad_conv_bc_bias: float32 [256], replicated
- grad_dt_bias: float32 [64], P('mp')
- grad_a_log: float32 [64], P('mp')
- grad_d_skip: float32 [64], P('mp')
- grad_gated_gain: float32 [4096], P('mp')
- grad_w_out: float32 [4096, 2048], P('mp', 'dp')
- rms_residual: float32 [], replicated
- rms_mixer: float32 [], replicated
The draws below stay inside these ranges and needn't reach their ends.
Inputs may be any that keep to these rules, and one draw needn't show every extreme that they name: `segments`: per token, the number of its document within its sequence of 1024 tokens, counted from 0 in order, or -1 for padding at the sequence's end. Documents hold 60 to 800 tokens, except the last of a sequence, which may be cut short. In every sequence one document holds tokens on both sides of its middle.
All inputs are finite; a program needn't handle non-finite values.
Results may differ from the reference program's by a relative error of at most 0.0064.
The reference program's roundings to bfloat16 on the way count: a program that leaves them out, or rounds other values in their place, can miss the bound.
Values may be sent and summed in bfloat16 or wider, within the bound.
A program may use at most 320 MiB of HBM per device.

```python
import jax
import jax.numpy as jnp
from jax import lax

D = 2048
HEADS = 64
NSTATE = 128
INNER = 4096
CONV = 4
BLOCK = 256
SEQ_LEN = 1024
TOKENS = 16384
DOC_MIN = 60
DOC_MAX = 800


def draw_segments(key, part):
    key = jax.random.fold_in(key, 11)
    number = TOKENS // SEQ_LEN
    most_docs = SEQ_LEN // DOC_MIN + 2
    length_key = jax.random.fold_in(key, 1)
    pad_key = jax.random.fold_in(key, 2)
    pick_key = jax.random.fold_in(key, 3)
    lengths = jax.random.randint(length_key, (number, most_docs), DOC_MIN + 1, DOC_MAX)
    chosen = jax.random.randint(pick_key, (), 0, number)
    rows = jnp.arange(number, dtype=jnp.int32)
    lengths = jnp.where((rows == chosen)[:, None], DOC_MIN + 1, lengths)
    ends = jnp.cumsum(lengths, axis=1)
    middle = SEQ_LEN // 2
    ends = jnp.where(ends == middle, ends + 1, ends)
    places = jnp.arange(SEQ_LEN, dtype=jnp.int32)
    doc_ids = jnp.sum((ends[:, None, :] <= places[None, :, None]).astype(jnp.int32), axis=2)
    padding = jax.random.randint(pad_key, (number, 1), 0, DOC_MIN)
    padding = jnp.where((rows == chosen)[:, None], 0, padding)
    doc_ids = jnp.where(places[None, :] >= SEQ_LEN - padding, -1, doc_ids)
    return doc_ids.reshape(TOKENS).astype(jnp.int32)


def raised(entries, rng, source, target, parts, factor):
    owner, partner = [(jnp.arange(entries.shape[axis_at]) // (entries.shape[axis_at] // parts)).reshape([-1 if axis == axis_at else 1 for axis in range(entries.ndim)]) for axis_at in (source, target)]
    chosen = jax.random.permutation(rng, parts)[partner]
    strong = (owner == chosen) | (owner == (partner + parts // 2) % parts)
    return jnp.where(strong, factor * entries, entries)


def block_levels(stream_key, extent, pieces, least, largest):
    factor_of = 1.0
    for dim, blocks in pieces:
        steps = jax.random.uniform(jax.random.fold_in(jax.random.fold_in(stream_key, 6), dim), (blocks,), jnp.float32, least / len(pieces), largest / len(pieces))
        factor_of = factor_of * jnp.repeat(jnp.exp(steps), extent[dim] // blocks).reshape((-1,) + (1,) * (len(extent) - 1 - dim))
    return factor_of


def gaussian(key, dims, scale, most, split=(), held_as=jnp.bfloat16):
    drawn = jax.random.normal(key, dims, jnp.float32) * scale
    if len(split) > 0:
        drawn = block_levels(key, dims, split, -0.22, 0.18) * drawn
    return jnp.clip(drawn, min=-most, max=most).astype(held_as)


def gaussian_with(own_key, dims, scale, most, split, heavy, kind=jnp.bfloat16):
    values = scale * jax.random.normal(own_key, dims, jnp.float32)
    if split:
        values = values * block_levels(own_key, dims, split, -0.22, 0.18)
    return jnp.clip(raised(values, jax.random.fold_in(own_key, 3), *heavy), -most, most).astype(kind)


def setup_inputs(seed: int = 0) -> dict:
    streams_of = jax.random.split(jax.random.key(seed), 17)
    return {
        "hidden_in": gaussian_with(streams_of[0], (TOKENS, D), 1.0, 6.0, ((0, 32),), (0, 1, 32, 2.75)),
        "segments": draw_segments(jax.random.fold_in(streams_of[16], 71), 0),
        "norm_gain": jnp.clip(1.0 + 0.15 * jax.random.normal(streams_of[2], (D,), jnp.float32), 0.25, 1.75),
        "w_zx": gaussian(streams_of[3], (D, 2, INNER), D ** -0.5, 0.125, ((0, 16), (2, 2))),
        "w_dt": gaussian(streams_of[4], (D, HEADS), D ** -0.5, 0.125, ((0, 16), (1, 2))),
        "w_bc": gaussian(streams_of[5], (D, 2 * NSTATE), D ** -0.5, 0.125, ((0, 16),)),
        "conv_x": gaussian(streams_of[6], (CONV, INNER), CONV ** -0.5, 3.0, ((1, 2),), jnp.float32),
        "conv_x_bias": gaussian(streams_of[7], (INNER,), 0.5, 3.0, ((0, 2),), jnp.float32),
        "conv_bc": gaussian(streams_of[8], (CONV, 2 * NSTATE), CONV ** -0.5, 3.0, (), jnp.float32),
        "conv_bc_bias": gaussian(streams_of[9], (2 * NSTATE,), 0.5, 3.0, (), jnp.float32),
        "dt_bias": jnp.clip(-6.5 + 4.0 * jax.random.uniform(streams_of[10], (HEADS,), jnp.float32) ** block_levels(streams_of[10], (HEADS,), ((0, 2),), -0.2, 0.2), -6.5, -2.5),
        "a_log": jnp.clip(2.77 * jax.random.uniform(streams_of[11], (HEADS,), jnp.float32) ** block_levels(streams_of[11], (HEADS,), ((0, 2),), -0.2, 0.2), 0.0, 2.77),
        "d_skip": jnp.clip(0.5 + 1.0 * jax.random.uniform(streams_of[12], (HEADS,), jnp.float32) ** block_levels(streams_of[12], (HEADS,), ((0, 2),), -0.2, 0.2), 0.5, 1.5),
        "gated_gain": jnp.clip(1.0 + 0.15 * jax.random.normal(streams_of[13], (INNER,), jnp.float32), 0.25, 1.75),
        "w_out": gaussian(streams_of[14], (INNER, D), INNER ** -0.5, 0.09375, ((0, 2), (1, 16))),
        "cotangent": gaussian_with(streams_of[15], (TOKENS, D), 1.0, 6.0, ((0, 32),), (0, 1, 32, 2.75)),
    }


EPSILON = 1e-05
HIGH = lax.Precision.HIGHEST

@jax.custom_vjp
def low(v):
    return lax.optimization_barrier(v.astype(jnp.bfloat16)).astype(jnp.float32)

@jax.custom_vjp
def low_back(v):
    return v

def low_keep(v):
    return (low(v), None)

def low_pass(kept, grad):
    return (grad,)

def back_keep(v):
    return (v, None)

def back_low(kept, grad):
    return (low(grad),)
low.defvjp(low_keep, low_pass)
low_back.defvjp(back_keep, back_low)

def segment_conv(inputs, taps, bias, segment_ids):
    reach = taps.shape[0]
    result = bias[None, :] + taps[reach - 1][None, :] * inputs
    for offset in range(1, reach):
        moved = jnp.concatenate([jnp.zeros((offset, inputs.shape[1]), inputs.dtype), inputs[:-offset]], axis=0)
        earlier = jnp.concatenate([jnp.full((offset,), -2, jnp.int32), segment_ids[:-offset]])
        same_doc = (earlier == segment_ids)[:, None]
        result = result + taps[reach - 1 - offset][None, :] * jnp.where(same_doc, moved, 0.0)
    return result

def block_terms(operands):
    block_x, block_dt, block_cum, block_b, block_c, block_seg = operands
    size = block_seg.shape[0]
    causal = lax.broadcasted_iota(jnp.int32, (size, size), 0) >= lax.broadcasted_iota(jnp.int32, (size, size), 1)
    same_doc = causal & (block_seg[:, None] == block_seg[None, :])
    scores = jnp.dot(block_c, block_b.T, precision=HIGH)
    spread = block_cum[:, None, :] - block_cum[None, :, :]
    decay = jnp.exp(jnp.where(same_doc[:, :, None], spread, -jnp.inf))
    mixing = scores[:, :, None] * decay * block_dt[None, :, :]
    within = jnp.einsum('tsh,shp->thp', mixing, block_x, precision=HIGH)
    last_keep = (block_seg == block_seg[-1]).astype(block_cum.dtype)[:, None]
    tail_weight = jnp.exp(block_cum[-1][None, :] - block_cum) * block_dt * last_keep
    weighted_x = tail_weight[:, :, None] * block_x
    state = jnp.einsum('shp,sn->hpn', weighted_x, block_b, precision=HIGH)
    return (within, state)

def blocked_scan(values, step_sizes, decay_rates, b_rows, c_rows, segment_ids):
    length, head_count, width = values.shape
    nstate = b_rows.shape[1]
    number = length // BLOCK
    x_blocks = values.reshape(number, BLOCK, head_count, width)
    dt_blocks = step_sizes.reshape(number, BLOCK, head_count)
    cum_blocks = jnp.cumsum((step_sizes * decay_rates[None, :]).reshape(number, BLOCK, head_count), axis=1)
    b_blocks = b_rows.reshape(number, BLOCK, nstate)
    c_blocks = c_rows.reshape(number, BLOCK, nstate)
    seg_blocks = segment_ids.reshape(number, BLOCK)
    before = jnp.concatenate([jnp.full((1,), -2, jnp.int32), seg_blocks[:-1, -1]])
    within, states = lax.map(jax.checkpoint(block_terms), (x_blocks, dt_blocks, cum_blocks, b_blocks, c_blocks, seg_blocks))

    def carry_step(state, operands):
        block_state, block_cum, block_seg, prior = operands
        keep_flag = (block_seg[-1] == prior).astype(state.dtype)
        after = state * (jnp.exp(block_cum[-1]) * keep_flag)[:, None, None] + block_state
        return (after, state)
    start_state = jnp.zeros((head_count, width, nstate), values.dtype)
    _, entering = lax.scan(carry_step, start_state, (states, cum_blocks, seg_blocks, before))
    linked = (seg_blocks == before[:, None]).astype(values.dtype)[:, :, None] * jnp.exp(cum_blocks)
    across = jnp.einsum('ctn,chpn->cthp', c_blocks, entering, precision=HIGH) * linked[..., None]
    return (within + across).reshape(length, head_count, width)

def conv_states(proj_bc, taps, tap_bias, segment_ids):
    return jax.nn.silu(segment_conv(proj_bc, taps, tap_bias, segment_ids))

def head_mixer(proj_zx, state_inputs, proj_dt, taps, tap_bias, step_bias, rate_logs, skip_gain, segment_ids):
    inner_width = taps.shape[1]
    head_count = step_bias.shape[0]
    length = proj_zx.shape[0]
    gate_part = proj_zx[:, :inner_width]
    values = proj_zx[:, inner_width:]
    conv_values = jax.nn.silu(segment_conv(values, taps, tap_bias, segment_ids))
    conv_values = conv_values.reshape(length, head_count, inner_width // head_count)
    nstate = state_inputs.shape[1] // 2
    step_sizes = jax.nn.softplus(proj_dt + step_bias)
    decay_rates = -jnp.exp(rate_logs)
    scanned = blocked_scan(conv_values, step_sizes, decay_rates, state_inputs[:, :nstate], state_inputs[:, nstate:], segment_ids)
    scanned = scanned + skip_gain[None, :, None] * conv_values
    return scanned.reshape(length, inner_width) * jax.nn.silu(gate_part)

def forward_layer(inputs, segment_ids, norm_gain, w_zx, w_dt, w_bc, conv_x, conv_x_bias, conv_bc, conv_bc_bias, dt_bias, a_log, d_skip, gated_gain, w_out):
    normed = low(inputs * lax.rsqrt(lax.optimization_barrier(jnp.mean(inputs * inputs, axis=-1, keepdims=True)) + EPSILON) * norm_gain)
    inner_width = conv_x.shape[1]
    proj_zx = low_back(jnp.dot(normed, w_zx.reshape(w_zx.shape[0], 2 * inner_width), precision=HIGH))
    proj_bc = low_back(jnp.dot(normed, w_bc, precision=HIGH))
    proj_dt = low_back(jnp.dot(normed, w_dt, precision=HIGH))
    state_inputs = conv_states(proj_bc, conv_bc, conv_bc_bias, segment_ids)
    gated = head_mixer(proj_zx, state_inputs, proj_dt, conv_x, conv_x_bias, dt_bias, a_log, d_skip, segment_ids)
    scaled = low(gated * lax.rsqrt(lax.optimization_barrier(jnp.mean(gated * gated, axis=-1, keepdims=True)) + EPSILON) * gated_gain)
    return jnp.dot(scaled, w_out, precision=HIGH)

def reference(hidden_in, segments, norm_gain, w_zx, w_dt, w_bc, conv_x, conv_x_bias, conv_bc, conv_bc_bias, dt_bias, a_log, d_skip, gated_gain, w_out, cotangent):
    params = tuple((p.astype(jnp.float32) for p in (norm_gain, w_zx, w_dt, w_bc, conv_x, conv_x_bias, conv_bc, conv_bc_bias, dt_bias, a_log, d_skip, gated_gain, w_out)))
    number = TOKENS // SEQ_LEN
    model_width = hidden_in.shape[1]
    all_inputs = hidden_in.astype(jnp.float32).reshape(number, SEQ_LEN, model_width)
    all_cot = cotangent.astype(jnp.float32).reshape(number, SEQ_LEN, model_width)
    all_segs = segments.reshape(number, SEQ_LEN)

    def one_sequence(carry, item):
        grads, totals = carry
        inputs, cot_rows, segment_ids = item

        def layer_fn(inputs, *weights):
            return forward_layer(inputs, segment_ids, *weights)
        mixer_out, pullback = jax.vjp(layer_fn, inputs, *params)
        pulled = pullback(cot_rows)
        d_inputs = cot_rows + pulled[0]
        grads = tuple((a + b for a, b in zip(grads, pulled[1:])))
        usable = (segment_ids >= 0).astype(jnp.float32)[:, None]
        totals = (totals[0] + jnp.sum(usable * inputs * inputs), totals[1] + jnp.sum(usable * mixer_out * mixer_out), totals[2] + jnp.sum(usable))
        return ((grads, totals), ((inputs + mixer_out).astype(jnp.bfloat16), d_inputs))
    zero_grads = tuple((jnp.zeros_like(p) for p in params))
    zero_totals = (jnp.zeros((), jnp.float32), jnp.zeros((), jnp.float32), jnp.zeros((), jnp.float32))
    (grads, totals), (outputs, d_all) = lax.scan(one_sequence, (zero_grads, zero_totals), (all_inputs, all_cot, all_segs))
    rms_residual = jnp.sqrt(totals[0] / (totals[2] * model_width))
    rms_mixer = jnp.sqrt(totals[1] / (totals[2] * model_width))
    return (outputs.reshape(TOKENS, model_width), d_all.reshape(TOKENS, model_width), grads[0], grads[1], grads[2], grads[3], grads[4], grads[5], grads[6], grads[7], grads[8], grads[9], grads[10], grads[11], grads[12], rms_residual, rms_mixer)
```

```python
import functools

import jax
import jax.numpy as jnp
from jax import lax
from jax.experimental import pallas as pl
from jax.experimental.pallas import tpu as pltpu
from jax.sharding import PartitionSpec as P

BLOCK = 256
LANES = 128
TILE = 256
WIDTH = 64
GROUP = TILE // WIDTH
EPSILON = 1e-05
HIGH = lax.Precision.HIGHEST
BF16 = jnp.bfloat16
F32 = jnp.float32
VMEM_LIMIT = 56 * 2**20

NN = (((1,), (0,)), ((), ()))
NT = (((1,), (1,)), ((), ()))
TN = (((0,), (0,)), ((), ()))


def dot(a, b, dims=NN, precision=None):
    return lax.dot_general(a, b, dims, precision=precision, preferred_element_type=F32)


def low_dot(a, b, dims=NN):
    return dot(a.astype(BF16), b.astype(BF16), dims)


def flip(a, axis, bit):
    size = lax.axis_size(axis)
    return lax.ppermute(a, axis, [(i, i ^ bit) for i in range(size)])


def sigmoid(q):
    return 1.0 / (1.0 + jnp.exp(-q))


def owner_block(number, dp, extent):
    y, z, x = number // (extent // 2), (number // 2) % (extent // 4), number % 2
    return jnp.bitwise_xor(dp - lax.rem(dp, 2), (y * 2) + (z * 4) + x)


def norm_kernel(place_ref, hidden_ref, cot_ref, gain_ref, normed_ref, cot_out_ref, inv_ref, *, extent):
    u = hidden_ref[...].astype(F32)
    inv = lax.rsqrt(jnp.mean(u * u, axis=-1, keepdims=True) + EPSILON)
    inv_ref[...] = inv
    for number in range(extent):
        start = pl.multiple_of(owner_block(number, place_ref[0], extent) * LANES, LANES)
        piece = hidden_ref[:, pl.ds(start, LANES)].astype(F32)
        gain = gain_ref[:, pl.ds(start, LANES)]
        normed_ref[:, number * LANES : (number + 1) * LANES] = (piece * inv * gain).astype(BF16)
        cot_out_ref[:, number * LANES : (number + 1) * LANES] = cot_ref[:, pl.ds(start, LANES)]


def input_norm(hidden, cot, gain, dp, extent):
    rows, width = hidden.shape
    if width // extent != LANES:
        u = hidden.astype(F32)
        inv = lax.rsqrt(jnp.mean(u * u, axis=-1, keepdims=True) + EPSILON)
        normed = (u * inv * gain).astype(BF16)
        order = owner_block(jnp.arange(extent), dp, extent)

        def arranged(a):
            return jnp.take(a.reshape(rows, extent, -1), order, axis=1).reshape(rows, width)

        return arranged(normed), arranged(cot), inv
    step = 128
    tile = pl.BlockSpec((step, width), lambda i: (i, 0))
    return pl.pallas_call(
        functools.partial(norm_kernel, extent=extent),
        grid=(rows // step,),
        in_specs=[
            pl.BlockSpec(memory_space=pltpu.SMEM),
            tile,
            tile,
            pl.BlockSpec((1, width), lambda i: (0, 0)),
        ],
        out_specs=[tile, tile, pl.BlockSpec((step, 1), lambda i: (i, 0))],
        out_shape=[
            jax.ShapeDtypeStruct((rows, width), BF16),
            jax.ShapeDtypeStruct((rows, width), BF16),
            jax.ShapeDtypeStruct((rows, 1), F32),
        ],
        compiler_params=pltpu.CompilerParams(vmem_limit_bytes=VMEM_LIMIT),
    )(dp.reshape(1), hidden, cot, gain.reshape(1, width))


def restore_kernel(place_ref, in_ref, out_ref, *, extent):
    for number in range(extent):
        start = pl.multiple_of(owner_block(number, place_ref[0], extent) * LANES, LANES)
        out_ref[:, pl.ds(start, LANES)] = in_ref[:, number * LANES : (number + 1) * LANES]


def restore_order(a, dp, extent):
    rows, width = a.shape
    if width // extent != LANES:
        order = owner_block(jnp.arange(extent), dp, extent)
        back = jnp.argsort(order)
        return jnp.take(a.reshape(rows, extent, -1), back, axis=1).reshape(rows, width)
    step = 128
    tile = pl.BlockSpec((step, width), lambda i: (i, 0))
    return pl.pallas_call(
        functools.partial(restore_kernel, extent=extent),
        grid=(rows // step,),
        in_specs=[pl.BlockSpec(memory_space=pltpu.SMEM), tile],
        out_specs=tile,
        out_shape=jax.ShapeDtypeStruct((rows, width), a.dtype),
        compiler_params=pltpu.CompilerParams(vmem_limit_bytes=VMEM_LIMIT),
    )(dp.reshape(1), a)


DT, CUM, SEG, VALID, LINK, KEEP, INV, CROSS = 0, 4, 8, 9, 12, 13, 14, 15
COLS = 16
TAPS, BIAS, SKIP, GAIN = 0, 4, 5, 6


def spread(col, first):
    rows = col.shape[0]
    lane = lax.broadcasted_iota(jnp.int32, (rows, TILE), 1)
    wide = jnp.broadcast_to(col[:, first : first + 1], (rows, TILE))
    for head in range(1, GROUP):
        wide = jnp.where(
            lane < head * WIDTH,
            wide,
            jnp.broadcast_to(col[:, first + head : first + head + 1], (rows, TILE)),
        )
    return wide


def conv_of(v, col_ref, par_ref):
    result = par_ref[BIAS : BIAS + 1, :] + par_ref[TAPS + 3 : TAPS + 4, :] * v
    for offset in range(1, 4):
        valid = col_ref[:, VALID + offset - 1 : VALID + offset]
        result = result + par_ref[TAPS + 3 - offset : TAPS + 4 - offset, :] * (
            pltpu.roll(v, offset, 0) * valid
        )
    return result


def pair_mask(seg_col, seg_row, transposed):
    down = lax.broadcasted_iota(jnp.int32, (BLOCK, BLOCK), 0)
    across = lax.broadcasted_iota(jnp.int32, (BLOCK, BLOCK), 1)
    causal = down <= across if transposed else down >= across
    return causal & (seg_col == seg_row)


def forward_kernel(z_ref, dyn_ref, bc_ref, col_ref, row_ref, par_ref, y_ref, state_ref, sum_ref, xs_ref, carry_ref):
    blocks = xs_ref.shape[0] // BLOCK
    conv = conv_of(z_ref[:, TILE:], col_ref, par_ref)
    xs_ref[...] = conv * sigmoid(conv)
    carry_ref[...] = jnp.zeros_like(carry_ref)

    def one_block(number, carried):
        rows = pl.ds(pl.multiple_of(number * BLOCK, BLOCK), BLOCK)
        b_rows, c_rows = bc_ref[rows, :LANES], bc_ref[rows, LANES:]
        col = col_ref[rows, :]
        scores = dot(c_rows, b_rows, NT, HIGH)
        mask = pair_mask(col[:, SEG : SEG + 1], row_ref[GROUP : GROUP + 1, rows], False)
        scores = jnp.where(mask, scores, 0.0)
        x = xs_ref[rows, :]
        cum_wide = spread(col, CUM)
        dtx = x * spread(col, DT)
        dtx_low = dtx.astype(BF16)
        parts = []
        for head in range(GROUP):
            gap = col[:, CUM + head : CUM + head + 1] - row_ref[head : head + 1, rows]
            mixing = scores * jnp.exp(jnp.minimum(gap, 0.0))
            parts.append(dot(mixing.astype(BF16), dtx_low[:, head * WIDTH : (head + 1) * WIDTH]))
        within = jnp.concatenate(parts, axis=1)
        state = carry_ref[...]
        state_ref[number] = state
        decay = jnp.exp(cum_wide) * col[:, LINK : LINK + 1]
        y = within + low_dot(c_rows, state) * decay + par_ref[SKIP : SKIP + 1, :] * x
        weight = jnp.exp(cum_wide[BLOCK - 1 :, :] - cum_wide) * col[:, KEEP : KEEP + 1]
        carry_ref[...] = state * decay[BLOCK - 1 :, :] + low_dot(b_rows, dtx * weight, TN)
        y_ref[rows, :] = y
        z = z_ref[rows, :TILE]
        yg = y * z * sigmoid(z)
        first = jnp.sum(yg * yg, axis=1, keepdims=True)
        second = jnp.sum(yg * par_ref[GAIN : GAIN + 1, :] * dyn_ref[rows, :], axis=1, keepdims=True)
        lane = lax.broadcasted_iota(jnp.int32, (BLOCK, 8), 1)
        sum_ref[rows, :] = jnp.where(lane == 0, first, jnp.where(lane == 1, second, 0.0))
        return carried

    lax.fori_loop(0, blocks, one_block, 0)


def backward_kernel(
    z_ref, y_ref, dyn_ref, bc_ref, col_ref, row_ref, par_ref, state_ref, dbc_in_ref,
    dzx_ref, yn_ref, dbc_ref, steps_ref, small_ref, xs_ref, dconv_ref, carry_ref,
):
    blocks = xs_ref.shape[0] // BLOCK
    conv = conv_of(z_ref[:, TILE:], col_ref, par_ref)
    gate = sigmoid(conv)
    xs_ref[...] = conv * gate
    dconv_ref[...] = gate * (1.0 + conv * (1.0 - gate))
    carry_ref[...] = jnp.zeros_like(carry_ref)
    small_ref[...] = jnp.zeros_like(small_ref)
    down = lax.broadcasted_iota(jnp.int32, (BLOCK, BLOCK), 0)
    across = lax.broadcasted_iota(jnp.int32, (BLOCK, BLOCK), 1)

    def one_block(step, carried):
        number = blocks - 1 - step
        rows = pl.ds(pl.multiple_of(number * BLOCK, BLOCK), BLOCK)
        col = col_ref[rows, :]
        z, y, dyn = z_ref[rows, :TILE], y_ref[rows, :], dyn_ref[rows, :]
        gain = par_ref[GAIN : GAIN + 1, :]
        inv, cross = col[:, INV : INV + 1], col[:, CROSS : CROSS + 1]
        gate = sigmoid(z)
        silu = z * gate
        yg = y * silu
        yg_inv = yg * inv
        d_yg = inv * gain * dyn - yg * cross
        dzx_ref[rows, :TILE] = (d_yg * y * (gate * (1.0 + z * (1.0 - gate)))).astype(BF16)
        yn_ref[rows, :] = (yg_inv * gain).astype(BF16)
        small_ref[GAIN : GAIN + 1, :] += jnp.sum(dyn * yg_inv, axis=0, keepdims=True)
        e = d_yg * silu
        b_rows, c_rows = bc_ref[rows, :LANES], bc_ref[rows, LANES:]
        b_low, c_low = b_rows.astype(BF16), c_rows.astype(BF16)
        scores = dot(b_rows, c_rows, NT, HIGH)
        mask = pair_mask(col[:, SEG : SEG + 1], row_ref[GROUP : GROUP + 1, rows], True)
        scores = jnp.where(mask, scores, 0.0)
        x = xs_ref[rows, :]
        dt_wide, cum_wide = spread(col, DT), spread(col, CUM)
        dtx = x * dt_wide
        dtx_low, e_low = dtx.astype(BF16), e.astype(BF16)
        reach = (down >= across).astype(BF16)
        d_scores = jnp.zeros((BLOCK, BLOCK), F32)
        parts, between = [], []
        for head in range(GROUP):
            lanes = slice(head * WIDTH, (head + 1) * WIDTH)
            gap = row_ref[head : head + 1, rows] - col[:, CUM + head : CUM + head + 1]
            decay = jnp.exp(jnp.minimum(gap, 0.0))
            mixing = scores * decay
            parts.append(dot(mixing.astype(BF16), e_low[:, lanes]))
            d_mixing = dot(dtx_low[:, lanes], e_low[:, lanes], NT)
            d_scores = d_scores + d_mixing * decay
            later = dot((d_mixing * mixing).astype(BF16), reach)
            between.append(jnp.sum(jnp.where(down < across, later, 0.0), axis=0, keepdims=True))
        d_dtx = jnp.concatenate(parts, axis=1)
        d_scores = jnp.where(mask, d_scores, 0.0).astype(BF16)
        d_b = dot(d_scores, c_low)
        d_c = dot(d_scores, b_low, TN)
        state, d_state = state_ref[number], carry_ref[...]
        state_low, d_state_low = state.astype(BF16), d_state.astype(BF16)
        decay = jnp.exp(cum_wide) * col[:, LINK : LINK + 1]
        e_in = e * decay
        e_in_low = e_in.astype(BF16)
        from_state = e_in * dot(c_low, state_low)
        d_c = d_c + dot(e_in_low, state_low, NT)
        carry_ref[...] = decay[BLOCK - 1 :, :] * d_state + dot(c_low, e_in_low, TN)
        weight = jnp.exp(cum_wide[BLOCK - 1 :, :] - cum_wide) * col[:, KEEP : KEEP + 1]
        d_tail = weight * dot(b_low, d_state_low)
        to_state = d_tail * dtx
        d_b = d_b + low_dot(weight * dtx, d_state_low, NT)
        d_dtx = d_dtx + d_tail
        through = decay[BLOCK - 1 :, :] * jnp.sum(state * d_state, axis=0, keepdims=True)
        d_x = dt_wide * d_dtx + par_ref[SKIP : SKIP + 1, :] * e
        small_ref[SKIP : SKIP + 1, :] += jnp.sum(x * e, axis=0, keepdims=True)
        dconv_ref[rows, :] = dconv_ref[rows, :] * d_x
        dbc_ref[rows, :LANES] = dbc_in_ref[rows, :LANES] + d_b
        dbc_ref[rows, LANES:] = dbc_in_ref[rows, LANES:] + d_c
        owner = lax.broadcasted_iota(jnp.int32, (8, TILE), 1) // WIDTH
        pick = (owner == lax.broadcasted_iota(jnp.int32, (8, TILE), 0)).astype(F32)
        q_rows = dot(pick, from_state, NT, HIGH)
        p_rows = dot(pick, to_state, NT, HIGH)
        dt_rows = dot(pick, d_dtx * x, NT, HIGH)
        const = dot(pick, jnp.broadcast_to(through, (8, TILE)), NT, HIGH)[:, :1]
        run = (
            dot(q_rows, (down >= across).astype(F32), NN, HIGH)
            + dot(p_rows, (down < across).astype(F32), NN, HIGH)
            + const
        )
        steps_ref[:GROUP, rows] = run[:GROUP] + jnp.concatenate(between, axis=0)
        steps_ref[GROUP:, rows] = dt_rows[:GROUP]
        return carried

    lax.fori_loop(0, blocks, one_block, 0)
    v, d_conv = z_ref[:, TILE:], dconv_ref[...]
    length = v.shape[0]
    d_v = par_ref[TAPS + 3 : TAPS + 4, :] * d_conv
    small_ref[TAPS + 3 : TAPS + 4, :] = jnp.sum(d_conv * v, axis=0, keepdims=True)
    small_ref[BIAS : BIAS + 1, :] = jnp.sum(d_conv, axis=0, keepdims=True)
    for offset in range(1, 4):
        place = TAPS + 3 - offset
        counted = d_conv * col_ref[:, VALID + offset - 1 : VALID + offset]
        small_ref[place : place + 1, :] = jnp.sum(
            counted * pltpu.roll(v, offset, 0), axis=0, keepdims=True
        )
        d_v = d_v + par_ref[place : place + 1, :] * pltpu.roll(counted, length - offset, 0)
    dzx_ref[:, TILE:] = d_v.astype(BF16)


def by_sequence(rows, width):
    return pl.BlockSpec((rows, width), lambda i: (i, 0))


def whole(shape):
    return pl.BlockSpec(shape, lambda i: (0,) * len(shape))


def run_forward(zv, dyn, bc, col, row, par, length):
    tokens = zv.shape[0]
    number, blocks = tokens // length, length // BLOCK
    return pl.pallas_call(
        forward_kernel,
        grid=(number,),
        in_specs=[
            by_sequence(length, 2 * TILE),
            by_sequence(length, TILE),
            by_sequence(length, 2 * LANES),
            by_sequence(length, COLS),
            pl.BlockSpec((8, length), lambda i: (0, i)),
            whole((8, TILE)),
        ],
        out_specs=[
            by_sequence(length, TILE),
            pl.BlockSpec((blocks, LANES, TILE), lambda i: (i, 0, 0)),
            by_sequence(length, 8),
        ],
        out_shape=[
            jax.ShapeDtypeStruct((tokens, TILE), F32),
            jax.ShapeDtypeStruct((number * blocks, LANES, TILE), F32),
            jax.ShapeDtypeStruct((tokens, 8), F32),
        ],
        scratch_shapes=[pltpu.VMEM((length, TILE), F32), pltpu.VMEM((LANES, TILE), F32)],
        compiler_params=pltpu.CompilerParams(vmem_limit_bytes=VMEM_LIMIT),
        cost_estimate=pl.CostEstimate(flops=10**10, bytes_accessed=10**7, transcendentals=10**7),
    )(zv, dyn, bc, col, row, par)


def run_backward(zv, y, dyn, bc, col, row, par, state, dbc, length):
    tokens = zv.shape[0]
    number, blocks = tokens // length, length // BLOCK
    return pl.pallas_call(
        backward_kernel,
        grid=(number,),
        in_specs=[
            by_sequence(length, 2 * TILE),
            by_sequence(length, TILE),
            by_sequence(length, TILE),
            by_sequence(length, 2 * LANES),
            by_sequence(length, COLS),
            pl.BlockSpec((8, length), lambda i: (0, i)),
            whole((8, TILE)),
            pl.BlockSpec((blocks, LANES, TILE), lambda i: (i, 0, 0)),
            by_sequence(length, 2 * LANES),
        ],
        out_specs=[
            by_sequence(length, 2 * TILE),
            by_sequence(length, TILE),
            by_sequence(length, 2 * LANES),
            pl.BlockSpec((8, length), lambda i: (0, i)),
            pl.BlockSpec((8, TILE), lambda i: (i, 0)),
        ],
        out_shape=[
            jax.ShapeDtypeStruct((tokens, 2 * TILE), BF16),
            jax.ShapeDtypeStruct((tokens, TILE), BF16),
            jax.ShapeDtypeStruct((tokens, 2 * LANES), F32),
            jax.ShapeDtypeStruct((8, tokens), F32),
            jax.ShapeDtypeStruct((8 * number, TILE), F32),
        ],
        scratch_shapes=[
            pltpu.VMEM((length, TILE), F32),
            pltpu.VMEM((length, TILE), F32),
            pltpu.VMEM((LANES, TILE), F32),
        ],
        compiler_params=pltpu.CompilerParams(vmem_limit_bytes=VMEM_LIMIT),
        cost_estimate=pl.CostEstimate(flops=2 * 10**10, bytes_accessed=10**7, transcendentals=10**7),
    )(zv, y, dyn, bc, col, row, par, state, dbc)


def segment_conv(inputs, taps, bias, masks):
    reach = taps.shape[0]
    result = bias[None, :] + taps[reach - 1][None, :] * inputs
    for offset in range(1, reach):
        moved = jnp.concatenate(
            [jnp.zeros((offset, inputs.shape[1]), inputs.dtype), inputs[:-offset]], axis=0
        )
        result = result + taps[reach - 1 - offset][None, :] * (
            moved * masks[:, offset - 1 : offset]
        )
    return result


def sequence_masks(ids):
    masks = []
    for offset in range(1, 4):
        earlier = jnp.concatenate([jnp.full((offset,), -2, jnp.int32), ids[:-offset]])
        masks.append(earlier == ids)
    blocks = ids.reshape(-1, BLOCK)
    last = blocks[:, -1]
    before = jnp.concatenate([jnp.full((1,), -2, jnp.int32), last[:-1]])
    masks.append((blocks == before[:, None]).reshape(-1))
    masks.append((blocks == last[:, None]).reshape(-1))
    return jnp.stack(masks, axis=1).astype(F32)


def local(
    hidden_in,
    segments,
    norm_gain,
    w_zx,
    w_dt,
    w_bc,
    conv_x,
    conv_x_bias,
    conv_bc,
    conv_bc_bias,
    dt_bias,
    a_log,
    d_skip,
    gated_gain,
    w_out,
    cotangent,
):
    dp, mp = lax.axis_index("dp"), lax.axis_index("mp")
    extent = lax.axis_size("dp")
    far = extent // 4
    x_side = lax.rem(dp, 2)
    rows, width = hidden_in.shape
    length = segments.shape[0]
    inner = conv_x.shape[1]
    inner_total = inner * lax.axis_size("mp")
    heads = dt_bias.shape[0]
    quarter, own_heads = inner // 2, heads // 2
    tiles = quarter // TILE
    depth = w_zx.shape[0]

    def by_side(own, other, axis):
        return jnp.where(
            x_side == 0,
            jnp.concatenate([own, other], axis=axis),
            jnp.concatenate([other, own], axis=axis),
        )

    def by_core(own, other, axis):
        return jnp.where(
            mp == 0,
            jnp.concatenate([own, other], axis=axis),
            jnp.concatenate([other, own], axis=axis),
        )

    def of_side(a, side, axis):
        size = a.shape[axis] // 2
        return lax.dynamic_slice_in_dim(a, side * size, size, axis)

    packed = jnp.concatenate([w_zx[:, 0], w_zx[:, 1], w_out.T], axis=1)
    packed = packed.reshape(depth, 3, 2, tiles, TILE).transpose(2, 3, 0, 1, 4)
    packed = packed.reshape(2, tiles, depth, 3 * TILE)
    small_weights = jnp.concatenate([w_bc, w_dt], axis=1)
    small_other = flip(small_weights, "dp", 1)
    packed_own = lax.dynamic_index_in_dim(packed, x_side, 0, False)
    packed_other = flip(lax.dynamic_index_in_dim(packed, 1 - x_side, 0, False), "dp", 1)

    def gathered(piece):
        near = [piece] + [flip(piece, "dp", 4 * k) for k in range(1, far)]
        return near + [flip(p, "dp", 2) for p in near]

    bc_weight = jnp.concatenate(gathered(by_side(small_weights, small_other, 0)), axis=0)

    normed, cot, inverse_rows = input_norm(hidden_in, cotangent, norm_gain, dp, extent)

    def both_sequences(a):
        near = flip(a, "dp", 1)
        return by_core(a, flip(a, "mp", 1), 0), by_core(near, flip(near, "mp", 1), 0)

    normed_own, normed_near = both_sequences(normed)
    normed_all = jnp.concatenate([normed_own, normed_near], axis=0)
    weights = []
    for tile in range(tiles):
        piece = by_side(packed_own[tile], packed_other[tile], 0)
        weights.append(jnp.concatenate(gathered(piece), axis=0))
    cot_all = jnp.concatenate(both_sequences(cot), axis=0)
    ids = (segments, flip(segments, "dp", 1))

    proj_small = dot(normed_all, bc_weight)
    proj_bc = proj_small[:, : 2 * LANES]
    proj_dt = of_side(proj_small[:, 2 * LANES :], x_side, 1)
    masks = [sequence_masks(one) for one in ids]

    def state_part(values, taps, bias, mask):
        return jax.nn.silu(segment_conv(values, taps, bias, mask))

    bc_own, state_back = jax.vjp(
        lambda values, taps, bias: state_part(values, taps, bias, masks[0]),
        proj_bc[:length],
        conv_bc,
        conv_bc_bias,
    )
    bc_near = state_part(proj_bc[length:], conv_bc, conv_bc_bias, masks[1])
    bc = jnp.concatenate([bc_own, bc_near], axis=0)
    side_bias = of_side(dt_bias, x_side, 0)
    rate = -jnp.exp(of_side(a_log, x_side, 0))
    raw_dt = proj_dt + side_bias
    dt = jax.nn.softplus(raw_dt)
    tokens = dt.shape[0]
    lower = (jnp.arange(BLOCK)[:, None] >= jnp.arange(BLOCK)[None, :]).astype(F32)
    cum = jnp.einsum(
        "ts,csh->cth", lower, (dt * rate).reshape(-1, BLOCK, own_heads), precision=HIGH
    ).reshape(tokens, own_heads)
    mask_all = jnp.concatenate(masks, axis=0)
    ids_all = jnp.concatenate(ids, axis=0).astype(F32)
    cum_rows = cum.T

    def tile_of(a, tile):
        return of_side(a, x_side, a.ndim - 1)[..., tile * TILE : (tile + 1) * TILE]

    skip_wide = jnp.repeat(d_skip, WIDTH)
    params, cols, row_sets = [], [], []
    for tile in range(tiles):
        params.append(
            jnp.concatenate(
                [
                    tile_of(conv_x, tile),
                    tile_of(conv_x_bias, tile)[None],
                    tile_of(skip_wide, tile)[None],
                    tile_of(gated_gain, tile)[None],
                    jnp.zeros((1, TILE), F32),
                ],
                axis=0,
            )
        )
        own = slice(tile * GROUP, (tile + 1) * GROUP)
        cols.append(
            jnp.concatenate([dt[:, own], cum[:, own], ids_all[:, None], mask_all], axis=1)
        )
        row_sets.append(
            jnp.concatenate(
                [cum_rows[own], ids_all[None], jnp.zeros((3, tokens), F32)], axis=0
            )
        )

    zvs, dyns, ys, states, sums = [], [], [], [], 0.0
    for tile in range(tiles):
        dyns.append(dot(cot_all, weights[tile][:, 2 * TILE :]))
        zvs.append(dot(normed_all, weights[tile][:, : 2 * TILE]))
        y, state, part = run_forward(
            zvs[tile],
            dyns[tile],
            bc,
            jnp.pad(cols[tile], ((0, 0), (0, 2))),
            row_sets[tile],
            params[tile],
            length,
        )
        ys.append(y)
        states.append(state)
        sums = sums + part[:, :2]
    sums = sums + flip(sums, "mp", 1)
    near = flip(sums, "dp", 1)
    sums = sums + jnp.concatenate([near[length:], near[:length]], axis=0)
    inverse_gated = lax.rsqrt(sums[:, :1] / inner_total + EPSILON)
    cross = inverse_gated * inverse_gated * inverse_gated / inner_total * sums[:, 1:2]

    dzxs, yns, mine, theirs, d_steps, smalls = [], [], [], [], [], []
    dbc = jnp.zeros((tokens, 2 * LANES), F32)
    half = width // 2
    for tile in range(tiles):
        dzx, yn, dbc, steps, small = run_backward(
            zvs[tile],
            ys[tile],
            dyns[tile],
            bc,
            jnp.concatenate([cols[tile], inverse_gated, cross], axis=1),
            row_sets[tile],
            params[tile],
            states[tile],
            dbc,
            length,
        )
        dzxs.append(dzx)
        yns.append(yn)
        d_steps.append(steps)
        smalls.append(small[:8] + small[8:])

        def share(start):
            part = slice(start, start + half)
            return jnp.concatenate(
                [dot(normed_all[:, part], dzx, TN), dot(cot_all[:, part], yn, TN)], axis=1
            )

        sent = flip(share(half).astype(BF16), "dp", 2)
        total = (share(0) + sent.astype(F32)).reshape(far, 2 * depth, 3 * TILE)
        out = total.astype(BF16)
        total = total[0]
        for k in range(1, far):
            total = total + flip(out[k], "dp", 4 * k).astype(F32)
        mine.append(of_side(total, x_side, 0))
        theirs.append(flip(of_side(total, 1 - x_side, 0).astype(BF16), "dp", 1).astype(F32))

    def assembled(parts):
        stacked = jnp.stack([p.reshape(depth, 3, TILE) for p in parts], axis=2)
        return stacked.reshape(depth, 3, quarter)

    full = by_side(assembled(mine), assembled(theirs), 2)
    grad_zx_weight = full[:, :2]
    grad_out_weight = full[:, 2].T

    dbc = dbc + flip(dbc, "mp", 1)
    dbc = dbc[:length] + flip(dbc[length:], "dp", 1)
    d_bc, grad_conv_bc, grad_conv_bc_bias = state_back(dbc)
    bc_grad = d_bc.astype(BF16)

    steps = jnp.concatenate([s[:GROUP] for s in d_steps], axis=0).T
    direct = jnp.concatenate([s[GROUP:] for s in d_steps], axis=0).T
    d_dt = (direct + rate * steps) * jax.nn.sigmoid(raw_dt)
    grad_dt_bias = jnp.sum(d_dt, axis=0)
    grad_a_log = jnp.sum(steps * dt, axis=0) * rate
    dt_grad = d_dt.astype(BF16)

    def placed(a):
        zero = jnp.zeros_like(a)
        return by_side(a, zero, a.ndim - 1)

    small_grad = jnp.concatenate(
        [
            dot(normed_own, lax.dynamic_slice_in_dim(bc_grad, mp * LANES, LANES, 1), TN),
            placed(dot(normed_all, dt_grad, TN)),
        ],
        axis=1,
    )
    small_grad = small_grad.reshape(2 * far, 2, depth, -1)
    small_grad = of_side(small_grad, x_side, 1) + flip(
        of_side(small_grad, 1 - x_side, 1).astype(BF16), "dp", 1
    ).astype(F32)
    small_grad = small_grad.reshape(2, far, depth, -1)
    small_grad = small_grad[0] + flip(small_grad[1].astype(BF16), "dp", 2).astype(F32)
    out = small_grad.astype(BF16)
    small_grad = small_grad[0]
    for k in range(1, far):
        small_grad = small_grad + flip(out[k], "dp", 4 * k).astype(F32)
    grad_dt_weight = small_grad[:, LANES:]
    own_bc = small_grad[:, :LANES]
    grad_bc_weight = by_core(own_bc, flip(own_bc, "mp", 1), 1)

    def token_sum(products):
        def part(core):
            return products(lambda a: of_side(a.reshape(2, 2, rows, -1), core, 1).reshape(2 * rows, -1))

        total = part(mp) + flip(part(1 - mp).astype(BF16), "mp", 1).astype(F32)
        return total[:rows] + flip(total[rows:].astype(BF16), "dp", 1).astype(F32)

    out_all = jnp.concatenate([w[:, 2 * TILE :] for w in weights], axis=1)
    yn_all = jnp.concatenate(yns, axis=1)
    mixer_out = restore_order(token_sum(lambda pick: dot(pick(yn_all), out_all, NT)), dp, extent)
    inputs = hidden_in.astype(F32)
    residual_out = (inputs + mixer_out).astype(BF16)
    usable = (lax.dynamic_slice_in_dim(segments, mp * rows, rows, 0) >= 0).astype(F32)[:, None]
    totals = jnp.stack(
        [
            jnp.sum(usable * inputs * inputs),
            jnp.sum(usable * mixer_out * mixer_out),
            jnp.sum(usable),
        ]
    )

    zv_all = jnp.concatenate([w[:, : 2 * TILE] for w in weights], axis=1)
    dt_weight = of_side(bc_weight[:, 2 * LANES :], x_side, 1)
    dzx_all = jnp.concatenate(dzxs, axis=1)
    d_normed = token_sum(
        lambda pick: dot(pick(dzx_all), zv_all, NT) + dot(pick(dt_grad), dt_weight, NT)
    )
    d_normed = d_normed + dot(
        lax.dynamic_slice_in_dim(bc_grad, mp * rows, rows, 0), bc_weight[:, : 2 * LANES], NT
    )
    d_normed = restore_order(d_normed, dp, extent)
    grad_norm_gain = jnp.sum(d_normed * inputs * inverse_rows, axis=0)
    inverse_cube_rows = inverse_rows * inverse_rows * inverse_rows
    input_grad = (
        cotangent.astype(F32)
        + inverse_rows * norm_gain * d_normed
        - inputs
        * inverse_cube_rows
        * jnp.mean(inputs * norm_gain * d_normed, axis=-1, keepdims=True)
    )

    def summed(a, axes):
        for axis in axes:
            bit = 1
            while bit < lax.axis_size(axis):
                a = a + flip(a, axis, bit)
                bit *= 2
        return a

    small = jnp.concatenate(smalls, axis=1)
    channel = placed(small[: GAIN + 1])
    skip_grad = jnp.sum(channel[SKIP].reshape(heads, WIDTH), axis=1)
    pieces = [
        channel[TAPS:BIAS],
        channel[BIAS],
        grad_conv_bc,
        grad_conv_bc_bias,
        placed(grad_dt_bias),
        placed(grad_a_log),
        skip_grad,
        channel[GAIN],
    ]
    flat = summed(jnp.concatenate([p.reshape(-1) for p in pieces]), ("dp",))
    small_sums, start = [], 0
    for piece in pieces:
        small_sums.append(flat[start : start + piece.size].reshape(piece.shape))
        start += piece.size
    last = summed(jnp.concatenate([grad_norm_gain, totals]), ("mp", "dp"))
    grad_norm_gain = last[:width]
    sum_inputs, sum_mixer, usable_count = last[width], last[width + 1], last[width + 2]
    rms_residual = jnp.sqrt(sum_inputs / (usable_count * width))
    rms_mixer = jnp.sqrt(sum_mixer / (usable_count * width))
    return (
        residual_out,
        input_grad,
        grad_norm_gain,
        grad_zx_weight,
        grad_dt_weight,
        grad_bc_weight,
        small_sums[0],
        small_sums[1],
        small_sums[2],
        small_sums[3],
        small_sums[4],
        small_sums[5],
        small_sums[6],
        small_sums[7],
        grad_out_weight,
        rms_residual,
        rms_mixer,
    )


def solution(mesh):
    in_specs = (
        P(("dp", "mp"), None),
        P("dp"),
        P(),
        P("dp", None, "mp"),
        P("dp", "mp"),
        P("dp", None),
        P(None, "mp"),
        P("mp"),
        P(),
        P(),
        P("mp"),
        P("mp"),
        P("mp"),
        P("mp"),
        P("mp", "dp"),
        P(("dp", "mp"), None),
    )
    out_specs = (
        P(("dp", "mp"), None),
        P(("dp", "mp"), None),
        P(),
        P("dp", None, "mp"),
        P("dp", "mp"),
        P("dp", None),
        P(None, "mp"),
        P("mp"),
        P(),
        P(),
        P("mp"),
        P("mp"),
        P("mp"),
        P("mp"),
        P("mp", "dp"),
        P(),
        P(),
    )
    return jax.shard_map(local, mesh=mesh, in_specs=in_specs, out_specs=out_specs, check_vma=False)
```

```python
import functools

import jax
import jax.numpy as jnp
from jax import lax
from jax.experimental import pallas as pl
from jax.experimental.pallas import tpu as pltpu
from jax.sharding import PartitionSpec as P

BLOCK = 256
LANES = 128
TILE = 256
WIDTH = 64
GROUP = TILE // WIDTH
EPSILON = 1e-05
HIGH = lax.Precision.HIGHEST
BF16 = jnp.bfloat16
F32 = jnp.float32
VMEM_LIMIT = 58 * 2**20

NN = (((1,), (0,)), ((), ()))
NT = (((1,), (1,)), ((), ()))
TN = (((0,), (0,)), ((), ()))


def dot(a, b, dims=NN, precision=None):
    return lax.dot_general(a, b, dims, precision=precision, preferred_element_type=F32)


def low_dot(a, b, dims=NN):
    return dot(a.astype(BF16), b.astype(BF16), dims)


def flip(a, axis, bit):
    size = lax.axis_size(axis)
    return lax.ppermute(a, axis, [(i, i ^ bit) for i in range(size)])


def sigmoid(q):
    return 1.0 / (1.0 + jnp.exp(-q))


def owner_block(number, dp, extent):
    y, z, x = number // (extent // 2), (number // 2) % (extent // 4), number % 2
    return jnp.bitwise_xor(dp - lax.rem(dp, 2), (y * 2) + (z * 4) + x)


def norm_kernel(place_ref, hidden_ref, cot_ref, gain_ref, normed_ref, cot_out_ref, inv_ref, *, extent):
    u = hidden_ref[...].astype(F32)
    inv = lax.rsqrt(jnp.mean(u * u, axis=-1, keepdims=True) + EPSILON)
    inv_ref[...] = inv
    for number in range(extent):
        start = pl.multiple_of(owner_block(number, place_ref[0], extent) * LANES, LANES)
        piece = hidden_ref[:, pl.ds(start, LANES)].astype(F32)
        gain = gain_ref[:, pl.ds(start, LANES)]
        normed_ref[:, number * LANES : (number + 1) * LANES] = (piece * inv * gain).astype(BF16)
        cot_out_ref[:, number * LANES : (number + 1) * LANES] = cot_ref[:, pl.ds(start, LANES)]


def input_norm(hidden, cot, gain, dp, extent):
    rows, width = hidden.shape
    if width // extent != LANES:
        u = hidden.astype(F32)
        inv = lax.rsqrt(jnp.mean(u * u, axis=-1, keepdims=True) + EPSILON)
        normed = (u * inv * gain).astype(BF16)
        order = owner_block(jnp.arange(extent), dp, extent)

        def arranged(a):
            return jnp.take(a.reshape(rows, extent, -1), order, axis=1).reshape(rows, width)

        return arranged(normed), arranged(cot), inv
    step = 128
    tile = pl.BlockSpec((step, width), lambda i: (i, 0))
    return pl.pallas_call(
        functools.partial(norm_kernel, extent=extent),
        grid=(rows // step,),
        in_specs=[
            pl.BlockSpec(memory_space=pltpu.SMEM),
            tile,
            tile,
            pl.BlockSpec((1, width), lambda i: (0, 0)),
        ],
        out_specs=[tile, tile, pl.BlockSpec((step, 1), lambda i: (i, 0))],
        out_shape=[
            jax.ShapeDtypeStruct((rows, width), BF16),
            jax.ShapeDtypeStruct((rows, width), BF16),
            jax.ShapeDtypeStruct((rows, 1), F32),
        ],
        compiler_params=pltpu.CompilerParams(vmem_limit_bytes=VMEM_LIMIT),
    )(dp.reshape(1), hidden, cot, gain.reshape(1, width))


def restore_kernel(place_ref, in_ref, out_ref, *, extent):
    for number in range(extent):
        start = pl.multiple_of(owner_block(number, place_ref[0], extent) * LANES, LANES)
        out_ref[:, pl.ds(start, LANES)] = in_ref[:, number * LANES : (number + 1) * LANES]


def restore_order(a, dp, extent):
    rows, width = a.shape
    if width // extent != LANES:
        order = owner_block(jnp.arange(extent), dp, extent)
        back = jnp.argsort(order)
        return jnp.take(a.reshape(rows, extent, -1), back, axis=1).reshape(rows, width)
    step = 128
    tile = pl.BlockSpec((step, width), lambda i: (i, 0))
    return pl.pallas_call(
        functools.partial(restore_kernel, extent=extent),
        grid=(rows // step,),
        in_specs=[pl.BlockSpec(memory_space=pltpu.SMEM), tile],
        out_specs=tile,
        out_shape=jax.ShapeDtypeStruct((rows, width), a.dtype),
        compiler_params=pltpu.CompilerParams(vmem_limit_bytes=VMEM_LIMIT),
    )(dp.reshape(1), a)


VALID, LINK, KEEP, SEG = 0, 3, 4, 5
COLS = 8
HEADS = 16
TAPS, BIAS, SKIP, GAIN = 0, 4, 5, 6
ANY = pl.BlockSpec(memory_space=pl.ANY)


def iota(shape, axis):
    return lax.broadcasted_iota(jnp.int32, shape, axis)


def thirds(a):
    high = a.astype(BF16)
    rest = a - high.astype(F32)
    mid = rest.astype(BF16)
    return [high, mid, (rest - mid.astype(F32)).astype(BF16)]


def halves(a):
    high = a.astype(BF16)
    return [high, (a - high.astype(F32)).astype(BF16)]


def conv_of(v, col_ref, par_ref, length):
    result = par_ref[BIAS : BIAS + 1, :] + par_ref[TAPS + 3 : TAPS + 4, :] * v
    for offset in range(1, 4):
        valid = col_ref[:, VALID + offset - 1 : VALID + offset]
        result = result + par_ref[TAPS + 3 - offset : TAPS + 4 - offset, :] * (
            pltpu.roll(v, offset, 0) * valid
        )
    return result


def pair_mask(seg_col, seg_row, transposed):
    down, across = iota((BLOCK, BLOCK), 0), iota((BLOCK, BLOCK), 1)
    causal = down <= across if transposed else down >= across
    return causal & (seg_col == seg_row)


def table_kernel(
    normed_ref, weight_ref, seg_col_ref, seg_row_ref, par_ref, head_ref,
    proj_ref, bc_ref, wide_ref, col_ref, row_ref, score_ref, turned_ref,
):
    length = seg_col_ref.shape[0]
    proj = dot(normed_ref[...], weight_ref[...])
    proj_ref[...] = proj[:, : 2 * LANES]
    raw = proj[:, 2 * LANES :] + head_ref[0:1, :HEADS]
    dt = jnp.maximum(raw, 0.0) + jnp.log1p(jnp.exp(-jnp.abs(raw)))
    step = dt * head_ref[1:2, :HEADS]
    seg = seg_col_ref[...]
    place = iota((length, 1), 0)
    number = place // BLOCK
    before, last = jnp.full((length, 1), -2.0, F32), jnp.zeros((length, 1), F32)
    for block in range(length // BLOCK):
        end = seg[(block + 1) * BLOCK - 1 : (block + 1) * BLOCK, :]
        last = jnp.where(number == block, end, last)
        before = jnp.where(number == block + 1, end, before)
    lower = (iota((BLOCK, BLOCK), 0) >= iota((BLOCK, BLOCK), 1)).astype(F32)
    upper = (iota((BLOCK, BLOCK), 0) <= iota((BLOCK, BLOCK), 1)).astype(F32)
    eye = (iota((BLOCK, BLOCK), 0) == iota((BLOCK, BLOCK), 1)).astype(F32)
    cums = []
    for block in range(length // BLOCK):
        rows = slice(block * BLOCK, (block + 1) * BLOCK)
        cums.append(dot(lower, step[rows], NN, HIGH))
        cum_rows = dot(step[rows], upper, TN, HIGH)
        raw_rows = dot(raw[rows], eye, TN, HIGH)
        for tile in range(HEADS // GROUP):
            heads = slice(tile * GROUP, (tile + 1) * GROUP)
            row_ref[tile * 8 : (tile + 1) * 8, rows] = jnp.concatenate(
                [cum_rows[heads], raw_rows[heads]], axis=0
            )
    cum = jnp.concatenate(cums, axis=0)
    lane = iota((length, COLS), 1)
    col = jnp.zeros((length, COLS), F32)
    for offset in range(1, 4):
        valid = (pltpu.roll(seg, offset, 0) == seg) & (place >= offset)
        col = jnp.where(lane == VALID + offset - 1, valid.astype(F32), col)
    col = jnp.where(lane == LINK, (seg == before).astype(F32), col)
    col = jnp.where(lane == KEEP, (seg == last).astype(F32), col)
    col_ref[...] = jnp.where(lane == SEG, seg, col)
    wide_ref[...] = jnp.concatenate(
        thirds(dt) + thirds(cum) + [jnp.zeros((length, LANES - 6 * HEADS), BF16)], axis=1
    )
    conv = conv_of(proj_ref[...], col_ref, par_ref, length)
    bc_ref[...] = conv * sigmoid(conv)
    for block in range(length // BLOCK):
        rows = slice(block * BLOCK, (block + 1) * BLOCK)
        b_rows, c_rows = bc_ref[rows, :LANES], bc_ref[rows, LANES:]
        seg_col, seg_row = seg[rows], seg_row_ref[:, rows]
        score_ref[rows, :] = jnp.where(
            pair_mask(seg_col, seg_row, False), dot(c_rows, b_rows, NT, HIGH), 0.0
        )
        turned_ref[rows, :] = jnp.where(
            pair_mask(seg_col, seg_row, True), dot(b_rows, c_rows, NT, HIGH), 0.0
        )


def forward_kernel(*refs, pieces):
    (
        normed_ref, cot_ref, bc_ref, wide_ref, pick_ref, col_ref, row_ref, score_ref, par_ref, sum_in_ref,
        w_ref, z_ref, dyn_ref, y_ref, state_ref, sum_ref, xs_ref, carry_ref,
    ) = refs[pieces:]
    length = xs_ref.shape[0]
    blocks = length // BLOCK

    @pl.when(pl.program_id(0) == 0)
    def _():
        depth = refs[0].shape[0]
        for number in range(pieces):
            w_ref[number * depth : (number + 1) * depth, :] = refs[number][...]

    def project(number, carried):
        rows = pl.ds(pl.multiple_of(number * BLOCK, BLOCK), BLOCK)
        z_ref[rows, :] = dot(normed_ref[rows, :], w_ref[:, : 2 * TILE])
        dyn_ref[rows, :] = dot(cot_ref[rows, :], w_ref[:, 2 * TILE :])
        return carried

    lax.fori_loop(0, blocks, project, 0)
    conv = conv_of(z_ref[:, TILE:], col_ref, par_ref, length)
    xs_ref[...] = conv * sigmoid(conv)
    carry_ref[...] = jnp.zeros_like(carry_ref)

    def one_block(number, carried):
        rows = pl.ds(pl.multiple_of(number * BLOCK, BLOCK), BLOCK)
        b_rows, c_rows = bc_ref[rows, :LANES], bc_ref[rows, LANES:]
        col = col_ref[rows, :]
        scores = score_ref[rows, :]
        x = xs_ref[rows, :]
        wide = dot(wide_ref[rows, :], pick_ref[...])
        dt_wide, cum_wide = wide[:, :TILE], wide[:, TILE:]
        dtx = x * dt_wide
        dtx_low = dtx.astype(BF16)
        parts = []
        for head in range(GROUP):
            gap = cum_wide[:, head * WIDTH : head * WIDTH + 1] - row_ref[head : head + 1, rows]
            mixing = scores * jnp.exp(jnp.minimum(gap, 0.0))
            parts.append(dot(mixing.astype(BF16), dtx_low[:, head * WIDTH : (head + 1) * WIDTH]))
        within = jnp.concatenate(parts, axis=1)
        state = carry_ref[...]
        state_ref[number] = state
        decay = jnp.exp(cum_wide) * col[:, LINK : LINK + 1]
        y = within + low_dot(c_rows, state) * decay + par_ref[SKIP : SKIP + 1, :] * x
        weight = jnp.exp(cum_wide[BLOCK - 1 :, :] - cum_wide) * col[:, KEEP : KEEP + 1]
        carry_ref[...] = state * decay[BLOCK - 1 :, :] + low_dot(b_rows, dtx * weight, TN)
        y_ref[rows, :] = y
        z = z_ref[rows, :TILE]
        yg = y * z * sigmoid(z)
        first = jnp.sum(yg * yg, axis=1, keepdims=True)
        second = jnp.sum(yg * par_ref[GAIN : GAIN + 1, :] * dyn_ref[rows, :], axis=1, keepdims=True)
        lane = iota((BLOCK, 8), 1)
        sum_ref[rows, :] = sum_in_ref[rows, :] + jnp.where(
            lane == 0, first, jnp.where(lane == 1, second, 0.0)
        )
        return carried

    lax.fori_loop(0, blocks, one_block, 0)


def backward_tile(
    origin, z_ref, y_ref, dyn_ref, bc_ref, wide_ref, pick_ref, col_ref, row_ref, seg_ref, turned_ref, norm_ref,
    par_ref, state_ref, grad_ref, dbc_ref, step_row_ref, step_col_ref, small_ref, turn_ref, xs_ref, dconv_ref,
    carry_ref,
):
    length = xs_ref.shape[0]
    blocks = length // BLOCK
    conv = conv_of(z_ref[:, TILE:], col_ref, par_ref, length)
    gate = sigmoid(conv)
    xs_ref[...] = conv * gate
    dconv_ref[...] = gate * (1.0 + conv * (1.0 - gate))
    carry_ref[...] = jnp.zeros_like(carry_ref)
    small_ref[...] = jnp.zeros_like(small_ref)
    down, across = iota((BLOCK, BLOCK), 0), iota((BLOCK, BLOCK), 1)

    def one_block(step, carried):
        number = blocks - 1 - step
        rows = pl.ds(pl.multiple_of(number * BLOCK, BLOCK), BLOCK)
        col = col_ref[rows, :]
        z, y, dyn = z_ref[rows, :TILE], y_ref[rows, :], dyn_ref[rows, :]
        gain = par_ref[GAIN : GAIN + 1, :]
        inv, cross = norm_ref[rows, 0:1], norm_ref[rows, 1:2]
        gate = sigmoid(z)
        silu = z * gate
        yg = y * silu
        yg_inv = yg * inv
        d_yg = inv * gain * dyn - yg * cross
        grad_ref[rows, :TILE] = (d_yg * y * (gate * (1.0 + z * (1.0 - gate)))).astype(BF16)
        grad_ref[rows, 2 * TILE :] = (yg_inv * gain).astype(BF16)
        small_ref[GAIN : GAIN + 1, :] += jnp.sum(dyn * yg_inv, axis=0, keepdims=True)
        e = d_yg * silu
        b_rows, c_rows = bc_ref[rows, :LANES], bc_ref[rows, LANES:]
        b_low, c_low = b_rows.astype(BF16), c_rows.astype(BF16)
        scores = turned_ref[rows, :]
        x = xs_ref[rows, :]
        wide = dot(wide_ref[rows, :], pick_ref[...])
        dt_wide, cum_wide = wide[:, :TILE], wide[:, TILE:]
        dtx = x * dt_wide
        dtx_low, e_low = dtx.astype(BF16), e.astype(BF16)
        reach = (down >= across).astype(BF16)
        d_scores = jnp.zeros((BLOCK, BLOCK), F32)
        parts, between = [], []
        for head in range(GROUP):
            lanes = slice(head * WIDTH, (head + 1) * WIDTH)
            gap = row_ref[head : head + 1, rows] - cum_wide[:, head * WIDTH : head * WIDTH + 1]
            decay = jnp.exp(jnp.minimum(gap, 0.0))
            mixing = scores * decay
            parts.append(dot(mixing.astype(BF16), e_low[:, lanes]))
            d_mixing = dot(dtx_low[:, lanes], e_low[:, lanes], NT)
            d_scores = d_scores + d_mixing * decay
            later = dot((d_mixing * mixing).astype(BF16), reach)
            between.append(jnp.sum(jnp.where(down < across, later, 0.0), axis=0, keepdims=True))
        d_dtx = jnp.concatenate(parts, axis=1)
        mask = pair_mask(col[:, SEG : SEG + 1], seg_ref[:, rows], True)
        d_scores = jnp.where(mask, d_scores, 0.0).astype(BF16)
        d_b = dot(d_scores, c_low)
        d_c = dot(d_scores, b_low, TN)
        state, d_state = state_ref[number], carry_ref[...]
        state_low, d_state_low = state.astype(BF16), d_state.astype(BF16)
        decay = jnp.exp(cum_wide) * col[:, LINK : LINK + 1]
        e_in = e * decay
        e_in_low = e_in.astype(BF16)
        from_state = e_in * dot(c_low, state_low)
        d_c = d_c + dot(e_in_low, state_low, NT)
        carry_ref[...] = decay[BLOCK - 1 :, :] * d_state + dot(c_low, e_in_low, TN)
        weight = jnp.exp(cum_wide[BLOCK - 1 :, :] - cum_wide) * col[:, KEEP : KEEP + 1]
        d_tail = weight * dot(b_low, d_state_low)
        to_state = d_tail * dtx
        d_b = d_b + low_dot(weight * dtx, d_state_low, NT)
        d_dtx = d_dtx + d_tail
        through = decay[BLOCK - 1 :, :] * jnp.sum(state * d_state, axis=0, keepdims=True)
        d_x = dt_wide * d_dtx + par_ref[SKIP : SKIP + 1, :] * e
        small_ref[SKIP : SKIP + 1, :] += jnp.sum(x * e, axis=0, keepdims=True)
        dconv_ref[rows, :] = dconv_ref[rows, :] * d_x
        spot = pl.ds(pl.multiple_of(origin + number * BLOCK, BLOCK), BLOCK)
        dbc_ref[spot, :LANES] += d_b
        dbc_ref[spot, LANES:] += d_c
        owner = (iota((TILE, 8), 0) // WIDTH == iota((TILE, 8), 1)).astype(BF16)

        def head_sum(a):
            return sum(dot(part, owner) for part in halves(a))

        after = (down <= across).astype(BF16)
        prior = (down > across).astype(BF16)
        run = sum(dot(after, part) for part in halves(head_sum(from_state)))
        run = run + sum(dot(prior, part) for part in halves(head_sum(to_state)))
        run = run + head_sum(jnp.broadcast_to(through, (8, TILE)))[:1]
        step_col_ref[rows, 0:8] = run
        step_col_ref[rows, 8:16] = head_sum(d_dtx * x)
        step_row_ref[:, rows] = jnp.concatenate(between + between, axis=0)
        return carried

    lax.fori_loop(0, blocks, one_block, 0)
    v, d_conv = z_ref[:, TILE:], dconv_ref[...]
    d_v = par_ref[TAPS + 3 : TAPS + 4, :] * d_conv
    small_ref[TAPS + 3 : TAPS + 4, :] = jnp.sum(d_conv * v, axis=0, keepdims=True)
    small_ref[BIAS : BIAS + 1, :] = jnp.sum(d_conv, axis=0, keepdims=True)
    for offset in range(1, 4):
        place = TAPS + 3 - offset
        counted = d_conv * col_ref[:, VALID + offset - 1 : VALID + offset]
        small_ref[place : place + 1, :] = jnp.sum(
            counted * pltpu.roll(v, offset, 0), axis=0, keepdims=True
        )
        d_v = d_v + par_ref[place : place + 1, :] * pltpu.roll(counted, length - offset, 0)
    grad_ref[:, TILE : 2 * TILE] = d_v.astype(BF16)
    for number in range(blocks):
        rows = slice(number * BLOCK, (number + 1) * BLOCK)
        spot = pl.ds(pl.multiple_of(origin + number * BLOCK, BLOCK), BLOCK)
        turn_ref[:, spot] = grad_ref[rows, :].T


def backward_kernel(
    normed_ref, cot_ref, z_ref, y_ref, dyn_ref, bc_ref, wide_ref, pick_ref, col_ref, row_ref, seg_ref,
    turned_ref, norm_ref, par_ref, state_ref,
    grad_ref, dbc_ref, step_row_ref, step_col_ref, small_ref, far_out_ref, near_out_ref, total_ref,
    turn_ref, xs_ref, dconv_ref, carry_ref, stream_ref, far_ref, near_ref, y_recv_ref, z_send_ref, z_own_ref,
    z_recv_ref, stream_sem, out_sem, y_send_sem, y_recv_sem, z_send_sem, z_recv_sem,
    *, inside, tiles, spans,
):
    tile, sequence = pl.program_id(0), pl.program_id(1)
    length = xs_ref.shape[0]
    parts = turn_ref.shape[0], near_ref.shape[2]
    halves_of = near_ref.shape[0]
    dp, mp = lax.axis_index("dp"), lax.axis_index("mp")

    def partner(bits):
        return (jnp.bitwise_xor(dp, bits), mp)

    def y_copy(number, part):
        slot = lax.rem(number, 2)
        return pltpu.make_async_remote_copy(
            src_ref=far_ref.at[part],
            dst_ref=y_recv_ref.at[slot, part],
            send_sem=y_send_sem.at[part],
            recv_sem=y_recv_sem.at[slot, part],
            device_id=partner(2),
            device_id_type=pl.DeviceIdType.MESH,
        )

    def z_copy(number, k):
        slot = lax.rem(number, 2)
        return pltpu.make_async_remote_copy(
            src_ref=z_send_ref.at[k - 1],
            dst_ref=z_recv_ref.at[slot, k - 1],
            send_sem=z_send_sem.at[k - 1],
            recv_sem=z_recv_sem.at[slot, k - 1],
            device_id=partner(4 * k),
            device_id_type=pl.DeviceIdType.MESH,
        )

    def finish(number):
        slot = lax.rem(number, 2)
        total = z_own_ref[...]
        for k in range(1, spans):
            z_copy(number, k).wait()
            total = total + z_recv_ref[slot, k - 1].astype(F32)
        total_ref[number] = total

    def pass_on(number):
        slot = lax.rem(number, 2)
        for part in range(spans):
            y_copy(number, part).wait()
            whole_part = near_ref[part] + y_recv_ref[slot, part].astype(F32)
            if part == 0:
                z_own_ref[...] = whole_part
            else:
                z_send_ref[part - 1] = whole_part.astype(BF16)
                z_copy(number, part).start()

    @pl.when((tile == 0) & (sequence == 0))
    def _():
        dbc_ref[...] = jnp.zeros_like(dbc_ref)
        if inside:
            barrier = pltpu.get_barrier_semaphore()
            others = [2] + [4 * k for k in range(1, spans)]
            for bits in others:
                pl.semaphore_signal(
                    barrier, inc=1, device_id=partner(bits), device_id_type=pl.DeviceIdType.MESH
                )
            pl.semaphore_wait(barrier, len(others))

    if inside > 1:

        @pl.when((sequence == 1) & (tile >= 2) & (tile < inside + 2))
        def _():
            finish(tile - 2)

    if inside:

        @pl.when((sequence == 1) & (tile >= 1) & (tile < inside + 1))
        def _():
            pass_on(tile - 1)

    backward_tile(
        sequence * length, z_ref, y_ref, dyn_ref, bc_ref, wide_ref, pick_ref, col_ref, row_ref, seg_ref,
        turned_ref, norm_ref, par_ref, state_ref, grad_ref, dbc_ref, step_row_ref, step_col_ref, small_ref,
        turn_ref, xs_ref, dconv_ref, carry_ref,
    )

    def fetch(number, slot):
        lanes = pl.ds(pl.multiple_of(number * parts[1], LANES), parts[1])
        return [
            pltpu.make_async_copy(ref.at[:, lanes], stream_ref.at[slot, at], stream_sem.at[slot, at])
            for at, ref in enumerate((normed_ref, cot_ref))
        ]

    def out_copies():
        place = tile - inside
        return [
            pltpu.make_async_copy(far_ref, far_out_ref.at[place], out_sem.at[0]),
            pltpu.make_async_copy(near_ref, near_out_ref.at[place], out_sem.at[1]),
        ]

    @pl.when(sequence == 1)
    def _():
        for copy in fetch(halves_of, 0):
            copy.start()

        def one_part(step, carried):
            number = lax.rem(step + halves_of, 2 * halves_of)
            slot = lax.rem(step, 2)

            @pl.when(step + 1 < 2 * halves_of)
            def _():
                for copy in fetch(lax.rem(step + 1 + halves_of, 2 * halves_of), lax.rem(step + 1, 2)):
                    copy.start()

            for copy in fetch(number, slot):
                copy.wait()
            upper = dot(turn_ref[: 2 * TILE, :], stream_ref[slot, 0])
            lower = dot(turn_ref[2 * TILE :, :], stream_ref[slot, 1])

            @pl.when(step < halves_of)
            def _():
                far_ref[step, : 2 * TILE, :] = upper.astype(BF16)
                far_ref[step, 2 * TILE :, :] = lower.astype(BF16)

            @pl.when(step >= halves_of)
            def _():
                near_ref[step - halves_of, : 2 * TILE, :] = upper
                near_ref[step - halves_of, 2 * TILE :, :] = lower

            return carried

        def run(first, last):
            lax.fori_loop(first, last, one_part, 0)

        run(0, halves_of)
        if inside:

            @pl.when(tile < inside)
            def _():
                for part in range(spans):
                    y_copy(tile, part).start()

        run(halves_of, 2 * halves_of)
        if inside < tiles:

            @pl.when(tile >= inside)
            def _():
                for copy in out_copies():
                    copy.start()
                for copy in out_copies():
                    copy.wait()

    if inside:

        @pl.when((sequence == 1) & (tile == tiles - 1))
        def _():
            finish(tile - 1)


def by_sequence(rows, width):
    return pl.BlockSpec((rows, width), lambda i: (i, 0))


def by_columns(rows, length):
    return pl.BlockSpec((rows, length), lambda i: (0, i))


def whole(shape):
    return pl.BlockSpec(shape, lambda i: (0,) * len(shape))


def shaped(shape, kind=F32):
    return jax.ShapeDtypeStruct(shape, kind)


def cost(flops):
    return pl.CostEstimate(flops=int(flops), bytes_accessed=10**7, transcendentals=10**6)


def run_tables(normed, weight, ids, par, head, length):
    tokens, width = normed.shape
    cols = weight.shape[1]
    return pl.pallas_call(
        table_kernel,
        grid=(tokens // length,),
        in_specs=[
            by_sequence(length, width),
            whole((width, cols)),
            by_sequence(length, 1),
            by_columns(1, length),
            whole((8, 2 * LANES)),
            whole((8, LANES)),
        ],
        out_specs=[
            by_sequence(length, 2 * LANES),
            by_sequence(length, 2 * LANES),
            by_sequence(length, LANES),
            by_sequence(length, COLS),
            by_columns(2 * HEADS, length),
            by_sequence(length, BLOCK),
            by_sequence(length, BLOCK),
        ],
        out_shape=[
            shaped((tokens, 2 * LANES)),
            shaped((tokens, 2 * LANES)),
            shaped((tokens, LANES), BF16),
            shaped((tokens, COLS)),
            shaped((2 * HEADS, tokens)),
            shaped((tokens, BLOCK)),
            shaped((tokens, BLOCK)),
        ],
        compiler_params=pltpu.CompilerParams(vmem_limit_bytes=VMEM_LIMIT),
        cost_estimate=cost(1e10),
    )(normed, weight, ids[:, None], ids[None, :], par, head)


def pick_table(tile):
    row, lane = jnp.arange(LANES)[:, None], jnp.arange(2 * TILE)[None, :]
    head = tile * GROUP + (lane % TILE) // WIDTH
    return ((row % HEADS == head) & (row // (3 * HEADS) == lane // TILE)).astype(BF16)


def run_forward(pieces, normed, cot, bc, wide, col, rows, score, par, sums, tile, length):
    tokens, width = normed.shape
    number, blocks = tokens // length, length // BLOCK
    return pl.pallas_call(
        functools.partial(forward_kernel, pieces=len(pieces)),
        grid=(number,),
        in_specs=[whole(p.shape) for p in pieces]
        + [
            by_sequence(length, width),
            by_sequence(length, width),
            by_sequence(length, 2 * LANES),
            by_sequence(length, LANES),
            whole((LANES, 2 * TILE)),
            by_sequence(length, COLS),
            pl.BlockSpec((8, length), lambda i: (tile, i)),
            by_sequence(length, BLOCK),
            whole((8, TILE)),
            by_sequence(length, 8),
        ],
        out_specs=[
            whole((width, 3 * TILE)),
            by_sequence(length, 2 * TILE),
            by_sequence(length, TILE),
            by_sequence(length, TILE),
            pl.BlockSpec((blocks, LANES, TILE), lambda i: (i, 0, 0)),
            by_sequence(length, 8),
        ],
        out_shape=[
            shaped((width, 3 * TILE), BF16),
            shaped((tokens, 2 * TILE)),
            shaped((tokens, TILE)),
            shaped((tokens, TILE)),
            shaped((number * blocks, LANES, TILE)),
            shaped((tokens, 8)),
        ],
        scratch_shapes=[pltpu.VMEM((length, TILE), F32), pltpu.VMEM((LANES, TILE), F32)],
        compiler_params=pltpu.CompilerParams(vmem_limit_bytes=VMEM_LIMIT),
        cost_estimate=cost(2e10),
    )(*pieces, normed, cot, bc, wide, pick_table(tile), col, rows, score, par, sums)


def run_backward(normed, cot, zv, y, dyn, bc, wide, col, rows, ids, turned, norms, par, state, length, spans):
    tiles, tokens = zv.shape[:2]
    width = normed.shape[1]
    number, blocks = tokens // length, length // BLOCK
    part = 2 * LANES
    near = width // part // 2
    inside = tiles - 1 if near == spans else 0

    def by_tile(size, cols):
        return pl.BlockSpec((None, size, cols), lambda j, i: (j, i, 0))

    def shared(size, cols):
        return pl.BlockSpec((size, cols), lambda j, i: (i, 0))

    def fixed(*shape):
        return pl.BlockSpec((None,) + shape, lambda j, i: (j,) + (0,) * len(shape))

    params = dict(vmem_limit_bytes=VMEM_LIMIT)
    if inside:
        params.update(collective_id=1, has_side_effects=True)
    return inside, pl.pallas_call(
        functools.partial(backward_kernel, inside=inside, tiles=tiles, spans=spans),
        grid=(tiles, number),
        in_specs=[
            ANY,
            ANY,
            by_tile(length, 2 * TILE),
            by_tile(length, TILE),
            by_tile(length, TILE),
            shared(length, 2 * LANES),
            shared(length, LANES),
            fixed(LANES, 2 * TILE),
            shared(length, COLS),
            pl.BlockSpec((8, length), lambda j, i: (j, i)),
            pl.BlockSpec((1, length), lambda j, i: (0, i)),
            shared(length, BLOCK),
            shared(length, 8),
            fixed(8, TILE),
            pl.BlockSpec((None, blocks, LANES, TILE), lambda j, i: (j, i, 0, 0)),
        ],
        out_specs=[
            by_tile(length, 3 * TILE),
            pl.BlockSpec((tokens, 2 * LANES), lambda j, i: (0, 0)),
            pl.BlockSpec((8, length), lambda j, i: (j, i)),
            by_tile(length, 16),
            pl.BlockSpec((None, None, 8, TILE), lambda j, i: (j, i, 0, 0)),
            ANY,
            ANY,
            pl.BlockSpec((max(inside, 1), 3 * TILE, part), lambda j, i: (0, 0, 0)),
        ],
        out_shape=[
            shaped((tiles, tokens, 3 * TILE), BF16),
            shaped((tokens, 2 * LANES)),
            shaped((tiles * 8, tokens)),
            shaped((tiles, tokens, 16)),
            shaped((tiles, number, 8, TILE)),
            shaped((tiles - inside, near, 3 * TILE, part), BF16),
            shaped((tiles - inside, near, 3 * TILE, part)),
            shaped((max(inside, 1), 3 * TILE, part)),
        ],
        scratch_shapes=[
            pltpu.VMEM((3 * TILE, tokens), BF16),
            pltpu.VMEM((length, TILE), F32),
            pltpu.VMEM((length, TILE), F32),
            pltpu.VMEM((LANES, TILE), F32),
            pltpu.VMEM((2, 2, tokens, part), BF16),
            pltpu.VMEM((near, 3 * TILE, part), BF16),
            pltpu.VMEM((near, 3 * TILE, part), F32),
            pltpu.VMEM((2, near, 3 * TILE, part), BF16),
            pltpu.VMEM((3, 3 * TILE, part), BF16),
            pltpu.VMEM((3 * TILE, part), F32),
            pltpu.VMEM((2, 3, 3 * TILE, part), BF16),
            pltpu.SemaphoreType.DMA((2, 2)),
            pltpu.SemaphoreType.DMA((2,)),
            pltpu.SemaphoreType.DMA((near,)),
            pltpu.SemaphoreType.DMA((2, near)),
            pltpu.SemaphoreType.DMA((3,)),
            pltpu.SemaphoreType.DMA((2, 3)),
        ],
        compiler_params=pltpu.CompilerParams(**params),
        cost_estimate=cost(2e11),
    )(
        normed, cot, zv, y, dyn, bc, wide, jnp.stack([pick_table(tile) for tile in range(tiles)]), col, rows,
        ids[None, :], turned, norms, par, state,
    )


def segment_conv(inputs, taps, bias, masks):
    reach = taps.shape[0]
    result = bias[None, :] + taps[reach - 1][None, :] * inputs
    for offset in range(1, reach):
        moved = jnp.concatenate(
            [jnp.zeros((offset, inputs.shape[1]), inputs.dtype), inputs[:-offset]], axis=0
        )
        result = result + taps[reach - 1 - offset][None, :] * (
            moved * masks[:, offset - 1 : offset]
        )
    return result


def local(
    hidden_in,
    segments,
    norm_gain,
    w_zx,
    w_dt,
    w_bc,
    conv_x,
    conv_x_bias,
    conv_bc,
    conv_bc_bias,
    dt_bias,
    a_log,
    d_skip,
    gated_gain,
    w_out,
    cotangent,
):
    dp, mp = lax.axis_index("dp"), lax.axis_index("mp")
    extent = lax.axis_size("dp")
    far = extent // 4
    x_side = lax.rem(dp, 2)
    rows, width = hidden_in.shape
    length = segments.shape[0]
    inner = conv_x.shape[1]
    inner_total = inner * lax.axis_size("mp")
    heads = dt_bias.shape[0]
    quarter, own_heads = inner // 2, heads // 2
    tiles = quarter // TILE
    depth = w_zx.shape[0]

    def by_side(own, other, axis):
        return jnp.where(
            x_side == 0,
            jnp.concatenate([own, other], axis=axis),
            jnp.concatenate([other, own], axis=axis),
        )

    def by_core(own, other, axis):
        return jnp.where(
            mp == 0,
            jnp.concatenate([own, other], axis=axis),
            jnp.concatenate([other, own], axis=axis),
        )

    def of_side(a, side, axis):
        size = a.shape[axis] // 2
        return lax.dynamic_slice_in_dim(a, side * size, size, axis)

    packed = jnp.concatenate([w_zx[:, 0], w_zx[:, 1], w_out.T], axis=1)
    packed = packed.reshape(depth, 3, 2, tiles, TILE).transpose(2, 3, 0, 1, 4)
    packed = packed.reshape(2, tiles, depth, 3 * TILE)

    def small_weights(side):
        return jnp.concatenate([w_bc, of_side(w_dt, side, 1)], axis=1)

    small_other = flip(small_weights(1 - x_side), "dp", 1)
    packed_own = lax.dynamic_index_in_dim(packed, x_side, 0, False)
    packed_other = flip(lax.dynamic_index_in_dim(packed, 1 - x_side, 0, False), "dp", 1)

    def gathered(piece):
        near = [piece] + [flip(piece, "dp", 4 * k) for k in range(1, far)]
        return near + [flip(p, "dp", 2) for p in near]

    bc_weight = jnp.concatenate(
        gathered(by_side(small_weights(x_side), small_other, 0)), axis=0
    )

    normed, cot, inverse_rows = input_norm(hidden_in, cotangent, norm_gain, dp, extent)

    def both_sequences(a):
        near = flip(a, "dp", 1)
        return by_core(a, flip(a, "mp", 1), 0), by_core(near, flip(near, "mp", 1), 0)

    normed_own, normed_near = both_sequences(normed)
    normed_all = jnp.concatenate([normed_own, normed_near], axis=0)
    pieces = [gathered(by_side(packed_own[tile], packed_other[tile], 0)) for tile in range(tiles)]
    cot_all = jnp.concatenate(both_sequences(cot), axis=0)
    ids = (segments, flip(segments, "dp", 1))

    ids_all = jnp.concatenate(ids, axis=0).astype(F32)
    side_bias = of_side(dt_bias, x_side, 0)
    rate = -jnp.exp(of_side(a_log, x_side, 0))
    bc_par = jnp.concatenate([conv_bc, conv_bc_bias[None], jnp.zeros((3, 2 * LANES), F32)], axis=0)
    head_par = jnp.pad(jnp.stack([side_bias, rate]), ((0, 6), (0, LANES - own_heads)))
    proj_bc, bc, wide, col, rows_all, score, turned = run_tables(
        normed_all, bc_weight, ids_all, bc_par, head_par, length
    )
    tokens = normed_all.shape[0]

    def tile_of(a, tile):
        return of_side(a, x_side, a.ndim - 1)[..., tile * TILE : (tile + 1) * TILE]

    skip_wide = jnp.repeat(d_skip, WIDTH)
    params = [
        jnp.concatenate(
            [
                tile_of(conv_x, tile),
                tile_of(conv_x_bias, tile)[None],
                tile_of(skip_wide, tile)[None],
                tile_of(gated_gain, tile)[None],
                jnp.zeros((1, TILE), F32),
            ],
            axis=0,
        )
        for tile in range(tiles)
    ]

    weights, zvs, dyns, ys, states = [], [], [], [], []
    sums = jnp.zeros((tokens, 8), F32)
    for tile in range(tiles):
        weight, zv, dyn, y, state, sums = run_forward(
            pieces[tile], normed_all, cot_all, bc, wide, col, rows_all, score, params[tile], sums, tile, length
        )
        weights.append(weight)
        zvs.append(zv)
        dyns.append(dyn)
        ys.append(y)
        states.append(state)
    sums = sums + flip(sums, "mp", 1)
    near = flip(sums, "dp", 1)
    sums = sums + jnp.concatenate([near[length:], near[:length]], axis=0)
    inverse_gated = lax.rsqrt(sums[:, :1] / inner_total + EPSILON)
    cross = inverse_gated * inverse_gated * inverse_gated / inner_total * sums[:, 1:2]
    lane = jnp.arange(8)[None, :]
    norms = jnp.where(lane == 0, inverse_gated, jnp.where(lane == 1, cross, 0.0))

    inside, (grads, dbc, step_rows, step_cols, smalls, far_share, near_share, inner_totals) = run_backward(
        normed_all, cot_all, jnp.stack(zvs), jnp.stack(ys), jnp.stack(dyns), bc, wide, col, rows_all, ids_all,
        turned, norms, jnp.stack(params), jnp.stack(states), length, far,
    )

    def spread_sum(far_part, near_part):
        def arranged(a):
            return a.transpose(1, 0, 2).reshape(3 * TILE, far, 2 * depth).transpose(1, 0, 2)

        total = arranged(near_part) + arranged(flip(far_part, "dp", 2)).astype(F32)
        out = total.astype(BF16)
        total = total[0]
        for k in range(1, far):
            total = total + flip(out[k], "dp", 4 * k).astype(F32)
        return total

    totals_of = [inner_totals[tile] for tile in range(inside)]
    totals_of += [spread_sum(far_share[at], near_share[at]) for at in range(tiles - inside)]
    stacked = jnp.stack(totals_of)
    mine = of_side(stacked, x_side, 2)
    theirs = flip(of_side(stacked, 1 - x_side, 2).astype(BF16), "dp", 1).astype(F32)

    def assembled(parts):
        return parts.reshape(tiles, 3, TILE, depth).transpose(1, 0, 2, 3).reshape(3, quarter, depth)

    full = by_side(assembled(mine), assembled(theirs), 1)
    grad_zx_weight = full[:2].transpose(2, 0, 1)
    grad_out_weight = full[2]

    dbc = dbc + flip(dbc, "mp", 1)
    dbc = dbc[:length] + flip(dbc[length:], "dp", 1)
    own_masks = col[:length, VALID : VALID + 3]
    _, state_back = jax.vjp(
        lambda values, taps, bias: jax.nn.silu(segment_conv(values, taps, bias, own_masks)),
        proj_bc[:length],
        conv_bc,
        conv_bc_bias,
    )
    d_bc, grad_conv_bc, grad_conv_bc_bias = state_back(dbc)
    bc_grad = d_bc.astype(BF16)

    raw_dt = rows_all.reshape(tiles, 2, GROUP, tokens)[:, 1].reshape(own_heads, tokens)
    run_steps = step_cols.transpose(0, 2, 1)
    steps = (step_rows.reshape(tiles, 8, tokens)[:, :GROUP] + run_steps[:, :GROUP]).reshape(own_heads, tokens)
    direct = run_steps[:, 8 : 8 + GROUP].reshape(own_heads, tokens)
    d_dt = (direct + rate[:, None] * steps) * jax.nn.sigmoid(raw_dt)
    grad_dt_bias = jnp.sum(d_dt, axis=1)
    grad_a_log = jnp.sum(steps * jax.nn.softplus(raw_dt), axis=1) * rate
    dt_grad = d_dt.T.astype(BF16)

    def placed(a):
        zero = jnp.zeros_like(a)
        return by_side(a, zero, a.ndim - 1)

    small_grad = jnp.concatenate(
        [
            dot(normed_own, lax.dynamic_slice_in_dim(bc_grad, mp * LANES, LANES, 1), TN),
            placed(dot(normed_all, dt_grad, TN)),
        ],
        axis=1,
    )
    small_grad = small_grad.reshape(2 * far, 2, depth, -1)
    small_grad = of_side(small_grad, x_side, 1) + flip(
        of_side(small_grad, 1 - x_side, 1).astype(BF16), "dp", 1
    ).astype(F32)
    small_grad = small_grad.reshape(2, far, depth, -1)
    small_grad = small_grad[0] + flip(small_grad[1].astype(BF16), "dp", 2).astype(F32)
    out = small_grad.astype(BF16)
    small_grad = small_grad[0]
    for k in range(1, far):
        small_grad = small_grad + flip(out[k], "dp", 4 * k).astype(F32)
    grad_dt_weight = small_grad[:, LANES:]
    own_bc = small_grad[:, :LANES]
    grad_bc_weight = by_core(own_bc, flip(own_bc, "mp", 1), 1)

    def token_sum(products):
        def part(core):
            return products(lambda a: of_side(a.reshape(2, 2, rows, -1), core, 1).reshape(2 * rows, -1))

        total = part(mp) + flip(part(1 - mp).astype(BF16), "mp", 1).astype(F32)
        return total[:rows] + flip(total[rows:].astype(BF16), "dp", 1).astype(F32)

    out_all = jnp.concatenate([w[:, 2 * TILE :] for w in weights], axis=1)
    yn_all = jnp.concatenate([g[:, 2 * TILE :] for g in grads], axis=1)
    mixer_out = restore_order(token_sum(lambda pick: dot(pick(yn_all), out_all, NT)), dp, extent)
    inputs = hidden_in.astype(F32)
    residual_out = (inputs + mixer_out).astype(BF16)
    usable = (lax.dynamic_slice_in_dim(segments, mp * rows, rows, 0) >= 0).astype(F32)[:, None]
    totals = jnp.stack(
        [
            jnp.sum(usable * inputs * inputs),
            jnp.sum(usable * mixer_out * mixer_out),
            jnp.sum(usable),
        ]
    )

    zv_all = jnp.concatenate([w[:, : 2 * TILE] for w in weights], axis=1)
    dt_weight = bc_weight[:, 2 * LANES :]
    dzx_all = jnp.concatenate([g[:, : 2 * TILE] for g in grads], axis=1)
    d_normed = token_sum(
        lambda pick: dot(pick(dzx_all), zv_all, NT) + dot(pick(dt_grad), dt_weight, NT)
    )
    d_normed = d_normed + dot(
        lax.dynamic_slice_in_dim(bc_grad, mp * rows, rows, 0), bc_weight[:, : 2 * LANES], NT
    )
    d_normed = restore_order(d_normed, dp, extent)
    grad_norm_gain = jnp.sum(d_normed * inputs * inverse_rows, axis=0)
    inverse_cube_rows = inverse_rows * inverse_rows * inverse_rows
    input_grad = (
        cotangent.astype(F32)
        + inverse_rows * norm_gain * d_normed
        - inputs
        * inverse_cube_rows
        * jnp.mean(inputs * norm_gain * d_normed, axis=-1, keepdims=True)
    )

    def summed(a, axes):
        for axis in axes:
            bit = 1
            while bit < lax.axis_size(axis):
                a = a + flip(a, axis, bit)
                bit *= 2
        return a

    small = jnp.sum(smalls, axis=1).transpose(1, 0, 2).reshape(8, quarter)
    channel = placed(small[: GAIN + 1])
    skip_grad = jnp.sum(channel[SKIP].reshape(heads, WIDTH), axis=1)
    pieces = [
        channel[TAPS:BIAS],
        channel[BIAS],
        grad_conv_bc,
        grad_conv_bc_bias,
        placed(grad_dt_bias),
        placed(grad_a_log),
        skip_grad,
        channel[GAIN],
    ]
    flat = summed(jnp.concatenate([p.reshape(-1) for p in pieces]), ("dp",))
    small_sums, start = [], 0
    for piece in pieces:
        small_sums.append(flat[start : start + piece.size].reshape(piece.shape))
        start += piece.size
    last = summed(jnp.concatenate([grad_norm_gain, totals]), ("mp", "dp"))
    grad_norm_gain = last[:width]
    sum_inputs, sum_mixer, usable_count = last[width], last[width + 1], last[width + 2]
    rms_residual = jnp.sqrt(sum_inputs / (usable_count * width))
    rms_mixer = jnp.sqrt(sum_mixer / (usable_count * width))
    return (
        residual_out,
        input_grad,
        grad_norm_gain,
        grad_zx_weight,
        grad_dt_weight,
        grad_bc_weight,
        small_sums[0],
        small_sums[1],
        small_sums[2],
        small_sums[3],
        small_sums[4],
        small_sums[5],
        small_sums[6],
        small_sums[7],
        grad_out_weight,
        rms_residual,
        rms_mixer,
    )


def solution(mesh):
    in_specs = (
        P(("dp", "mp"), None),
        P("dp"),
        P(),
        P("dp", None, "mp"),
        P("dp", "mp"),
        P("dp", None),
        P(None, "mp"),
        P("mp"),
        P(),
        P(),
        P("mp"),
        P("mp"),
        P("mp"),
        P("mp"),
        P("mp", "dp"),
        P(("dp", "mp"), None),
    )
    out_specs = (
        P(("dp", "mp"), None),
        P(("dp", "mp"), None),
        P(),
        P("dp", None, "mp"),
        P("dp", "mp"),
        P("dp", None),
        P(None, "mp"),
        P("mp"),
        P(),
        P(),
        P("mp"),
        P("mp"),
        P("mp"),
        P("mp"),
        P("mp", "dp"),
        P(),
        P(),
    )
    return jax.shard_map(local, mesh=mesh, in_specs=in_specs, out_specs=out_specs, check_vma=False)
```

```python
import functools

import jax
import jax.numpy as jnp
from jax import lax
from jax.experimental import pallas as pl
from jax.experimental.pallas import tpu as pltpu
from jax.sharding import PartitionSpec as P

BLOCK = 256
LANES = 128
TILE = 256
WIDTH = 64
GROUP = TILE // WIDTH
EPSILON = 1e-05
HIGH = lax.Precision.HIGHEST
BF16 = jnp.bfloat16
F32 = jnp.float32
VMEM_LIMIT = 58 * 2**20

NN = (((1,), (0,)), ((), ()))
NT = (((1,), (1,)), ((), ()))
TN = (((0,), (0,)), ((), ()))


def dot(a, b, dims=NN, precision=None):
    return lax.dot_general(a, b, dims, precision=precision, preferred_element_type=F32)


def low_dot(a, b, dims=NN):
    return dot(a.astype(BF16), b.astype(BF16), dims)


def flip(a, axis, bit):
    size = lax.axis_size(axis)
    return lax.ppermute(a, axis, [(i, i ^ bit) for i in range(size)])


def sigmoid(q):
    return 1.0 / (1.0 + jnp.exp(-q))


def owner_block(number, dp, extent):
    y, z, x = number // (extent // 2), (number // 2) % (extent // 4), number % 2
    return jnp.bitwise_xor(dp - lax.rem(dp, 2), (y * 2) + (z * 4) + x)


def norm_kernel(place_ref, hidden_ref, cot_ref, gain_ref, normed_ref, cot_out_ref, inv_ref, *, extent):
    u = hidden_ref[...].astype(F32)
    inv = lax.rsqrt(jnp.mean(u * u, axis=-1, keepdims=True) + EPSILON)
    inv_ref[...] = inv
    for number in range(extent):
        start = pl.multiple_of(owner_block(number, place_ref[0], extent) * LANES, LANES)
        piece = hidden_ref[:, pl.ds(start, LANES)].astype(F32)
        gain = gain_ref[:, pl.ds(start, LANES)]
        normed_ref[:, number * LANES : (number + 1) * LANES] = (piece * inv * gain).astype(BF16)
        cot_out_ref[:, number * LANES : (number + 1) * LANES] = cot_ref[:, pl.ds(start, LANES)]


def input_norm(hidden, cot, gain, dp, extent):
    rows, width = hidden.shape
    if width // extent != LANES:
        u = hidden.astype(F32)
        inv = lax.rsqrt(jnp.mean(u * u, axis=-1, keepdims=True) + EPSILON)
        normed = (u * inv * gain).astype(BF16)
        order = owner_block(jnp.arange(extent), dp, extent)

        def arranged(a):
            return jnp.take(a.reshape(rows, extent, -1), order, axis=1).reshape(rows, width)

        return arranged(normed), arranged(cot), inv
    step = 128
    tile = pl.BlockSpec((step, width), lambda i: (i, 0))
    return pl.pallas_call(
        functools.partial(norm_kernel, extent=extent),
        grid=(rows // step,),
        in_specs=[
            pl.BlockSpec(memory_space=pltpu.SMEM),
            tile,
            tile,
            pl.BlockSpec((1, width), lambda i: (0, 0)),
        ],
        out_specs=[tile, tile, pl.BlockSpec((step, 1), lambda i: (i, 0))],
        out_shape=[
            jax.ShapeDtypeStruct((rows, width), BF16),
            jax.ShapeDtypeStruct((rows, width), BF16),
            jax.ShapeDtypeStruct((rows, 1), F32),
        ],
        compiler_params=pltpu.CompilerParams(vmem_limit_bytes=VMEM_LIMIT),
    )(dp.reshape(1), hidden, cot, gain.reshape(1, width))


def restore_kernel(place_ref, in_ref, out_ref, *, extent):
    for number in range(extent):
        start = pl.multiple_of(owner_block(number, place_ref[0], extent) * LANES, LANES)
        out_ref[:, pl.ds(start, LANES)] = in_ref[:, number * LANES : (number + 1) * LANES]


def restore_order(a, dp, extent):
    rows, width = a.shape
    if width // extent != LANES:
        order = owner_block(jnp.arange(extent), dp, extent)
        back = jnp.argsort(order)
        return jnp.take(a.reshape(rows, extent, -1), back, axis=1).reshape(rows, width)
    step = 128
    tile = pl.BlockSpec((step, width), lambda i: (i, 0))
    return pl.pallas_call(
        functools.partial(restore_kernel, extent=extent),
        grid=(rows // step,),
        in_specs=[pl.BlockSpec(memory_space=pltpu.SMEM), tile],
        out_specs=tile,
        out_shape=jax.ShapeDtypeStruct((rows, width), a.dtype),
        compiler_params=pltpu.CompilerParams(vmem_limit_bytes=VMEM_LIMIT),
    )(dp.reshape(1), a)


VALID, LINK, KEEP, SEG = 0, 3, 4, 5
COLS = 8
HEADS = 16
TAPS, BIAS, SKIP, GAIN = 0, 4, 5, 6
ANY = pl.BlockSpec(memory_space=pl.ANY)


def iota(shape, axis):
    return lax.broadcasted_iota(jnp.int32, shape, axis)


def thirds(a):
    high = a.astype(BF16)
    rest = a - high.astype(F32)
    mid = rest.astype(BF16)
    return [high, mid, (rest - mid.astype(F32)).astype(BF16)]


def halves(a):
    high = a.astype(BF16)
    return [high, (a - high.astype(F32)).astype(BF16)]


def conv_of(v, col, par_ref):
    result = par_ref[BIAS : BIAS + 1, :] + par_ref[TAPS + 3 : TAPS + 4, :] * v
    for offset in range(1, 4):
        valid = col[:, VALID + offset - 1 : VALID + offset]
        result = result + par_ref[TAPS + 3 - offset : TAPS + 4 - offset, :] * (
            pltpu.roll(v, offset, 0) * valid
        )
    return result


def pair_mask(seg_col, seg_row, transposed):
    down, across = iota((BLOCK, BLOCK), 0), iota((BLOCK, BLOCK), 1)
    causal = down <= across if transposed else down >= across
    return causal & (seg_col == seg_row)


def table_part(
    origin, length, normed_ref, weight_ref, seg_col_ref, seg_row_ref, par_ref, head_ref,
    proj_ref, bc_ref, wide_ref, col_ref, row_ref, score_ref, turned_ref,
):
    every = pl.ds(origin, length)
    blocks = length // BLOCK

    def spot(block):
        return pl.ds(pl.multiple_of(origin + block * BLOCK, BLOCK), BLOCK)

    proj = dot(normed_ref[every, :], weight_ref[...])
    proj_ref[every, :] = proj[:, : 2 * LANES]
    raw = proj[:, 2 * LANES : 2 * LANES + HEADS] + head_ref[0:1, :HEADS]
    dt = jnp.maximum(raw, 0.0) + jnp.log1p(jnp.exp(-jnp.abs(raw)))
    step = dt * head_ref[1:2, :HEADS]
    seg = seg_col_ref[every, :]
    place = iota((length, 1), 0)
    number = place // BLOCK
    before, last = jnp.full((length, 1), -2.0, F32), jnp.zeros((length, 1), F32)
    for block in range(blocks):
        end = seg[(block + 1) * BLOCK - 1 : (block + 1) * BLOCK, :]
        last = jnp.where(number == block, end, last)
        before = jnp.where(number == block + 1, end, before)
    lower = (iota((BLOCK, BLOCK), 0) >= iota((BLOCK, BLOCK), 1)).astype(F32)
    upper = (iota((BLOCK, BLOCK), 0) <= iota((BLOCK, BLOCK), 1)).astype(F32)
    eye = (iota((BLOCK, BLOCK), 0) == iota((BLOCK, BLOCK), 1)).astype(F32)
    cums = []
    for block in range(blocks):
        rows = slice(block * BLOCK, (block + 1) * BLOCK)
        cums.append(dot(lower, step[rows], NN, HIGH))
        cum_rows = dot(step[rows], upper, TN, HIGH)
        raw_rows = dot(raw[rows], eye, TN, HIGH)
        for tile in range(HEADS // GROUP):
            heads = slice(tile * GROUP, (tile + 1) * GROUP)
            row_ref[tile * 8 : (tile + 1) * 8, spot(block)] = jnp.concatenate(
                [cum_rows[heads], raw_rows[heads]], axis=0
            )
    cum = jnp.concatenate(cums, axis=0)
    lane = iota((length, COLS), 1)
    col = jnp.zeros((length, COLS), F32)
    for offset in range(1, 4):
        valid = (pltpu.roll(seg, offset, 0) == seg) & (place >= offset)
        col = jnp.where(lane == VALID + offset - 1, valid.astype(F32), col)
    col = jnp.where(lane == LINK, (seg == before).astype(F32), col)
    col = jnp.where(lane == KEEP, (seg == last).astype(F32), col)
    col = jnp.where(lane == SEG, seg, col)
    col_ref[every, :] = col
    wide_ref[every, :] = jnp.concatenate(
        thirds(dt) + thirds(cum) + [jnp.zeros((length, LANES - 6 * HEADS), BF16)], axis=1
    )
    conv = conv_of(proj[:, : 2 * LANES], col, par_ref)
    bc_ref[every, :] = conv * sigmoid(conv)
    for block in range(blocks):
        rows = slice(block * BLOCK, (block + 1) * BLOCK)
        at = spot(block)
        b_rows, c_rows = bc_ref[at, :LANES], bc_ref[at, LANES:]
        seg_col, seg_row = seg[rows], seg_row_ref[:, at]
        score_ref[at, :] = jnp.where(
            pair_mask(seg_col, seg_row, False), dot(c_rows, b_rows, NT, HIGH), 0.0
        )
        turned_ref[at, :] = jnp.where(
            pair_mask(seg_col, seg_row, True), dot(b_rows, c_rows, NT, HIGH), 0.0
        )


def table_kernel(*refs):
    table_part(0, refs[0].shape[0], *refs)


def forward_tile(
    origin, first_row, normed_ref, cot_ref, w_ref, bc_ref, wide_ref, pick_ref, col_ref, row_ref, score_ref,
    par_ref, z_ref, dyn_ref, y_ref, state_ref, sum_ref, xs_ref, carry_ref,
):
    length = xs_ref.shape[0]
    blocks = length // BLOCK

    def spot(number):
        return pl.ds(pl.multiple_of(origin + number * BLOCK, BLOCK), BLOCK)

    def project(number, carried):
        rows = pl.ds(pl.multiple_of(number * BLOCK, BLOCK), BLOCK)
        z_ref[rows, :] = dot(normed_ref[spot(number), :], w_ref[:, : 2 * TILE])
        dyn_ref[rows, :] = dot(cot_ref[spot(number), :], w_ref[:, 2 * TILE :])
        return carried

    lax.fori_loop(0, blocks, project, 0)
    conv = conv_of(z_ref[:, TILE:], col_ref[pl.ds(origin, length), :], par_ref)
    xs_ref[...] = conv * sigmoid(conv)
    carry_ref[...] = jnp.zeros_like(carry_ref)
    ones = jnp.ones((8, TILE), BF16)

    def row_sum(a):
        return sum(dot(ones, part, NT) for part in halves(a))

    def one_block(number, carried):
        rows, at = pl.ds(pl.multiple_of(number * BLOCK, BLOCK), BLOCK), spot(number)
        b_rows, c_rows = bc_ref[at, :LANES], bc_ref[at, LANES:]
        col = col_ref[at, :]
        scores = score_ref[at, :]
        x = xs_ref[rows, :]
        wide = dot(wide_ref[at, :], pick_ref[...])
        dt_wide, cum_wide = wide[:, :TILE], wide[:, TILE:]
        cum_rows = row_ref[pl.ds(first_row, 8), at]
        dtx = x * dt_wide
        dtx_low = dtx.astype(BF16)
        parts = []
        for head in range(GROUP):
            gap = cum_wide[:, head * WIDTH : head * WIDTH + 1] - cum_rows[head : head + 1, :]
            mixing = scores * jnp.exp(jnp.minimum(gap, 0.0))
            parts.append(dot(mixing.astype(BF16), dtx_low[:, head * WIDTH : (head + 1) * WIDTH]))
        within = jnp.concatenate(parts, axis=1)
        state = carry_ref[...]
        state_ref[number] = state
        decay = jnp.exp(cum_wide) * col[:, LINK : LINK + 1]
        y = within + low_dot(c_rows, state) * decay + par_ref[SKIP : SKIP + 1, :] * x
        weight = jnp.exp(cum_wide[BLOCK - 1 :, :] - cum_wide) * col[:, KEEP : KEEP + 1]
        carry_ref[...] = state * decay[BLOCK - 1 :, :] + low_dot(b_rows, dtx * weight, TN)
        y_ref[rows, :] = y
        z = z_ref[rows, :TILE]
        yg = y * z * sigmoid(z)
        first = row_sum(yg * yg)
        second = row_sum(yg * par_ref[GAIN : GAIN + 1, :] * dyn_ref[rows, :])
        place = iota((8, BLOCK), 0)
        sum_ref[:, at] += jnp.where(place == 0, first, jnp.where(place == 1, second, 0.0))
        return carried

    lax.fori_loop(0, blocks, one_block, 0)


def forward_kernel(*refs, pieces):
    normed_ref, cot_ref, bc_ref, wide_ref, pick_ref, col_ref, row_ref, score_ref, par_ref = refs[pieces : pieces + 9]
    w_ref, z_ref, dyn_ref, y_ref, state_ref, sum_ref, xs_ref, carry_ref = refs[pieces + 9 :]

    @pl.when(pl.program_id(0) == 0)
    def _():
        depth = refs[0].shape[0]
        for number in range(pieces):
            w_ref[number * depth : (number + 1) * depth, :] = refs[number][...]

    sum_ref[...] = jnp.zeros_like(sum_ref)
    forward_tile(
        0, 0, normed_ref, cot_ref, w_ref, bc_ref, wide_ref, pick_ref, col_ref, row_ref, score_ref, par_ref,
        z_ref, dyn_ref, y_ref, state_ref, sum_ref, xs_ref, carry_ref,
    )


def gather_kernel(
    normed_ref, cot_ref, own_ref, other_ref, small_own_ref, small_other_ref, seg_col_ref, seg_row_ref,
    bc_par_ref, head_ref, pick_ref, par_ref,
    normed_out, cot_out, w_out, small_out, z_ref, dyn_ref, y_ref, state_ref, proj_out, bc_out, wide_out, col_out, row_out,
    turned_out, norm_ref,
    normed_all, cot_all, w_all, small_all, proj_all, bc_all, wide_all, col_all, row_all, score_all, turned_all,
    sum_ref, sum_recv, xs_ref, carry_ref,
    here_sem, out_sem, act_send, act_recv, x_send, x_recv, z_send, z_recv, y_send, y_recv, sum_send, sum_recv_sem,
    *, tiles, spans, inner_total,
):
    tile, sequence = pl.program_id(0), pl.program_id(1)
    length = xs_ref.shape[0]
    rows = normed_ref.shape[0]
    depth = own_ref.shape[1]
    part = 2 * depth
    dp, mp = lax.axis_index("dp"), lax.axis_index("mp")
    side = lax.rem(dp, 2)
    mine = pl.ds(pl.multiple_of(mp * rows, rows), rows)
    theirs = pl.ds(pl.multiple_of(length + mp * rows, rows), rows)
    slab = pl.ds(pl.multiple_of(side * depth, depth), depth)
    other_core = (dp, 1 - mp)

    def along(bits):
        return (jnp.bitwise_xor(dp, bits), mp)

    def remote(src, dst, send, recv, device):
        return pltpu.make_async_remote_copy(
            src_ref=src, dst_ref=dst, send_sem=send, recv_sem=recv, device_id=device,
            device_id_type=pl.DeviceIdType.MESH,
        )

    arrays = ((normed_ref, normed_all), (cot_ref, cot_all))

    def act_here(a):
        return pltpu.make_async_copy(arrays[a][0], arrays[a][1].at[mine, :], here_sem.at[a])

    def act_core(a):
        return remote(
            arrays[a][0], arrays[a][1].at[mine, :], act_send.at[a, 0], act_recv.at[a, 0], other_core
        )

    def act_x(a):
        return remote(
            arrays[a][0], arrays[a][1].at[theirs, :], act_send.at[a, 1], act_recv.at[a, 1], along(1)
        )

    def act_pass(a):
        return remote(
            arrays[a][1].at[theirs, :], arrays[a][1].at[theirs, :], act_send.at[a, 2], act_recv.at[a, 2], other_core
        )

    def weight_of(number):
        return small_all if number == 0 else w_all.at[number - 1]

    def w_here(number):
        src = small_own_ref if number == 0 else own_ref.at[number - 1]
        return pltpu.make_async_copy(src, weight_of(number).at[slab, :], here_sem.at[2 + number])

    def w_x(number):
        src = small_other_ref if number == 0 else other_ref.at[number - 1]
        return remote(src, weight_of(number).at[slab, :], x_send.at[number], x_recv.at[number], along(1))

    def w_z(number, k):
        ref = weight_of(number)
        return remote(
            ref.at[pl.ds(0, part), :], ref.at[pl.ds(k * part, part), :],
            z_send.at[number, k - 1], z_recv.at[number, k - 1], along(4 * k),
        )

    def w_y(number, k):
        ref = weight_of(number)
        return remote(
            ref.at[pl.ds(k * part, part), :], ref.at[pl.ds((spans + k) * part, part), :],
            y_send.at[number, k], y_recv.at[number, k], along(2),
        )

    def begin_z(number):
        w_here(number).wait()
        w_x(number).wait_recv()
        for k in range(1, spans):
            w_z(number, k).start()
        w_y(number, 0).start()

    def begin_y(number):
        for k in range(1, spans):
            w_z(number, k).wait_recv()
            w_y(number, k).start()

    def complete(number):
        for k in range(spans):
            w_y(number, k).wait_recv()

    tables = (
        (normed_all, normed_out), (cot_all, cot_out), (proj_all, proj_out), (bc_all, bc_out),
        (wide_all, wide_out), (col_all, col_out), (row_all, row_out), (turned_all, turned_out),
        (small_all, small_out),
    )

    def table_out(at):
        return pltpu.make_async_copy(tables[at][0], tables[at][1], out_sem.at[at])

    def weight_out(number):
        return pltpu.make_async_copy(w_all.at[number], w_out.at[number], out_sem.at[len(tables) + number])

    def make_tables(origin):
        table_part(
            origin, length, normed_all, small_all, seg_col_ref, seg_row_ref, bc_par_ref, head_ref,
            proj_all, bc_all, wide_all, col_all, row_all, score_all, turned_all,
        )

    @pl.when((tile == 0) & (sequence == 0))
    def _():
        barrier = pltpu.get_barrier_semaphore()
        partners = [along(1), along(2), other_core] + [along(4 * k) for k in range(1, spans)]
        for device in partners:
            pl.semaphore_signal(barrier, inc=1, device_id=device, device_id_type=pl.DeviceIdType.MESH)
        for number in range(tiles + 1):
            w_here(number).start()
        act_here(0).start()
        act_here(1).start()
        sum_ref[...] = jnp.zeros_like(sum_ref)
        pl.semaphore_wait(barrier, len(partners))
        w_x(0).start()
        w_x(1).start()
        act_core(0).start()
        act_core(1).start()
        act_x(0).start()
        begin_z(0)
        begin_z(1)
        for number in range(2, tiles + 1):
            w_x(number).start()
        act_x(1).start()
        begin_y(0)
        begin_z(2)
        act_here(0).wait()
        act_core(0).wait_recv()
        complete(0)
        make_tables(0)
        begin_y(1)
        act_x(0).wait_recv()
        act_pass(0).start()
        act_here(1).wait()
        act_core(1).wait_recv()

    for number in range(tiles):

        @pl.when((tile == number) & (sequence == 0))
        def _(number=number):
            if number + 3 <= tiles:
                begin_z(number + 3)
            if number + 2 <= tiles:
                begin_y(number + 2)
            complete(number + 1)
            weight_out(number).start()

    @pl.when((tile == 0) & (sequence == 1))
    def _():
        act_pass(0).wait_recv()
        make_tables(length)
        act_x(1).wait_recv()
        act_pass(1).start()
        act_pass(1).wait_recv()
        for at in range(len(tables)):
            table_out(at).start()

    forward_tile(
        sequence * length, tile * 8, normed_all, cot_all, w_all.at[tile], bc_all, wide_all, pick_ref, col_all,
        row_all, score_all, par_ref, z_ref, dyn_ref, y_ref, state_ref, sum_ref, xs_ref, carry_ref,
    )

    @pl.when((tile == tiles - 1) & (sequence == 1))
    def _():
        between = remote(sum_ref, sum_recv.at[0], sum_send.at[0], sum_recv_sem.at[0], other_core)
        between.start()
        between.wait()
        sum_ref[...] += sum_recv[0]
        across = remote(sum_ref, sum_recv.at[1], sum_send.at[1], sum_recv_sem.at[1], along(1))
        across.start()
        across.wait()
        norm_ref[...] = norm_rows(
            sum_ref[...] + jnp.concatenate([sum_recv[1, :, length:], sum_recv[1, :, :length]], axis=1),
            inner_total,
        )
        for a in range(2):
            act_core(a).wait_send()
            act_x(a).wait_send()
            act_pass(a).wait_send()
        for number in range(tiles + 1):
            w_x(number).wait_send()
            for k in range(1, spans):
                w_z(number, k).wait_send()
            for k in range(spans):
                w_y(number, k).wait_send()
        for at in range(len(tables)):
            table_out(at).wait()
        for number in range(tiles):
            weight_out(number).wait()


def norm_rows(sums, inner_total):
    inverse = lax.rsqrt(sums[0:1] / inner_total + EPSILON)
    cross = inverse * inverse * inverse / inner_total * sums[1:2]
    return jnp.concatenate([inverse, cross, jnp.zeros((6, sums.shape[1]), F32)], axis=0)


def backward_tile(
    origin, z_ref, y_ref, dyn_ref, bc_ref, wide_ref, pick_ref, col_ref, row_ref, seg_ref, turned_ref, norm_ref,
    par_ref, state_ref, grad_ref, dbc_ref, step_row_ref, step_col_ref, small_ref, turn_ref, xs_ref, dconv_ref,
    carry_ref,
):
    length = xs_ref.shape[0]
    blocks = length // BLOCK
    conv = conv_of(z_ref[:, TILE:], col_ref[...], par_ref)
    gate = sigmoid(conv)
    xs_ref[...] = conv * gate
    dconv_ref[...] = gate * (1.0 + conv * (1.0 - gate))
    carry_ref[...] = jnp.zeros_like(carry_ref)
    small_ref[...] = jnp.zeros_like(small_ref)
    down, across = iota((BLOCK, BLOCK), 0), iota((BLOCK, BLOCK), 1)

    def one_block(step, carried):
        number = blocks - 1 - step
        rows = pl.ds(pl.multiple_of(number * BLOCK, BLOCK), BLOCK)
        col = col_ref[rows, :]
        z, y, dyn = z_ref[rows, :TILE], y_ref[rows, :], dyn_ref[rows, :]
        gain = par_ref[GAIN : GAIN + 1, :]
        norms = dot(norm_ref[:, rows], (iota((8, 8), 0) == iota((8, 8), 1)).astype(F32), TN, HIGH)
        inv, cross = norms[:, 0:1], norms[:, 1:2]
        gate = sigmoid(z)
        silu = z * gate
        yg = y * silu
        yg_inv = yg * inv
        d_yg = inv * gain * dyn - yg * cross
        grad_ref[rows, :TILE] = (d_yg * y * (gate * (1.0 + z * (1.0 - gate)))).astype(BF16)
        grad_ref[rows, 2 * TILE :] = (yg_inv * gain).astype(BF16)
        small_ref[GAIN : GAIN + 1, :] += jnp.sum(dyn * yg_inv, axis=0, keepdims=True)
        e = d_yg * silu
        b_rows, c_rows = bc_ref[rows, :LANES], bc_ref[rows, LANES:]
        b_low, c_low = b_rows.astype(BF16), c_rows.astype(BF16)
        scores = turned_ref[rows, :]
        x = xs_ref[rows, :]
        wide = dot(wide_ref[rows, :], pick_ref[...])
        dt_wide, cum_wide = wide[:, :TILE], wide[:, TILE:]
        dtx = x * dt_wide
        dtx_low, e_low = dtx.astype(BF16), e.astype(BF16)
        reach = (down >= across).astype(BF16)
        d_scores = jnp.zeros((BLOCK, BLOCK), F32)
        parts, between = [], []
        for head in range(GROUP):
            lanes = slice(head * WIDTH, (head + 1) * WIDTH)
            gap = row_ref[head : head + 1, rows] - cum_wide[:, head * WIDTH : head * WIDTH + 1]
            decay = jnp.exp(jnp.minimum(gap, 0.0))
            mixing = scores * decay
            parts.append(dot(mixing.astype(BF16), e_low[:, lanes]))
            d_mixing = dot(dtx_low[:, lanes], e_low[:, lanes], NT)
            d_scores = d_scores + d_mixing * decay
            later = dot((d_mixing * mixing).astype(BF16), reach)
            between.append(jnp.sum(jnp.where(down < across, later, 0.0), axis=0, keepdims=True))
        d_dtx = jnp.concatenate(parts, axis=1)
        mask = pair_mask(col[:, SEG : SEG + 1], seg_ref[:, rows], True)
        d_scores = jnp.where(mask, d_scores, 0.0).astype(BF16)
        d_b = dot(d_scores, c_low)
        d_c = dot(d_scores, b_low, TN)
        state, d_state = state_ref[number], carry_ref[...]
        state_low, d_state_low = state.astype(BF16), d_state.astype(BF16)
        decay = jnp.exp(cum_wide) * col[:, LINK : LINK + 1]
        e_in = e * decay
        e_in_low = e_in.astype(BF16)
        from_state = e_in * dot(c_low, state_low)
        d_c = d_c + dot(e_in_low, state_low, NT)
        carry_ref[...] = decay[BLOCK - 1 :, :] * d_state + dot(c_low, e_in_low, TN)
        weight = jnp.exp(cum_wide[BLOCK - 1 :, :] - cum_wide) * col[:, KEEP : KEEP + 1]
        d_tail = weight * dot(b_low, d_state_low)
        to_state = d_tail * dtx
        d_b = d_b + low_dot(weight * dtx, d_state_low, NT)
        d_dtx = d_dtx + d_tail
        through = decay[BLOCK - 1 :, :] * jnp.sum(state * d_state, axis=0, keepdims=True)
        d_x = dt_wide * d_dtx + par_ref[SKIP : SKIP + 1, :] * e
        small_ref[SKIP : SKIP + 1, :] += jnp.sum(x * e, axis=0, keepdims=True)
        dconv_ref[rows, :] = dconv_ref[rows, :] * d_x
        spot = pl.ds(pl.multiple_of(origin + number * BLOCK, BLOCK), BLOCK)
        dbc_ref[spot, :LANES] += d_b
        dbc_ref[spot, LANES:] += d_c
        owner = (iota((TILE, 8), 0) // WIDTH == iota((TILE, 8), 1)).astype(BF16)

        def head_sum(a):
            return sum(dot(part, owner) for part in halves(a))

        after = (down <= across).astype(BF16)
        prior = (down > across).astype(BF16)
        run = sum(dot(after, part) for part in halves(head_sum(from_state)))
        run = run + sum(dot(prior, part) for part in halves(head_sum(to_state)))
        run = run + head_sum(jnp.broadcast_to(through, (8, TILE)))[:1]
        step_col_ref[rows, 0:8] = run
        step_col_ref[rows, 8:16] = head_sum(d_dtx * x)
        step_row_ref[:, rows] = jnp.concatenate(between + between, axis=0)
        return carried

    lax.fori_loop(0, blocks, one_block, 0)
    v, d_conv = z_ref[:, TILE:], dconv_ref[...]
    d_v = par_ref[TAPS + 3 : TAPS + 4, :] * d_conv
    small_ref[TAPS + 3 : TAPS + 4, :] = jnp.sum(d_conv * v, axis=0, keepdims=True)
    small_ref[BIAS : BIAS + 1, :] = jnp.sum(d_conv, axis=0, keepdims=True)
    for offset in range(1, 4):
        place = TAPS + 3 - offset
        counted = d_conv * col_ref[:, VALID + offset - 1 : VALID + offset]
        small_ref[place : place + 1, :] = jnp.sum(
            counted * pltpu.roll(v, offset, 0), axis=0, keepdims=True
        )
        d_v = d_v + par_ref[place : place + 1, :] * pltpu.roll(counted, length - offset, 0)
    grad_ref[:, TILE : 2 * TILE] = d_v.astype(BF16)
    for number in range(blocks):
        rows = slice(number * BLOCK, (number + 1) * BLOCK)
        spot = pl.ds(pl.multiple_of(origin + number * BLOCK, BLOCK), BLOCK)
        turn_ref[:, spot] = grad_ref[rows, :].T


def backward_kernel(
    normed_ref, cot_ref, z_ref, y_ref, dyn_ref, bc_ref, wide_ref, pick_ref, col_ref, row_ref, seg_ref,
    turned_ref, norm_ref, par_ref, state_ref,
    grad_ref, dbc_ref, step_row_ref, step_col_ref, small_ref, far_out_ref, near_out_ref, total_ref,
    turn_ref, xs_ref, dconv_ref, carry_ref, stream_ref, far_ref, near_ref, y_recv_ref, z_send_ref, z_own_ref,
    z_recv_ref, stream_sem, out_sem, y_send_sem, y_recv_sem, z_send_sem, z_recv_sem,
    *, inside, tiles, spans,
):
    tile, sequence = pl.program_id(0), pl.program_id(1)
    length = xs_ref.shape[0]
    parts = turn_ref.shape[0], near_ref.shape[2]
    halves_of = near_ref.shape[0]
    dp, mp = lax.axis_index("dp"), lax.axis_index("mp")

    def partner(bits):
        return (jnp.bitwise_xor(dp, bits), mp)

    def y_copy(number, part):
        slot = lax.rem(number, 2)
        return pltpu.make_async_remote_copy(
            src_ref=far_ref.at[part],
            dst_ref=y_recv_ref.at[slot, part],
            send_sem=y_send_sem.at[part],
            recv_sem=y_recv_sem.at[slot, part],
            device_id=partner(2),
            device_id_type=pl.DeviceIdType.MESH,
        )

    def z_copy(number, k):
        slot = lax.rem(number, 2)
        return pltpu.make_async_remote_copy(
            src_ref=z_send_ref.at[k - 1],
            dst_ref=z_recv_ref.at[slot, k - 1],
            send_sem=z_send_sem.at[k - 1],
            recv_sem=z_recv_sem.at[slot, k - 1],
            device_id=partner(4 * k),
            device_id_type=pl.DeviceIdType.MESH,
        )

    def finish(number):
        slot = lax.rem(number, 2)
        total = z_own_ref[...]
        for k in range(1, spans):
            z_copy(number, k).wait()
            total = total + z_recv_ref[slot, k - 1].astype(F32)
        total_ref[number] = total

    def pass_on(number):
        slot = lax.rem(number, 2)
        for part in range(spans):
            y_copy(number, part).wait()
            whole_part = near_ref[part] + y_recv_ref[slot, part].astype(F32)
            if part == 0:
                z_own_ref[...] = whole_part
            else:
                z_send_ref[part - 1] = whole_part.astype(BF16)
                z_copy(number, part).start()

    @pl.when((tile == 0) & (sequence == 0))
    def _():
        dbc_ref[...] = jnp.zeros_like(dbc_ref)
        if inside:
            barrier = pltpu.get_barrier_semaphore()
            others = [2] + [4 * k for k in range(1, spans)]
            for bits in others:
                pl.semaphore_signal(
                    barrier, inc=1, device_id=partner(bits), device_id_type=pl.DeviceIdType.MESH
                )
            pl.semaphore_wait(barrier, len(others))

    if inside > 1:

        @pl.when((sequence == 1) & (tile >= 2) & (tile < inside + 2))
        def _():
            finish(tile - 2)

    if inside:

        @pl.when((sequence == 1) & (tile >= 1) & (tile < inside + 1))
        def _():
            pass_on(tile - 1)

    backward_tile(
        sequence * length, z_ref, y_ref, dyn_ref, bc_ref, wide_ref, pick_ref, col_ref, row_ref, seg_ref,
        turned_ref, norm_ref, par_ref, state_ref, grad_ref, dbc_ref, step_row_ref, step_col_ref, small_ref,
        turn_ref, xs_ref, dconv_ref, carry_ref,
    )

    def fetch(number, slot):
        lanes = pl.ds(pl.multiple_of(number * parts[1], LANES), parts[1])
        return [
            pltpu.make_async_copy(ref.at[:, lanes], stream_ref.at[slot, at], stream_sem.at[slot, at])
            for at, ref in enumerate((normed_ref, cot_ref))
        ]

    def out_copies():
        place = tile - inside
        return [
            pltpu.make_async_copy(far_ref, far_out_ref.at[place], out_sem.at[0]),
            pltpu.make_async_copy(near_ref, near_out_ref.at[place], out_sem.at[1]),
        ]

    @pl.when(sequence == 1)
    def _():
        for copy in fetch(halves_of, 0):
            copy.start()

        def one_part(step, carried):
            number = lax.rem(step + halves_of, 2 * halves_of)
            slot = lax.rem(step, 2)

            @pl.when(step + 1 < 2 * halves_of)
            def _():
                for copy in fetch(lax.rem(step + 1 + halves_of, 2 * halves_of), lax.rem(step + 1, 2)):
                    copy.start()

            for copy in fetch(number, slot):
                copy.wait()
            upper = dot(turn_ref[: 2 * TILE, :], stream_ref[slot, 0])
            lower = dot(turn_ref[2 * TILE :, :], stream_ref[slot, 1])

            @pl.when(step < halves_of)
            def _():
                far_ref[step, : 2 * TILE, :] = upper.astype(BF16)
                far_ref[step, 2 * TILE :, :] = lower.astype(BF16)

            @pl.when(step >= halves_of)
            def _():
                near_ref[step - halves_of, : 2 * TILE, :] = upper
                near_ref[step - halves_of, 2 * TILE :, :] = lower

            return carried

        def run(first, last):
            lax.fori_loop(first, last, one_part, 0)

        run(0, halves_of)
        if inside:

            @pl.when(tile < inside)
            def _():
                for part in range(spans):
                    y_copy(tile, part).start()

        run(halves_of, 2 * halves_of)
        if inside < tiles:

            @pl.when(tile >= inside)
            def _():
                for copy in out_copies():
                    copy.start()
                for copy in out_copies():
                    copy.wait()

    if inside:

        @pl.when((sequence == 1) & (tile == tiles - 1))
        def _():
            finish(tile - 1)


def by_sequence(rows, width):
    return pl.BlockSpec((rows, width), lambda i: (i, 0))


def by_columns(rows, length):
    return pl.BlockSpec((rows, length), lambda i: (0, i))


def whole(shape):
    return pl.BlockSpec(shape, lambda i: (0,) * len(shape))


def shaped(shape, kind=F32):
    return jax.ShapeDtypeStruct(shape, kind)


def cost(flops):
    return pl.CostEstimate(flops=int(flops), bytes_accessed=10**7, transcendentals=10**6)


def run_tables(normed, weight, ids, par, head, length):
    tokens, width = normed.shape
    cols = weight.shape[1]
    return pl.pallas_call(
        table_kernel,
        grid=(tokens // length,),
        in_specs=[
            by_sequence(length, width),
            whole((width, cols)),
            by_sequence(length, 1),
            by_columns(1, length),
            whole((8, 2 * LANES)),
            whole((8, LANES)),
        ],
        out_specs=[
            by_sequence(length, 2 * LANES),
            by_sequence(length, 2 * LANES),
            by_sequence(length, LANES),
            by_sequence(length, COLS),
            by_columns(2 * HEADS, length),
            by_sequence(length, BLOCK),
            by_sequence(length, BLOCK),
        ],
        out_shape=[
            shaped((tokens, 2 * LANES)),
            shaped((tokens, 2 * LANES)),
            shaped((tokens, LANES), BF16),
            shaped((tokens, COLS)),
            shaped((2 * HEADS, tokens)),
            shaped((tokens, BLOCK)),
            shaped((tokens, BLOCK)),
        ],
        compiler_params=pltpu.CompilerParams(vmem_limit_bytes=VMEM_LIMIT),
        cost_estimate=cost(1e10),
    )(normed, weight, ids[:, None], ids[None, :], par, head)


def pick_table(tile):
    row, lane = jnp.arange(LANES)[:, None], jnp.arange(2 * TILE)[None, :]
    head = tile * GROUP + (lane % TILE) // WIDTH
    return ((row % HEADS == head) & (row // (3 * HEADS) == lane // TILE)).astype(BF16)


def run_forward(pieces, normed, cot, bc, wide, col, rows, score, par, tile, length):
    tokens, width = normed.shape
    number, blocks = tokens // length, length // BLOCK
    return pl.pallas_call(
        functools.partial(forward_kernel, pieces=len(pieces)),
        grid=(number,),
        in_specs=[whole(p.shape) for p in pieces]
        + [
            by_sequence(length, width),
            by_sequence(length, width),
            by_sequence(length, 2 * LANES),
            by_sequence(length, LANES),
            whole((LANES, 2 * TILE)),
            by_sequence(length, COLS),
            pl.BlockSpec((8, length), lambda i: (tile, i)),
            by_sequence(length, BLOCK),
            whole((8, TILE)),
        ],
        out_specs=[
            whole((width, 3 * TILE)),
            by_sequence(length, 2 * TILE),
            by_sequence(length, TILE),
            by_sequence(length, TILE),
            pl.BlockSpec((blocks, LANES, TILE), lambda i: (i, 0, 0)),
            by_columns(8, length),
        ],
        out_shape=[
            shaped((width, 3 * TILE), BF16),
            shaped((tokens, 2 * TILE)),
            shaped((tokens, TILE)),
            shaped((tokens, TILE)),
            shaped((number * blocks, LANES, TILE)),
            shaped((8, tokens)),
        ],
        scratch_shapes=[pltpu.VMEM((length, TILE), F32), pltpu.VMEM((LANES, TILE), F32)],
        compiler_params=pltpu.CompilerParams(vmem_limit_bytes=VMEM_LIMIT),
        cost_estimate=cost(2e10),
    )(*pieces, normed, cot, bc, wide, pick_table(tile), col, rows, score, par)


def run_gather(normed, cot, own, other, small_own, small_other, ids, bc_par, head_par, pars, length, spans, inner_total):
    rows, width = normed.shape
    tiles, _, cols = own.shape
    small_cols = small_own.shape[1]
    tokens, blocks = 2 * length, length // BLOCK

    def by_tile(size, count):
        return pl.BlockSpec((None, size, count), lambda j, i: (j, i, 0))

    def fixed(*shape):
        return pl.BlockSpec((None,) + shape, lambda j, i: (j,) + (0,) * len(shape))

    def constant(*shape):
        return pl.BlockSpec(shape, lambda j, i: (0,) * len(shape))

    dma = pltpu.SemaphoreType.DMA
    table_shapes = [
        ((tokens, 2 * LANES), F32),
        ((tokens, 2 * LANES), F32),
        ((tokens, LANES), BF16),
        ((tokens, COLS), F32),
        ((2 * HEADS, tokens), F32),
        ((tokens, BLOCK), F32),
    ]
    return pl.pallas_call(
        functools.partial(gather_kernel, tiles=tiles, spans=spans, inner_total=inner_total),
        grid=(tiles, 2),
        in_specs=[ANY] * 6
        + [
            constant(tokens, 1),
            constant(1, tokens),
            constant(8, 2 * LANES),
            constant(8, LANES),
            fixed(LANES, 2 * TILE),
            fixed(8, TILE),
        ],
        out_specs=[
            ANY,
            ANY,
            ANY,
            ANY,
            by_tile(length, 2 * TILE),
            by_tile(length, TILE),
            by_tile(length, TILE),
            pl.BlockSpec((None, blocks, LANES, TILE), lambda j, i: (j, i, 0, 0)),
        ]
        + [ANY] * 6
        + [constant(8, tokens)],
        out_shape=[
            shaped((tokens, width), BF16),
            shaped((tokens, width), BF16),
            shaped((tiles, width, cols), BF16),
            shaped((width, small_cols), BF16),
            shaped((tiles, tokens, 2 * TILE)),
            shaped((tiles, tokens, TILE)),
            shaped((tiles, tokens, TILE)),
            shaped((tiles, 2 * blocks, LANES, TILE)),
        ]
        + [shaped(*one) for one in table_shapes]
        + [shaped((8, tokens))],
        scratch_shapes=[
            pltpu.VMEM((tokens, width), BF16),
            pltpu.VMEM((tokens, width), BF16),
            pltpu.VMEM((tiles, width, cols), BF16),
            pltpu.VMEM((width, small_cols), BF16),
        ]
        + [pltpu.VMEM(*one) for one in table_shapes[:5]]
        + [
            pltpu.VMEM((tokens, BLOCK), F32),
            pltpu.VMEM((tokens, BLOCK), F32),
            pltpu.VMEM((8, tokens), F32),
            pltpu.VMEM((2, 8, tokens), F32),
            pltpu.VMEM((length, TILE), F32),
            pltpu.VMEM((LANES, TILE), F32),
            dma((3 + tiles,)),
            dma((9 + tiles,)),
            dma((2, 3)),
            dma((2, 3)),
            dma((1 + tiles,)),
            dma((1 + tiles,)),
            dma((1 + tiles, spans - 1)),
            dma((1 + tiles, spans - 1)),
            dma((1 + tiles, spans)),
            dma((1 + tiles, spans)),
            dma((2,)),
            dma((2,)),
        ],
        compiler_params=pltpu.CompilerParams(
            vmem_limit_bytes=VMEM_LIMIT, collective_id=2, has_side_effects=True
        ),
        cost_estimate=cost(2e11),
    )(
        normed, cot, own, other, small_own, small_other, ids[:, None], ids[None, :], bc_par, head_par,
        jnp.stack([pick_table(tile) for tile in range(tiles)]), pars,
    )


def run_backward(normed, cot, zv, y, dyn, bc, wide, col, rows, ids, turned, norms, par, state, length, spans):
    tiles, tokens = zv.shape[:2]
    width = normed.shape[1]
    number, blocks = tokens // length, length // BLOCK
    part = 2 * LANES
    near = width // part // 2
    inside = tiles - 1 if near == spans else 0

    def by_tile(size, cols):
        return pl.BlockSpec((None, size, cols), lambda j, i: (j, i, 0))

    def shared(size, cols):
        return pl.BlockSpec((size, cols), lambda j, i: (i, 0))

    def fixed(*shape):
        return pl.BlockSpec((None,) + shape, lambda j, i: (j,) + (0,) * len(shape))

    params = dict(vmem_limit_bytes=VMEM_LIMIT)
    if inside:
        params.update(collective_id=1, has_side_effects=True)
    return inside, pl.pallas_call(
        functools.partial(backward_kernel, inside=inside, tiles=tiles, spans=spans),
        grid=(tiles, number),
        in_specs=[
            ANY,
            ANY,
            by_tile(length, 2 * TILE),
            by_tile(length, TILE),
            by_tile(length, TILE),
            shared(length, 2 * LANES),
            shared(length, LANES),
            fixed(LANES, 2 * TILE),
            shared(length, COLS),
            pl.BlockSpec((8, length), lambda j, i: (j, i)),
            pl.BlockSpec((1, length), lambda j, i: (0, i)),
            shared(length, BLOCK),
            pl.BlockSpec((8, length), lambda j, i: (0, i)),
            fixed(8, TILE),
            pl.BlockSpec((None, blocks, LANES, TILE), lambda j, i: (j, i, 0, 0)),
        ],
        out_specs=[
            by_tile(length, 3 * TILE),
            pl.BlockSpec((tokens, 2 * LANES), lambda j, i: (0, 0)),
            pl.BlockSpec((8, length), lambda j, i: (j, i)),
            by_tile(length, 16),
            pl.BlockSpec((None, None, 8, TILE), lambda j, i: (j, i, 0, 0)),
            ANY,
            ANY,
            pl.BlockSpec((max(inside, 1), 3 * TILE, part), lambda j, i: (0, 0, 0)),
        ],
        out_shape=[
            shaped((tiles, tokens, 3 * TILE), BF16),
            shaped((tokens, 2 * LANES)),
            shaped((tiles * 8, tokens)),
            shaped((tiles, tokens, 16)),
            shaped((tiles, number, 8, TILE)),
            shaped((tiles - inside, near, 3 * TILE, part), BF16),
            shaped((tiles - inside, near, 3 * TILE, part)),
            shaped((max(inside, 1), 3 * TILE, part)),
        ],
        scratch_shapes=[
            pltpu.VMEM((3 * TILE, tokens), BF16),
            pltpu.VMEM((length, TILE), F32),
            pltpu.VMEM((length, TILE), F32),
            pltpu.VMEM((LANES, TILE), F32),
            pltpu.VMEM((2, 2, tokens, part), BF16),
            pltpu.VMEM((near, 3 * TILE, part), BF16),
            pltpu.VMEM((near, 3 * TILE, part), F32),
            pltpu.VMEM((2, near, 3 * TILE, part), BF16),
            pltpu.VMEM((3, 3 * TILE, part), BF16),
            pltpu.VMEM((3 * TILE, part), F32),
            pltpu.VMEM((2, 3, 3 * TILE, part), BF16),
            pltpu.SemaphoreType.DMA((2, 2)),
            pltpu.SemaphoreType.DMA((2,)),
            pltpu.SemaphoreType.DMA((near,)),
            pltpu.SemaphoreType.DMA((2, near)),
            pltpu.SemaphoreType.DMA((3,)),
            pltpu.SemaphoreType.DMA((2, 3)),
        ],
        compiler_params=pltpu.CompilerParams(**params),
        cost_estimate=cost(2e11),
    )(
        normed, cot, zv, y, dyn, bc, wide, jnp.stack([pick_table(tile) for tile in range(tiles)]), col, rows,
        ids[None, :], turned, norms, par, state,
    )


def segment_conv(inputs, taps, bias, masks):
    reach = taps.shape[0]
    result = bias[None, :] + taps[reach - 1][None, :] * inputs
    for offset in range(1, reach):
        moved = jnp.concatenate(
            [jnp.zeros((offset, inputs.shape[1]), inputs.dtype), inputs[:-offset]], axis=0
        )
        result = result + taps[reach - 1 - offset][None, :] * (
            moved * masks[:, offset - 1 : offset]
        )
    return result


def local(
    hidden_in,
    segments,
    norm_gain,
    w_zx,
    w_dt,
    w_bc,
    conv_x,
    conv_x_bias,
    conv_bc,
    conv_bc_bias,
    dt_bias,
    a_log,
    d_skip,
    gated_gain,
    w_out,
    cotangent,
):
    dp, mp = lax.axis_index("dp"), lax.axis_index("mp")
    extent = lax.axis_size("dp")
    far = extent // 4
    x_side = lax.rem(dp, 2)
    rows, width = hidden_in.shape
    length = segments.shape[0]
    inner = conv_x.shape[1]
    inner_total = inner * lax.axis_size("mp")
    heads = dt_bias.shape[0]
    quarter, own_heads = inner // 2, heads // 2
    tiles = quarter // TILE
    depth = w_zx.shape[0]

    def by_side(own, other, axis):
        return jnp.where(
            x_side == 0,
            jnp.concatenate([own, other], axis=axis),
            jnp.concatenate([other, own], axis=axis),
        )

    def by_core(own, other, axis):
        return jnp.where(
            mp == 0,
            jnp.concatenate([own, other], axis=axis),
            jnp.concatenate([other, own], axis=axis),
        )

    def of_side(a, side, axis):
        size = a.shape[axis] // 2
        return lax.dynamic_slice_in_dim(a, side * size, size, axis)

    packed = jnp.concatenate([w_zx[:, 0], w_zx[:, 1], w_out.T], axis=1)
    packed = packed.reshape(depth, 3, 2, tiles, TILE).transpose(2, 3, 0, 1, 4)
    packed = packed.reshape(2, tiles, depth, 3 * TILE)

    def small_weights(side):
        filler = jnp.zeros((depth, LANES - own_heads), BF16)
        return jnp.concatenate([w_bc, of_side(w_dt, side, 1), filler], axis=1)

    packed_own = lax.dynamic_index_in_dim(packed, x_side, 0, False)
    packed_other = lax.dynamic_index_in_dim(packed, 1 - x_side, 0, False)

    def gathered(piece):
        near = [piece] + [flip(piece, "dp", 4 * k) for k in range(1, far)]
        return near + [flip(p, "dp", 2) for p in near]

    normed, cot, inverse_rows = input_norm(hidden_in, cotangent, norm_gain, dp, extent)

    ids = (segments, flip(segments, "dp", 1))
    ids_all = jnp.concatenate(ids, axis=0).astype(F32)
    side_bias = of_side(dt_bias, x_side, 0)
    rate = -jnp.exp(of_side(a_log, x_side, 0))
    bc_par = jnp.concatenate([conv_bc, conv_bc_bias[None], jnp.zeros((3, 2 * LANES), F32)], axis=0)
    head_par = jnp.pad(jnp.stack([side_bias, rate]), ((0, 6), (0, LANES - own_heads)))
    params = jnp.concatenate(
        [
            of_side(conv_x, x_side, 1),
            of_side(conv_x_bias, x_side, 0)[None],
            of_side(jnp.repeat(d_skip, WIDTH), x_side, 0)[None],
            of_side(gated_gain, x_side, 0)[None],
            jnp.zeros((1, quarter), F32),
        ],
        axis=0,
    )
    params = params.reshape(8, tiles, TILE).transpose(1, 0, 2)
    tokens = 2 * length
    if depth == LANES:
        (
            normed_all, cot_all, weights, bc_weight, zvs, dyns, ys, states, proj_bc, bc, wide, col, rows_all, turned, norms,
        ) = run_gather(
            normed, cot, packed_own, packed_other, small_weights(x_side), small_weights(1 - x_side), ids_all,
            bc_par, head_par, params, length, far, inner_total,
        )
    else:

        def both_sequences(a):
            near = flip(a, "dp", 1)
            return jnp.concatenate(
                [by_core(a, flip(a, "mp", 1), 0), by_core(near, flip(near, "mp", 1), 0)], axis=0
            )

        normed_all, cot_all = both_sequences(normed), both_sequences(cot)
        packed_other = flip(packed_other, "dp", 1)
        small_other = flip(small_weights(1 - x_side), "dp", 1)
        bc_weight = jnp.concatenate(gathered(by_side(small_weights(x_side), small_other, 0)), axis=0)
        proj_bc, bc, wide, col, rows_all, score, turned = run_tables(
            normed_all, bc_weight, ids_all, bc_par, head_par, length
        )
        results = []
        for tile in range(tiles):
            pieces = gathered(by_side(packed_own[tile], packed_other[tile], 0))
            results.append(
                run_forward(
                    pieces, normed_all, cot_all, bc, wide, col, rows_all, score, params[tile], tile, length
                )
            )
        weights, zvs, dyns, ys, states, sums = [jnp.stack(part) for part in zip(*results)]
        sums = jnp.sum(sums, axis=0)
        sums = sums + flip(sums, "mp", 1)
        near = flip(sums, "dp", 1)
        sums = sums + jnp.concatenate([near[:, length:], near[:, :length]], axis=1)
        norms = norm_rows(sums, inner_total)

    inside, (grads, dbc, step_rows, step_cols, smalls, far_share, near_share, inner_totals) = run_backward(
        normed_all, cot_all, zvs, ys, dyns, bc, wide, col, rows_all, ids_all, turned, norms, params, states,
        length, far,
    )

    def spread_sum(far_part, near_part):
        def arranged(a):
            return a.transpose(1, 0, 2).reshape(3 * TILE, far, 2 * depth).transpose(1, 0, 2)

        total = arranged(near_part) + arranged(flip(far_part, "dp", 2)).astype(F32)
        out = total.astype(BF16)
        total = total[0]
        for k in range(1, far):
            total = total + flip(out[k], "dp", 4 * k).astype(F32)
        return total

    totals_of = [inner_totals[tile] for tile in range(inside)]
    totals_of += [spread_sum(far_share[at], near_share[at]) for at in range(tiles - inside)]
    stacked = jnp.stack(totals_of)
    mine = of_side(stacked, x_side, 2)
    theirs = flip(of_side(stacked, 1 - x_side, 2).astype(BF16), "dp", 1).astype(F32)

    def assembled(parts):
        return parts.reshape(tiles, 3, TILE, depth).transpose(1, 0, 2, 3).reshape(3, quarter, depth)

    full = by_side(assembled(mine), assembled(theirs), 1)
    grad_zx_weight = full[:2].transpose(2, 0, 1)
    grad_out_weight = full[2]

    dbc = dbc + flip(dbc, "mp", 1)
    dbc = dbc[:length] + flip(dbc[length:], "dp", 1)
    own_masks = col[:length, VALID : VALID + 3]
    _, state_back = jax.vjp(
        lambda values, taps, bias: jax.nn.silu(segment_conv(values, taps, bias, own_masks)),
        proj_bc[:length],
        conv_bc,
        conv_bc_bias,
    )
    d_bc, grad_conv_bc, grad_conv_bc_bias = state_back(dbc)
    bc_grad = d_bc.astype(BF16)

    raw_dt = rows_all.reshape(tiles, 2, GROUP, tokens)[:, 1].reshape(own_heads, tokens)
    run_steps = step_cols.transpose(0, 2, 1)
    steps = (step_rows.reshape(tiles, 8, tokens)[:, :GROUP] + run_steps[:, :GROUP]).reshape(own_heads, tokens)
    direct = run_steps[:, 8 : 8 + GROUP].reshape(own_heads, tokens)
    d_dt = (direct + rate[:, None] * steps) * jax.nn.sigmoid(raw_dt)
    grad_dt_bias = jnp.sum(d_dt, axis=1)
    grad_a_log = jnp.sum(steps * jax.nn.softplus(raw_dt), axis=1) * rate
    dt_grad = d_dt.T.astype(BF16)

    def placed(a):
        zero = jnp.zeros_like(a)
        return by_side(a, zero, a.ndim - 1)

    small_grad = jnp.concatenate(
        [
            dot(normed_all[:length], lax.dynamic_slice_in_dim(bc_grad, mp * LANES, LANES, 1), TN),
            placed(dot(normed_all, dt_grad, TN)),
        ],
        axis=1,
    )
    small_grad = small_grad.reshape(2 * far, 2, depth, -1)
    small_grad = of_side(small_grad, x_side, 1) + flip(
        of_side(small_grad, 1 - x_side, 1).astype(BF16), "dp", 1
    ).astype(F32)
    small_grad = small_grad.reshape(2, far, depth, -1)
    small_grad = small_grad[0] + flip(small_grad[1].astype(BF16), "dp", 2).astype(F32)
    out = small_grad.astype(BF16)
    small_grad = small_grad[0]
    for k in range(1, far):
        small_grad = small_grad + flip(out[k], "dp", 4 * k).astype(F32)
    grad_dt_weight = small_grad[:, LANES:]
    own_bc = small_grad[:, :LANES]
    grad_bc_weight = by_core(own_bc, flip(own_bc, "mp", 1), 1)

    def token_sum(products):
        def part(core):
            return products(lambda a: of_side(a.reshape(2, 2, rows, -1), core, 1).reshape(2 * rows, -1))

        total = part(mp) + flip(part(1 - mp).astype(BF16), "mp", 1).astype(F32)
        return total[:rows] + flip(total[rows:].astype(BF16), "dp", 1).astype(F32)

    out_all = jnp.concatenate([w[:, 2 * TILE :] for w in weights], axis=1)
    yn_all = jnp.concatenate([g[:, 2 * TILE :] for g in grads], axis=1)
    mixer_out = restore_order(token_sum(lambda pick: dot(pick(yn_all), out_all, NT)), dp, extent)
    inputs = hidden_in.astype(F32)
    residual_out = (inputs + mixer_out).astype(BF16)
    usable = (lax.dynamic_slice_in_dim(segments, mp * rows, rows, 0) >= 0).astype(F32)[:, None]
    totals = jnp.stack(
        [
            jnp.sum(usable * inputs * inputs),
            jnp.sum(usable * mixer_out * mixer_out),
            jnp.sum(usable),
        ]
    )

    zv_all = jnp.concatenate([w[:, : 2 * TILE] for w in weights], axis=1)
    dt_weight = bc_weight[:, 2 * LANES : 2 * LANES + own_heads]
    dzx_all = jnp.concatenate([g[:, : 2 * TILE] for g in grads], axis=1)
    d_normed = token_sum(
        lambda pick: dot(pick(dzx_all), zv_all, NT) + dot(pick(dt_grad), dt_weight, NT)
    )
    d_normed = d_normed + dot(
        lax.dynamic_slice_in_dim(bc_grad, mp * rows, rows, 0), bc_weight[:, : 2 * LANES], NT
    )
    d_normed = restore_order(d_normed, dp, extent)
    grad_norm_gain = jnp.sum(d_normed * inputs * inverse_rows, axis=0)
    inverse_cube_rows = inverse_rows * inverse_rows * inverse_rows
    input_grad = (
        cotangent.astype(F32)
        + inverse_rows * norm_gain * d_normed
        - inputs
        * inverse_cube_rows
        * jnp.mean(inputs * norm_gain * d_normed, axis=-1, keepdims=True)
    )

    def summed(a, axes):
        for axis in axes:
            bit = 1
            while bit < lax.axis_size(axis):
                a = a + flip(a, axis, bit)
                bit *= 2
        return a

    small = jnp.sum(smalls, axis=1).transpose(1, 0, 2).reshape(8, quarter)
    channel = placed(small[: GAIN + 1])
    skip_grad = jnp.sum(channel[SKIP].reshape(heads, WIDTH), axis=1)
    pieces = [
        channel[TAPS:BIAS],
        channel[BIAS],
        grad_conv_bc,
        grad_conv_bc_bias,
        placed(grad_dt_bias),
        placed(grad_a_log),
        skip_grad,
        channel[GAIN],
    ]
    flat = summed(jnp.concatenate([p.reshape(-1) for p in pieces]), ("dp",))
    small_sums, start = [], 0
    for piece in pieces:
        small_sums.append(flat[start : start + piece.size].reshape(piece.shape))
        start += piece.size
    last = summed(jnp.concatenate([grad_norm_gain, totals]), ("mp", "dp"))
    grad_norm_gain = last[:width]
    sum_inputs, sum_mixer, usable_count = last[width], last[width + 1], last[width + 2]
    rms_residual = jnp.sqrt(sum_inputs / (usable_count * width))
    rms_mixer = jnp.sqrt(sum_mixer / (usable_count * width))
    return (
        residual_out,
        input_grad,
        grad_norm_gain,
        grad_zx_weight,
        grad_dt_weight,
        grad_bc_weight,
        small_sums[0],
        small_sums[1],
        small_sums[2],
        small_sums[3],
        small_sums[4],
        small_sums[5],
        small_sums[6],
        small_sums[7],
        grad_out_weight,
        rms_residual,
        rms_mixer,
    )


def solution(mesh):
    in_specs = (
        P(("dp", "mp"), None),
        P("dp"),
        P(),
        P("dp", None, "mp"),
        P("dp", "mp"),
        P("dp", None),
        P(None, "mp"),
        P("mp"),
        P(),
        P(),
        P("mp"),
        P("mp"),
        P("mp"),
        P("mp"),
        P("mp", "dp"),
        P(("dp", "mp"), None),
    )
    out_specs = (
        P(("dp", "mp"), None),
        P(("dp", "mp"), None),
        P(),
        P("dp", None, "mp"),
        P("dp", "mp"),
        P("dp", None),
        P(None, "mp"),
        P("mp"),
        P(),
        P(),
        P("mp"),
        P("mp"),
        P("mp"),
        P("mp"),
        P("mp", "dp"),
        P(),
        P(),
    )
    return jax.shard_map(local, mesh=mesh, in_specs=in_specs, out_specs=out_specs, check_vma=False)
```

```python
import functools

import jax
import jax.numpy as jnp
from jax import lax
from jax.experimental import pallas as pl
from jax.experimental.pallas import tpu as pltpu
from jax.sharding import PartitionSpec as P

BLOCK = 256
LANES = 128
TILE = 256
WIDTH = 64
GROUP = TILE // WIDTH
EPSILON = 1e-05
HIGH = lax.Precision.HIGHEST
BF16 = jnp.bfloat16
F32 = jnp.float32
VMEM_LIMIT = 58 * 2**20

NN = (((1,), (0,)), ((), ()))
NT = (((1,), (1,)), ((), ()))
TN = (((0,), (0,)), ((), ()))


def dot(a, b, dims=NN, precision=None):
    return lax.dot_general(a, b, dims, precision=precision, preferred_element_type=F32)


def low_dot(a, b, dims=NN):
    return dot(a.astype(BF16), b.astype(BF16), dims)


def flip(a, axis, bit):
    size = lax.axis_size(axis)
    return lax.ppermute(a, axis, [(i, i ^ bit) for i in range(size)])


def sigmoid(q):
    return 1.0 / (1.0 + jnp.exp(-q))


def owner_block(number, dp, extent):
    y, z, x = number // (extent // 2), (number // 2) % (extent // 4), number % 2
    return jnp.bitwise_xor(dp - lax.rem(dp, 2), (y * 2) + (z * 4) + x)


def norm_kernel(place_ref, hidden_ref, cot_ref, gain_ref, normed_ref, cot_out_ref, inv_ref, *, extent):
    u = hidden_ref[...].astype(F32)
    inv = lax.rsqrt(jnp.mean(u * u, axis=-1, keepdims=True) + EPSILON)
    inv_ref[...] = inv
    for number in range(extent):
        start = pl.multiple_of(owner_block(number, place_ref[0], extent) * LANES, LANES)
        piece = hidden_ref[:, pl.ds(start, LANES)].astype(F32)
        gain = gain_ref[:, pl.ds(start, LANES)]
        normed_ref[:, number * LANES : (number + 1) * LANES] = (piece * inv * gain).astype(BF16)
        cot_out_ref[:, number * LANES : (number + 1) * LANES] = cot_ref[:, pl.ds(start, LANES)]


def input_norm(hidden, cot, gain, dp, extent):
    rows, width = hidden.shape
    if width // extent != LANES:
        u = hidden.astype(F32)
        inv = lax.rsqrt(jnp.mean(u * u, axis=-1, keepdims=True) + EPSILON)
        normed = (u * inv * gain).astype(BF16)
        order = owner_block(jnp.arange(extent), dp, extent)

        def arranged(a):
            return jnp.take(a.reshape(rows, extent, -1), order, axis=1).reshape(rows, width)

        return arranged(normed), arranged(cot), inv
    step = 128
    tile = pl.BlockSpec((step, width), lambda i: (i, 0))
    return pl.pallas_call(
        functools.partial(norm_kernel, extent=extent),
        grid=(rows // step,),
        in_specs=[
            pl.BlockSpec(memory_space=pltpu.SMEM),
            tile,
            tile,
            pl.BlockSpec((1, width), lambda i: (0, 0)),
        ],
        out_specs=[tile, tile, pl.BlockSpec((step, 1), lambda i: (i, 0))],
        out_shape=[
            jax.ShapeDtypeStruct((rows, width), BF16),
            jax.ShapeDtypeStruct((rows, width), BF16),
            jax.ShapeDtypeStruct((rows, 1), F32),
        ],
        compiler_params=pltpu.CompilerParams(vmem_limit_bytes=VMEM_LIMIT),
    )(dp.reshape(1), hidden, cot, gain.reshape(1, width))


def restore_kernel(place_ref, in_ref, out_ref, *, extent):
    for number in range(extent):
        start = pl.multiple_of(owner_block(number, place_ref[0], extent) * LANES, LANES)
        out_ref[:, pl.ds(start, LANES)] = in_ref[:, number * LANES : (number + 1) * LANES]


def restore_order(a, dp, extent):
    rows, width = a.shape
    if width // extent != LANES:
        order = owner_block(jnp.arange(extent), dp, extent)
        back = jnp.argsort(order)
        return jnp.take(a.reshape(rows, extent, -1), back, axis=1).reshape(rows, width)
    step = 128
    tile = pl.BlockSpec((step, width), lambda i: (i, 0))
    return pl.pallas_call(
        functools.partial(restore_kernel, extent=extent),
        grid=(rows // step,),
        in_specs=[pl.BlockSpec(memory_space=pltpu.SMEM), tile],
        out_specs=tile,
        out_shape=jax.ShapeDtypeStruct((rows, width), a.dtype),
        compiler_params=pltpu.CompilerParams(vmem_limit_bytes=VMEM_LIMIT),
    )(dp.reshape(1), a)


VALID, LINK, KEEP, SEG = 0, 3, 4, 5
COLS = 8
HEADS = 16
TAPS, BIAS, SKIP, GAIN = 0, 4, 5, 6
STEPS, OUT, SHARE = 2 * TILE, 2 * TILE + 16, 3 * TILE + 16
ANY = pl.BlockSpec(memory_space=pl.ANY)


def iota(shape, axis):
    return lax.broadcasted_iota(jnp.int32, shape, axis)


def thirds(a):
    high = a.astype(BF16)
    rest = a - high.astype(F32)
    mid = rest.astype(BF16)
    return [high, mid, (rest - mid.astype(F32)).astype(BF16)]


def halves(a):
    high = a.astype(BF16)
    return [high, (a - high.astype(F32)).astype(BF16)]


def conv_of(v, col, par_ref):
    result = par_ref[BIAS : BIAS + 1, :] + par_ref[TAPS + 3 : TAPS + 4, :] * v
    for offset in range(1, 4):
        valid = col[:, VALID + offset - 1 : VALID + offset]
        result = result + par_ref[TAPS + 3 - offset : TAPS + 4 - offset, :] * (
            pltpu.roll(v, offset, 0) * valid
        )
    return result


def pair_mask(seg_col, seg_row, transposed):
    down, across = iota((BLOCK, BLOCK), 0), iota((BLOCK, BLOCK), 1)
    causal = down <= across if transposed else down >= across
    return causal & (seg_col == seg_row)


def table_part(
    origin, length, normed_ref, weight_ref, seg_col_ref, seg_row_ref, par_ref, head_ref,
    proj_ref, bc_ref, wide_ref, col_ref, row_ref, score_ref, turned_ref,
):
    every = pl.ds(origin, length)
    blocks = length // BLOCK

    def spot(block):
        return pl.ds(pl.multiple_of(origin + block * BLOCK, BLOCK), BLOCK)

    proj = dot(normed_ref[every, :], weight_ref[...])
    proj_ref[every, :] = proj[:, : 2 * LANES]
    raw = proj[:, 2 * LANES : 2 * LANES + HEADS] + head_ref[0:1, :HEADS]
    dt = jnp.maximum(raw, 0.0) + jnp.log1p(jnp.exp(-jnp.abs(raw)))
    step = dt * head_ref[1:2, :HEADS]
    seg = seg_col_ref[every, :]
    place = iota((length, 1), 0)
    number = place // BLOCK
    before, last = jnp.full((length, 1), -2.0, F32), jnp.zeros((length, 1), F32)
    for block in range(blocks):
        end = seg[(block + 1) * BLOCK - 1 : (block + 1) * BLOCK, :]
        last = jnp.where(number == block, end, last)
        before = jnp.where(number == block + 1, end, before)
    lower = (iota((BLOCK, BLOCK), 0) >= iota((BLOCK, BLOCK), 1)).astype(F32)
    upper = (iota((BLOCK, BLOCK), 0) <= iota((BLOCK, BLOCK), 1)).astype(F32)
    eye = (iota((BLOCK, BLOCK), 0) == iota((BLOCK, BLOCK), 1)).astype(F32)
    cums = []
    for block in range(blocks):
        rows = slice(block * BLOCK, (block + 1) * BLOCK)
        cums.append(dot(lower, step[rows], NN, HIGH))
        cum_rows = dot(step[rows], upper, TN, HIGH)
        raw_rows = dot(raw[rows], eye, TN, HIGH)
        for tile in range(HEADS // GROUP):
            heads = slice(tile * GROUP, (tile + 1) * GROUP)
            row_ref[tile * 8 : (tile + 1) * 8, spot(block)] = jnp.concatenate(
                [cum_rows[heads], raw_rows[heads]], axis=0
            )
    cum = jnp.concatenate(cums, axis=0)
    lane = iota((length, COLS), 1)
    col = jnp.zeros((length, COLS), F32)
    for offset in range(1, 4):
        valid = (pltpu.roll(seg, offset, 0) == seg) & (place >= offset)
        col = jnp.where(lane == VALID + offset - 1, valid.astype(F32), col)
    col = jnp.where(lane == LINK, (seg == before).astype(F32), col)
    col = jnp.where(lane == KEEP, (seg == last).astype(F32), col)
    col = jnp.where(lane == SEG, seg, col)
    col_ref[every, :] = col
    wide_ref[every, :] = jnp.concatenate(
        thirds(dt) + thirds(cum) + [jnp.zeros((length, LANES - 6 * HEADS), BF16)], axis=1
    )
    conv = conv_of(proj[:, : 2 * LANES], col, par_ref)
    bc_ref[every, :] = conv * sigmoid(conv)
    for block in range(blocks):
        rows = slice(block * BLOCK, (block + 1) * BLOCK)
        at = spot(block)
        b_rows, c_rows = bc_ref[at, :LANES], bc_ref[at, LANES:]
        seg_col, seg_row = seg[rows], seg_row_ref[:, at]
        score_ref[at, :] = jnp.where(
            pair_mask(seg_col, seg_row, False), dot(c_rows, b_rows, NT, HIGH), 0.0
        )
        turned_ref[at, :] = jnp.where(
            pair_mask(seg_col, seg_row, True), dot(b_rows, c_rows, NT, HIGH), 0.0
        )


def table_kernel(*refs):
    table_part(0, refs[0].shape[0], *refs)


def forward_tile(
    origin, first_row, normed_ref, cot_ref, w_ref, bc_ref, wide_ref, pick_ref, col_ref, row_ref, score_ref,
    par_ref, z_ref, dyn_ref, y_ref, state_ref, sum_ref, xs_ref, carry_ref,
):
    length = xs_ref.shape[0]
    blocks = length // BLOCK

    def spot(number):
        return pl.ds(pl.multiple_of(origin + number * BLOCK, BLOCK), BLOCK)

    def project(number, carried):
        rows = pl.ds(pl.multiple_of(number * BLOCK, BLOCK), BLOCK)
        z_ref[rows, :] = dot(normed_ref[spot(number), :], w_ref[:, : 2 * TILE])
        dyn_ref[rows, :] = dot(cot_ref[spot(number), :], w_ref[:, 2 * TILE :])
        return carried

    lax.fori_loop(0, blocks, project, 0)
    conv = conv_of(z_ref[:, TILE:], col_ref[pl.ds(origin, length), :], par_ref)
    xs_ref[...] = conv * sigmoid(conv)
    carry_ref[...] = jnp.zeros_like(carry_ref)
    ones = jnp.ones((8, TILE), BF16)

    def row_sum(a):
        return sum(dot(ones, part, NT) for part in halves(a))

    def one_block(number, carried):
        rows, at = pl.ds(pl.multiple_of(number * BLOCK, BLOCK), BLOCK), spot(number)
        b_rows, c_rows = bc_ref[at, :LANES], bc_ref[at, LANES:]
        col = col_ref[at, :]
        scores = score_ref[at, :]
        x = xs_ref[rows, :]
        wide = dot(wide_ref[at, :], pick_ref[...])
        dt_wide, cum_wide = wide[:, :TILE], wide[:, TILE:]
        cum_rows = row_ref[pl.ds(first_row, 8), at]
        dtx = x * dt_wide
        dtx_low = dtx.astype(BF16)
        parts = []
        for head in range(GROUP):
            gap = cum_wide[:, head * WIDTH : head * WIDTH + 1] - cum_rows[head : head + 1, :]
            mixing = scores * jnp.exp(jnp.minimum(gap, 0.0))
            parts.append(dot(mixing.astype(BF16), dtx_low[:, head * WIDTH : (head + 1) * WIDTH]))
        within = jnp.concatenate(parts, axis=1)
        state = carry_ref[...]
        state_ref[number] = state
        decay = jnp.exp(cum_wide) * col[:, LINK : LINK + 1]
        y = within + low_dot(c_rows, state) * decay + par_ref[SKIP : SKIP + 1, :] * x
        weight = jnp.exp(cum_wide[BLOCK - 1 :, :] - cum_wide) * col[:, KEEP : KEEP + 1]
        carry_ref[...] = state * decay[BLOCK - 1 :, :] + low_dot(b_rows, dtx * weight, TN)
        y_ref[rows, :] = y
        z = z_ref[rows, :TILE]
        yg = y * z * sigmoid(z)
        first = row_sum(yg * yg)
        second = row_sum(yg * par_ref[GAIN : GAIN + 1, :] * dyn_ref[rows, :])
        place = iota((8, BLOCK), 0)
        sum_ref[:, at] += jnp.where(place == 0, first, jnp.where(place == 1, second, 0.0))
        return carried

    lax.fori_loop(0, blocks, one_block, 0)


def forward_kernel(*refs, pieces):
    normed_ref, cot_ref, bc_ref, wide_ref, pick_ref, col_ref, row_ref, score_ref, par_ref = refs[pieces : pieces + 9]
    w_ref, z_ref, dyn_ref, y_ref, state_ref, sum_ref, xs_ref, carry_ref = refs[pieces + 9 :]

    @pl.when(pl.program_id(0) == 0)
    def _():
        depth = refs[0].shape[0]
        for number in range(pieces):
            w_ref[number * depth : (number + 1) * depth, :] = refs[number][...]

    sum_ref[...] = jnp.zeros_like(sum_ref)
    forward_tile(
        0, 0, normed_ref, cot_ref, w_ref, bc_ref, wide_ref, pick_ref, col_ref, row_ref, score_ref, par_ref,
        z_ref, dyn_ref, y_ref, state_ref, sum_ref, xs_ref, carry_ref,
    )


def gather_kernel(
    normed_ref, cot_ref, own_ref, other_ref, small_own_ref, small_other_ref, seg_col_ref, seg_row_ref,
    bc_par_ref, head_ref, pick_ref, par_ref,
    normed_out, cot_out, w_out, small_out, z_ref, dyn_ref, y_ref, state_ref, proj_out, bc_out, wide_out, col_out, row_out,
    turned_out, norm_ref,
    normed_all, cot_all, w_all, small_all, proj_all, bc_all, wide_all, col_all, row_all, score_all, turned_all,
    sum_ref, sum_recv, xs_ref, carry_ref,
    here_sem, out_sem, act_send, act_recv, x_send, x_recv, z_send, z_recv, y_send, y_recv, sum_send, sum_recv_sem,
    *, tiles, spans, inner_total,
):
    tile, sequence = pl.program_id(0), pl.program_id(1)
    length = xs_ref.shape[0]
    rows = normed_ref.shape[0]
    depth = own_ref.shape[1]
    part = 2 * depth
    dp, mp = lax.axis_index("dp"), lax.axis_index("mp")
    side = lax.rem(dp, 2)
    mine = pl.ds(pl.multiple_of(mp * rows, rows), rows)
    theirs = pl.ds(pl.multiple_of(length + mp * rows, rows), rows)
    slab = pl.ds(pl.multiple_of(side * depth, depth), depth)
    other_core = (dp, 1 - mp)

    def along(bits):
        return (jnp.bitwise_xor(dp, bits), mp)

    def remote(src, dst, send, recv, device):
        return pltpu.make_async_remote_copy(
            src_ref=src, dst_ref=dst, send_sem=send, recv_sem=recv, device_id=device,
            device_id_type=pl.DeviceIdType.MESH,
        )

    arrays = ((normed_ref, normed_all), (cot_ref, cot_all))

    def act_here(a):
        return pltpu.make_async_copy(arrays[a][0], arrays[a][1].at[mine, :], here_sem.at[a])

    def act_core(a):
        return remote(
            arrays[a][0], arrays[a][1].at[mine, :], act_send.at[a, 0], act_recv.at[a, 0], other_core
        )

    def act_x(a):
        return remote(
            arrays[a][0], arrays[a][1].at[theirs, :], act_send.at[a, 1], act_recv.at[a, 1], along(1)
        )

    def act_pass(a):
        return remote(
            arrays[a][1].at[theirs, :], arrays[a][1].at[theirs, :], act_send.at[a, 2], act_recv.at[a, 2], other_core
        )

    def weight_of(number):
        return small_all if number == 0 else w_all.at[number - 1]

    def w_here(number):
        src = small_own_ref if number == 0 else own_ref.at[number - 1]
        return pltpu.make_async_copy(src, weight_of(number).at[slab, :], here_sem.at[2 + number])

    def w_x(number):
        src = small_other_ref if number == 0 else other_ref.at[number - 1]
        return remote(src, weight_of(number).at[slab, :], x_send.at[number], x_recv.at[number], along(1))

    def w_z(number, k):
        ref = weight_of(number)
        return remote(
            ref.at[pl.ds(0, part), :], ref.at[pl.ds(k * part, part), :],
            z_send.at[number, k - 1], z_recv.at[number, k - 1], along(4 * k),
        )

    def w_y(number, k):
        ref = weight_of(number)
        return remote(
            ref.at[pl.ds(k * part, part), :], ref.at[pl.ds((spans + k) * part, part), :],
            y_send.at[number, k], y_recv.at[number, k], along(2),
        )

    def begin_z(number):
        w_here(number).wait()
        w_x(number).wait_recv()
        for k in range(1, spans):
            w_z(number, k).start()
        w_y(number, 0).start()

    def begin_y(number):
        for k in range(1, spans):
            w_z(number, k).wait_recv()
            w_y(number, k).start()

    def complete(number):
        for k in range(spans):
            w_y(number, k).wait_recv()

    tables = (
        (normed_all, normed_out), (cot_all, cot_out), (proj_all, proj_out), (bc_all, bc_out),
        (wide_all, wide_out), (col_all, col_out), (row_all, row_out), (turned_all, turned_out),
        (small_all, small_out),
    )

    def table_out(at):
        return pltpu.make_async_copy(tables[at][0], tables[at][1], out_sem.at[at])

    def weight_out(number):
        return pltpu.make_async_copy(w_all.at[number], w_out.at[number], out_sem.at[len(tables) + number])

    def make_tables(origin):
        table_part(
            origin, length, normed_all, small_all, seg_col_ref, seg_row_ref, bc_par_ref, head_ref,
            proj_all, bc_all, wide_all, col_all, row_all, score_all, turned_all,
        )

    @pl.when((tile == 0) & (sequence == 0))
    def _():
        barrier = pltpu.get_barrier_semaphore()
        partners = [along(1), along(2), other_core] + [along(4 * k) for k in range(1, spans)]
        for device in partners:
            pl.semaphore_signal(barrier, inc=1, device_id=device, device_id_type=pl.DeviceIdType.MESH)
        for number in range(tiles + 1):
            w_here(number).start()
        act_here(0).start()
        act_here(1).start()
        sum_ref[...] = jnp.zeros_like(sum_ref)
        pl.semaphore_wait(barrier, len(partners))
        w_x(0).start()
        w_x(1).start()
        act_core(0).start()
        act_core(1).start()
        act_x(0).start()
        begin_z(0)
        begin_z(1)
        for number in range(2, tiles + 1):
            w_x(number).start()
        act_x(1).start()
        begin_y(0)
        begin_z(2)
        act_here(0).wait()
        act_core(0).wait_recv()
        complete(0)
        make_tables(0)
        begin_y(1)
        act_x(0).wait_recv()
        act_pass(0).start()
        act_here(1).wait()
        act_core(1).wait_recv()

    for number in range(tiles):

        @pl.when((tile == number) & (sequence == 0))
        def _(number=number):
            if number + 3 <= tiles:
                begin_z(number + 3)
            if number + 2 <= tiles:
                begin_y(number + 2)
            complete(number + 1)
            weight_out(number).start()

    @pl.when((tile == 0) & (sequence == 1))
    def _():
        act_pass(0).wait_recv()
        make_tables(length)
        act_x(1).wait_recv()
        act_pass(1).start()
        act_pass(1).wait_recv()
        for at in range(len(tables)):
            table_out(at).start()

    forward_tile(
        sequence * length, tile * 8, normed_all, cot_all, w_all.at[tile], bc_all, wide_all, pick_ref, col_all,
        row_all, score_all, par_ref, z_ref, dyn_ref, y_ref, state_ref, sum_ref, xs_ref, carry_ref,
    )

    @pl.when((tile == tiles - 1) & (sequence == 1))
    def _():
        between = remote(sum_ref, sum_recv.at[0], sum_send.at[0], sum_recv_sem.at[0], other_core)
        between.start()
        between.wait()
        sum_ref[...] += sum_recv[0]
        across = remote(sum_ref, sum_recv.at[1], sum_send.at[1], sum_recv_sem.at[1], along(1))
        across.start()
        across.wait()
        norm_ref[...] = norm_rows(
            sum_ref[...] + jnp.concatenate([sum_recv[1, :, length:], sum_recv[1, :, :length]], axis=1),
            inner_total,
        )
        for a in range(2):
            act_core(a).wait_send()
            act_x(a).wait_send()
            act_pass(a).wait_send()
        for number in range(tiles + 1):
            w_x(number).wait_send()
            for k in range(1, spans):
                w_z(number, k).wait_send()
            for k in range(spans):
                w_y(number, k).wait_send()
        for at in range(len(tables)):
            table_out(at).wait()
        for number in range(tiles):
            weight_out(number).wait()


def norm_rows(sums, inner_total):
    inverse = lax.rsqrt(sums[0:1] / inner_total + EPSILON)
    cross = inverse * inverse * inverse / inner_total * sums[1:2]
    return jnp.concatenate([inverse, cross, jnp.zeros((6, sums.shape[1]), F32)], axis=0)


def backward_tile(
    origin, z_ref, y_ref, dyn_ref, bc_ref, wide_ref, pick_ref, col_ref, row_ref, seg_ref, turned_ref, norm_ref,
    par_ref, rate_ref, state_ref, grad_ref, dbc_ref, dt_ref, head_ref, small_ref, turn_ref, xs_ref, dconv_ref,
    carry_ref,
):
    length = xs_ref.shape[0]
    blocks = length // BLOCK
    conv = conv_of(z_ref[:, TILE:], col_ref[...], par_ref)
    gate = sigmoid(conv)
    xs_ref[...] = conv * gate
    dconv_ref[...] = gate * (1.0 + conv * (1.0 - gate))
    carry_ref[...] = jnp.zeros_like(carry_ref)
    small_ref[...] = jnp.zeros_like(small_ref)
    head_ref[...] = jnp.zeros_like(head_ref)
    down, across = iota((BLOCK, BLOCK), 0), iota((BLOCK, BLOCK), 1)

    def one_block(step, carried):
        number = blocks - 1 - step
        rows = pl.ds(pl.multiple_of(number * BLOCK, BLOCK), BLOCK)
        col = col_ref[rows, :]
        z, y, dyn = z_ref[rows, :TILE], y_ref[rows, :], dyn_ref[rows, :]
        gain = par_ref[GAIN : GAIN + 1, :]
        norms = dot(norm_ref[:, rows], (iota((8, 8), 0) == iota((8, 8), 1)).astype(F32), TN, HIGH)
        inv, cross = norms[:, 0:1], norms[:, 1:2]
        gate = sigmoid(z)
        silu = z * gate
        yg = y * silu
        yg_inv = yg * inv
        d_yg = inv * gain * dyn - yg * cross
        grad_ref[rows, :TILE] = (d_yg * y * (gate * (1.0 + z * (1.0 - gate)))).astype(BF16)
        grad_ref[rows, 2 * TILE :] = (yg_inv * gain).astype(BF16)
        small_ref[GAIN : GAIN + 1, :] += jnp.sum(dyn * yg_inv, axis=0, keepdims=True)
        e = d_yg * silu
        b_rows, c_rows = bc_ref[rows, :LANES], bc_ref[rows, LANES:]
        b_low, c_low = b_rows.astype(BF16), c_rows.astype(BF16)
        scores = turned_ref[rows, :]
        x = xs_ref[rows, :]
        wide = dot(wide_ref[rows, :], pick_ref[...])
        dt_wide, cum_wide = wide[:, :TILE], wide[:, TILE:]
        dtx = x * dt_wide
        dtx_low, e_low = dtx.astype(BF16), e.astype(BF16)
        reach = (down >= across).astype(BF16)
        d_scores = jnp.zeros((BLOCK, BLOCK), F32)
        parts, between = [], []
        for head in range(GROUP):
            lanes = slice(head * WIDTH, (head + 1) * WIDTH)
            gap = row_ref[head : head + 1, rows] - cum_wide[:, head * WIDTH : head * WIDTH + 1]
            decay = jnp.exp(jnp.minimum(gap, 0.0))
            mixing = scores * decay
            parts.append(dot(mixing.astype(BF16), e_low[:, lanes]))
            d_mixing = dot(dtx_low[:, lanes], e_low[:, lanes], NT)
            d_scores = d_scores + d_mixing * decay
            later = dot((d_mixing * mixing).astype(BF16), reach)
            between.append(jnp.sum(jnp.where(down < across, later, 0.0), axis=0, keepdims=True))
        d_dtx = jnp.concatenate(parts, axis=1)
        mask = pair_mask(col[:, SEG : SEG + 1], seg_ref[:, rows], True)
        d_scores = jnp.where(mask, d_scores, 0.0).astype(BF16)
        d_b = dot(d_scores, c_low)
        d_c = dot(d_scores, b_low, TN)
        state, d_state = state_ref[number], carry_ref[...]
        state_low, d_state_low = state.astype(BF16), d_state.astype(BF16)
        decay = jnp.exp(cum_wide) * col[:, LINK : LINK + 1]
        e_in = e * decay
        e_in_low = e_in.astype(BF16)
        from_state = e_in * dot(c_low, state_low)
        d_c = d_c + dot(e_in_low, state_low, NT)
        carry_ref[...] = decay[BLOCK - 1 :, :] * d_state + dot(c_low, e_in_low, TN)
        weight = jnp.exp(cum_wide[BLOCK - 1 :, :] - cum_wide) * col[:, KEEP : KEEP + 1]
        d_tail = weight * dot(b_low, d_state_low)
        to_state = d_tail * dtx
        d_b = d_b + low_dot(weight * dtx, d_state_low, NT)
        d_dtx = d_dtx + d_tail
        through = decay[BLOCK - 1 :, :] * jnp.sum(state * d_state, axis=0, keepdims=True)
        d_x = dt_wide * d_dtx + par_ref[SKIP : SKIP + 1, :] * e
        small_ref[SKIP : SKIP + 1, :] += jnp.sum(x * e, axis=0, keepdims=True)
        dconv_ref[rows, :] = dconv_ref[rows, :] * d_x
        spot = pl.ds(pl.multiple_of(origin + number * BLOCK, BLOCK), BLOCK)
        dbc_ref[spot, :LANES] += d_b
        dbc_ref[spot, LANES:] += d_c
        owner = (iota((TILE, 8), 0) // WIDTH == iota((TILE, 8), 1)).astype(BF16)

        def head_sum(a):
            return sum(dot(part, owner) for part in halves(a))

        after = (down <= across).astype(BF16)
        prior = (down > across).astype(BF16)
        run = sum(dot(after, part) for part in halves(head_sum(from_state)))
        run = run + sum(dot(prior, part) for part in halves(head_sum(to_state)))
        run = run + head_sum(jnp.broadcast_to(through, (8, TILE)))[:1]
        sums = jnp.concatenate(
            [run, head_sum(d_dtx * x), jnp.zeros((BLOCK, LANES - 16), F32)], axis=1
        ).T
        run_rows = sums[:GROUP] + jnp.concatenate(between, axis=0)
        raw = row_ref[GROUP : 2 * GROUP, rows]
        d_dt = (sums[8 : 8 + GROUP] + rate_ref[:GROUP, :1] * run_rows) * sigmoid(raw)
        dt = jnp.maximum(raw, 0.0) + jnp.log1p(jnp.exp(-jnp.abs(raw)))
        head_ref[:GROUP, :] += jnp.sum(d_dt, axis=1, keepdims=True)
        head_ref[GROUP:, :] += jnp.sum(run_rows * dt, axis=1, keepdims=True)
        d_dt = jnp.concatenate([d_dt, jnp.zeros((16 - GROUP, BLOCK), F32)], axis=0).astype(BF16)
        dt_ref[:, rows] = d_dt
        turn_ref[STEPS:OUT, spot] = d_dt
        return carried

    lax.fori_loop(0, blocks, one_block, 0)
    v, d_conv = z_ref[:, TILE:], dconv_ref[...]
    d_v = par_ref[TAPS + 3 : TAPS + 4, :] * d_conv
    small_ref[TAPS + 3 : TAPS + 4, :] = jnp.sum(d_conv * v, axis=0, keepdims=True)
    small_ref[BIAS : BIAS + 1, :] = jnp.sum(d_conv, axis=0, keepdims=True)
    for offset in range(1, 4):
        place = TAPS + 3 - offset
        counted = d_conv * col_ref[:, VALID + offset - 1 : VALID + offset]
        small_ref[place : place + 1, :] = jnp.sum(
            counted * pltpu.roll(v, offset, 0), axis=0, keepdims=True
        )
        d_v = d_v + par_ref[place : place + 1, :] * pltpu.roll(counted, length - offset, 0)
    grad_ref[:, TILE : 2 * TILE] = d_v.astype(BF16)
    for number in range(blocks):
        rows = slice(number * BLOCK, (number + 1) * BLOCK)
        spot = pl.ds(pl.multiple_of(origin + number * BLOCK, BLOCK), BLOCK)
        turned = grad_ref[rows, :].T
        turn_ref[:STEPS, spot] = turned[: 2 * TILE]
        turn_ref[OUT:, spot] = turned[2 * TILE :]


def backward_kernel(*refs, ties, inside, tiles, spans):
    (
        normed_ref, cot_ref, z_ref, y_ref, dyn_ref, bc_ref, wide_ref, pick_ref, col_ref, row_ref, seg_ref,
        turned_ref, norm_ref, par_ref, rate_ref, state_ref,
        grad_ref, dbc_ref, dt_ref, head_ref, small_ref, far_out_ref, near_out_ref, total_ref,
        turn_ref, xs_ref, dconv_ref, carry_ref, stream_ref, far_ref, near_ref, y_recv_ref, z_send_ref, z_own_ref,
        z_recv_ref, stream_sem, out_sem, y_send_sem, y_recv_sem, z_send_sem, z_recv_sem,
    ) = refs[ties:]
    tile, sequence = pl.program_id(0), pl.program_id(1)
    length = xs_ref.shape[0]
    parts = turn_ref.shape[0], near_ref.shape[2]
    halves_of = near_ref.shape[0]
    dp, mp = lax.axis_index("dp"), lax.axis_index("mp")

    def partner(bits):
        return (jnp.bitwise_xor(dp, bits), mp)

    def y_copy(number, part):
        slot = lax.rem(number, 2)
        return pltpu.make_async_remote_copy(
            src_ref=far_ref.at[part],
            dst_ref=y_recv_ref.at[slot, part],
            send_sem=y_send_sem.at[part],
            recv_sem=y_recv_sem.at[slot, part],
            device_id=partner(2),
            device_id_type=pl.DeviceIdType.MESH,
        )

    def z_copy(number, k):
        slot = lax.rem(number, 2)
        return pltpu.make_async_remote_copy(
            src_ref=z_send_ref.at[k - 1],
            dst_ref=z_recv_ref.at[slot, k - 1],
            send_sem=z_send_sem.at[k - 1],
            recv_sem=z_recv_sem.at[slot, k - 1],
            device_id=partner(4 * k),
            device_id_type=pl.DeviceIdType.MESH,
        )

    def finish(number):
        slot = lax.rem(number, 2)
        total = z_own_ref[...]
        for k in range(1, spans):
            z_copy(number, k).wait()
            total = total + z_recv_ref[slot, k - 1].astype(F32)
        total_ref[number] = total

    def pass_on(number):
        slot = lax.rem(number, 2)
        for part in range(spans):
            y_copy(number, part).wait()
            whole_part = near_ref[part] + y_recv_ref[slot, part].astype(F32)
            if part == 0:
                z_own_ref[...] = whole_part
            else:
                z_send_ref[part - 1] = whole_part.astype(BF16)
                z_copy(number, part).start()

    @pl.when((tile == 0) & (sequence == 0))
    def _():
        dbc_ref[...] = jnp.zeros_like(dbc_ref)
        if inside:
            barrier = pltpu.get_barrier_semaphore()
            others = [2] + [4 * k for k in range(1, spans)]
            for bits in others:
                pl.semaphore_signal(
                    barrier, inc=1, device_id=partner(bits), device_id_type=pl.DeviceIdType.MESH
                )
            pl.semaphore_wait(barrier, len(others))

    if inside > 1:

        @pl.when((sequence == 1) & (tile >= 2) & (tile < inside + 2))
        def _():
            finish(tile - 2)

    if inside:

        @pl.when((sequence == 1) & (tile >= 1) & (tile < inside + 1))
        def _():
            pass_on(tile - 1)

    backward_tile(
        sequence * length, z_ref, y_ref, dyn_ref, bc_ref, wide_ref, pick_ref, col_ref, row_ref, seg_ref,
        turned_ref, norm_ref, par_ref, rate_ref, state_ref, grad_ref, dbc_ref, dt_ref, head_ref, small_ref,
        turn_ref, xs_ref, dconv_ref, carry_ref,
    )

    def fetch(number, slot):
        lanes = pl.ds(pl.multiple_of(number * parts[1], LANES), parts[1])
        return [
            pltpu.make_async_copy(ref.at[:, lanes], stream_ref.at[slot, at], stream_sem.at[slot, at])
            for at, ref in enumerate((normed_ref, cot_ref))
        ]

    def out_copies():
        place = tile - inside
        return [
            pltpu.make_async_copy(far_ref, far_out_ref.at[place], out_sem.at[0]),
            pltpu.make_async_copy(near_ref, near_out_ref.at[place], out_sem.at[1]),
        ]

    @pl.when(sequence == 1)
    def _():
        for copy in fetch(halves_of, 0):
            copy.start()

        def one_part(step, carried):
            number = lax.rem(step + halves_of, 2 * halves_of)
            slot = lax.rem(step, 2)

            @pl.when(step + 1 < 2 * halves_of)
            def _():
                for copy in fetch(lax.rem(step + 1 + halves_of, 2 * halves_of), lax.rem(step + 1, 2)):
                    copy.start()

            for copy in fetch(number, slot):
                copy.wait()
            upper = dot(turn_ref[:OUT, :], stream_ref[slot, 0])
            lower = dot(turn_ref[OUT:, :], stream_ref[slot, 1])

            @pl.when(step < halves_of)
            def _():
                far_ref[step, :OUT, :] = upper.astype(BF16)
                far_ref[step, OUT:, :] = lower.astype(BF16)

            @pl.when(step >= halves_of)
            def _():
                near_ref[step - halves_of, :OUT, :] = upper
                near_ref[step - halves_of, OUT:, :] = lower

            return carried

        def run(first, last):
            lax.fori_loop(first, last, one_part, 0)

        run(0, halves_of)
        if inside:

            @pl.when(tile < inside)
            def _():
                for part in range(spans):
                    y_copy(tile, part).start()

        run(halves_of, 2 * halves_of)
        if inside < tiles:

            @pl.when(tile >= inside)
            def _():
                for copy in out_copies():
                    copy.start()
                for copy in out_copies():
                    copy.wait()

    if inside:

        @pl.when((sequence == 1) & (tile == tiles - 1))
        def _():
            finish(tile - 1)


def by_sequence(rows, width):
    return pl.BlockSpec((rows, width), lambda i: (i, 0))


def by_columns(rows, length):
    return pl.BlockSpec((rows, length), lambda i: (0, i))


def whole(shape):
    return pl.BlockSpec(shape, lambda i: (0,) * len(shape))


def shaped(shape, kind=F32):
    return jax.ShapeDtypeStruct(shape, kind)


def cost(flops):
    return pl.CostEstimate(flops=int(flops), bytes_accessed=10**7, transcendentals=10**6)


def run_tables(normed, weight, ids, par, head, length):
    tokens, width = normed.shape
    cols = weight.shape[1]
    return pl.pallas_call(
        table_kernel,
        grid=(tokens // length,),
        in_specs=[
            by_sequence(length, width),
            whole((width, cols)),
            by_sequence(length, 1),
            by_columns(1, length),
            whole((8, 2 * LANES)),
            whole((8, LANES)),
        ],
        out_specs=[
            by_sequence(length, 2 * LANES),
            by_sequence(length, 2 * LANES),
            by_sequence(length, LANES),
            by_sequence(length, COLS),
            by_columns(2 * HEADS, length),
            by_sequence(length, BLOCK),
            by_sequence(length, BLOCK),
        ],
        out_shape=[
            shaped((tokens, 2 * LANES)),
            shaped((tokens, 2 * LANES)),
            shaped((tokens, LANES), BF16),
            shaped((tokens, COLS)),
            shaped((2 * HEADS, tokens)),
            shaped((tokens, BLOCK)),
            shaped((tokens, BLOCK)),
        ],
        compiler_params=pltpu.CompilerParams(vmem_limit_bytes=VMEM_LIMIT),
        cost_estimate=cost(1e10),
    )(normed, weight, ids[:, None], ids[None, :], par, head)


def pick_table(tile):
    row, lane = jnp.arange(LANES)[:, None], jnp.arange(2 * TILE)[None, :]
    head = tile * GROUP + (lane % TILE) // WIDTH
    return ((row % HEADS == head) & (row // (3 * HEADS) == lane // TILE)).astype(BF16)


def run_forward(pieces, normed, cot, bc, wide, col, rows, score, par, tile, length):
    tokens, width = normed.shape
    number, blocks = tokens // length, length // BLOCK
    return pl.pallas_call(
        functools.partial(forward_kernel, pieces=len(pieces)),
        grid=(number,),
        in_specs=[whole(p.shape) for p in pieces]
        + [
            by_sequence(length, width),
            by_sequence(length, width),
            by_sequence(length, 2 * LANES),
            by_sequence(length, LANES),
            whole((LANES, 2 * TILE)),
            by_sequence(length, COLS),
            pl.BlockSpec((8, length), lambda i: (tile, i)),
            by_sequence(length, BLOCK),
            whole((8, TILE)),
        ],
        out_specs=[
            whole((width, 3 * TILE)),
            by_sequence(length, 2 * TILE),
            by_sequence(length, TILE),
            by_sequence(length, TILE),
            pl.BlockSpec((blocks, LANES, TILE), lambda i: (i, 0, 0)),
            by_columns(8, length),
        ],
        out_shape=[
            shaped((width, 3 * TILE), BF16),
            shaped((tokens, 2 * TILE)),
            shaped((tokens, TILE)),
            shaped((tokens, TILE)),
            shaped((number * blocks, LANES, TILE)),
            shaped((8, tokens)),
        ],
        scratch_shapes=[pltpu.VMEM((length, TILE), F32), pltpu.VMEM((LANES, TILE), F32)],
        compiler_params=pltpu.CompilerParams(vmem_limit_bytes=VMEM_LIMIT),
        cost_estimate=cost(2e10),
    )(*pieces, normed, cot, bc, wide, pick_table(tile), col, rows, score, par)


def run_gather(normed, cot, own, other, small_own, small_other, ids, bc_par, head_par, pars, length, spans, inner_total):
    rows, width = normed.shape
    tiles, _, cols = own.shape
    small_cols = small_own.shape[1]
    tokens, blocks = 2 * length, length // BLOCK

    def by_tile(size, count):
        return pl.BlockSpec((None, size, count), lambda j, i: (j, i, 0))

    def fixed(*shape):
        return pl.BlockSpec((None,) + shape, lambda j, i: (j,) + (0,) * len(shape))

    def constant(*shape):
        return pl.BlockSpec(shape, lambda j, i: (0,) * len(shape))

    dma = pltpu.SemaphoreType.DMA
    table_shapes = [
        ((tokens, 2 * LANES), F32),
        ((tokens, 2 * LANES), F32),
        ((tokens, LANES), BF16),
        ((tokens, COLS), F32),
        ((2 * HEADS, tokens), F32),
        ((tokens, BLOCK), F32),
    ]
    return pl.pallas_call(
        functools.partial(gather_kernel, tiles=tiles, spans=spans, inner_total=inner_total),
        grid=(tiles, 2),
        in_specs=[ANY] * 6
        + [
            constant(tokens, 1),
            constant(1, tokens),
            constant(8, 2 * LANES),
            constant(8, LANES),
            fixed(LANES, 2 * TILE),
            fixed(8, TILE),
        ],
        out_specs=[
            ANY,
            ANY,
            ANY,
            ANY,
            by_tile(length, 2 * TILE),
            by_tile(length, TILE),
            by_tile(length, TILE),
            pl.BlockSpec((None, blocks, LANES, TILE), lambda j, i: (j, i, 0, 0)),
        ]
        + [ANY] * 6
        + [constant(8, tokens)],
        out_shape=[
            shaped((tokens, width), BF16),
            shaped((tokens, width), BF16),
            shaped((tiles, width, cols), BF16),
            shaped((width, small_cols), BF16),
            shaped((tiles, tokens, 2 * TILE)),
            shaped((tiles, tokens, TILE)),
            shaped((tiles, tokens, TILE)),
            shaped((tiles, 2 * blocks, LANES, TILE)),
        ]
        + [shaped(*one) for one in table_shapes]
        + [shaped((8, tokens))],
        scratch_shapes=[
            pltpu.VMEM((tokens, width), BF16),
            pltpu.VMEM((tokens, width), BF16),
            pltpu.VMEM((tiles, width, cols), BF16),
            pltpu.VMEM((width, small_cols), BF16),
        ]
        + [pltpu.VMEM(*one) for one in table_shapes[:5]]
        + [
            pltpu.VMEM((tokens, BLOCK), F32),
            pltpu.VMEM((tokens, BLOCK), F32),
            pltpu.VMEM((8, tokens), F32),
            pltpu.VMEM((2, 8, tokens), F32),
            pltpu.VMEM((length, TILE), F32),
            pltpu.VMEM((LANES, TILE), F32),
            dma((3 + tiles,)),
            dma((9 + tiles,)),
            dma((2, 3)),
            dma((2, 3)),
            dma((1 + tiles,)),
            dma((1 + tiles,)),
            dma((1 + tiles, spans - 1)),
            dma((1 + tiles, spans - 1)),
            dma((1 + tiles, spans)),
            dma((1 + tiles, spans)),
            dma((2,)),
            dma((2,)),
        ],
        compiler_params=pltpu.CompilerParams(
            vmem_limit_bytes=VMEM_LIMIT, collective_id=2, has_side_effects=True
        ),
        cost_estimate=cost(2e11),
    )(
        normed, cot, own, other, small_own, small_other, ids[:, None], ids[None, :], bc_par, head_par,
        jnp.stack([pick_table(tile) for tile in range(tiles)]), pars,
    )


def run_backward(
    ties, normed, cot, zv, y, dyn, bc, wide, col, rows, ids, turned, norms, par, rate, state, length, spans
):
    tiles, tokens = zv.shape[:2]
    width = normed.shape[1]
    number, blocks = tokens // length, length // BLOCK
    part = 2 * LANES
    near = width // part // 2
    inside = tiles - 1 if near == spans else 0

    def by_tile(size, cols):
        return pl.BlockSpec((None, size, cols), lambda j, i: (j, i, 0))

    def shared(size, cols):
        return pl.BlockSpec((size, cols), lambda j, i: (i, 0))

    def fixed(*shape):
        return pl.BlockSpec((None,) + shape, lambda j, i: (j,) + (0,) * len(shape))

    params = dict(vmem_limit_bytes=VMEM_LIMIT)
    if inside:
        params.update(collective_id=1, has_side_effects=True)
    return inside, pl.pallas_call(
        functools.partial(backward_kernel, ties=len(ties), inside=inside, tiles=tiles, spans=spans),
        grid=(tiles, number),
        in_specs=[ANY for _ in ties]
        + [
            ANY,
            ANY,
            by_tile(length, 2 * TILE),
            by_tile(length, TILE),
            by_tile(length, TILE),
            shared(length, 2 * LANES),
            shared(length, LANES),
            fixed(LANES, 2 * TILE),
            shared(length, COLS),
            pl.BlockSpec((8, length), lambda j, i: (j, i)),
            pl.BlockSpec((1, length), lambda j, i: (0, i)),
            shared(length, BLOCK),
            pl.BlockSpec((8, length), lambda j, i: (0, i)),
            fixed(8, TILE),
            fixed(8, LANES),
            pl.BlockSpec((None, blocks, LANES, TILE), lambda j, i: (j, i, 0, 0)),
        ],
        out_specs=[
            by_tile(length, 3 * TILE),
            pl.BlockSpec((tokens, 2 * LANES), lambda j, i: (0, 0)),
            pl.BlockSpec((16, length), lambda j, i: (j, i)),
            pl.BlockSpec((None, None, 8, LANES), lambda j, i: (j, i, 0, 0)),
            pl.BlockSpec((None, None, 8, TILE), lambda j, i: (j, i, 0, 0)),
            ANY,
            ANY,
            pl.BlockSpec((max(inside, 1), SHARE, part), lambda j, i: (0, 0, 0)),
        ],
        out_shape=[
            shaped((tiles, tokens, 3 * TILE), BF16),
            shaped((tokens, 2 * LANES)),
            shaped((tiles * 16, tokens), BF16),
            shaped((tiles, number, 8, LANES)),
            shaped((tiles, number, 8, TILE)),
            shaped((tiles - inside, near, SHARE, part), BF16),
            shaped((tiles - inside, near, SHARE, part)),
            shaped((max(inside, 1), SHARE, part)),
        ],
        scratch_shapes=[
            pltpu.VMEM((SHARE, tokens), BF16),
            pltpu.VMEM((length, TILE), F32),
            pltpu.VMEM((length, TILE), F32),
            pltpu.VMEM((LANES, TILE), F32),
            pltpu.VMEM((2, 2, tokens, part), BF16),
            pltpu.VMEM((near, SHARE, part), BF16),
            pltpu.VMEM((near, SHARE, part), F32),
            pltpu.VMEM((2, near, SHARE, part), BF16),
            pltpu.VMEM((3, SHARE, part), BF16),
            pltpu.VMEM((SHARE, part), F32),
            pltpu.VMEM((2, 3, SHARE, part), BF16),
            pltpu.SemaphoreType.DMA((2, 2)),
            pltpu.SemaphoreType.DMA((2,)),
            pltpu.SemaphoreType.DMA((near,)),
            pltpu.SemaphoreType.DMA((2, near)),
            pltpu.SemaphoreType.DMA((3,)),
            pltpu.SemaphoreType.DMA((2, 3)),
        ],
        compiler_params=pltpu.CompilerParams(**params),
        cost_estimate=cost(2e11),
    )(
        *ties, normed, cot, zv, y, dyn, bc, wide, jnp.stack([pick_table(tile) for tile in range(tiles)]), col,
        rows, ids[None, :], turned, norms, par, rate, state,
    )


def mixer_kernel(place_ref, z_ref, y_ref, norm_ref, par_ref, w_ref, out_ref, *, spans):
    tiles, rows = y_ref.shape[:2]
    norms = dot(norm_ref[...], (iota((8, 8), 0) == iota((8, 8), 1)).astype(F32), TN, HIGH)
    parts = []
    for tile in range(tiles):
        z = z_ref[tile]
        yg = y_ref[tile] * (z * sigmoid(z))
        parts.append((yg * norms[:, 0:1] * par_ref[tile, GAIN : GAIN + 1, :]).astype(BF16))
    part = 2 * LANES
    for number in range(2 * spans):
        total = jnp.zeros((rows, part), F32)
        for tile in range(tiles):
            total = total + dot(parts[tile], w_ref[tile, number * part : (number + 1) * part, :], NT)
        out_ref[:, pl.ds(pair_start(number, place_ref[0], spans), part)] = total.astype(BF16)


def pair_start(number, dp, spans):
    bits = number // spans * 2 + number % spans * 4
    return pl.multiple_of(jnp.bitwise_xor(dp - lax.rem(dp, 2), bits) * LANES, 2 * LANES)


def run_mixer(place, zvs, ys, norms, params, weights, rows, spans):
    tiles, tokens, _ = ys.shape
    width = weights.shape[1]

    def at(i, place_ref):
        half = jnp.bitwise_xor(i // 2, place_ref[1])
        return i % 2 * 2 + half

    return pl.pallas_call(
        functools.partial(mixer_kernel, spans=spans),
        grid_spec=pltpu.PrefetchScalarGridSpec(
            num_scalar_prefetch=1,
            grid=(4,),
            in_specs=[
                pl.BlockSpec((tiles, rows, TILE), lambda i, p: (0, at(i, p), 0)),
                pl.BlockSpec((tiles, rows, TILE), lambda i, p: (0, at(i, p), 0)),
                pl.BlockSpec((8, rows), lambda i, p: (0, at(i, p))),
                pl.BlockSpec((tiles, 8, TILE), lambda i, p: (0, 0, 0)),
                pl.BlockSpec((tiles, width, TILE), lambda i, p: (0, 0, 2)),
            ],
            out_specs=pl.BlockSpec((None, rows, width), lambda i, p: (i, 0, 0)),
        ),
        out_shape=shaped((4, rows, width), BF16),
        compiler_params=pltpu.CompilerParams(vmem_limit_bytes=VMEM_LIMIT),
        cost_estimate=cost(1e10),
    )(place, zvs, ys, norms, params, weights)


def tail_kernel(
    hidden_ref, cot_ref, inv_ref, gain_ref, grads_hbm, weights_hbm, small_ref, dt_ref, far_hbm, near_ref,
    totals_ref, dbc_ref, proj_ref, col_ref, par_ref, normed_hbm, pack_ref, sums_ref,
    grad_out, mine_ref, theirs_ref, bc_out_ref, pack_out_ref, last_ref,
    grads_seq, wblk, acc_ref, give_ref, core_recv, own_ref, x_give, x_recv, y_recv, z_send, z_own, z_recv, w_send,
    dbc_core, dbc_x, dbc_low, dt_cols, normed_blk, bc_grad, bc_xs, bc_own, bc_xr, bc_yr, bc_zr, bc_core, pack_recv,
    last_recv,
    seq_sem, blk_sem, out_sem, core_send, core_rsem, xs_sem, xr_sem, ys_sem, yr_sem, zs_sem, zr_sem, ws_sem, wr_sem,
    ds_sem, dr_sem, bs_sem, br_sem, ps_sem, pr_sem, ls_sem, lr_sem,
    *, spans, inside, extent,
):
    tiles = grads_seq.shape[0]
    length = grads_seq.shape[1]
    rows, width = hidden_ref.shape
    part = 2 * LANES
    count = 2 * spans
    dp, mp = lax.axis_index("dp"), lax.axis_index("mp")
    side = lax.rem(dp, 2)
    ours = pl.ds(pl.multiple_of(side * LANES, LANES), LANES)
    others = pl.ds(pl.multiple_of((1 - side) * LANES, LANES), LANES)
    other_core = (dp, 1 - mp)

    def along(bits):
        return (jnp.bitwise_xor(dp, bits), mp)

    def remote(src, dst, send, recv, device):
        return pltpu.make_async_remote_copy(
            src_ref=src, dst_ref=dst, send_sem=send, recv_sem=recv, device_id=device,
            device_id_type=pl.DeviceIdType.MESH,
        )

    def lanes_of(number):
        return pl.ds(pair_start(number, dp, spans), part)

    def seq_fetch(sequence):
        return pltpu.make_async_copy(
            grads_hbm.at[:, pl.ds(sequence * length, length), pl.ds(0, 2 * TILE)], grads_seq, seq_sem.at[0]
        )

    def w_fetch(number, slot):
        at = pl.ds(pl.multiple_of(number * part, part), part)
        return pltpu.make_async_copy(
            weights_hbm.at[:, at, pl.ds(0, 2 * TILE)], wblk.at[slot], blk_sem.at[slot]
        )

    def normed_fetch(number, slot):
        at = pl.ds(pl.multiple_of(number * part, part), part)
        return pltpu.make_async_copy(
            normed_hbm.at[pl.ds(0, length), at], normed_blk.at[slot], blk_sem.at[2 + slot]
        )

    def core_copy(sequence, number):
        at = lanes_of(number)
        return remote(
            give_ref.at[:, at], core_recv.at[sequence, :, at], core_send.at[sequence, number],
            core_rsem.at[sequence, number], other_core,
        )

    def x_copy(number):
        at = lanes_of(number)
        return remote(x_give.at[:, at], x_recv.at[:, at], xs_sem.at[number], xr_sem.at[number], along(1))

    def y_copy(k):
        return remote(far_hbm.at[0, k], y_recv.at[k], ys_sem.at[k], yr_sem.at[k], along(2))

    def z_copy(k):
        return remote(z_send.at[k - 1], z_recv.at[k - 1], zs_sem.at[k - 1], zr_sem.at[k - 1], along(4 * k))

    def w_copy(tile):
        return remote(w_send.at[tile], theirs_ref.at[tile], ws_sem.at[tile], wr_sem.at[tile], along(1))

    dbc_between = remote(dbc_ref, dbc_core, ds_sem.at[0], dr_sem.at[0], other_core)
    dbc_across = remote(dbc_core.at[pl.ds(length, length), :], dbc_x, ds_sem.at[1], dr_sem.at[1], along(1))
    bc_x = remote(bc_xs, bc_xr, bs_sem.at[0], br_sem.at[0], along(1))
    bc_y = remote(bc_own.at[pl.ds(spans, spans)], bc_yr, bs_sem.at[1], br_sem.at[1], along(2))

    def bc_z(k):
        return remote(bc_own.at[k], bc_zr.at[k - 1], bs_sem.at[1 + k], br_sem.at[1 + k], along(4 * k))

    bc_between = remote(bc_own.at[0], bc_core, bs_sem.at[1 + spans], br_sem.at[1 + spans], other_core)
    bits = [1 << place for place in range(extent.bit_length() - 1)]

    def pack_copy(step):
        return remote(pack_out_ref, pack_recv.at[step], ps_sem.at[step], pr_sem.at[step], along(bits[step]))

    def pack_step(step):
        pack_copy(step).wait()
        pack_out_ref[...] += pack_recv[step]
        if step + 1 < len(bits):
            pack_copy(step + 1).start()

    def last_copy(step):
        device = along(bits[step]) if step < len(bits) else other_core
        return remote(last_ref, last_recv.at[step], ls_sem.at[step], lr_sem.at[step], device)

    def give_total(tile, total_ref):
        mine_ref[tile] = total_ref[:, ours]
        w_send[tile] = total_ref[:, others].astype(BF16)
        w_copy(tile).start()

    def products(sequence):
        dt_rows = jnp.concatenate(
            [
                dt_ref[tile * 16 : tile * 16 + GROUP, sequence * length : (sequence + 1) * length].astype(F32)
                for tile in range(tiles)
            ],
            axis=0,
        )
        dt_rows = jnp.concatenate([dt_rows, jnp.zeros((LANES - tiles * GROUP, length), F32)], axis=0)
        dt_cols[...] = dt_rows.T.astype(BF16)
        seq_fetch(sequence).wait()

        def one(number, carried):
            slot = lax.rem(number, 2)

            @pl.when(number + 1 < count)
            def _():
                w_fetch(number + 1, 1 - slot).start()

            w_fetch(number, slot).wait()
            at = pl.ds(pl.multiple_of(number * part, part), part)
            total = dot(dt_cols[...], small_ref[at, 2 * LANES :], NT)
            for tile in range(tiles):
                total = total + dot(grads_seq[tile], wblk[slot, tile], NT)
            acc_ref[...] = total
            lanes = lanes_of(number)
            away = pl.ds(pl.multiple_of((1 - mp) * rows, rows), rows)
            here = pl.ds(pl.multiple_of(mp * rows, rows), rows)
            give_ref[:, lanes] = acc_ref[away, :].astype(BF16)
            core_copy(sequence, number).start()
            own_ref[:, lanes] = acc_ref[here, :]
            return carried

        lax.fori_loop(0, count, one, 0)

    seq_fetch(1).start()
    w_fetch(0, 0).start()
    pack_out_ref[...] = pack_ref[...]
    barrier = pltpu.get_barrier_semaphore()
    partners = [along(1), along(2), other_core] + [along(4 * k) for k in range(1, spans)]
    for device in partners:
        pl.semaphore_signal(barrier, inc=1, device_id=device, device_id_type=pl.DeviceIdType.MESH)
    pl.semaphore_wait(barrier, len(partners))
    for k in range(spans):
        y_copy(k).start()
    dbc_between.start()
    pack_copy(0).start()
    for tile in range(inside):
        give_total(tile, totals_ref.at[tile])
    products(1)
    seq_fetch(0).start()
    w_fetch(0, 0).start()
    dbc_between.wait()
    dbc_core[...] += dbc_ref[...]
    dbc_across.start()
    pack_step(0)

    def pass_on(number, carried):
        core_copy(1, number).wait()
        lanes = lanes_of(number)
        x_give[:, lanes] = (own_ref[:, lanes] + core_recv[1, :, lanes].astype(F32)).astype(BF16)
        x_copy(number).start()
        return carried

    lax.fori_loop(0, count, pass_on, 0)
    products(0)
    pack_step(1)
    normed_fetch(0, 0).start()
    dbc_across.wait()
    conv = conv_of(proj_ref[...], col_ref[...], par_ref)
    gate = sigmoid(conv)
    d_conv = (dbc_core[:length, :] + dbc_x[...]) * (gate * (1.0 + conv * (1.0 - gate)))
    d_proj = par_ref[TAPS + 3 : TAPS + 4, :] * d_conv
    small = [None] * 4
    small[3] = jnp.sum(d_conv * proj_ref[...], axis=0, keepdims=True)
    for offset in range(1, 4):
        place = TAPS + 3 - offset
        counted = d_conv * col_ref[:, VALID + offset - 1 : VALID + offset]
        small[place] = jnp.sum(counted * pltpu.roll(proj_ref[...], offset, 0), axis=0, keepdims=True)
        d_proj = d_proj + par_ref[place : place + 1, :] * pltpu.roll(counted, length - offset, 0)
    small.append(jnp.sum(d_conv, axis=0, keepdims=True))
    conv_grads = jnp.concatenate(small + [jnp.zeros((3, part), F32)], axis=0)
    dbc_low[...] = d_proj.astype(BF16)
    for k in range(spans):
        y_copy(k).wait()
        total = near_ref[0, k] + y_recv[k].astype(F32)
        if k == 0:
            z_own[...] = total
        else:
            z_send[k - 1] = total.astype(BF16)
            z_copy(k).start()
    half = pl.ds(pl.multiple_of(mp * LANES, LANES), LANES)
    turned = dbc_low[:, half].T

    def bc_product(number, carried):
        slot = lax.rem(number, 2)

        @pl.when(number + 1 < count)
        def _():
            normed_fetch(number + 1, 1 - slot).start()

        normed_fetch(number, slot).wait()
        bc_grad[...] = dot(turned, normed_blk[slot])
        bc_own[number] = bc_grad[:, ours]
        bc_xs[number] = bc_grad[:, others]
        return carried

    lax.fori_loop(0, count, bc_product, 0)
    bc_x.start()
    pack_step(2)
    here = pl.ds(pl.multiple_of(mp * rows, rows), rows)

    def add_core(number, carried):
        core_copy(0, number).wait_recv()
        lanes = lanes_of(number)
        at = pl.ds(pl.multiple_of(number * part, part), part)
        own_ref[:, lanes] += core_recv[0, :, lanes].astype(F32) + dot(
            dbc_low[here, :], small_ref[at, : 2 * LANES], NT
        )
        return carried

    lax.fori_loop(0, count, add_core, 0)
    pack_step(3)
    for step in range(4, len(bits)):
        pack_step(step)
    bc_x.wait()
    bc_own[...] += bc_xr[...]
    bc_y.start()
    total = z_own[...]
    for k in range(1, spans):
        z_copy(k).wait()
        total = total + z_recv[k - 1].astype(F32)
    z_own[...] = total
    give_total(inside, z_own)
    bc_y.wait()
    bc_own[:spans] += bc_yr[...]
    for k in range(1, spans):
        bc_z(k).start()

    def add_x(number, carried):
        x_copy(number).wait_recv()
        lanes = lanes_of(number)
        own_ref[:, lanes] += x_recv[:, lanes].astype(F32)
        return carried

    lax.fori_loop(0, count, add_x, 0)
    last_ref[...] = jnp.zeros_like(last_ref)
    last_ref[:, part : 2 * part] = 0.5 * conv_grads
    last_ref[:, 2 * part : 2 * part + LANES] = sums_ref[...]
    step_rows = 64

    def finish(number, gain_sum):
        at = pl.ds(pl.multiple_of(number * step_rows, step_rows), step_rows)
        u, d_normed = hidden_ref[at, :].astype(F32), own_ref[at, :]
        inv = inv_ref[at, :]
        scaled = gain_ref[...] * d_normed
        mean = jnp.mean(u * scaled, axis=-1, keepdims=True)
        own_ref[at, :] = cot_ref[at, :].astype(F32) + inv * scaled - u * (inv * inv * inv * mean)
        return gain_sum + jnp.sum(d_normed * u * inv, axis=0, keepdims=True)

    gain_sum = lax.fori_loop(0, rows // step_rows, finish, jnp.zeros((1, width), F32))
    out = pltpu.make_async_copy(own_ref, grad_out, out_sem.at[0])
    out.start()
    for number in range(8):
        last_ref[number : number + 1, :part] = gain_sum[:, number * part : (number + 1) * part]
    for step in range(len(bits) + 1):
        last_copy(step).start()
        if step == 1:
            total = bc_own[0]
            for k in range(1, spans):
                bc_z(k).wait()
                total = total + bc_zr[k - 1]
            bc_own[0] = total
            bc_between.start()
        last_copy(step).wait()
        last_ref[...] += last_recv[step]
    bc_between.wait()
    first = jnp.where(mp == 0, 1.0, 0.0)
    bc_out_ref[:LANES, :] = first * bc_own[0] + (1.0 - first) * bc_core[...]
    bc_out_ref[LANES:, :] = (1.0 - first) * bc_own[0] + first * bc_core[...]
    for tile in range(inside + 1):
        w_copy(tile).wait()
    for number in range(count):
        core_copy(0, number).wait_send()
        x_copy(number).wait_send()
    out.wait()


def run_tail(
    hidden, cot, inv, gain, grads, weights, small, dts, far_share, near_share, totals, dbc, proj, col, bc_par,
    normed, pack, sums, length, spans, extent,
):
    rows, width = hidden.shape
    tiles, tokens = grads.shape[:2]
    part, inside = 2 * LANES, tiles - 1
    hops = extent.bit_length() - 1
    dma = pltpu.SemaphoreType.DMA

    def full(*shape):
        return pl.BlockSpec(shape, lambda i: (0,) * len(shape))

    return pl.pallas_call(
        functools.partial(tail_kernel, spans=spans, inside=inside, extent=extent),
        grid=(1,),
        in_specs=[
            full(rows, width),
            full(rows, width),
            full(rows, 1),
            full(1, width),
            ANY,
            ANY,
            full(*small.shape),
            full(*dts.shape),
            ANY,
            full(*near_share.shape),
            full(*totals.shape),
            full(*dbc.shape),
            full(length, part),
            full(length, COLS),
            full(8, part),
            ANY,
            full(*pack.shape),
            full(8, LANES),
        ],
        out_specs=[
            ANY,
            full(tiles, SHARE, LANES),
            full(tiles, SHARE, LANES),
            full(part, LANES),
            full(*pack.shape),
            full(8, 3 * part),
        ],
        out_shape=[
            shaped((rows, width)),
            shaped((tiles, SHARE, LANES)),
            shaped((tiles, SHARE, LANES), BF16),
            shaped((part, LANES)),
            shaped(pack.shape),
            shaped((8, 3 * part)),
        ],
        scratch_shapes=[
            pltpu.VMEM((tiles, length, 2 * TILE), BF16),
            pltpu.VMEM((2, tiles, part, 2 * TILE), BF16),
            pltpu.VMEM((length, part), F32),
            pltpu.VMEM((rows, width), BF16),
            pltpu.VMEM((2, rows, width), BF16),
            pltpu.VMEM((rows, width), F32),
            pltpu.VMEM((rows, width), BF16),
            pltpu.VMEM((rows, width), BF16),
            pltpu.VMEM((spans, SHARE, part), BF16),
            pltpu.VMEM((spans - 1, SHARE, part), BF16),
            pltpu.VMEM((SHARE, part), F32),
            pltpu.VMEM((spans - 1, SHARE, part), BF16),
            pltpu.VMEM((tiles, SHARE, LANES), BF16),
            pltpu.VMEM((tokens, part), F32),
            pltpu.VMEM((length, part), F32),
            pltpu.VMEM((length, part), BF16),
            pltpu.VMEM((length, LANES), BF16),
            pltpu.VMEM((2, length, part), BF16),
            pltpu.VMEM((LANES, part), F32),
            pltpu.VMEM((2 * spans, LANES, LANES), F32),
            pltpu.VMEM((2 * spans, LANES, LANES), F32),
            pltpu.VMEM((2 * spans, LANES, LANES), F32),
            pltpu.VMEM((spans, LANES, LANES), F32),
            pltpu.VMEM((spans - 1, LANES, LANES), F32),
            pltpu.VMEM((LANES, LANES), F32),
            pltpu.VMEM((hops,) + pack.shape, F32),
            pltpu.VMEM((hops + 1, 8, 3 * part), F32),
            dma((1,)),
            dma((4,)),
            dma((1,)),
            dma((2, 2 * spans)),
            dma((2, 2 * spans)),
            dma((2 * spans,)),
            dma((2 * spans,)),
            dma((spans,)),
            dma((spans,)),
            dma((spans - 1,)),
            dma((spans - 1,)),
            dma((tiles,)),
            dma((tiles,)),
            dma((2,)),
            dma((2,)),
            dma((2 + spans,)),
            dma((2 + spans,)),
            dma((hops,)),
            dma((hops,)),
            dma((hops + 1,)),
            dma((hops + 1,)),
        ],
        compiler_params=pltpu.CompilerParams(
            vmem_limit_bytes=VMEM_LIMIT, collective_id=3, has_side_effects=True
        ),
        cost_estimate=cost(1e11),
    )(
        hidden, cot, inv, gain, grads, weights, small, dts, far_share, near_share, totals, dbc, proj, col, bc_par,
        normed, pack, sums,
    )


def segment_conv(inputs, taps, bias, masks):
    reach = taps.shape[0]
    result = bias[None, :] + taps[reach - 1][None, :] * inputs
    for offset in range(1, reach):
        moved = jnp.concatenate(
            [jnp.zeros((offset, inputs.shape[1]), inputs.dtype), inputs[:-offset]], axis=0
        )
        result = result + taps[reach - 1 - offset][None, :] * (
            moved * masks[:, offset - 1 : offset]
        )
    return result


def local(
    hidden_in,
    segments,
    norm_gain,
    w_zx,
    w_dt,
    w_bc,
    conv_x,
    conv_x_bias,
    conv_bc,
    conv_bc_bias,
    dt_bias,
    a_log,
    d_skip,
    gated_gain,
    w_out,
    cotangent,
):
    dp, mp = lax.axis_index("dp"), lax.axis_index("mp")
    extent = lax.axis_size("dp")
    far = extent // 4
    x_side = lax.rem(dp, 2)
    rows, width = hidden_in.shape
    length = segments.shape[0]
    inner = conv_x.shape[1]
    inner_total = inner * lax.axis_size("mp")
    heads = dt_bias.shape[0]
    quarter, own_heads = inner // 2, heads // 2
    tiles = quarter // TILE
    depth = w_zx.shape[0]

    def by_side(own, other, axis):
        return jnp.where(
            x_side == 0,
            jnp.concatenate([own, other], axis=axis),
            jnp.concatenate([other, own], axis=axis),
        )

    def by_core(own, other, axis):
        return jnp.where(
            mp == 0,
            jnp.concatenate([own, other], axis=axis),
            jnp.concatenate([other, own], axis=axis),
        )

    def of_side(a, side, axis):
        size = a.shape[axis] // 2
        return lax.dynamic_slice_in_dim(a, side * size, size, axis)

    packed = jnp.concatenate([w_zx[:, 0], w_zx[:, 1], w_out.T], axis=1)
    packed = packed.reshape(depth, 3, 2, tiles, TILE).transpose(2, 3, 0, 1, 4)
    packed = packed.reshape(2, tiles, depth, 3 * TILE)

    def small_weights(side):
        filler = jnp.zeros((depth, LANES - own_heads), BF16)
        return jnp.concatenate([w_bc, of_side(w_dt, side, 1), filler], axis=1)

    packed_own = lax.dynamic_index_in_dim(packed, x_side, 0, False)
    packed_other = lax.dynamic_index_in_dim(packed, 1 - x_side, 0, False)

    def gathered(piece):
        near = [piece] + [flip(piece, "dp", 4 * k) for k in range(1, far)]
        return near + [flip(p, "dp", 2) for p in near]

    normed, cot, inverse_rows = input_norm(hidden_in, cotangent, norm_gain, dp, extent)

    ids = (segments, flip(segments, "dp", 1))
    ids_all = jnp.concatenate(ids, axis=0).astype(F32)
    side_bias = of_side(dt_bias, x_side, 0)
    rate = -jnp.exp(of_side(a_log, x_side, 0))
    bc_par = jnp.concatenate([conv_bc, conv_bc_bias[None], jnp.zeros((3, 2 * LANES), F32)], axis=0)
    head_par = jnp.pad(jnp.stack([side_bias, rate]), ((0, 6), (0, LANES - own_heads)))
    params = jnp.concatenate(
        [
            of_side(conv_x, x_side, 1),
            of_side(conv_x_bias, x_side, 0)[None],
            of_side(jnp.repeat(d_skip, WIDTH), x_side, 0)[None],
            of_side(gated_gain, x_side, 0)[None],
            jnp.zeros((1, quarter), F32),
        ],
        axis=0,
    )
    params = params.reshape(8, tiles, TILE).transpose(1, 0, 2)
    tokens = 2 * length
    if depth == LANES:
        (
            normed_all, cot_all, weights, bc_weight, zvs, dyns, ys, states, proj_bc, bc, wide, col, rows_all, turned, norms,
        ) = run_gather(
            normed, cot, packed_own, packed_other, small_weights(x_side), small_weights(1 - x_side), ids_all,
            bc_par, head_par, params, length, far, inner_total,
        )
    else:

        def both_sequences(a):
            near = flip(a, "dp", 1)
            return jnp.concatenate(
                [by_core(a, flip(a, "mp", 1), 0), by_core(near, flip(near, "mp", 1), 0)], axis=0
            )

        normed_all, cot_all = both_sequences(normed), both_sequences(cot)
        packed_other = flip(packed_other, "dp", 1)
        small_other = flip(small_weights(1 - x_side), "dp", 1)
        bc_weight = jnp.concatenate(gathered(by_side(small_weights(x_side), small_other, 0)), axis=0)
        proj_bc, bc, wide, col, rows_all, score, turned = run_tables(
            normed_all, bc_weight, ids_all, bc_par, head_par, length
        )
        results = []
        for tile in range(tiles):
            pieces = gathered(by_side(packed_own[tile], packed_other[tile], 0))
            results.append(
                run_forward(
                    pieces, normed_all, cot_all, bc, wide, col, rows_all, score, params[tile], tile, length
                )
            )
        weights, zvs, dyns, ys, states, sums = [jnp.stack(part) for part in zip(*results)]
        sums = jnp.sum(sums, axis=0)
        sums = sums + flip(sums, "mp", 1)
        near = flip(sums, "dp", 1)
        sums = sums + jnp.concatenate([near[:, length:], near[:, :length]], axis=1)
        norms = norm_rows(sums, inner_total)

    place = jnp.stack([dp, mp])
    inputs = hidden_in.astype(F32)
    usable = (lax.dynamic_slice_in_dim(segments, mp * rows, rows, 0) >= 0).astype(F32)[:, None]
    native = depth == LANES
    ties = []
    if native:
        mixer = run_mixer(place, zvs, ys, norms, params, weights, rows, far)
        ties = [mixer]
        mixer_near = flip(mixer[2:], "mp", 1)
        mixer_send = (mixer[1].astype(F32) + mixer_near[1].astype(F32)).astype(BF16)
        mixer_out = mixer[0].astype(F32) + mixer_near[0].astype(F32) + flip(mixer_send, "dp", 1).astype(F32)

    rate_rows = jnp.pad(rate.reshape(tiles, GROUP, 1), ((0, 0), (0, 8 - GROUP), (0, 0)))
    inside, (grads, dbc, dts, head_sums, smalls, far_share, near_share, inner_totals) = run_backward(
        ties, normed_all, cot_all, zvs, ys, dyns, bc, wide, col, rows_all, ids_all, turned, norms, params,
        jnp.broadcast_to(rate_rows, (tiles, 8, LANES)), states, length, far,
    )

    def placed(a):
        zero = jnp.zeros_like(a)
        return by_side(a, zero, a.ndim - 1)

    small = jnp.sum(smalls, axis=1).transpose(1, 0, 2).reshape(8, quarter)
    head_sums = jnp.sum(head_sums[..., 0], axis=1)
    grad_dt_bias = placed(head_sums[:, :GROUP].reshape(own_heads))
    grad_a_log = placed(head_sums[:, GROUP:].reshape(own_heads) * rate)
    channel = placed(small[: GAIN + 1])
    head_row = jnp.pad(jnp.concatenate([grad_dt_bias, grad_a_log]), (0, inner - 2 * heads))
    pack = jnp.concatenate([channel, head_row[None]], axis=0)

    def summed(a, axes):
        for axis in axes:
            bit = 1
            while bit < lax.axis_size(axis):
                a = a + flip(a, axis, bit)
                bit *= 2
        return a

    def mixer_sums(mixer_out):
        return jnp.stack(
            [
                jnp.sum(usable * inputs * inputs),
                jnp.sum(usable * mixer_out * mixer_out),
                jnp.sum(usable),
            ]
        )

    if native:
        sums = jnp.pad(mixer_sums(mixer_out)[None], ((0, 7), (0, LANES - 3)))
        input_grad, mine, theirs, grad_bc, pack, last = run_tail(
            hidden_in, cotangent, inverse_rows, norm_gain[None], grads, weights, bc_weight, dts, far_share,
            near_share, inner_totals, dbc, proj_bc, col, bc_par, normed_all, pack, sums, length, far, extent,
        )
        theirs = theirs.astype(F32)
        grad_bc_weight = grad_bc.T
        part = 2 * LANES
        grad_norm_gain = last[:, :part].reshape(width)
        grad_conv_bc, grad_conv_bc_bias = last[:4, part : 2 * part], last[4, part : 2 * part]
        totals = last[0, 2 * part : 2 * part + 3]
    else:

        def spread_sum(far_part, near_part):
            def arranged(a):
                return a.transpose(1, 0, 2).reshape(SHARE, far, 2 * depth).transpose(1, 0, 2)

            total = arranged(near_part) + arranged(flip(far_part, "dp", 2)).astype(F32)
            out = total.astype(BF16)
            total = total[0]
            for k in range(1, far):
                total = total + flip(out[k], "dp", 4 * k).astype(F32)
            return total

        stacked = jnp.stack([spread_sum(far_share[at], near_share[at]) for at in range(tiles)])
        mine = of_side(stacked, x_side, 2)
        theirs = flip(of_side(stacked, 1 - x_side, 2).astype(BF16), "dp", 1).astype(F32)

        dbc = dbc + flip(dbc, "mp", 1)
        dbc = dbc[:length] + flip(dbc[length:], "dp", 1)
        own_masks = col[:length, VALID : VALID + 3]
        _, state_back = jax.vjp(
            lambda values, taps, bias: jax.nn.silu(segment_conv(values, taps, bias, own_masks)),
            proj_bc[:length],
            conv_bc,
            conv_bc_bias,
        )
        d_bc, grad_conv_bc, grad_conv_bc_bias = state_back(dbc)
        bc_grad = d_bc.astype(BF16)
        small_grad = dot(normed_all[:length], lax.dynamic_slice_in_dim(bc_grad, mp * LANES, LANES, 1), TN)
        small_grad = small_grad.reshape(2 * far, 2, depth, -1)
        small_grad = of_side(small_grad, x_side, 1) + flip(of_side(small_grad, 1 - x_side, 1), "dp", 1)
        small_grad = small_grad.reshape(2, far, depth, -1)
        small_grad = small_grad[0] + flip(small_grad[1], "dp", 2)
        own_bc = small_grad[0]
        for k in range(1, far):
            own_bc = own_bc + flip(small_grad[k], "dp", 4 * k)
        grad_bc_weight = by_core(own_bc, flip(own_bc, "mp", 1), 1)

        def token_sum(products):
            def part(core):
                return products(
                    lambda a: of_side(a.reshape(2, 2, rows, -1), core, 1).reshape(2 * rows, -1)
                )

            total = part(mp) + flip(part(1 - mp).astype(BF16), "mp", 1).astype(F32)
            return total[:rows] + flip(total[rows:].astype(BF16), "dp", 1).astype(F32)

        out_all = jnp.concatenate([w[:, 2 * TILE :] for w in weights], axis=1)
        yn_all = jnp.concatenate([g[:, 2 * TILE :] for g in grads], axis=1)
        mixer_out = restore_order(token_sum(lambda pick: dot(pick(yn_all), out_all, NT)), dp, extent)
        zv_all = jnp.concatenate([w[:, : 2 * TILE] for w in weights], axis=1)
        dt_weight = bc_weight[:, 2 * LANES : 2 * LANES + own_heads]
        dzx_all = jnp.concatenate([g[:, : 2 * TILE] for g in grads], axis=1)
        dt_grad = dts.reshape(tiles, 16, tokens)[:, :GROUP].reshape(own_heads, tokens).T
        d_normed = token_sum(
            lambda pick: dot(pick(dzx_all), zv_all, NT) + dot(pick(dt_grad), dt_weight, NT)
        )
        d_normed = d_normed + dot(
            lax.dynamic_slice_in_dim(bc_grad, mp * rows, rows, 0), bc_weight[:, : 2 * LANES], NT
        )
        d_normed = restore_order(d_normed, dp, extent)
        grad_norm_gain = jnp.sum(d_normed * inputs * inverse_rows, axis=0)
        inverse_cube_rows = inverse_rows * inverse_rows * inverse_rows
        input_grad = (
            cotangent.astype(F32)
            + inverse_rows * norm_gain * d_normed
            - inputs
            * inverse_cube_rows
            * jnp.mean(inputs * norm_gain * d_normed, axis=-1, keepdims=True)
        )
        pack = summed(pack, ("dp",))
        conv_sums = jnp.concatenate([grad_conv_bc, grad_conv_bc_bias[None]], axis=0)
        conv_sums = summed(conv_sums, ("dp",))
        grad_conv_bc, grad_conv_bc_bias = conv_sums[:4], conv_sums[4]
        last = summed(jnp.concatenate([grad_norm_gain, mixer_sums(mixer_out)]), ("mp", "dp"))
        grad_norm_gain, totals = last[:width], last[width:]

    residual_out = (inputs + mixer_out).astype(BF16)

    def assembled(first, last_row):
        def columns(a):
            return a[:, first:last_row].reshape(-1, depth)

        return by_side(columns(mine), columns(theirs), 0)

    grad_zx_weight = jnp.stack([assembled(0, TILE).T, assembled(TILE, STEPS).T], axis=1)
    grad_dt_weight = assembled(STEPS, STEPS + GROUP).T
    grad_out_weight = assembled(OUT, SHARE)
    skip_grad = jnp.sum(pack[SKIP].reshape(heads, WIDTH), axis=1)
    sum_inputs, sum_mixer, usable_count = totals[0], totals[1], totals[2]
    rms_residual = jnp.sqrt(sum_inputs / (usable_count * width))
    rms_mixer = jnp.sqrt(sum_mixer / (usable_count * width))
    return (
        residual_out,
        input_grad,
        grad_norm_gain,
        grad_zx_weight,
        grad_dt_weight,
        grad_bc_weight,
        pack[TAPS:BIAS],
        pack[BIAS],
        grad_conv_bc,
        grad_conv_bc_bias,
        pack[GAIN + 1, :heads],
        pack[GAIN + 1, heads : 2 * heads],
        skip_grad,
        pack[GAIN],
        grad_out_weight,
        rms_residual,
        rms_mixer,
    )


def solution(mesh):
    in_specs = (
        P(("dp", "mp"), None),
        P("dp"),
        P(),
        P("dp", None, "mp"),
        P("dp", "mp"),
        P("dp", None),
        P(None, "mp"),
        P("mp"),
        P(),
        P(),
        P("mp"),
        P("mp"),
        P("mp"),
        P("mp"),
        P("mp", "dp"),
        P(("dp", "mp"), None),
    )
    out_specs = (
        P(("dp", "mp"), None),
        P(("dp", "mp"), None),
        P(),
        P("dp", None, "mp"),
        P("dp", "mp"),
        P("dp", None),
        P(None, "mp"),
        P("mp"),
        P(),
        P(),
        P("mp"),
        P("mp"),
        P("mp"),
        P("mp"),
        P("mp", "dp"),
        P(),
        P(),
    )
    return jax.shard_map(local, mesh=mesh, in_specs=in_specs, out_specs=out_specs, check_vma=False)
```

```python
import functools

import jax
import jax.numpy as jnp
from jax import lax
from jax.experimental import pallas as pl
from jax.experimental.pallas import tpu as pltpu
from jax.sharding import PartitionSpec as P

BLOCK = 256
LANES = 128
TILE = 256
WIDTH = 64
GROUP = TILE // WIDTH
EPSILON = 1e-05
HIGH = lax.Precision.HIGHEST
BF16 = jnp.bfloat16
F32 = jnp.float32
VMEM_LIMIT = 58 * 2**20

NN = (((1,), (0,)), ((), ()))
NT = (((1,), (1,)), ((), ()))
TN = (((0,), (0,)), ((), ()))


def dot(a, b, dims=NN, precision=None):
    return lax.dot_general(a, b, dims, precision=precision, preferred_element_type=F32)


def low_dot(a, b, dims=NN):
    return dot(a.astype(BF16), b.astype(BF16), dims)


def flip(a, axis, bit):
    size = lax.axis_size(axis)
    return lax.ppermute(a, axis, [(i, i ^ bit) for i in range(size)])


def sigmoid(q):
    return 1.0 / (1.0 + jnp.exp(-q))


def owner_block(number, dp, extent):
    y, z, x = number // (extent // 2), (number // 2) % (extent // 4), number % 2
    return jnp.bitwise_xor(dp - lax.rem(dp, 2), (y * 2) + (z * 4) + x)


def norm_kernel(place_ref, hidden_ref, cot_ref, gain_ref, normed_ref, cot_out_ref, inv_ref, *, extent):
    u = hidden_ref[...].astype(F32)
    inv = lax.rsqrt(jnp.mean(u * u, axis=-1, keepdims=True) + EPSILON)
    inv_ref[...] = inv
    for number in range(extent):
        start = pl.multiple_of(owner_block(number, place_ref[0], extent) * LANES, LANES)
        piece = hidden_ref[:, pl.ds(start, LANES)].astype(F32)
        gain = gain_ref[:, pl.ds(start, LANES)]
        normed_ref[:, number * LANES : (number + 1) * LANES] = (piece * inv * gain).astype(BF16)
        cot_out_ref[:, number * LANES : (number + 1) * LANES] = cot_ref[:, pl.ds(start, LANES)]


def input_norm(hidden, cot, gain, dp, extent):
    rows, width = hidden.shape
    if width // extent != LANES:
        u = hidden.astype(F32)
        inv = lax.rsqrt(jnp.mean(u * u, axis=-1, keepdims=True) + EPSILON)
        normed = (u * inv * gain).astype(BF16)
        order = owner_block(jnp.arange(extent), dp, extent)

        def arranged(a):
            return jnp.take(a.reshape(rows, extent, -1), order, axis=1).reshape(rows, width)

        return arranged(normed), arranged(cot), inv
    step = 128
    tile = pl.BlockSpec((step, width), lambda i: (i, 0))
    return pl.pallas_call(
        functools.partial(norm_kernel, extent=extent),
        grid=(rows // step,),
        in_specs=[
            pl.BlockSpec(memory_space=pltpu.SMEM),
            tile,
            tile,
            pl.BlockSpec((1, width), lambda i: (0, 0)),
        ],
        out_specs=[tile, tile, pl.BlockSpec((step, 1), lambda i: (i, 0))],
        out_shape=[
            jax.ShapeDtypeStruct((rows, width), BF16),
            jax.ShapeDtypeStruct((rows, width), BF16),
            jax.ShapeDtypeStruct((rows, 1), F32),
        ],
        compiler_params=pltpu.CompilerParams(vmem_limit_bytes=VMEM_LIMIT),
    )(dp.reshape(1), hidden, cot, gain.reshape(1, width))


def restore_kernel(place_ref, in_ref, out_ref, *, extent):
    for number in range(extent):
        start = pl.multiple_of(owner_block(number, place_ref[0], extent) * LANES, LANES)
        out_ref[:, pl.ds(start, LANES)] = in_ref[:, number * LANES : (number + 1) * LANES]


def restore_order(a, dp, extent):
    rows, width = a.shape
    if width // extent != LANES:
        order = owner_block(jnp.arange(extent), dp, extent)
        back = jnp.argsort(order)
        return jnp.take(a.reshape(rows, extent, -1), back, axis=1).reshape(rows, width)
    step = 128
    tile = pl.BlockSpec((step, width), lambda i: (i, 0))
    return pl.pallas_call(
        functools.partial(restore_kernel, extent=extent),
        grid=(rows // step,),
        in_specs=[pl.BlockSpec(memory_space=pltpu.SMEM), tile],
        out_specs=tile,
        out_shape=jax.ShapeDtypeStruct((rows, width), a.dtype),
        compiler_params=pltpu.CompilerParams(vmem_limit_bytes=VMEM_LIMIT),
    )(dp.reshape(1), a)


VALID, LINK, KEEP, SEG = 0, 3, 4, 5
COLS = 8
HEADS = 16
TAPS, BIAS, SKIP, GAIN = 0, 4, 5, 6
STEPS, OUT, SHARE = 2 * TILE, 2 * TILE + 16, 3 * TILE + 16
ANY = pl.BlockSpec(memory_space=pl.ANY)


def iota(shape, axis):
    return lax.broadcasted_iota(jnp.int32, shape, axis)


def thirds(a):
    high = a.astype(BF16)
    rest = a - high.astype(F32)
    mid = rest.astype(BF16)
    return [high, mid, (rest - mid.astype(F32)).astype(BF16)]


def halves(a):
    high = a.astype(BF16)
    return [high, (a - high.astype(F32)).astype(BF16)]


def conv_of(v, col, par_ref):
    result = par_ref[BIAS : BIAS + 1, :] + par_ref[TAPS + 3 : TAPS + 4, :] * v
    for offset in range(1, 4):
        valid = col[:, VALID + offset - 1 : VALID + offset]
        result = result + par_ref[TAPS + 3 - offset : TAPS + 4 - offset, :] * (
            pltpu.roll(v, offset, 0) * valid
        )
    return result


def pair_mask(seg_col, seg_row, transposed):
    down, across = iota((BLOCK, BLOCK), 0), iota((BLOCK, BLOCK), 1)
    causal = down <= across if transposed else down >= across
    return causal & (seg_col == seg_row)


def table_part(
    origin, length, normed_ref, weight_ref, seg_col_ref, seg_row_ref, par_ref, head_ref,
    proj_ref, bc_ref, wide_ref, col_ref, row_ref, score_ref, turned_ref,
):
    every = pl.ds(origin, length)
    blocks = length // BLOCK

    def spot(block):
        return pl.ds(pl.multiple_of(origin + block * BLOCK, BLOCK), BLOCK)

    proj = dot(normed_ref[every, :], weight_ref[...])
    proj_ref[every, :] = proj[:, : 2 * LANES]
    raw = proj[:, 2 * LANES : 2 * LANES + HEADS] + head_ref[0:1, :HEADS]
    dt = jnp.maximum(raw, 0.0) + jnp.log1p(jnp.exp(-jnp.abs(raw)))
    step = dt * head_ref[1:2, :HEADS]
    seg = seg_col_ref[every, :]
    place = iota((length, 1), 0)
    number = place // BLOCK
    before, last = jnp.full((length, 1), -2.0, F32), jnp.zeros((length, 1), F32)
    for block in range(blocks):
        end = seg[(block + 1) * BLOCK - 1 : (block + 1) * BLOCK, :]
        last = jnp.where(number == block, end, last)
        before = jnp.where(number == block + 1, end, before)
    lower = (iota((BLOCK, BLOCK), 0) >= iota((BLOCK, BLOCK), 1)).astype(F32)
    upper = (iota((BLOCK, BLOCK), 0) <= iota((BLOCK, BLOCK), 1)).astype(F32)
    eye = (iota((BLOCK, BLOCK), 0) == iota((BLOCK, BLOCK), 1)).astype(F32)
    cums = []
    for block in range(blocks):
        rows = slice(block * BLOCK, (block + 1) * BLOCK)
        cums.append(dot(lower, step[rows], NN, HIGH))
        cum_rows = dot(step[rows], upper, TN, HIGH)
        raw_rows = dot(raw[rows], eye, TN, HIGH)
        for tile in range(HEADS // GROUP):
            heads = slice(tile * GROUP, (tile + 1) * GROUP)
            row_ref[tile * 8 : (tile + 1) * 8, spot(block)] = jnp.concatenate(
                [cum_rows[heads], raw_rows[heads]], axis=0
            )
    cum = jnp.concatenate(cums, axis=0)
    lane = iota((length, COLS), 1)
    col = jnp.zeros((length, COLS), F32)
    for offset in range(1, 4):
        valid = (pltpu.roll(seg, offset, 0) == seg) & (place >= offset)
        col = jnp.where(lane == VALID + offset - 1, valid.astype(F32), col)
    col = jnp.where(lane == LINK, (seg == before).astype(F32), col)
    col = jnp.where(lane == KEEP, (seg == last).astype(F32), col)
    col = jnp.where(lane == SEG, seg, col)
    col_ref[every, :] = col
    wide_ref[every, :] = jnp.concatenate(
        thirds(dt) + thirds(cum) + [jnp.zeros((length, LANES - 6 * HEADS), BF16)], axis=1
    )
    conv = conv_of(proj[:, : 2 * LANES], col, par_ref)
    bc_ref[every, :] = conv * sigmoid(conv)
    for block in range(blocks):
        rows = slice(block * BLOCK, (block + 1) * BLOCK)
        at = spot(block)
        b_rows, c_rows = bc_ref[at, :LANES], bc_ref[at, LANES:]
        seg_col, seg_row = seg[rows], seg_row_ref[:, at]
        score_ref[at, :] = jnp.where(
            pair_mask(seg_col, seg_row, False), dot(c_rows, b_rows, NT, HIGH), 0.0
        )
        turned_ref[at, :] = jnp.where(
            pair_mask(seg_col, seg_row, True), dot(b_rows, c_rows, NT, HIGH), 0.0
        )


def table_kernel(*refs):
    table_part(0, refs[0].shape[0], *refs)


def forward_tile(
    origin, first_row, normed_ref, cot_ref, w_ref, bc_ref, wide_ref, pick_ref, col_ref, row_ref, score_ref,
    par_ref, z_ref, dyn_ref, y_ref, state_ref, sum_ref, xs_ref, carry_ref,
):
    length = xs_ref.shape[0]
    blocks = length // BLOCK

    def spot(number):
        return pl.ds(pl.multiple_of(origin + number * BLOCK, BLOCK), BLOCK)

    def project(number, carried):
        rows = pl.ds(pl.multiple_of(number * BLOCK, BLOCK), BLOCK)
        z_ref[rows, :] = dot(normed_ref[spot(number), :], w_ref[:, : 2 * TILE])
        dyn_ref[rows, :] = dot(cot_ref[spot(number), :], w_ref[:, 2 * TILE :])
        return carried

    lax.fori_loop(0, blocks, project, 0)
    conv = conv_of(z_ref[:, TILE:], col_ref[pl.ds(origin, length), :], par_ref)
    xs_ref[...] = conv * sigmoid(conv)
    carry_ref[...] = jnp.zeros_like(carry_ref)
    ones = jnp.ones((8, TILE), BF16)

    def row_sum(a):
        return sum(dot(ones, part, NT) for part in halves(a))

    def one_block(number, carried):
        rows, at = pl.ds(pl.multiple_of(number * BLOCK, BLOCK), BLOCK), spot(number)
        b_rows, c_rows = bc_ref[at, :LANES], bc_ref[at, LANES:]
        col = col_ref[at, :]
        scores = score_ref[at, :]
        x = xs_ref[rows, :]
        wide = dot(wide_ref[at, :], pick_ref[...])
        dt_wide, cum_wide = wide[:, :TILE], wide[:, TILE:]
        cum_rows = row_ref[pl.ds(first_row, 8), at]
        dtx = x * dt_wide
        dtx_low = dtx.astype(BF16)
        parts = []
        for head in range(GROUP):
            gap = cum_wide[:, head * WIDTH : head * WIDTH + 1] - cum_rows[head : head + 1, :]
            mixing = scores * jnp.exp(jnp.minimum(gap, 0.0))
            parts.append(dot(mixing.astype(BF16), dtx_low[:, head * WIDTH : (head + 1) * WIDTH]))
        within = jnp.concatenate(parts, axis=1)
        state = carry_ref[...]
        state_ref[number] = state
        decay = jnp.exp(cum_wide) * col[:, LINK : LINK + 1]
        y = within + low_dot(c_rows, state) * decay + par_ref[SKIP : SKIP + 1, :] * x
        weight = jnp.exp(cum_wide[BLOCK - 1 :, :] - cum_wide) * col[:, KEEP : KEEP + 1]
        carry_ref[...] = state * decay[BLOCK - 1 :, :] + low_dot(b_rows, dtx * weight, TN)
        y_ref[rows, :] = y
        z = z_ref[rows, :TILE]
        yg = y * z * sigmoid(z)
        first = row_sum(yg * yg)
        second = row_sum(yg * par_ref[GAIN : GAIN + 1, :] * dyn_ref[rows, :])
        place = iota((8, BLOCK), 0)
        sum_ref[:, at] += jnp.where(place == 0, first, jnp.where(place == 1, second, 0.0))
        return carried

    lax.fori_loop(0, blocks, one_block, 0)


def forward_kernel(*refs, pieces):
    normed_ref, cot_ref, bc_ref, wide_ref, pick_ref, col_ref, row_ref, score_ref, par_ref = refs[pieces : pieces + 9]
    w_ref, z_ref, dyn_ref, y_ref, state_ref, sum_ref, xs_ref, carry_ref = refs[pieces + 9 :]

    @pl.when(pl.program_id(0) == 0)
    def _():
        depth = refs[0].shape[0]
        for number in range(pieces):
            w_ref[number * depth : (number + 1) * depth, :] = refs[number][...]

    sum_ref[...] = jnp.zeros_like(sum_ref)
    forward_tile(
        0, 0, normed_ref, cot_ref, w_ref, bc_ref, wide_ref, pick_ref, col_ref, row_ref, score_ref, par_ref,
        z_ref, dyn_ref, y_ref, state_ref, sum_ref, xs_ref, carry_ref,
    )


def gather_kernel(
    normed_ref, cot_ref, own_ref, other_ref, small_own_ref, small_other_ref, seg_col_ref, seg_row_ref,
    bc_par_ref, head_ref, pick_ref, par_ref,
    normed_out, cot_out, w_out, small_out, z_ref, dyn_ref, y_ref, state_ref, proj_out, bc_out, wide_out, col_out, row_out,
    turned_out, norm_ref,
    normed_all, cot_all, w_all, small_all, proj_all, bc_all, wide_all, col_all, row_all, score_all, turned_all,
    sum_ref, sum_recv, xs_ref, carry_ref,
    here_sem, out_sem, act_send, act_recv, x_send, x_recv, z_send, z_recv, y_send, y_recv, sum_send, sum_recv_sem,
    *, tiles, spans, inner_total,
):
    tile, sequence = pl.program_id(0), pl.program_id(1)
    length = xs_ref.shape[0]
    rows = normed_ref.shape[0]
    depth = own_ref.shape[1]
    part = 2 * depth
    dp, mp = lax.axis_index("dp"), lax.axis_index("mp")
    side = lax.rem(dp, 2)
    mine = pl.ds(pl.multiple_of(mp * rows, rows), rows)
    theirs = pl.ds(pl.multiple_of(length + mp * rows, rows), rows)
    slab = pl.ds(pl.multiple_of(side * depth, depth), depth)
    other_core = (dp, 1 - mp)

    def along(bits):
        return (jnp.bitwise_xor(dp, bits), mp)

    def remote(src, dst, send, recv, device):
        return pltpu.make_async_remote_copy(
            src_ref=src, dst_ref=dst, send_sem=send, recv_sem=recv, device_id=device,
            device_id_type=pl.DeviceIdType.MESH,
        )

    arrays = ((normed_ref, normed_all), (cot_ref, cot_all))

    def act_here(a):
        return pltpu.make_async_copy(arrays[a][0], arrays[a][1].at[mine, :], here_sem.at[a])

    def act_core(a):
        return remote(
            arrays[a][0], arrays[a][1].at[mine, :], act_send.at[a, 0], act_recv.at[a, 0], other_core
        )

    def act_x(a):
        return remote(
            arrays[a][0], arrays[a][1].at[theirs, :], act_send.at[a, 1], act_recv.at[a, 1], along(1)
        )

    def act_pass(a):
        return remote(
            arrays[a][1].at[theirs, :], arrays[a][1].at[theirs, :], act_send.at[a, 2], act_recv.at[a, 2], other_core
        )

    def weight_of(number):
        return small_all if number == 0 else w_all.at[number - 1]

    def w_here(number):
        src = small_own_ref if number == 0 else own_ref.at[number - 1]
        return pltpu.make_async_copy(src, weight_of(number).at[slab, :], here_sem.at[2 + number])

    def w_x(number):
        src = small_other_ref if number == 0 else other_ref.at[number - 1]
        return remote(src, weight_of(number).at[slab, :], x_send.at[number], x_recv.at[number], along(1))

    def w_z(number, k):
        ref = weight_of(number)
        return remote(
            ref.at[pl.ds(0, part), :], ref.at[pl.ds(k * part, part), :],
            z_send.at[number, k - 1], z_recv.at[number, k - 1], along(4 * k),
        )

    def w_y(number, k):
        ref = weight_of(number)
        return remote(
            ref.at[pl.ds(k * part, part), :], ref.at[pl.ds((spans + k) * part, part), :],
            y_send.at[number, k], y_recv.at[number, k], along(2),
        )

    def begin_z(number):
        w_here(number).wait()
        w_x(number).wait_recv()
        for k in range(1, spans):
            w_z(number, k).start()
        w_y(number, 0).start()

    def begin_y(number):
        for k in range(1, spans):
            w_z(number, k).wait_recv()
            w_y(number, k).start()

    def complete(number):
        for k in range(spans):
            w_y(number, k).wait_recv()

    tables = (
        (normed_all, normed_out), (cot_all, cot_out), (proj_all, proj_out), (bc_all, bc_out),
        (wide_all, wide_out), (col_all, col_out), (row_all, row_out), (turned_all, turned_out),
        (small_all, small_out),
    )

    def table_out(at):
        return pltpu.make_async_copy(tables[at][0], tables[at][1], out_sem.at[at])

    def weight_out(number):
        return pltpu.make_async_copy(w_all.at[number], w_out.at[number], out_sem.at[len(tables) + number])

    def make_tables(origin):
        table_part(
            origin, length, normed_all, small_all, seg_col_ref, seg_row_ref, bc_par_ref, head_ref,
            proj_all, bc_all, wide_all, col_all, row_all, score_all, turned_all,
        )

    @pl.when((tile == 0) & (sequence == 0))
    def _():
        barrier = pltpu.get_barrier_semaphore()
        partners = [along(1), along(2), other_core] + [along(4 * k) for k in range(1, spans)]
        for device in partners:
            pl.semaphore_signal(barrier, inc=1, device_id=device, device_id_type=pl.DeviceIdType.MESH)
        for number in range(tiles + 1):
            w_here(number).start()
        act_here(0).start()
        act_here(1).start()
        sum_ref[...] = jnp.zeros_like(sum_ref)
        pl.semaphore_wait(barrier, len(partners))
        w_x(0).start()
        w_x(1).start()
        act_core(0).start()
        act_core(1).start()
        act_x(0).start()
        begin_z(0)
        begin_z(1)
        for number in range(2, tiles + 1):
            w_x(number).start()
        act_x(1).start()
        begin_y(0)
        begin_z(2)
        act_here(0).wait()
        act_core(0).wait_recv()
        complete(0)
        make_tables(0)
        begin_y(1)
        act_x(0).wait_recv()
        act_pass(0).start()
        act_here(1).wait()
        act_core(1).wait_recv()

    for number in range(tiles):

        @pl.when((tile == number) & (sequence == 0))
        def _(number=number):
            if number + 3 <= tiles:
                begin_z(number + 3)
            if number + 2 <= tiles:
                begin_y(number + 2)
            complete(number + 1)
            weight_out(number).start()

    @pl.when((tile == 0) & (sequence == 1))
    def _():
        act_pass(0).wait_recv()
        make_tables(length)
        act_x(1).wait_recv()
        act_pass(1).start()
        act_pass(1).wait_recv()
        for at in range(len(tables)):
            table_out(at).start()

    forward_tile(
        sequence * length, tile * 8, normed_all, cot_all, w_all.at[tile], bc_all, wide_all, pick_ref, col_all,
        row_all, score_all, par_ref, z_ref, dyn_ref, y_ref, state_ref, sum_ref, xs_ref, carry_ref,
    )

    @pl.when((tile == tiles - 1) & (sequence == 1))
    def _():
        between = remote(sum_ref, sum_recv.at[0], sum_send.at[0], sum_recv_sem.at[0], other_core)
        between.start()
        between.wait()
        sum_ref[...] += sum_recv[0]
        across = remote(sum_ref, sum_recv.at[1], sum_send.at[1], sum_recv_sem.at[1], along(1))
        across.start()
        across.wait()
        norm_ref[...] = norm_rows(
            sum_ref[...] + jnp.concatenate([sum_recv[1, :, length:], sum_recv[1, :, :length]], axis=1),
            inner_total,
        )
        for a in range(2):
            act_core(a).wait_send()
            act_x(a).wait_send()
            act_pass(a).wait_send()
        for number in range(tiles + 1):
            w_x(number).wait_send()
            for k in range(1, spans):
                w_z(number, k).wait_send()
            for k in range(spans):
                w_y(number, k).wait_send()
        for at in range(len(tables)):
            table_out(at).wait()
        for number in range(tiles):
            weight_out(number).wait()


def norm_rows(sums, inner_total):
    inverse = lax.rsqrt(sums[0:1] / inner_total + EPSILON)
    cross = inverse * inverse * inverse / inner_total * sums[1:2]
    return jnp.concatenate([inverse, cross, jnp.zeros((6, sums.shape[1]), F32)], axis=0)


def backward_tile(
    origin, z_ref, y_ref, dyn_ref, bc_ref, wide_ref, pick_ref, col_ref, row_ref, seg_ref, turned_ref, norm_ref,
    par_ref, rate_ref, state_ref, grad_ref, dbc_ref, dt_ref, head_ref, small_ref, turn_ref, halo_ref, carry_ref,
):
    length = z_ref.shape[0]
    blocks = length // BLOCK
    carry_ref[...] = jnp.zeros_like(carry_ref)
    small_ref[...] = jnp.zeros_like(small_ref)
    head_ref[...] = jnp.zeros_like(head_ref)
    halo_ref[...] = jnp.zeros_like(halo_ref)
    down, across = iota((BLOCK, BLOCK), 0), iota((BLOCK, BLOCK), 1)

    def one_block(step, carried):
        number = blocks - 1 - step
        start = pl.multiple_of(number * BLOCK, BLOCK)
        rows = pl.ds(start, BLOCK)
        col = col_ref[rows, :]
        v = z_ref[rows, TILE:]
        above = z_ref[pl.ds(pl.multiple_of(jnp.maximum(start - 8, 0), 8), 8), TILE:]
        joined = jnp.concatenate([above, v], axis=0)
        moved = [None] + [
            pltpu.roll(joined, offset, 0)[8:] * col[:, VALID + offset - 1 : VALID + offset]
            for offset in range(1, 4)
        ]
        conv = par_ref[BIAS : BIAS + 1, :] + par_ref[TAPS + 3 : TAPS + 4, :] * v
        for offset in range(1, 4):
            conv = conv + par_ref[TAPS + 3 - offset : TAPS + 4 - offset, :] * moved[offset]
        gate = sigmoid(conv)
        x = conv * gate
        slope = gate * (1.0 + conv * (1.0 - gate))
        z, y, dyn = z_ref[rows, :TILE], y_ref[rows, :], dyn_ref[rows, :]
        gain = par_ref[GAIN : GAIN + 1, :]
        inv, cross = norm_ref[rows, 0:1], norm_ref[rows, 1:2]
        gate = sigmoid(z)
        silu = z * gate
        yg = y * silu
        yg_inv = yg * inv
        d_yg = inv * gain * dyn - yg * cross
        grad_ref[rows, :TILE] = (d_yg * y * (gate * (1.0 + z * (1.0 - gate)))).astype(BF16)
        grad_ref[rows, 2 * TILE :] = (yg_inv * gain).astype(BF16)
        small_ref[GAIN : GAIN + 1, :] += jnp.sum(dyn * yg_inv, axis=0, keepdims=True)
        e = d_yg * silu
        b_low, c_low = bc_ref[rows, :LANES].astype(BF16), bc_ref[rows, LANES:].astype(BF16)
        scores = turned_ref[rows, :]
        wide = dot(wide_ref[rows, :], pick_ref[...])
        dt_wide, cum_wide = wide[:, :TILE], wide[:, TILE:]
        dtx = x * dt_wide
        dtx_low, e_low = dtx.astype(BF16), e.astype(BF16)
        reach = (down >= across).astype(BF16)
        d_scores = jnp.zeros((BLOCK, BLOCK), F32)
        parts, between = [], []
        for head in range(GROUP):
            lanes = slice(head * WIDTH, (head + 1) * WIDTH)
            gap = row_ref[head : head + 1, rows] - cum_wide[:, head * WIDTH : head * WIDTH + 1]
            decay = jnp.exp(jnp.minimum(gap, 0.0))
            mixing = scores * decay
            parts.append(dot(mixing.astype(BF16), e_low[:, lanes]))
            d_mixing = dot(dtx_low[:, lanes], e_low[:, lanes], NT)
            d_scores = d_scores + d_mixing * decay
            later = dot((d_mixing * mixing).astype(BF16), reach)
            between.append(jnp.sum(jnp.where(down < across, later, 0.0), axis=0, keepdims=True))
        d_dtx = jnp.concatenate(parts, axis=1)
        mask = pair_mask(col[:, SEG : SEG + 1], seg_ref[:, rows], True)
        d_scores = jnp.where(mask, d_scores, 0.0).astype(BF16)
        d_b = dot(d_scores, c_low)
        d_c = dot(d_scores, b_low, TN)
        state, d_state = state_ref[number], carry_ref[...]
        state_low, d_state_low = state.astype(BF16), d_state.astype(BF16)
        decay = jnp.exp(cum_wide) * col[:, LINK : LINK + 1]
        e_in = e * decay
        e_in_low = e_in.astype(BF16)
        from_state = e_in * dot(c_low, state_low)
        d_c = d_c + dot(e_in_low, state_low, NT)
        carry_ref[...] = decay[BLOCK - 1 :, :] * d_state + dot(c_low, e_in_low, TN)
        weight = jnp.exp(cum_wide[BLOCK - 1 :, :] - cum_wide) * col[:, KEEP : KEEP + 1]
        d_tail = weight * dot(b_low, d_state_low)
        to_state = d_tail * dtx
        d_b = d_b + low_dot(weight * dtx, d_state_low, NT)
        d_dtx = d_dtx + d_tail
        through = decay[BLOCK - 1 :, :] * jnp.sum(state * d_state, axis=0, keepdims=True)
        d_x = dt_wide * d_dtx + par_ref[SKIP : SKIP + 1, :] * e
        small_ref[SKIP : SKIP + 1, :] += jnp.sum(x * e, axis=0, keepdims=True)
        spot = pl.ds(pl.multiple_of(origin + start, BLOCK), BLOCK)
        dbc_ref[spot, :LANES] += d_b
        dbc_ref[spot, LANES:] += d_c
        d_conv = slope * d_x
        below = pl.ds(pl.multiple_of(jnp.minimum(start + BLOCK, length - 8), 8), 8)
        joined = jnp.concatenate([d_conv, halo_ref[...]], axis=0)
        halo_ref[...] = d_conv[:8]
        d_v = par_ref[TAPS + 3 : TAPS + 4, :] * d_conv
        small_ref[TAPS + 3 : TAPS + 4, :] += jnp.sum(d_conv * v, axis=0, keepdims=True)
        small_ref[BIAS : BIAS + 1, :] += jnp.sum(d_conv, axis=0, keepdims=True)
        valid = jnp.concatenate([col, col_ref[below, :]], axis=0)
        for offset in range(1, 4):
            place = TAPS + 3 - offset
            small_ref[place : place + 1, :] += jnp.sum(d_conv * moved[offset], axis=0, keepdims=True)
            counted = joined * valid[:, VALID + offset - 1 : VALID + offset]
            d_v = d_v + par_ref[place : place + 1, :] * pltpu.roll(counted, BLOCK + 8 - offset, 0)[:BLOCK]
        grad_ref[rows, TILE : 2 * TILE] = d_v.astype(BF16)
        owner = (iota((TILE, 8), 0) // WIDTH == iota((TILE, 8), 1)).astype(BF16)

        def head_sum(a):
            return sum(dot(part, owner) for part in halves(a))

        def token_sum(reached, a):
            both = dot(reached, jnp.concatenate(halves(a), axis=1))
            return both[:, :8] + both[:, 8:]

        run = token_sum((down <= across).astype(BF16), head_sum(from_state))
        run = run + token_sum((down > across).astype(BF16), head_sum(to_state))
        run = run + head_sum(jnp.broadcast_to(through, (8, TILE)))[:1]
        sums = jnp.concatenate(
            [run, head_sum(d_dtx * x), jnp.zeros((BLOCK, LANES - 16), F32)], axis=1
        ).T
        run_rows = sums[:GROUP] + jnp.concatenate(between, axis=0)
        raw = row_ref[GROUP : 2 * GROUP, rows]
        d_dt = (sums[8 : 8 + GROUP] + rate_ref[:GROUP, :1] * run_rows) * sigmoid(raw)
        dt = jnp.maximum(raw, 0.0) + jnp.log1p(jnp.exp(-jnp.abs(raw)))
        head_ref[:GROUP, :] += jnp.sum(d_dt, axis=1, keepdims=True)
        head_ref[GROUP:, :] += jnp.sum(run_rows * dt, axis=1, keepdims=True)
        d_dt = jnp.concatenate([d_dt, jnp.zeros((16 - GROUP, BLOCK), F32)], axis=0).astype(BF16)
        dt_ref[:, rows] = d_dt
        turn_ref[STEPS:OUT, spot] = d_dt
        turned = grad_ref[rows, :].T
        turn_ref[:STEPS, spot] = turned[: 2 * TILE]
        turn_ref[OUT:, spot] = turned[2 * TILE :]
        return carried

    lax.fori_loop(0, blocks, one_block, 0)


def backward_kernel(*refs, ties, inside, tiles, spans):
    (
        normed_ref, cot_ref, z_ref, y_ref, dyn_ref, bc_ref, wide_ref, pick_ref, col_ref, row_ref, seg_ref,
        turned_ref, norm_ref, par_ref, rate_ref, state_ref,
        grad_ref, dbc_ref, dt_ref, head_ref, small_ref, far_out_ref, near_out_ref, z_own_out, z_send_out,
        mine_ref, theirs_ref, dbc_x_ref,
        turn_ref, halo_ref, carry_ref, stream_ref, far_ref, near_ref, y_recv_ref, z_send_ref, z_own_ref,
        z_recv_ref, w_send_ref, w_recv_ref, dbc_core_ref, dbc_send_ref, dbc_recv_ref,
        stream_sem, out_sem, y_send_sem, y_recv_sem, z_send_sem, z_recv_sem, w_send_sem, w_recv_sem,
        d_send_sem, d_recv_sem,
    ) = refs[ties:]
    tile, turn = pl.program_id(0), pl.program_id(1)
    sequence = 1 - turn
    done = inside - 1
    length = z_ref.shape[0]
    part = near_ref.shape[2]
    halves_of = near_ref.shape[0]
    ahead = stream_ref.shape[0] - 1
    dp, mp = lax.axis_index("dp"), lax.axis_index("mp")
    side = lax.rem(dp, 2)

    def partner(bits):
        return (jnp.bitwise_xor(dp, bits), mp)

    def remote(src, dst, send, recv, device):
        return pltpu.make_async_remote_copy(
            src_ref=src, dst_ref=dst, send_sem=send, recv_sem=recv, device_id=device,
            device_id_type=pl.DeviceIdType.MESH,
        )

    def y_copy(number, at):
        slot = lax.rem(number, 2)
        return remote(
            far_ref.at[at], y_recv_ref.at[slot, at], y_send_sem.at[at], y_recv_sem.at[slot, at], partner(2)
        )

    def z_copy(number, k):
        slot = lax.rem(number, 2)
        return remote(
            z_send_ref.at[k - 1], z_recv_ref.at[slot, k - 1], z_send_sem.at[k - 1], z_recv_sem.at[slot, k - 1],
            partner(4 * k),
        )

    def w_copy(number):
        return remote(
            w_send_ref.at[number], w_recv_ref.at[number], w_send_sem.at[number], w_recv_sem.at[number], partner(1)
        )

    def finish(number):
        slot = lax.rem(number, 2)
        total = z_own_ref[...]
        for k in range(1, spans):
            z_copy(number, k).wait()
            total = total + z_recv_ref[slot, k - 1].astype(F32)
        z_own_ref[...] = total
        mine_ref[number] = z_own_ref[:, pl.ds(pl.multiple_of(side * LANES, LANES), LANES)]
        w_send_ref[number] = z_own_ref[:, pl.ds(pl.multiple_of((1 - side) * LANES, LANES), LANES)].astype(BF16)
        w_copy(number).start()

    def pass_on(number):
        slot = lax.rem(number, 2)
        for at in range(spans):
            y_copy(number, at).wait()
            whole_part = near_ref[at] + y_recv_ref[slot, at].astype(F32)
            if at == 0:
                z_own_ref[...] = whole_part
            else:
                z_send_ref[at - 1] = whole_part.astype(BF16)

                @pl.when(number < done)
                def _(at=at):
                    z_copy(number, at).start()

    def z_out():
        return [
            pltpu.make_async_copy(z_own_ref, z_own_out, out_sem.at[2]),
            pltpu.make_async_copy(z_send_ref, z_send_out, out_sem.at[3]),
        ]

    def dbc_core():
        src = dbc_ref.at[pl.ds(length, length), :]
        return remote(src, dbc_core_ref, d_send_sem.at[0], d_recv_sem.at[0], (dp, 1 - mp))

    def dbc_x():
        return remote(dbc_send_ref, dbc_recv_ref, d_send_sem.at[1], d_recv_sem.at[1], partner(1))

    @pl.when((tile == 0) & (turn == 0))
    def _():
        dbc_ref[...] = jnp.zeros_like(dbc_ref)
        if inside:
            barrier = pltpu.get_barrier_semaphore()
            others = [partner(1), partner(2), (dp, 1 - mp)] + [partner(4 * k) for k in range(1, spans)]
            for device in others:
                pl.semaphore_signal(barrier, inc=1, device_id=device, device_id_type=pl.DeviceIdType.MESH)
            pl.semaphore_wait(barrier, len(others))

    def fetch(step):
        number = lax.rem(step + halves_of, 2 * halves_of)
        slot = lax.rem(step, ahead + 1)
        lanes = pl.ds(pl.multiple_of(number * part, LANES), part)
        return [
            pltpu.make_async_copy(ref.at[:, lanes], stream_ref.at[slot, at], stream_sem.at[slot, at])
            for at, ref in enumerate((normed_ref, cot_ref))
        ]

    @pl.when(turn == 1)
    def _():
        for step in range(ahead):
            for copy in fetch(step):
                copy.start()

    if inside:

        @pl.when((tile == tiles - 1) & (turn == 1))
        def _():
            dbc_core().start()

    backward_tile(
        sequence * length, z_ref, y_ref, dyn_ref, bc_ref, wide_ref, pick_ref, col_ref, row_ref, seg_ref,
        turned_ref, norm_ref, par_ref, rate_ref, state_ref, grad_ref, dbc_ref, dt_ref, head_ref, small_ref,
        turn_ref, halo_ref, carry_ref,
    )

    if inside:

        @pl.when((tile == tiles - 1) & (turn == 1))
        def _():
            dbc_core().wait()
            dbc_send_ref[...] = (dbc_ref[length:, :] + dbc_core_ref[...]).astype(BF16)
            dbc_x().start()

        @pl.when((turn == 1) & (tile >= 2) & (tile < done + 2))
        def _():
            finish(tile - 2)

        @pl.when((turn == 1) & (tile >= 1) & (tile <= inside))
        def _():
            pass_on(tile - 1)

        @pl.when((turn == 1) & (tile == inside))
        def _():
            for copy in z_out():
                copy.start()

    def out_copies():
        place = tile - inside
        return [
            pltpu.make_async_copy(far_ref, far_out_ref.at[place], out_sem.at[0]),
            pltpu.make_async_copy(near_ref, near_out_ref.at[place], out_sem.at[1]),
        ]

    @pl.when(turn == 1)
    def _():
        def one_part(step, carried):
            slot = lax.rem(step, ahead + 1)

            @pl.when(step + ahead < 2 * halves_of)
            def _():
                for copy in fetch(step + ahead):
                    copy.start()

            for copy in fetch(step):
                copy.wait()
            upper = dot(turn_ref[:OUT, :], stream_ref[slot, 0])
            lower = dot(turn_ref[OUT:, :], stream_ref[slot, 1])

            @pl.when(step < halves_of)
            def _():
                far_ref[step, :OUT, :] = upper.astype(BF16)
                far_ref[step, OUT:, :] = lower.astype(BF16)
                if inside:

                    @pl.when(tile < inside)
                    def _():
                        y_copy(tile, step).start()

            @pl.when(step >= halves_of)
            def _():
                near_ref[step - halves_of, :OUT, :] = upper
                near_ref[step - halves_of, OUT:, :] = lower

            return carried

        lax.fori_loop(0, 2 * halves_of, one_part, 0)

        @pl.when(tile >= inside)
        def _():
            for copy in out_copies():
                copy.start()
            for copy in out_copies():
                copy.wait()

    if inside:

        @pl.when((turn == 1) & (tile == tiles - 1))
        def _():
            for copy in z_out():
                copy.wait()
            for number in range(done):
                w_copy(number).wait()
            theirs_ref[...] = w_recv_ref[...]
            dbc_x().wait()
            dbc_x_ref[...] = dbc_recv_ref[...]


def by_sequence(rows, width):
    return pl.BlockSpec((rows, width), lambda i: (i, 0))


def by_columns(rows, length):
    return pl.BlockSpec((rows, length), lambda i: (0, i))


def whole(shape):
    return pl.BlockSpec(shape, lambda i: (0,) * len(shape))


def shaped(shape, kind=F32):
    return jax.ShapeDtypeStruct(shape, kind)


def cost(flops):
    return pl.CostEstimate(flops=int(flops), bytes_accessed=10**7, transcendentals=10**6)


def run_tables(normed, weight, ids, par, head, length):
    tokens, width = normed.shape
    cols = weight.shape[1]
    return pl.pallas_call(
        table_kernel,
        grid=(tokens // length,),
        in_specs=[
            by_sequence(length, width),
            whole((width, cols)),
            by_sequence(length, 1),
            by_columns(1, length),
            whole((8, 2 * LANES)),
            whole((8, LANES)),
        ],
        out_specs=[
            by_sequence(length, 2 * LANES),
            by_sequence(length, 2 * LANES),
            by_sequence(length, LANES),
            by_sequence(length, COLS),
            by_columns(2 * HEADS, length),
            by_sequence(length, BLOCK),
            by_sequence(length, BLOCK),
        ],
        out_shape=[
            shaped((tokens, 2 * LANES)),
            shaped((tokens, 2 * LANES)),
            shaped((tokens, LANES), BF16),
            shaped((tokens, COLS)),
            shaped((2 * HEADS, tokens)),
            shaped((tokens, BLOCK)),
            shaped((tokens, BLOCK)),
        ],
        compiler_params=pltpu.CompilerParams(vmem_limit_bytes=VMEM_LIMIT),
        cost_estimate=cost(1e10),
    )(normed, weight, ids[:, None], ids[None, :], par, head)


def pick_table(tile):
    row, lane = jnp.arange(LANES)[:, None], jnp.arange(2 * TILE)[None, :]
    head = tile * GROUP + (lane % TILE) // WIDTH
    return ((row % HEADS == head) & (row // (3 * HEADS) == lane // TILE)).astype(BF16)


def run_forward(pieces, normed, cot, bc, wide, col, rows, score, par, tile, length):
    tokens, width = normed.shape
    number, blocks = tokens // length, length // BLOCK
    return pl.pallas_call(
        functools.partial(forward_kernel, pieces=len(pieces)),
        grid=(number,),
        in_specs=[whole(p.shape) for p in pieces]
        + [
            by_sequence(length, width),
            by_sequence(length, width),
            by_sequence(length, 2 * LANES),
            by_sequence(length, LANES),
            whole((LANES, 2 * TILE)),
            by_sequence(length, COLS),
            pl.BlockSpec((8, length), lambda i: (tile, i)),
            by_sequence(length, BLOCK),
            whole((8, TILE)),
        ],
        out_specs=[
            whole((width, 3 * TILE)),
            by_sequence(length, 2 * TILE),
            by_sequence(length, TILE),
            by_sequence(length, TILE),
            pl.BlockSpec((blocks, LANES, TILE), lambda i: (i, 0, 0)),
            by_columns(8, length),
        ],
        out_shape=[
            shaped((width, 3 * TILE), BF16),
            shaped((tokens, 2 * TILE)),
            shaped((tokens, TILE)),
            shaped((tokens, TILE)),
            shaped((number * blocks, LANES, TILE)),
            shaped((8, tokens)),
        ],
        scratch_shapes=[pltpu.VMEM((length, TILE), F32), pltpu.VMEM((LANES, TILE), F32)],
        compiler_params=pltpu.CompilerParams(vmem_limit_bytes=VMEM_LIMIT),
        cost_estimate=cost(2e10),
    )(*pieces, normed, cot, bc, wide, pick_table(tile), col, rows, score, par)


def run_gather(normed, cot, own, other, small_own, small_other, ids, bc_par, head_par, pars, length, spans, inner_total):
    rows, width = normed.shape
    tiles, _, cols = own.shape
    small_cols = small_own.shape[1]
    tokens, blocks = 2 * length, length // BLOCK

    def by_tile(size, count):
        return pl.BlockSpec((None, size, count), lambda j, i: (j, i, 0))

    def fixed(*shape):
        return pl.BlockSpec((None,) + shape, lambda j, i: (j,) + (0,) * len(shape))

    def constant(*shape):
        return pl.BlockSpec(shape, lambda j, i: (0,) * len(shape))

    dma = pltpu.SemaphoreType.DMA
    table_shapes = [
        ((tokens, 2 * LANES), F32),
        ((tokens, 2 * LANES), F32),
        ((tokens, LANES), BF16),
        ((tokens, COLS), F32),
        ((2 * HEADS, tokens), F32),
        ((tokens, BLOCK), F32),
    ]
    return pl.pallas_call(
        functools.partial(gather_kernel, tiles=tiles, spans=spans, inner_total=inner_total),
        grid=(tiles, 2),
        in_specs=[ANY] * 6
        + [
            constant(tokens, 1),
            constant(1, tokens),
            constant(8, 2 * LANES),
            constant(8, LANES),
            fixed(LANES, 2 * TILE),
            fixed(8, TILE),
        ],
        out_specs=[
            ANY,
            ANY,
            ANY,
            ANY,
            by_tile(length, 2 * TILE),
            by_tile(length, TILE),
            by_tile(length, TILE),
            pl.BlockSpec((None, blocks, LANES, TILE), lambda j, i: (j, i, 0, 0)),
        ]
        + [ANY] * 6
        + [constant(8, tokens)],
        out_shape=[
            shaped((tokens, width), BF16),
            shaped((tokens, width), BF16),
            shaped((tiles, width, cols), BF16),
            shaped((width, small_cols), BF16),
            shaped((tiles, tokens, 2 * TILE)),
            shaped((tiles, tokens, TILE)),
            shaped((tiles, tokens, TILE)),
            shaped((tiles, 2 * blocks, LANES, TILE)),
        ]
        + [shaped(*one) for one in table_shapes]
        + [shaped((8, tokens))],
        scratch_shapes=[
            pltpu.VMEM((tokens, width), BF16),
            pltpu.VMEM((tokens, width), BF16),
            pltpu.VMEM((tiles, width, cols), BF16),
            pltpu.VMEM((width, small_cols), BF16),
        ]
        + [pltpu.VMEM(*one) for one in table_shapes[:5]]
        + [
            pltpu.VMEM((tokens, BLOCK), F32),
            pltpu.VMEM((tokens, BLOCK), F32),
            pltpu.VMEM((8, tokens), F32),
            pltpu.VMEM((2, 8, tokens), F32),
            pltpu.VMEM((length, TILE), F32),
            pltpu.VMEM((LANES, TILE), F32),
            dma((3 + tiles,)),
            dma((9 + tiles,)),
            dma((2, 3)),
            dma((2, 3)),
            dma((1 + tiles,)),
            dma((1 + tiles,)),
            dma((1 + tiles, spans - 1)),
            dma((1 + tiles, spans - 1)),
            dma((1 + tiles, spans)),
            dma((1 + tiles, spans)),
            dma((2,)),
            dma((2,)),
        ],
        compiler_params=pltpu.CompilerParams(
            vmem_limit_bytes=VMEM_LIMIT, collective_id=2, has_side_effects=True
        ),
        cost_estimate=cost(2e11),
    )(
        normed, cot, own, other, small_own, small_other, ids[:, None], ids[None, :], bc_par, head_par,
        jnp.stack([pick_table(tile) for tile in range(tiles)]), pars,
    )


def run_backward(
    ties, normed, cot, zv, y, dyn, bc, wide, col, rows, ids, turned, norms, par, rate, state, length, spans
):
    tiles, tokens = zv.shape[:2]
    width = normed.shape[1]
    number, blocks = tokens // length, length // BLOCK
    part = 2 * LANES
    near = width // part // 2
    inside = tiles - 1 if near == spans else 0
    done = max(inside - 1, 1)
    hops = 3

    def by_tile(size, cols):
        return pl.BlockSpec((None, size, cols), lambda j, i: (j, 1 - i, 0))

    def shared(size, cols):
        return pl.BlockSpec((size, cols), lambda j, i: (1 - i, 0))

    def fixed(*shape):
        return pl.BlockSpec((None,) + shape, lambda j, i: (j,) + (0,) * len(shape))

    def constant(*shape):
        return pl.BlockSpec(shape, lambda j, i: (0,) * len(shape))

    dma = pltpu.SemaphoreType.DMA
    params = dict(vmem_limit_bytes=VMEM_LIMIT)
    if inside:
        params.update(collective_id=1, has_side_effects=True)
    return inside, pl.pallas_call(
        functools.partial(backward_kernel, ties=len(ties), inside=inside, tiles=tiles, spans=spans),
        grid=(tiles, number),
        in_specs=[ANY for _ in ties]
        + [
            ANY,
            ANY,
            by_tile(length, 2 * TILE),
            by_tile(length, TILE),
            by_tile(length, TILE),
            shared(length, 2 * LANES),
            shared(length, LANES),
            fixed(LANES, 2 * TILE),
            shared(length, COLS),
            pl.BlockSpec((8, length), lambda j, i: (j, 1 - i)),
            pl.BlockSpec((1, length), lambda j, i: (0, 1 - i)),
            shared(length, BLOCK),
            shared(length, 8),
            fixed(8, TILE),
            fixed(8, LANES),
            pl.BlockSpec((None, blocks, LANES, TILE), lambda j, i: (j, 1 - i, 0, 0)),
        ],
        out_specs=[
            by_tile(length, 3 * TILE),
            constant(tokens, 2 * LANES),
            pl.BlockSpec((16, length), lambda j, i: (j, 1 - i)),
            pl.BlockSpec((None, None, 8, LANES), lambda j, i: (j, 1 - i, 0, 0)),
            pl.BlockSpec((None, None, 8, TILE), lambda j, i: (j, 1 - i, 0, 0)),
            ANY,
            ANY,
            ANY,
            ANY,
            constant(done, SHARE, LANES),
            constant(done, SHARE, LANES),
            constant(length, part),
        ],
        out_shape=[
            shaped((tiles, tokens, 3 * TILE), BF16),
            shaped((tokens, 2 * LANES)),
            shaped((tiles * 16, tokens), BF16),
            shaped((tiles, number, 8, LANES)),
            shaped((tiles, number, 8, TILE)),
            shaped((tiles - inside, near, SHARE, part), BF16),
            shaped((tiles - inside, near, SHARE, part)),
            shaped((SHARE, part)),
            shaped((hops, SHARE, part), BF16),
            shaped((done, SHARE, LANES)),
            shaped((done, SHARE, LANES), BF16),
            shaped((length, part), BF16),
        ],
        scratch_shapes=[
            pltpu.VMEM((SHARE, tokens), BF16),
            pltpu.VMEM((8, TILE), F32),
            pltpu.VMEM((LANES, TILE), F32),
            pltpu.VMEM((4, 2, tokens, part), BF16),
            pltpu.VMEM((near, SHARE, part), BF16),
            pltpu.VMEM((near, SHARE, part), F32),
            pltpu.VMEM((2, near, SHARE, part), BF16),
            pltpu.VMEM((hops, SHARE, part), BF16),
            pltpu.VMEM((SHARE, part), F32),
            pltpu.VMEM((2, hops, SHARE, part), BF16),
            pltpu.VMEM((done, SHARE, LANES), BF16),
            pltpu.VMEM((done, SHARE, LANES), BF16),
            pltpu.VMEM((length, part), F32),
            pltpu.VMEM((length, part), BF16),
            pltpu.VMEM((length, part), BF16),
            dma((4, 2)),
            dma((4,)),
            dma((near,)),
            dma((2, near)),
            dma((hops,)),
            dma((2, hops)),
            dma((done,)),
            dma((done,)),
            dma((2,)),
            dma((2,)),
        ],
        compiler_params=pltpu.CompilerParams(**params),
        cost_estimate=cost(2e11),
    )(
        *ties, normed, cot, zv, y, dyn, bc, wide, jnp.stack([pick_table(tile) for tile in range(tiles)]), col,
        rows, ids[None, :], turned, norms, par, rate, state,
    )


def mixer_kernel(
    z_hbm, y_hbm, norm_ref, par_ref, w_ref, own_ref, give_ref,
    z_buf, y_buf, norm_buf, away, recv, z_sem, y_sem, send_sem, recv_sem, *, spans, length,
):
    tiles, rows = z_buf.shape[1:3]
    dp, mp = lax.axis_index("dp"), lax.axis_index("mp")
    part = 2 * LANES
    order = ((1, 1 - mp), (0, 1 - mp), (1, mp), (0, mp))

    def rows_of(step):
        sequence, half = order[step]
        return pl.ds(pl.multiple_of(sequence * length + half * rows, rows), rows)

    def fetch(step):
        slot = step % 2
        at = rows_of(step)
        return [
            pltpu.make_async_copy(z_hbm.at[:, at, pl.ds(0, TILE)], z_buf.at[slot], z_sem.at[slot]),
            pltpu.make_async_copy(y_hbm.at[:, at, :], y_buf.at[slot], y_sem.at[slot]),
        ]

    def core_copy(step):
        return pltpu.make_async_remote_copy(
            src_ref=away.at[step], dst_ref=recv.at[step], send_sem=send_sem.at[step], recv_sem=recv_sem.at[step],
            device_id=(dp, 1 - mp), device_id_type=pl.DeviceIdType.MESH,
        )

    for copy in fetch(0):
        copy.start()
    barrier = pltpu.get_barrier_semaphore()
    pl.semaphore_signal(barrier, inc=1, device_id=(dp, 1 - mp), device_id_type=pl.DeviceIdType.MESH)
    pl.semaphore_wait(barrier, 1)
    for step in range(4):
        if step < 3:
            for copy in fetch(step + 1):
                copy.start()
        for copy in fetch(step):
            copy.wait()
        norm_buf[...] = norm_ref[rows_of(step), :]
        parts = []
        for tile in range(tiles):
            z = z_buf[step % 2, tile]
            yg = y_buf[step % 2, tile] * (z * sigmoid(z))
            parts.append((yg * norm_buf[:, 0:1] * par_ref[tile, GAIN : GAIN + 1, :]).astype(BF16))
        if step >= 2:
            core_copy(step - 2).wait()

        def columns(number, carried, step=step, parts=parts):
            at = pl.ds(pl.multiple_of(number * part, part), part)
            total = dot(parts[0], w_ref[0, at, :], NT)
            for tile in range(1, tiles):
                total = total + dot(parts[tile], w_ref[tile, at, :], NT)
            lanes = pl.ds(pair_start(number, dp, spans), part)
            if step < 2:
                away[step, :, lanes] = total.astype(BF16)
            elif step == 2:
                give_ref[:, lanes] = (total + recv[0, :, lanes].astype(F32)).astype(BF16)
            else:
                own_ref[:, lanes] = total + recv[1, :, lanes].astype(F32)
            return carried

        lax.fori_loop(0, 2 * spans, columns, 0)
        if step < 2:
            core_copy(step).start()


def pair_start(number, dp, spans):
    bits = number // spans * 2 + number % spans * 4
    return pl.multiple_of(jnp.bitwise_xor(dp - lax.rem(dp, 2), bits) * LANES, 2 * LANES)


def run_mixer(zvs, ys, norms, params, weights, rows, length, spans):
    tiles, tokens, _ = ys.shape
    width = weights.shape[1]
    dma = pltpu.SemaphoreType.DMA
    return pl.pallas_call(
        functools.partial(mixer_kernel, spans=spans, length=length),
        grid=(1,),
        in_specs=[
            ANY,
            ANY,
            pl.BlockSpec((tokens, 8), lambda i: (0, 0)),
            pl.BlockSpec((tiles, 8, TILE), lambda i: (0, 0, 0)),
            pl.BlockSpec((tiles, width, TILE), lambda i: (0, 0, 2)),
        ],
        out_specs=[
            pl.BlockSpec((rows, width), lambda i: (0, 0)),
            pl.BlockSpec((rows, width), lambda i: (0, 0)),
        ],
        out_shape=[shaped((rows, width)), shaped((rows, width), BF16)],
        scratch_shapes=[
            pltpu.VMEM((2, tiles, rows, TILE), F32),
            pltpu.VMEM((2, tiles, rows, TILE), F32),
            pltpu.VMEM((rows, 8), F32),
            pltpu.VMEM((2, rows, width), BF16),
            pltpu.VMEM((2, rows, width), BF16),
            dma((2,)),
            dma((2,)),
            dma((2,)),
            dma((2,)),
        ],
        compiler_params=pltpu.CompilerParams(
            vmem_limit_bytes=VMEM_LIMIT, collective_id=4, has_side_effects=True
        ),
        cost_estimate=cost(1e10),
    )(zvs, ys, norms, params, weights)


def tail_kernel(
    hidden_ref, cot_ref, inv_ref, gain_ref, grads_hbm, weights_hbm, small_ref, dt_ref, far_hbm, near_ref,
    z_own_ref, z_send_hbm, mine_ref, theirs_ref, dbc_ref, dbc_x_ref, proj_ref, col_ref, par_ref, normed_hbm,
    smalls_ref, heads_ref, rate_ref, sums_ref,
    grad_out, zx_ref, out_ref, steps_ref, bc_out_ref, pack_out_ref, last_ref,
    grads_seq, wblk, acc_ref, give_ref, core_recv, own_ref, x_give, x_recv, y_recv, z_send, z_own, z_recv, w_send,
    w_recv, dbc_core, dbc_low, dt_cols, normed_blk, bc_grad, bc_xs, bc_own, bc_xr, bc_yr, bc_zr, bc_core,
    pack_recv, last_recv,
    seq_sem, blk_sem, out_sem, core_send, core_rsem, xs_sem, xr_sem, ys_sem, yr_sem, zs_sem, zr_sem, ws_sem, wr_sem,
    ds_sem, dr_sem, bs_sem, br_sem, ps_sem, pr_sem, ls_sem, lr_sem,
    *, spans, inside, extent,
):
    tiles = grads_seq.shape[0]
    length = grads_seq.shape[1]
    rows, width = hidden_ref.shape
    part = 2 * LANES
    count = 2 * spans
    dp, mp = lax.axis_index("dp"), lax.axis_index("mp")
    side = lax.rem(dp, 2)
    ours = pl.ds(pl.multiple_of(side * LANES, LANES), LANES)
    others = pl.ds(pl.multiple_of((1 - side) * LANES, LANES), LANES)
    other_core = (dp, 1 - mp)

    def along(bits):
        return (jnp.bitwise_xor(dp, bits), mp)

    def remote(src, dst, send, recv, device):
        return pltpu.make_async_remote_copy(
            src_ref=src, dst_ref=dst, send_sem=send, recv_sem=recv, device_id=device,
            device_id_type=pl.DeviceIdType.MESH,
        )

    def lanes_of(number):
        return pl.ds(pair_start(number, dp, spans), part)

    def seq_fetch(sequence):
        return pltpu.make_async_copy(
            grads_hbm.at[:, pl.ds(sequence * length, length), pl.ds(0, 2 * TILE)], grads_seq, seq_sem.at[0]
        )

    def w_fetch(number, slot):
        at = pl.ds(pl.multiple_of(number * part, part), part)
        return pltpu.make_async_copy(
            weights_hbm.at[:, at, pl.ds(0, 2 * TILE)], wblk.at[slot], blk_sem.at[slot]
        )

    def normed_fetch(number, slot):
        at = pl.ds(pl.multiple_of(number * part, part), part)
        return pltpu.make_async_copy(
            normed_hbm.at[pl.ds(0, length), at], normed_blk.at[slot], blk_sem.at[2 + slot]
        )

    def core_copy(sequence, number):
        at = lanes_of(number)
        return remote(
            give_ref.at[:, at], core_recv.at[sequence, :, at], core_send.at[sequence, number],
            core_rsem.at[sequence, number], other_core,
        )

    def x_copy(number):
        at = lanes_of(number)
        return remote(x_give.at[:, at], x_recv.at[:, at], xs_sem.at[number], xr_sem.at[number], along(1))

    def y_copy(k):
        return remote(far_hbm.at[0, k], y_recv.at[k], ys_sem.at[k], yr_sem.at[k], along(2))

    def z_copy(number, k):
        src = z_send_hbm if number == 0 else z_send
        return remote(
            src.at[k - 1], z_recv.at[number, k - 1], zs_sem.at[number, k - 1], zr_sem.at[number, k - 1],
            along(4 * k),
        )

    def w_copy(number):
        return remote(w_send.at[number], w_recv.at[number], ws_sem.at[number], wr_sem.at[number], along(1))

    dbc_between = remote(dbc_ref, dbc_core, ds_sem.at[0], dr_sem.at[0], other_core)
    bc_x = remote(bc_xs, bc_xr, bs_sem.at[0], br_sem.at[0], along(1))
    bc_y = remote(bc_own.at[pl.ds(spans, spans)], bc_yr, bs_sem.at[1], br_sem.at[1], along(2))

    def bc_z(k):
        return remote(bc_own.at[k], bc_zr.at[k - 1], bs_sem.at[1 + k], br_sem.at[1 + k], along(4 * k))

    bc_between = remote(bc_own.at[0], bc_core, bs_sem.at[1 + spans], br_sem.at[1 + spans], other_core)
    bits = [1 << place for place in range(extent.bit_length() - 1)]

    def pack_copy(step):
        return remote(pack_out_ref, pack_recv.at[step], ps_sem.at[step], pr_sem.at[step], along(bits[step]))

    def pack_step(step):
        pack_copy(step).wait()
        pack_out_ref[...] += pack_recv[step]
        if step + 1 < len(bits):
            pack_copy(step + 1).start()

    def last_copy(step):
        device = along(bits[step]) if step < len(bits) else other_core
        return remote(last_ref, last_recv.at[step], ls_sem.at[step], lr_sem.at[step], device)

    def emit(tile, share, owner):
        channels = (owner * tiles + tile) * TILE
        for plane in range(2):
            lanes = pl.ds(pl.multiple_of(plane * 2 * tiles * TILE + channels, TILE), TILE)
            zx_ref[:, lanes] = share[plane * TILE : (plane + 1) * TILE, :].astype(F32).T
        out_ref[pl.ds(pl.multiple_of(channels, TILE), TILE), :] = share[OUT:, :].astype(F32)
        steps_ref[tile, owner] = share[STEPS : STEPS + 16, :].astype(F32)[:8]

    def give_total(number, total_ref):
        w_send[number] = total_ref[:, others].astype(BF16)
        w_copy(number).start()
        emit(inside - 1 + number, total_ref[:, ours], side)

    def finish_z(number, own):
        total = own[...]
        for k in range(1, spans):
            z_copy(number, k).wait()
            total = total + z_recv[number, k - 1].astype(F32)
        z_own[...] = total
        give_total(number, z_own)

    def products(sequence):
        dt_rows = jnp.concatenate(
            [
                dt_ref[tile * 16 : tile * 16 + GROUP, sequence * length : (sequence + 1) * length].astype(F32)
                for tile in range(tiles)
            ],
            axis=0,
        )
        dt_rows = jnp.concatenate([dt_rows, jnp.zeros((LANES - tiles * GROUP, length), F32)], axis=0)
        dt_cols[...] = dt_rows.T.astype(BF16)
        seq_fetch(sequence).wait()

        def one(number, carried):
            slot = lax.rem(number, 2)

            @pl.when(number + 1 < count)
            def _():
                w_fetch(number + 1, 1 - slot).start()

            w_fetch(number, slot).wait()
            at = pl.ds(pl.multiple_of(number * part, part), part)
            total = dot(dt_cols[...], small_ref[at, 2 * LANES :], NT)
            for tile in range(tiles):
                total = total + dot(grads_seq[tile], wblk[slot, tile], NT)
            acc_ref[...] = total
            lanes = lanes_of(number)
            away = pl.ds(pl.multiple_of((1 - mp) * rows, rows), rows)
            here = pl.ds(pl.multiple_of(mp * rows, rows), rows)
            give_ref[:, lanes] = acc_ref[away, :].astype(BF16)
            core_copy(sequence, number).start()
            own_ref[:, lanes] = acc_ref[here, :]
            return carried

        lax.fori_loop(0, count, one, 0)

    seq_fetch(1).start()
    w_fetch(0, 0).start()
    barrier = pltpu.get_barrier_semaphore()
    partners = [along(1), along(2), other_core] + [along(4 * k) for k in range(1, spans)]
    for device in partners:
        pl.semaphore_signal(barrier, inc=1, device_id=device, device_id_type=pl.DeviceIdType.MESH)
    pl.semaphore_wait(barrier, len(partners))
    for k in range(spans):
        y_copy(k).start()
    for k in range(1, spans):
        z_copy(0, k).start()
    dbc_between.start()
    pack_out_ref[...] = jnp.zeros_like(pack_out_ref)
    head_row = jnp.zeros((1, LANES), F32)
    for tile in range(tiles):
        lanes = pl.ds(pl.multiple_of((side * tiles + tile) * TILE, TILE), TILE)
        pack_out_ref[: GAIN + 1, lanes] = (smalls_ref[tile, 0] + smalls_ref[tile, 1])[: GAIN + 1]
        heads = heads_ref[tile, 0] + heads_ref[tile, 1]
        heads = jnp.concatenate([heads[:GROUP], heads[GROUP:] * rate_ref[tile, :GROUP]], axis=0)
        row = iota((8, LANES), 0)
        target = (row // GROUP) * 2 * HEADS + side * HEADS + tile * GROUP + row % GROUP
        head_row = head_row + jnp.sum(
            jnp.where(iota((8, LANES), 1) == target, heads, 0.0), axis=0, keepdims=True
        )
    pack_out_ref[GAIN + 1 : GAIN + 2, :LANES] = head_row
    pack_copy(0).start()
    products(1)
    seq_fetch(0).start()
    w_fetch(0, 0).start()
    pack_step(0)

    def pass_on(number, carried):
        core_copy(1, number).wait()
        lanes = lanes_of(number)
        x_give[:, lanes] = (own_ref[:, lanes] + core_recv[1, :, lanes].astype(F32)).astype(BF16)
        x_copy(number).start()
        return carried

    lax.fori_loop(0, count, pass_on, 0)
    products(0)
    pack_step(1)
    normed_fetch(0, 0).start()
    dbc_between.wait()
    conv = conv_of(proj_ref[...], col_ref[...], par_ref)
    gate = sigmoid(conv)
    d_conv = (dbc_ref[...] + dbc_core[...] + dbc_x_ref[...].astype(F32)) * (gate * (1.0 + conv * (1.0 - gate)))
    d_proj = par_ref[TAPS + 3 : TAPS + 4, :] * d_conv
    small = [None] * 4
    small[3] = jnp.sum(d_conv * proj_ref[...], axis=0, keepdims=True)
    for offset in range(1, 4):
        place = TAPS + 3 - offset
        counted = d_conv * col_ref[:, VALID + offset - 1 : VALID + offset]
        small[place] = jnp.sum(counted * pltpu.roll(proj_ref[...], offset, 0), axis=0, keepdims=True)
        d_proj = d_proj + par_ref[place : place + 1, :] * pltpu.roll(counted, length - offset, 0)
    small.append(jnp.sum(d_conv, axis=0, keepdims=True))
    conv_grads = jnp.concatenate(small + [jnp.zeros((3, part), F32)], axis=0)
    dbc_low[...] = d_proj.astype(BF16)
    finish_z(0, z_own_ref)
    for tile in range(inside - 1):
        emit(tile, mine_ref[tile], side)
        emit(tile, theirs_ref[tile], 1 - side)
    for k in range(spans):
        y_copy(k).wait()
        total = near_ref[0, k] + y_recv[k].astype(F32)
        if k == 0:
            z_own[...] = total
        else:
            z_send[k - 1] = total.astype(BF16)
            z_copy(1, k).start()
    half = pl.ds(pl.multiple_of(mp * LANES, LANES), LANES)
    turned = dbc_low[:, half].T

    def bc_product(number, carried):
        slot = lax.rem(number, 2)

        @pl.when(number + 1 < count)
        def _():
            normed_fetch(number + 1, 1 - slot).start()

        normed_fetch(number, slot).wait()
        bc_grad[...] = dot(turned, normed_blk[slot])
        bc_own[number] = bc_grad[:, ours]
        bc_xs[number] = bc_grad[:, others]
        return carried

    lax.fori_loop(0, count, bc_product, 0)
    bc_x.start()
    pack_step(2)
    here = pl.ds(pl.multiple_of(mp * rows, rows), rows)

    def add_core(number, carried):
        core_copy(0, number).wait_recv()
        lanes = lanes_of(number)
        at = pl.ds(pl.multiple_of(number * part, part), part)
        own_ref[:, lanes] += core_recv[0, :, lanes].astype(F32) + dot(
            dbc_low[here, :], small_ref[at, : 2 * LANES], NT
        )
        return carried

    lax.fori_loop(0, count, add_core, 0)
    pack_step(3)
    for step in range(4, len(bits)):
        pack_step(step)
    bc_x.wait()
    bc_own[...] += bc_xr[...]
    bc_y.start()
    finish_z(1, z_own)
    bc_y.wait()
    bc_own[:spans] += bc_yr[...]
    for k in range(1, spans):
        bc_z(k).start()

    def add_x(number, carried):
        x_copy(number).wait_recv()
        lanes = lanes_of(number)
        own_ref[:, lanes] += x_recv[:, lanes].astype(F32)
        return carried

    lax.fori_loop(0, count, add_x, 0)
    last_ref[...] = jnp.zeros_like(last_ref)
    last_ref[:, part : 2 * part] = 0.5 * conv_grads
    last_ref[:, 2 * part : 2 * part + LANES] = sums_ref[...]
    step_rows = 64

    def finish(number, gain_sum):
        at = pl.ds(pl.multiple_of(number * step_rows, step_rows), step_rows)
        u, d_normed = hidden_ref[at, :].astype(F32), own_ref[at, :]
        inv = inv_ref[at, :]
        scaled = gain_ref[...] * d_normed
        mean = jnp.mean(u * scaled, axis=-1, keepdims=True)
        own_ref[at, :] = cot_ref[at, :].astype(F32) + inv * scaled - u * (inv * inv * inv * mean)
        return gain_sum + jnp.sum(d_normed * u * inv, axis=0, keepdims=True)

    gain_sum = lax.fori_loop(0, rows // step_rows, finish, jnp.zeros((1, width), F32))
    out = pltpu.make_async_copy(own_ref, grad_out, out_sem.at[0])
    out.start()
    for number in range(8):
        last_ref[number : number + 1, :part] = gain_sum[:, number * part : (number + 1) * part]
    for step in range(len(bits) + 1):
        last_copy(step).start()
        if step == 1:
            total = bc_own[0]
            for k in range(1, spans):
                bc_z(k).wait()
                total = total + bc_zr[k - 1]
            bc_own[0] = total
            bc_between.start()
        last_copy(step).wait()
        last_ref[...] += last_recv[step]
    bc_between.wait()
    first = jnp.where(mp == 0, 1.0, 0.0)
    bc_out_ref[:LANES, :] = first * bc_own[0] + (1.0 - first) * bc_core[...]
    bc_out_ref[LANES:, :] = (1.0 - first) * bc_own[0] + first * bc_core[...]
    for number in range(2):
        w_copy(number).wait()
        emit(inside - 1 + number, w_recv[number], 1 - side)
    for number in range(count):
        core_copy(0, number).wait_send()
        x_copy(number).wait_send()
    out.wait()


def run_tail(
    hidden, cot, inv, gain, grads, weights, small, dts, far_share, near_share, z_own, z_send, mine, theirs, dbc,
    dbc_x, proj, col, bc_par, normed, smalls, heads, rate, sums, length, spans, extent,
):
    rows, width = hidden.shape
    tiles, tokens = grads.shape[:2]
    part, inside = 2 * LANES, tiles - 1
    hops = extent.bit_length() - 1
    channels = 2 * tiles * TILE
    dma = pltpu.SemaphoreType.DMA

    def full(*shape):
        return pl.BlockSpec(shape, lambda i: (0,) * len(shape))

    return pl.pallas_call(
        functools.partial(tail_kernel, spans=spans, inside=inside, extent=extent),
        grid=(1,),
        in_specs=[
            full(rows, width),
            full(rows, width),
            full(rows, 1),
            full(1, width),
            ANY,
            ANY,
            full(*small.shape),
            full(*dts.shape),
            ANY,
            full(*near_share.shape),
            full(*z_own.shape),
            ANY,
            full(*mine.shape),
            full(*theirs.shape),
            full(length, part),
            full(length, part),
            full(length, part),
            full(length, COLS),
            full(8, part),
            ANY,
            full(*smalls.shape),
            full(*heads.shape),
            full(*rate.shape),
            full(8, LANES),
        ],
        out_specs=[
            ANY,
            full(LANES, 2 * channels),
            full(channels, LANES),
            full(tiles, 2, 8, LANES),
            full(part, LANES),
            full(8, channels),
            full(8, 3 * part),
        ],
        out_shape=[
            shaped((rows, width)),
            shaped((LANES, 2 * channels)),
            shaped((channels, LANES)),
            shaped((tiles, 2, 8, LANES)),
            shaped((part, LANES)),
            shaped((8, channels)),
            shaped((8, 3 * part)),
        ],
        scratch_shapes=[
            pltpu.VMEM((tiles, length, 2 * TILE), BF16),
            pltpu.VMEM((2, tiles, part, 2 * TILE), BF16),
            pltpu.VMEM((length, part), F32),
            pltpu.VMEM((rows, width), BF16),
            pltpu.VMEM((2, rows, width), BF16),
            pltpu.VMEM((rows, width), F32),
            pltpu.VMEM((rows, width), BF16),
            pltpu.VMEM((rows, width), BF16),
            pltpu.VMEM((spans, SHARE, part), BF16),
            pltpu.VMEM((spans - 1, SHARE, part), BF16),
            pltpu.VMEM((SHARE, part), F32),
            pltpu.VMEM((2, spans - 1, SHARE, part), BF16),
            pltpu.VMEM((2, SHARE, LANES), BF16),
            pltpu.VMEM((2, SHARE, LANES), BF16),
            pltpu.VMEM((length, part), F32),
            pltpu.VMEM((length, part), BF16),
            pltpu.VMEM((length, LANES), BF16),
            pltpu.VMEM((2, length, part), BF16),
            pltpu.VMEM((LANES, part), F32),
            pltpu.VMEM((2 * spans, LANES, LANES), F32),
            pltpu.VMEM((2 * spans, LANES, LANES), F32),
            pltpu.VMEM((2 * spans, LANES, LANES), F32),
            pltpu.VMEM((spans, LANES, LANES), F32),
            pltpu.VMEM((spans - 1, LANES, LANES), F32),
            pltpu.VMEM((LANES, LANES), F32),
            pltpu.VMEM((hops, 8, channels), F32),
            pltpu.VMEM((hops + 1, 8, 3 * part), F32),
            dma((1,)),
            dma((4,)),
            dma((1,)),
            dma((2, 2 * spans)),
            dma((2, 2 * spans)),
            dma((2 * spans,)),
            dma((2 * spans,)),
            dma((spans,)),
            dma((spans,)),
            dma((2, spans - 1)),
            dma((2, spans - 1)),
            dma((2,)),
            dma((2,)),
            dma((1,)),
            dma((1,)),
            dma((2 + spans,)),
            dma((2 + spans,)),
            dma((hops,)),
            dma((hops,)),
            dma((hops + 1,)),
            dma((hops + 1,)),
        ],
        compiler_params=pltpu.CompilerParams(
            vmem_limit_bytes=VMEM_LIMIT, collective_id=3, has_side_effects=True
        ),
        cost_estimate=cost(1e11),
    )(
        hidden, cot, inv, gain, grads, weights, small, dts, far_share, near_share, z_own, z_send, mine, theirs, dbc,
        dbc_x, proj, col, bc_par, normed, smalls, heads, rate, sums,
    )


def segment_conv(inputs, taps, bias, masks):
    reach = taps.shape[0]
    result = bias[None, :] + taps[reach - 1][None, :] * inputs
    for offset in range(1, reach):
        moved = jnp.concatenate(
            [jnp.zeros((offset, inputs.shape[1]), inputs.dtype), inputs[:-offset]], axis=0
        )
        result = result + taps[reach - 1 - offset][None, :] * (
            moved * masks[:, offset - 1 : offset]
        )
    return result


def local(
    hidden_in,
    segments,
    norm_gain,
    w_zx,
    w_dt,
    w_bc,
    conv_x,
    conv_x_bias,
    conv_bc,
    conv_bc_bias,
    dt_bias,
    a_log,
    d_skip,
    gated_gain,
    w_out,
    cotangent,
):
    dp, mp = lax.axis_index("dp"), lax.axis_index("mp")
    extent = lax.axis_size("dp")
    far = extent // 4
    x_side = lax.rem(dp, 2)
    rows, width = hidden_in.shape
    length = segments.shape[0]
    inner = conv_x.shape[1]
    inner_total = inner * lax.axis_size("mp")
    heads = dt_bias.shape[0]
    quarter, own_heads = inner // 2, heads // 2
    tiles = quarter // TILE
    depth = w_zx.shape[0]

    def by_side(own, other, axis):
        return jnp.where(
            x_side == 0,
            jnp.concatenate([own, other], axis=axis),
            jnp.concatenate([other, own], axis=axis),
        )

    def by_core(own, other, axis):
        return jnp.where(
            mp == 0,
            jnp.concatenate([own, other], axis=axis),
            jnp.concatenate([other, own], axis=axis),
        )

    def of_side(a, side, axis):
        size = a.shape[axis] // 2
        return lax.dynamic_slice_in_dim(a, side * size, size, axis)

    packed = jnp.concatenate([w_zx[:, 0], w_zx[:, 1], w_out.T], axis=1)
    packed = packed.reshape(depth, 3, 2, tiles, TILE).transpose(2, 3, 0, 1, 4)
    packed = packed.reshape(2, tiles, depth, 3 * TILE)

    def small_weights(side):
        filler = jnp.zeros((depth, LANES - own_heads), BF16)
        return jnp.concatenate([w_bc, of_side(w_dt, side, 1), filler], axis=1)

    packed_own = lax.dynamic_index_in_dim(packed, x_side, 0, False)
    packed_other = lax.dynamic_index_in_dim(packed, 1 - x_side, 0, False)

    def gathered(piece):
        near = [piece] + [flip(piece, "dp", 4 * k) for k in range(1, far)]
        return near + [flip(p, "dp", 2) for p in near]

    normed, cot, inverse_rows = input_norm(hidden_in, cotangent, norm_gain, dp, extent)

    ids = (segments, flip(segments, "dp", 1))
    ids_all = jnp.concatenate(ids, axis=0).astype(F32)
    side_bias = of_side(dt_bias, x_side, 0)
    rate = -jnp.exp(of_side(a_log, x_side, 0))
    bc_par = jnp.concatenate([conv_bc, conv_bc_bias[None], jnp.zeros((3, 2 * LANES), F32)], axis=0)
    head_par = jnp.pad(jnp.stack([side_bias, rate]), ((0, 6), (0, LANES - own_heads)))
    params = jnp.concatenate(
        [
            of_side(conv_x, x_side, 1),
            of_side(conv_x_bias, x_side, 0)[None],
            of_side(jnp.repeat(d_skip, WIDTH), x_side, 0)[None],
            of_side(gated_gain, x_side, 0)[None],
            jnp.zeros((1, quarter), F32),
        ],
        axis=0,
    )
    params = params.reshape(8, tiles, TILE).transpose(1, 0, 2)
    tokens = 2 * length
    if depth == LANES:
        (
            normed_all, cot_all, weights, bc_weight, zvs, dyns, ys, states, proj_bc, bc, wide, col, rows_all, turned, norms,
        ) = run_gather(
            normed, cot, packed_own, packed_other, small_weights(x_side), small_weights(1 - x_side), ids_all,
            bc_par, head_par, params, length, far, inner_total,
        )
    else:

        def both_sequences(a):
            near = flip(a, "dp", 1)
            return jnp.concatenate(
                [by_core(a, flip(a, "mp", 1), 0), by_core(near, flip(near, "mp", 1), 0)], axis=0
            )

        normed_all, cot_all = both_sequences(normed), both_sequences(cot)
        packed_other = flip(packed_other, "dp", 1)
        small_other = flip(small_weights(1 - x_side), "dp", 1)
        bc_weight = jnp.concatenate(gathered(by_side(small_weights(x_side), small_other, 0)), axis=0)
        proj_bc, bc, wide, col, rows_all, score, turned = run_tables(
            normed_all, bc_weight, ids_all, bc_par, head_par, length
        )
        results = []
        for tile in range(tiles):
            pieces = gathered(by_side(packed_own[tile], packed_other[tile], 0))
            results.append(
                run_forward(
                    pieces, normed_all, cot_all, bc, wide, col, rows_all, score, params[tile], tile, length
                )
            )
        weights, zvs, dyns, ys, states, sums = [jnp.stack(part) for part in zip(*results)]
        sums = jnp.sum(sums, axis=0)
        sums = sums + flip(sums, "mp", 1)
        near = flip(sums, "dp", 1)
        sums = sums + jnp.concatenate([near[:, length:], near[:, :length]], axis=1)
        norms = norm_rows(sums, inner_total)

    inputs = hidden_in.astype(F32)
    usable = (lax.dynamic_slice_in_dim(segments, mp * rows, rows, 0) >= 0).astype(F32)[:, None]
    native = depth == LANES
    norm_cols = norms.T
    ties = []
    if native:
        mixer_own, mixer_give = run_mixer(zvs, ys, norm_cols, params, weights, rows, length, far)
        ties = [mixer_own]
        mixer_out = mixer_own + flip(mixer_give, "dp", 1).astype(F32)

    rate_rows = jnp.pad(rate.reshape(tiles, GROUP, 1), ((0, 0), (0, 8 - GROUP), (0, 0)))
    rate_rows = jnp.broadcast_to(rate_rows, (tiles, 8, LANES))
    inside, results = run_backward(
        ties, normed_all, cot_all, zvs, ys, dyns, bc, wide, col, rows_all, ids_all, turned, norm_cols, params,
        rate_rows, states, length, far,
    )
    (
        grads, dbc, dts, head_sums, smalls, far_share, near_share, z_own, z_send, mine, theirs, dbc_x,
    ) = results

    def placed(a):
        return by_side(a, jnp.zeros_like(a), a.ndim - 1)

    def summed(a, axes):
        for axis in axes:
            bit = 1
            while bit < lax.axis_size(axis):
                a = a + flip(a, axis, bit)
                bit *= 2
        return a

    def mixer_sums(mixer_out):
        return jnp.stack(
            [
                jnp.sum(usable * inputs * inputs),
                jnp.sum(usable * mixer_out * mixer_out),
                jnp.sum(usable),
            ]
        )

    if native:
        sums = jnp.pad(mixer_sums(mixer_out)[None], ((0, 7), (0, LANES - 3)))
        input_grad, grad_zx, grad_out_weight, grad_steps, grad_bc, pack, last = run_tail(
            hidden_in, cotangent, inverse_rows, norm_gain[None], grads, weights, bc_weight, dts, far_share,
            near_share, z_own, z_send, mine, theirs, dbc, dbc_x, proj_bc, col, bc_par, normed_all, smalls,
            head_sums, rate_rows, sums, length, far, extent,
        )
        grad_zx_weight = grad_zx.reshape(depth, 2, inner)
        grad_dt_weight = grad_steps[:, :, :GROUP].transpose(1, 0, 2, 3).reshape(heads, depth).T
        grad_bc_weight = grad_bc.T
        part = 2 * LANES
        grad_norm_gain = last[:, :part].reshape(width)
        grad_conv_bc, grad_conv_bc_bias = last[:4, part : 2 * part], last[4, part : 2 * part]
        totals = last[0, 2 * part : 2 * part + 3]
    else:

        def spread_sum(far_part, near_part):
            def arranged(a):
                return a.transpose(1, 0, 2).reshape(SHARE, far, 2 * depth).transpose(1, 0, 2)

            total = arranged(near_part) + arranged(flip(far_part, "dp", 2)).astype(F32)
            out = total.astype(BF16)
            total = total[0]
            for k in range(1, far):
                total = total + flip(out[k], "dp", 4 * k).astype(F32)
            return total

        stacked = jnp.stack([spread_sum(far_share[at], near_share[at]) for at in range(tiles)])
        mine = of_side(stacked, x_side, 2)
        theirs = flip(of_side(stacked, 1 - x_side, 2).astype(BF16), "dp", 1).astype(F32)

        dbc = dbc + flip(dbc, "mp", 1)
        dbc = dbc[:length] + flip(dbc[length:], "dp", 1)
        own_masks = col[:length, VALID : VALID + 3]
        _, state_back = jax.vjp(
            lambda values, taps, bias: jax.nn.silu(segment_conv(values, taps, bias, own_masks)),
            proj_bc[:length],
            conv_bc,
            conv_bc_bias,
        )
        d_bc, grad_conv_bc, grad_conv_bc_bias = state_back(dbc)
        bc_grad = d_bc.astype(BF16)
        small_grad = dot(normed_all[:length], lax.dynamic_slice_in_dim(bc_grad, mp * LANES, LANES, 1), TN)
        small_grad = small_grad.reshape(2 * far, 2, depth, -1)
        small_grad = of_side(small_grad, x_side, 1) + flip(of_side(small_grad, 1 - x_side, 1), "dp", 1)
        small_grad = small_grad.reshape(2, far, depth, -1)
        small_grad = small_grad[0] + flip(small_grad[1], "dp", 2)
        own_bc = small_grad[0]
        for k in range(1, far):
            own_bc = own_bc + flip(small_grad[k], "dp", 4 * k)
        grad_bc_weight = by_core(own_bc, flip(own_bc, "mp", 1), 1)

        def token_sum(products):
            def part(core):
                return products(
                    lambda a: of_side(a.reshape(2, 2, rows, -1), core, 1).reshape(2 * rows, -1)
                )

            total = part(mp) + flip(part(1 - mp).astype(BF16), "mp", 1).astype(F32)
            return total[:rows] + flip(total[rows:].astype(BF16), "dp", 1).astype(F32)

        out_all = jnp.concatenate([w[:, 2 * TILE :] for w in weights], axis=1)
        yn_all = jnp.concatenate([g[:, 2 * TILE :] for g in grads], axis=1)
        mixer_out = restore_order(token_sum(lambda pick: dot(pick(yn_all), out_all, NT)), dp, extent)
        zv_all = jnp.concatenate([w[:, : 2 * TILE] for w in weights], axis=1)
        dt_weight = bc_weight[:, 2 * LANES : 2 * LANES + own_heads]
        dzx_all = jnp.concatenate([g[:, : 2 * TILE] for g in grads], axis=1)
        dt_grad = dts.reshape(tiles, 16, tokens)[:, :GROUP].reshape(own_heads, tokens).T
        d_normed = token_sum(
            lambda pick: dot(pick(dzx_all), zv_all, NT) + dot(pick(dt_grad), dt_weight, NT)
        )
        d_normed = d_normed + dot(
            lax.dynamic_slice_in_dim(bc_grad, mp * rows, rows, 0), bc_weight[:, : 2 * LANES], NT
        )
        d_normed = restore_order(d_normed, dp, extent)
        grad_norm_gain = jnp.sum(d_normed * inputs * inverse_rows, axis=0)
        inverse_cube_rows = inverse_rows * inverse_rows * inverse_rows
        input_grad = (
            cotangent.astype(F32)
            + inverse_rows * norm_gain * d_normed
            - inputs
            * inverse_cube_rows
            * jnp.mean(inputs * norm_gain * d_normed, axis=-1, keepdims=True)
        )
        small = jnp.sum(smalls, axis=1).transpose(1, 0, 2).reshape(8, quarter)
        head_sums = jnp.sum(head_sums[..., 0], axis=1)
        grad_dt_bias = placed(head_sums[:, :GROUP].reshape(own_heads))
        grad_a_log = placed(head_sums[:, GROUP:].reshape(own_heads) * rate)
        head_row = jnp.pad(jnp.concatenate([grad_dt_bias, grad_a_log]), (0, inner - 2 * heads))
        pack = jnp.concatenate([placed(small[: GAIN + 1]), head_row[None]], axis=0)
        pack = summed(pack, ("dp",))
        conv_sums = jnp.concatenate([grad_conv_bc, grad_conv_bc_bias[None]], axis=0)
        conv_sums = summed(conv_sums, ("dp",))
        grad_conv_bc, grad_conv_bc_bias = conv_sums[:4], conv_sums[4]
        last = summed(jnp.concatenate([grad_norm_gain, mixer_sums(mixer_out)]), ("mp", "dp"))
        grad_norm_gain, totals = last[:width], last[width:]

        def assembled(first, last_row):
            def columns(a):
                return a[:, first:last_row].reshape(-1, depth)

            return by_side(columns(mine), columns(theirs), 0)

        grad_zx_weight = jnp.stack([assembled(0, TILE).T, assembled(TILE, STEPS).T], axis=1)
        grad_dt_weight = assembled(STEPS, STEPS + GROUP).T
        grad_out_weight = assembled(OUT, SHARE)

    residual_out = (inputs + mixer_out).astype(BF16)
    skip_grad = jnp.sum(pack[SKIP].reshape(heads, WIDTH), axis=1)
    sum_inputs, sum_mixer, usable_count = totals[0], totals[1], totals[2]
    rms_residual = jnp.sqrt(sum_inputs / (usable_count * width))
    rms_mixer = jnp.sqrt(sum_mixer / (usable_count * width))
    return (
        residual_out,
        input_grad,
        grad_norm_gain,
        grad_zx_weight,
        grad_dt_weight,
        grad_bc_weight,
        pack[TAPS:BIAS],
        pack[BIAS],
        grad_conv_bc,
        grad_conv_bc_bias,
        pack[GAIN + 1, :heads],
        pack[GAIN + 1, heads : 2 * heads],
        skip_grad,
        pack[GAIN],
        grad_out_weight,
        rms_residual,
        rms_mixer,
    )


def solution(mesh):
    in_specs = (
        P(("dp", "mp"), None),
        P("dp"),
        P(),
        P("dp", None, "mp"),
        P("dp", "mp"),
        P("dp", None),
        P(None, "mp"),
        P("mp"),
        P(),
        P(),
        P("mp"),
        P("mp"),
        P("mp"),
        P("mp"),
        P("mp", "dp"),
        P(("dp", "mp"), None),
    )
    out_specs = (
        P(("dp", "mp"), None),
        P(("dp", "mp"), None),
        P(),
        P("dp", None, "mp"),
        P("dp", "mp"),
        P("dp", None),
        P(None, "mp"),
        P("mp"),
        P(),
        P(),
        P("mp"),
        P("mp"),
        P("mp"),
        P("mp"),
        P("mp", "dp"),
        P(),
        P(),
    )
    return jax.shard_map(local, mesh=mesh, in_specs=in_specs, out_specs=out_specs, check_vma=False)
```

```python
import functools

import jax
import jax.numpy as jnp
import numpy as np
from jax import lax
from jax.experimental import pallas as pl
from jax.experimental.pallas import tpu as pltpu
from jax.sharding import PartitionSpec as P

BLOCK = 256
LANES = 128
TILE = 256
WIDTH = 64
GROUP = TILE // WIDTH
EPSILON = 1e-05
HIGH = lax.Precision.HIGHEST
BF16 = jnp.bfloat16
F32 = jnp.float32
VMEM_LIMIT = 60 * 2**20

NN = (((1,), (0,)), ((), ()))
NT = (((1,), (1,)), ((), ()))
TN = (((0,), (0,)), ((), ()))


def dot(a, b, dims=NN, precision=None):
    return lax.dot_general(a, b, dims, precision=precision, preferred_element_type=F32)


def low_dot(a, b, dims=NN):
    return dot(a.astype(BF16), b.astype(BF16), dims)


def flip(a, axis, bit):
    size = lax.axis_size(axis)
    return lax.ppermute(a, axis, [(i, i ^ bit) for i in range(size)])


def sigmoid(q):
    return 1.0 / (1.0 + jnp.exp(-q))


def owner_block(number, dp, extent):
    y, z, x = number // (extent // 2), (number // 2) % (extent // 4), number % 2
    return jnp.bitwise_xor(dp - lax.rem(dp, 2), (y * 2) + (z * 4) + x)


def norm_kernel(place_ref, hidden_ref, cot_ref, gain_ref, normed_ref, cot_out_ref, inv_ref, *, extent):
    u = hidden_ref[...].astype(F32)
    inv = lax.rsqrt(jnp.mean(u * u, axis=-1, keepdims=True) + EPSILON)
    inv_ref[...] = inv
    for number in range(extent):
        start = pl.multiple_of(owner_block(number, place_ref[0], extent) * LANES, LANES)
        piece = hidden_ref[:, pl.ds(start, LANES)].astype(F32)
        gain = gain_ref[:, pl.ds(start, LANES)]
        normed_ref[:, number * LANES : (number + 1) * LANES] = (piece * inv * gain).astype(BF16)
        cot_out_ref[:, number * LANES : (number + 1) * LANES] = cot_ref[:, pl.ds(start, LANES)]


def input_norm(hidden, cot, gain, dp, extent):
    rows, width = hidden.shape
    if width // extent != LANES:
        u = hidden.astype(F32)
        inv = lax.rsqrt(jnp.mean(u * u, axis=-1, keepdims=True) + EPSILON)
        normed = (u * inv * gain).astype(BF16)
        order = owner_block(jnp.arange(extent), dp, extent)

        def arranged(a):
            return jnp.take(a.reshape(rows, extent, -1), order, axis=1).reshape(rows, width)

        return arranged(normed), arranged(cot), inv
    step = 128
    tile = pl.BlockSpec((step, width), lambda i: (i, 0))
    return pl.pallas_call(
        functools.partial(norm_kernel, extent=extent),
        grid=(rows // step,),
        in_specs=[
            pl.BlockSpec(memory_space=pltpu.SMEM),
            tile,
            tile,
            pl.BlockSpec((1, width), lambda i: (0, 0)),
        ],
        out_specs=[tile, tile, pl.BlockSpec((step, 1), lambda i: (i, 0))],
        out_shape=[
            jax.ShapeDtypeStruct((rows, width), BF16),
            jax.ShapeDtypeStruct((rows, width), BF16),
            jax.ShapeDtypeStruct((rows, 1), F32),
        ],
        compiler_params=pltpu.CompilerParams(vmem_limit_bytes=VMEM_LIMIT),
    )(dp.reshape(1), hidden, cot, gain.reshape(1, width))


def restore_kernel(place_ref, in_ref, out_ref, *, extent):
    for number in range(extent):
        start = pl.multiple_of(owner_block(number, place_ref[0], extent) * LANES, LANES)
        out_ref[:, pl.ds(start, LANES)] = in_ref[:, number * LANES : (number + 1) * LANES]


def restore_order(a, dp, extent):
    rows, width = a.shape
    if width // extent != LANES:
        order = owner_block(jnp.arange(extent), dp, extent)
        back = jnp.argsort(order)
        return jnp.take(a.reshape(rows, extent, -1), back, axis=1).reshape(rows, width)
    step = 128
    tile = pl.BlockSpec((step, width), lambda i: (i, 0))
    return pl.pallas_call(
        functools.partial(restore_kernel, extent=extent),
        grid=(rows // step,),
        in_specs=[pl.BlockSpec(memory_space=pltpu.SMEM), tile],
        out_specs=tile,
        out_shape=jax.ShapeDtypeStruct((rows, width), a.dtype),
        compiler_params=pltpu.CompilerParams(vmem_limit_bytes=VMEM_LIMIT),
    )(dp.reshape(1), a)


VALID, LINK, KEEP, SEG = 0, 3, 4, 5
COLS = 8
HEADS = 16
TAPS, BIAS, SKIP, GAIN = 0, 4, 5, 6
STEPS, OUT, SHARE = 2 * TILE, 2 * TILE + 16, 3 * TILE + 16
ANY = pl.BlockSpec(memory_space=pl.ANY)


def iota(shape, axis):
    return lax.broadcasted_iota(jnp.int32, shape, axis)


def thirds(a):
    high = a.astype(BF16)
    rest = a - high.astype(F32)
    mid = rest.astype(BF16)
    return [high, mid, (rest - mid.astype(F32)).astype(BF16)]


def halves(a):
    high = a.astype(BF16)
    return [high, (a - high.astype(F32)).astype(BF16)]


def conv_of(v, col, par_ref):
    result = par_ref[BIAS : BIAS + 1, :] + par_ref[TAPS + 3 : TAPS + 4, :] * v
    for offset in range(1, 4):
        valid = col[:, VALID + offset - 1 : VALID + offset]
        result = result + par_ref[TAPS + 3 - offset : TAPS + 4 - offset, :] * (
            pltpu.roll(v, offset, 0) * valid
        )
    return result


def pair_mask(seg_col, seg_row, transposed):
    down, across = iota((BLOCK, BLOCK), 0), iota((BLOCK, BLOCK), 1)
    causal = down <= across if transposed else down >= across
    return causal & (seg_col == seg_row)


def table_part(
    origin, length, normed_ref, weight_ref, seg_col_ref, seg_row_ref, par_ref, head_ref,
    proj_ref, bc_ref, wide_ref, col_ref, row_ref, score_ref, turned_ref,
):
    every = pl.ds(origin, length)
    blocks = length // BLOCK

    def spot(block):
        return pl.ds(pl.multiple_of(origin + block * BLOCK, BLOCK), BLOCK)

    proj = dot(normed_ref[every, :], weight_ref[...])
    proj_ref[every, :] = proj[:, : 2 * LANES]
    raw = jnp.where(
        head_ref[2:3, :HEADS] == 0.0,
        proj[:, 2 * LANES : 2 * LANES + HEADS],
        proj[:, 2 * LANES + HEADS : 2 * LANES + 2 * HEADS],
    )
    raw = raw + head_ref[0:1, :HEADS]
    dt = jnp.maximum(raw, 0.0) + jnp.log1p(jnp.exp(-jnp.abs(raw)))
    step = dt * head_ref[1:2, :HEADS]
    seg = seg_col_ref[every, :]
    place = iota((length, 1), 0)
    number = place // BLOCK
    before, last = jnp.full((length, 1), -2.0, F32), jnp.zeros((length, 1), F32)
    for block in range(blocks):
        end = seg[(block + 1) * BLOCK - 1 : (block + 1) * BLOCK, :]
        last = jnp.where(number == block, end, last)
        before = jnp.where(number == block + 1, end, before)
    lower = (iota((BLOCK, BLOCK), 0) >= iota((BLOCK, BLOCK), 1)).astype(F32)
    upper = (iota((BLOCK, BLOCK), 0) <= iota((BLOCK, BLOCK), 1)).astype(F32)
    eye = (iota((BLOCK, BLOCK), 0) == iota((BLOCK, BLOCK), 1)).astype(F32)
    cums = []
    for block in range(blocks):
        rows = slice(block * BLOCK, (block + 1) * BLOCK)
        cums.append(dot(lower, step[rows], NN, HIGH))
        cum_rows = dot(step[rows], upper, TN, HIGH)
        raw_rows = dot(raw[rows], eye, TN, HIGH)
        for tile in range(HEADS // GROUP):
            heads = slice(tile * GROUP, (tile + 1) * GROUP)
            row_ref[tile * 8 : (tile + 1) * 8, spot(block)] = jnp.concatenate(
                [cum_rows[heads], raw_rows[heads]], axis=0
            )
    cum = jnp.concatenate(cums, axis=0)
    lane = iota((length, COLS), 1)
    col = jnp.zeros((length, COLS), F32)
    for offset in range(1, 4):
        valid = (pltpu.roll(seg, offset, 0) == seg) & (place >= offset)
        col = jnp.where(lane == VALID + offset - 1, valid.astype(F32), col)
    col = jnp.where(lane == LINK, (seg == before).astype(F32), col)
    col = jnp.where(lane == KEEP, (seg == last).astype(F32), col)
    col = jnp.where(lane == SEG, seg, col)
    col_ref[every, :] = col
    wide_ref[every, :] = jnp.concatenate(
        thirds(dt) + thirds(cum) + [jnp.zeros((length, LANES - 6 * HEADS), BF16)], axis=1
    )
    conv = conv_of(proj[:, : 2 * LANES], col, par_ref)
    bc_ref[every, :] = conv * sigmoid(conv)
    for block in range(blocks):
        rows = slice(block * BLOCK, (block + 1) * BLOCK)
        at = spot(block)
        b_rows, c_rows = bc_ref[at, :LANES], bc_ref[at, LANES:]
        seg_col, seg_row = seg[rows], seg_row_ref[:, at]
        score_ref[at, :] = jnp.where(
            pair_mask(seg_col, seg_row, False), dot(c_rows, b_rows, NT, HIGH), 0.0
        )
        turned_ref[at, :] = jnp.where(
            pair_mask(seg_col, seg_row, True), dot(b_rows, c_rows, NT, HIGH), 0.0
        )


def table_kernel(*refs):
    table_part(0, refs[0].shape[0], *refs)


def forward_tile(
    origin, first_row, normed_ref, cot_ref, w_ref, bc_ref, wide_ref, pick_ref, col_ref, row_ref, score_ref,
    par_ref, z_ref, dyn_ref, y_ref, state_ref, sum_ref, carry_ref,
):
    length = z_ref.shape[0]
    blocks = length // BLOCK

    def spot(number):
        return pl.ds(pl.multiple_of(origin + number * BLOCK, BLOCK), BLOCK)


    def project(number, carried):
        rows = pl.ds(pl.multiple_of(number * 2 * BLOCK, 2 * BLOCK), 2 * BLOCK)
        at = pl.ds(pl.multiple_of(origin + number * 2 * BLOCK, 2 * BLOCK), 2 * BLOCK)
        z_ref[rows, :] = dot(normed_ref[at, :], w_ref[:, : 2 * TILE])
        dyn_ref[rows, :] = dot(cot_ref[at, :], w_ref[:, 2 * TILE :])
        return carried

    lax.fori_loop(0, blocks // 2, project, 0)
    carry_ref[...] = jnp.zeros_like(carry_ref)

    def row_sum(a):
        return jnp.sum(a, axis=1, keepdims=True)

    def one_block(number, carried):
        rows, at = pl.ds(pl.multiple_of(number * BLOCK, BLOCK), BLOCK), spot(number)
        b_rows, c_rows = bc_ref[at, :LANES], bc_ref[at, LANES:]
        col = col_ref[at, :]
        scores = score_ref[at, :]
        start = number * BLOCK
        v = z_ref[rows, TILE:]
        above = z_ref[pl.ds(pl.multiple_of(jnp.maximum(start - 8, 0), 8), 8), TILE:]
        joined = jnp.concatenate([above, v], axis=0)
        conv = par_ref[BIAS : BIAS + 1, :] + par_ref[TAPS + 3 : TAPS + 4, :] * v
        for offset in range(1, 4):
            moved = pltpu.roll(joined, offset, 0)[8:] * col[:, VALID + offset - 1 : VALID + offset]
            conv = conv + par_ref[TAPS + 3 - offset : TAPS + 4 - offset, :] * moved
        x = conv * sigmoid(conv)
        wide = dot(wide_ref[at, :], pick_ref[...])
        dt_wide, cum_wide = wide[:, :TILE], wide[:, TILE:]
        cum_rows = row_ref[pl.ds(first_row, 8), at]
        dtx = x * dt_wide
        dtx_low = dtx.astype(BF16)
        parts = []
        for head in range(GROUP):
            gap = cum_wide[:, head * WIDTH : head * WIDTH + 1] - cum_rows[head : head + 1, :]
            mixing = scores * jnp.exp(jnp.minimum(gap, 0.0))
            parts.append(dot(mixing.astype(BF16), dtx_low[:, head * WIDTH : (head + 1) * WIDTH]))
        within = jnp.concatenate(parts, axis=1)
        state = carry_ref[...]
        state_ref[number] = state
        decay = jnp.exp(cum_wide) * col[:, LINK : LINK + 1]
        y = within + low_dot(c_rows, state) * decay + par_ref[SKIP : SKIP + 1, :] * x
        weight = jnp.exp(cum_wide[BLOCK - 1 :, :] - cum_wide) * col[:, KEEP : KEEP + 1]
        carry_ref[...] = state * decay[BLOCK - 1 :, :] + low_dot(b_rows, dtx * weight, TN)
        y_ref[rows, :] = y
        z = z_ref[rows, :TILE]
        yg = y * z * sigmoid(z)
        first = row_sum(yg * yg)
        second = row_sum(yg * par_ref[GAIN : GAIN + 1, :] * dyn_ref[rows, :])
        both = jnp.concatenate([first, second, jnp.zeros((BLOCK, LANES - 2), F32)], axis=1).T
        sum_ref[:, at] += both[:8]
        return carried

    lax.fori_loop(0, blocks, one_block, 0)


def forward_kernel(*refs, pieces):
    normed_ref, cot_ref, bc_ref, wide_ref, pick_ref, col_ref, row_ref, score_ref, par_ref = refs[pieces : pieces + 9]
    w_ref, z_ref, dyn_ref, y_ref, state_ref, sum_ref, carry_ref = refs[pieces + 9 :]

    @pl.when(pl.program_id(0) == 0)
    def _():
        depth = refs[0].shape[0]
        for number in range(pieces):
            w_ref[number * depth : (number + 1) * depth, :] = refs[number][...]

    sum_ref[...] = jnp.zeros_like(sum_ref)
    forward_tile(
        0, 0, normed_ref, cot_ref, w_ref, bc_ref, wide_ref, pick_ref, col_ref, row_ref, score_ref, par_ref,
        z_ref, dyn_ref, y_ref, state_ref, sum_ref, carry_ref,
    )


def step_of(step):
    early = step < 4
    return jnp.where(early, step % 2, step // 2), jnp.where(early, step // 2, step % 2)


def gather_kernel(
    normed_ref, cot_ref, own_ref, other_ref, small_own_ref, seg_col_ref, seg_row_ref,
    bc_par_ref, head_ref, pick_ref, par_ref,
    normed_out, cot_out, w_out, small_out, z_ref, dyn_ref, y_ref, state_ref, proj_out, bc_out, wide_out, col_out, row_out,
    turned_out, norm_ref,
    normed_all, cot_all, w_all, small_all, proj_all, bc_all, wide_all, col_all, row_all, score_all, turned_all,
    sum_ref, sum_recv, carry_ref, small_side, small_mine, small_theirs,
    here_sem, out_sem, act_send, act_recv, x_send, x_recv, z_send, z_recv, y_send, y_recv, sum_send, sum_recv_sem,
    *, tiles, spans, inner_total,
):
    tile, sequence = step_of(pl.program_id(0))
    length = z_ref.shape[0]
    rows = normed_ref.shape[0]
    depth = own_ref.shape[1]
    part = 2 * depth
    dp, mp = lax.axis_index("dp"), lax.axis_index("mp")
    side = lax.rem(dp, 2)
    mine = pl.ds(pl.multiple_of(mp * rows, rows), rows)
    theirs = pl.ds(pl.multiple_of(length + mp * rows, rows), rows)
    slab = pl.ds(pl.multiple_of(side * depth, depth), depth)
    other_core = (dp, 1 - mp)

    def along(bits):
        return (jnp.bitwise_xor(dp, bits), mp)

    def remote(src, dst, send, recv, device):
        return pltpu.make_async_remote_copy(
            src_ref=src, dst_ref=dst, send_sem=send, recv_sem=recv, device_id=device,
            device_id_type=pl.DeviceIdType.MESH,
        )

    arrays = ((normed_ref, normed_all), (cot_ref, cot_all))

    def act_here(a):
        return pltpu.make_async_copy(arrays[a][0], arrays[a][1].at[mine, :], here_sem.at[a])

    def act_core(a):
        return remote(
            arrays[a][0], arrays[a][1].at[mine, :], act_send.at[a, 0], act_recv.at[a, 0], other_core
        )

    def act_x(a):
        return remote(
            arrays[a][0], arrays[a][1].at[theirs, :], act_send.at[a, 1], act_recv.at[a, 1], along(1)
        )

    def act_pass(a):
        return remote(
            arrays[a][1].at[theirs, :], arrays[a][1].at[theirs, :], act_send.at[a, 2], act_recv.at[a, 2], other_core
        )

    def weight_of(number):
        return small_side.at[side] if number == 0 else w_all.at[number - 1]

    def w_here(number):
        if number == 0:
            return pltpu.make_async_copy(
                small_own_ref, weight_of(0).at[pl.ds(0, depth), :], here_sem.at[2]
            )
        return pltpu.make_async_copy(
            own_ref.at[number - 1], weight_of(number).at[slab, :], here_sem.at[2 + number]
        )

    def w_x(number):
        if number == 0:
            src, dst = small_side.at[side], small_side.at[side]
        else:
            src, dst = other_ref.at[number - 1], weight_of(number).at[slab, :]
        return remote(src, dst, x_send.at[number], x_recv.at[number], along(1))

    def rows_at(number, at):
        size = depth if number == 0 else part
        return weight_of(number).at[pl.ds(at * size, size), :]

    def w_z(number, k):
        return remote(
            rows_at(number, 0), rows_at(number, k), z_send.at[number, k - 1], z_recv.at[number, k - 1], along(4 * k)
        )

    def w_y(number, k):
        return remote(
            rows_at(number, k), rows_at(number, spans + k), y_send.at[number, k], y_recv.at[number, k], along(2)
        )

    def small_core():
        return remote(small_mine, small_theirs, sum_send.at[2], sum_recv_sem.at[2], other_core)

    def gather_small():
        for k in range(2 * spans):
            for at in range(2):
                small_mine[k * part + at * depth : k * part + (at + 1) * depth, :] = small_side[
                    at, k * depth : (k + 1) * depth, :LANES
                ]
                small_all[k * part + at * depth : k * part + (at + 1) * depth, 2 * LANES :] = small_side[
                    at, k * depth : (k + 1) * depth, LANES:
                ]
        small_core().start()
        small_core().wait_recv()
        first = mp == 0
        small_all[:, :LANES] = jnp.where(first, small_mine[...], small_theirs[...])
        small_all[:, LANES : 2 * LANES] = jnp.where(first, small_theirs[...], small_mine[...])

    def begin_z(number):
        w_here(number).wait()
        if number:
            w_x(number).wait_recv()
        for k in range(1, spans):
            w_z(number, k).start()
        w_y(number, 0).start()

    def begin_y(number):
        for k in range(1, spans):
            w_z(number, k).wait_recv()
            w_y(number, k).start()

    def complete(number):
        for k in range(spans):
            w_y(number, k).wait_recv()

    tables = (
        (normed_all, normed_out), (cot_all, cot_out), (proj_all, proj_out), (bc_all, bc_out),
        (wide_all, wide_out), (col_all, col_out), (row_all, row_out), (turned_all, turned_out),
        (small_all, small_out),
    )

    def table_out(at):
        return pltpu.make_async_copy(tables[at][0], tables[at][1], out_sem.at[at])

    def weight_out(number):
        return pltpu.make_async_copy(w_all.at[number], w_out.at[number], out_sem.at[len(tables) + number])

    def make_tables(origin):
        table_part(
            origin, length, normed_all, small_all, seg_col_ref, seg_row_ref, bc_par_ref, head_ref,
            proj_all, bc_all, wide_all, col_all, row_all, score_all, turned_all,
        )

    @pl.when((tile == 0) & (sequence == 0))
    def _():
        barrier = pltpu.get_barrier_semaphore()
        partners = [along(1), along(2), other_core] + [along(4 * k) for k in range(1, spans)]
        for device in partners:
            pl.semaphore_signal(barrier, inc=1, device_id=device, device_id_type=pl.DeviceIdType.MESH)
        for number in range(tiles + 1):
            w_here(number).start()
        act_here(0).start()
        act_here(1).start()
        sum_ref[...] = jnp.zeros_like(sum_ref)
        pl.semaphore_wait(barrier, len(partners))
        w_x(1).start()
        w_x(2).start()
        begin_z(0)
        act_core(0).start()
        act_core(1).start()
        begin_z(1)
        begin_y(0)
        complete(0)
        w_x(0).start()
        act_x(0).start()
        for number in range(3, tiles + 1):
            w_x(number).start()
        act_x(1).start()
        begin_z(2)
        act_here(0).wait()
        act_core(0).wait_recv()
        w_x(0).wait_recv()
        gather_small()
        make_tables(0)
        begin_y(1)
        act_x(0).wait_recv()
        act_pass(0).start()
        act_here(1).wait()
        act_core(1).wait_recv()

    @pl.when((tile == 1) & (sequence == 0))
    def _():
        act_pass(0).wait_recv()
        make_tables(length)

    for number in range(tiles):

        @pl.when((tile == number) & (sequence == 0))
        def _(number=number):
            if number + 3 <= tiles:
                begin_z(number + 3)
            if number < 2:
                begin_y(number + 2)
            complete(number + 1)
            weight_out(number).start()

    for number in range(2, tiles - 1):

        @pl.when((tile == number - 1) & (sequence == 1))
        def _(number=number):
            begin_y(number + 2)

    @pl.when((tile == 0) & (sequence == 1))
    def _():
        act_x(1).wait_recv()
        act_pass(1).start()
        act_pass(1).wait_recv()
        for at in range(len(tables)):
            table_out(at).start()

    forward_tile(
        sequence * length, tile * 8, normed_all, cot_all, w_all.at[tile], bc_all, wide_all, pick_ref, col_all,
        row_all, score_all, par_ref, z_ref, dyn_ref, y_ref, state_ref, sum_ref, carry_ref,
    )

    @pl.when((tile == tiles - 1) & (sequence == 1))
    def _():
        between = remote(sum_ref, sum_recv.at[0], sum_send.at[0], sum_recv_sem.at[0], other_core)
        between.start()
        between.wait()
        sum_ref[...] += sum_recv[0]
        across = remote(sum_ref, sum_recv.at[1], sum_send.at[1], sum_recv_sem.at[1], along(1))
        across.start()
        across.wait()
        norm_ref[...] = norm_rows(
            sum_ref[...] + jnp.concatenate([sum_recv[1, :, length:], sum_recv[1, :, :length]], axis=1),
            inner_total,
        )
        small_core().wait_send()
        for a in range(2):
            act_core(a).wait_send()
            act_x(a).wait_send()
            act_pass(a).wait_send()
        for number in range(tiles + 1):
            w_x(number).wait_send()
            for k in range(1, spans):
                w_z(number, k).wait_send()
            for k in range(spans):
                w_y(number, k).wait_send()
        for at in range(len(tables)):
            table_out(at).wait()
        for number in range(tiles):
            weight_out(number).wait()


def norm_rows(sums, inner_total):
    inverse = lax.rsqrt(sums[0:1] / inner_total + EPSILON)
    cross = inverse * inverse * inverse / inner_total * sums[1:2]
    return jnp.concatenate([inverse, cross, jnp.zeros((6, sums.shape[1]), F32)], axis=0)


def backward_tile(
    origin, z_ref, y_ref, dyn_ref, bc_ref, wide_ref, pick_ref, col_ref, row_ref, seg_ref, turned_ref, norm_ref,
    par_ref, rate_ref, state_ref, grad_ref, dbc_ref, dt_ref, head_ref, small_ref, turn_ref, halo_ref, carry_ref,
):
    length = z_ref.shape[0]
    blocks = length // BLOCK
    carry_ref[...] = jnp.zeros_like(carry_ref)
    small_ref[...] = jnp.zeros_like(small_ref)
    head_ref[...] = jnp.zeros_like(head_ref)
    halo_ref[...] = jnp.zeros_like(halo_ref)
    down, across = iota((BLOCK, BLOCK), 0), iota((BLOCK, BLOCK), 1)

    def one_block(step, carried):
        number = blocks - 1 - step
        start = pl.multiple_of(number * BLOCK, BLOCK)
        rows = pl.ds(start, BLOCK)
        col = col_ref[rows, :]
        v = z_ref[rows, TILE:]
        above = z_ref[pl.ds(pl.multiple_of(jnp.maximum(start - 8, 0), 8), 8), TILE:]
        joined = jnp.concatenate([above, v], axis=0)
        moved = [None] + [
            pltpu.roll(joined, offset, 0)[8:] * col[:, VALID + offset - 1 : VALID + offset]
            for offset in range(1, 4)
        ]
        conv = par_ref[BIAS : BIAS + 1, :] + par_ref[TAPS + 3 : TAPS + 4, :] * v
        for offset in range(1, 4):
            conv = conv + par_ref[TAPS + 3 - offset : TAPS + 4 - offset, :] * moved[offset]
        gate = sigmoid(conv)
        x = conv * gate
        slope = gate * (1.0 + conv * (1.0 - gate))
        z, y, dyn = z_ref[rows, :TILE], y_ref[rows, :], dyn_ref[rows, :]
        gain = par_ref[GAIN : GAIN + 1, :]
        inv, cross = norm_ref[rows, 0:1], norm_ref[rows, 1:2]
        gate = sigmoid(z)
        silu = z * gate
        yg = y * silu
        yg_inv = yg * inv
        d_yg = inv * gain * dyn - yg * cross
        grad_ref[rows, :TILE] = (d_yg * y * (gate * (1.0 + z * (1.0 - gate)))).astype(BF16)
        grad_ref[rows, 2 * TILE :] = (yg_inv * gain).astype(BF16)
        small_ref[GAIN : GAIN + 1, :] += jnp.sum(dyn * yg_inv, axis=0, keepdims=True)
        e = d_yg * silu
        b_low, c_low = bc_ref[rows, :LANES].astype(BF16), bc_ref[rows, LANES:].astype(BF16)
        scores = turned_ref[rows, :]
        wide = dot(wide_ref[rows, :], pick_ref[...])
        dt_wide, cum_wide = wide[:, :TILE], wide[:, TILE:]
        dtx = x * dt_wide
        dtx_low, e_low = dtx.astype(BF16), e.astype(BF16)
        d_scores = jnp.zeros((BLOCK, BLOCK), F32)
        parts, leaving, arriving = [], [], []
        for head in range(GROUP):
            lanes = slice(head * WIDTH, (head + 1) * WIDTH)
            gap = row_ref[head : head + 1, rows] - cum_wide[:, head * WIDTH : head * WIDTH + 1]
            decay = jnp.exp(jnp.minimum(gap, 0.0))
            mixing = scores * decay
            parts.append(dot(mixing.astype(BF16), e_low[:, lanes]))
            d_mixing = dot(dtx_low[:, lanes], e_low[:, lanes], NT)
            d_scores = d_scores + d_mixing * decay
            pairs = d_mixing * mixing
            leaving.append(jnp.sum(pairs, axis=1, keepdims=True))
            arriving.append(jnp.sum(pairs, axis=0, keepdims=True))
        d_dtx = jnp.concatenate(parts, axis=1)
        mask = pair_mask(col[:, SEG : SEG + 1], seg_ref[:, rows], True)
        d_scores = jnp.where(mask, d_scores, 0.0).astype(BF16)
        d_b = dot(d_scores, c_low)
        d_c = dot(d_scores, b_low, TN)
        state, d_state = state_ref[number], carry_ref[...]
        state_low, d_state_low = state.astype(BF16), d_state.astype(BF16)
        decay = jnp.exp(cum_wide) * col[:, LINK : LINK + 1]
        e_in = e * decay
        e_in_low = e_in.astype(BF16)
        from_state = e_in * dot(c_low, state_low)
        d_c = d_c + dot(e_in_low, state_low, NT)
        carry_ref[...] = decay[BLOCK - 1 :, :] * d_state + dot(c_low, e_in_low, TN)
        weight = jnp.exp(cum_wide[BLOCK - 1 :, :] - cum_wide) * col[:, KEEP : KEEP + 1]
        d_tail = weight * dot(b_low, d_state_low)
        to_state = d_tail * dtx
        d_b = d_b + low_dot(weight * dtx, d_state_low, NT)
        d_dtx = d_dtx + d_tail
        through = decay[BLOCK - 1 :, :] * jnp.sum(state * d_state, axis=0, keepdims=True)
        d_x = dt_wide * d_dtx + par_ref[SKIP : SKIP + 1, :] * e
        small_ref[SKIP : SKIP + 1, :] += jnp.sum(x * e, axis=0, keepdims=True)
        spot = pl.ds(pl.multiple_of(origin + start, BLOCK), BLOCK)
        dbc_ref[spot, :LANES] += d_b
        dbc_ref[spot, LANES:] += d_c
        d_conv = slope * d_x
        below = pl.ds(pl.multiple_of(jnp.minimum(start + BLOCK, length - 8), 8), 8)
        joined = jnp.concatenate([d_conv, halo_ref[...]], axis=0)
        halo_ref[...] = d_conv[:8]
        d_v = par_ref[TAPS + 3 : TAPS + 4, :] * d_conv
        small_ref[TAPS + 3 : TAPS + 4, :] += jnp.sum(d_conv * v, axis=0, keepdims=True)
        small_ref[BIAS : BIAS + 1, :] += jnp.sum(d_conv, axis=0, keepdims=True)
        valid = jnp.concatenate([col, col_ref[below, :]], axis=0)
        for offset in range(1, 4):
            place = TAPS + 3 - offset
            small_ref[place : place + 1, :] += jnp.sum(d_conv * moved[offset], axis=0, keepdims=True)
            counted = joined * valid[:, VALID + offset - 1 : VALID + offset]
            d_v = d_v + par_ref[place : place + 1, :] * pltpu.roll(counted, BLOCK + 8 - offset, 0)[:BLOCK]
        grad_ref[rows, TILE : 2 * TILE] = d_v.astype(BF16)
        owner = (iota((TILE, 8), 0) // WIDTH == iota((TILE, 8), 1)).astype(BF16)

        def head_sum(a):
            return sum(dot(part, owner) for part in halves(a))

        through = through + jnp.sum(from_state, axis=0, keepdims=True)
        sums = jnp.concatenate(
            [head_sum(to_state - from_state), head_sum(d_dtx * x)]
            + leaving
            + [jnp.zeros((BLOCK, LANES - 16 - GROUP), F32)],
            axis=1,
        ).T
        change = sums[:GROUP] + sums[16 : 16 + GROUP] - jnp.concatenate(arriving, axis=0)
        terms = jnp.concatenate(
            thirds(change) + [jnp.zeros((16 - 3 * GROUP, BLOCK), BF16)], axis=0
        )
        before = dot(terms, (down < across).astype(BF16))
        const = head_sum(jnp.broadcast_to(through, (8, TILE))).T[:GROUP, :1]
        run_rows = before[:GROUP] + before[GROUP : 2 * GROUP] + before[2 * GROUP : 3 * GROUP] + const
        raw = row_ref[GROUP : 2 * GROUP, rows]
        d_dt = (sums[8 : 8 + GROUP] + rate_ref[:GROUP, :1] * run_rows) * sigmoid(raw)
        dt = jnp.maximum(raw, 0.0) + jnp.log1p(jnp.exp(-jnp.abs(raw)))
        head_ref[:GROUP, :] += jnp.sum(d_dt, axis=1, keepdims=True)
        head_ref[GROUP:, :] += jnp.sum(run_rows * dt, axis=1, keepdims=True)
        d_dt = jnp.concatenate([d_dt, jnp.zeros((16 - GROUP, BLOCK), F32)], axis=0).astype(BF16)
        dt_ref[:, rows] = d_dt
        turn_ref[STEPS:OUT, spot] = d_dt
        turned = grad_ref[rows, :].T
        turn_ref[:STEPS, spot] = turned[: 2 * TILE]
        turn_ref[OUT:, spot] = turned[2 * TILE :]
        return carried

    lax.fori_loop(0, blocks, one_block, 0)


def backward_kernel(*refs, ties, inside, tiles, spans):
    (
        normed_ref, cot_ref, z_ref, y_ref, dyn_ref, bc_ref, wide_ref, pick_ref, col_ref, row_ref, seg_ref,
        turned_ref, norm_ref, par_ref, rate_ref, state_ref,
        grad_ref, dbc_ref, dt_ref, head_ref, small_ref, far_out_ref, near_out_ref, z_own_out, z_send_out,
        mine_ref, theirs_ref, dbc_x_ref,
        turn_ref, halo_ref, carry_ref, stream_ref, far_ref, near_ref, y_recv_ref, z_send_ref, z_own_ref,
        z_recv_ref, w_send_ref, w_recv_ref, dbc_core_ref, dbc_send_ref, dbc_recv_ref,
        stream_sem, out_sem, y_send_sem, y_recv_sem, z_send_sem, z_recv_sem, w_send_sem, w_recv_sem,
        d_send_sem, d_recv_sem,
    ) = refs[ties:]
    tile, turn = pl.program_id(0), pl.program_id(1)
    sequence = 1 - turn
    done = inside - 1
    length = z_ref.shape[0]
    part = near_ref.shape[2]
    halves_of = near_ref.shape[0]
    ahead = stream_ref.shape[0] - 1
    dp, mp = lax.axis_index("dp"), lax.axis_index("mp")
    side = lax.rem(dp, 2)

    def partner(bits):
        return (jnp.bitwise_xor(dp, bits), mp)

    def remote(src, dst, send, recv, device):
        return pltpu.make_async_remote_copy(
            src_ref=src, dst_ref=dst, send_sem=send, recv_sem=recv, device_id=device,
            device_id_type=pl.DeviceIdType.MESH,
        )

    def y_copy(number, at):
        slot = lax.rem(number, 2)
        return remote(
            far_ref.at[at], y_recv_ref.at[slot, at], y_send_sem.at[at], y_recv_sem.at[slot, at], partner(2)
        )

    def z_copy(number, k):
        slot = lax.rem(number, 2)
        return remote(
            z_send_ref.at[k - 1], z_recv_ref.at[slot, k - 1], z_send_sem.at[k - 1], z_recv_sem.at[slot, k - 1],
            partner(4 * k),
        )

    def w_copy(number):
        return remote(
            w_send_ref.at[number], w_recv_ref.at[number], w_send_sem.at[number], w_recv_sem.at[number], partner(1)
        )

    def finish(number):
        slot = lax.rem(number, 2)
        total = z_own_ref[...]
        for k in range(1, spans):
            z_copy(number, k).wait()
            total = total + z_recv_ref[slot, k - 1].astype(F32)
        z_own_ref[...] = total
        mine_ref[number] = z_own_ref[:, pl.ds(pl.multiple_of(side * LANES, LANES), LANES)]
        w_send_ref[number] = z_own_ref[:, pl.ds(pl.multiple_of((1 - side) * LANES, LANES), LANES)].astype(BF16)
        w_copy(number).start()

    def pass_on(number):
        slot = lax.rem(number, 2)
        for at in range(spans):
            y_copy(number, at).wait()
            whole_part = near_ref[at] + y_recv_ref[slot, at].astype(F32)
            if at == 0:
                z_own_ref[...] = whole_part
            else:
                z_send_ref[at - 1] = whole_part.astype(BF16)

                @pl.when(number < done)
                def _(at=at):
                    z_copy(number, at).start()

    def z_out():
        return [
            pltpu.make_async_copy(z_own_ref, z_own_out, out_sem.at[2]),
            pltpu.make_async_copy(z_send_ref, z_send_out, out_sem.at[3]),
        ]

    def dbc_core():
        src = dbc_ref.at[pl.ds(length, length), :]
        return remote(src, dbc_core_ref, d_send_sem.at[0], d_recv_sem.at[0], (dp, 1 - mp))

    def dbc_x():
        return remote(dbc_send_ref, dbc_recv_ref, d_send_sem.at[1], d_recv_sem.at[1], partner(1))

    @pl.when((tile == 0) & (turn == 0))
    def _():
        dbc_ref[...] = jnp.zeros_like(dbc_ref)
        if inside:
            barrier = pltpu.get_barrier_semaphore()
            others = [partner(1), partner(2), (dp, 1 - mp)] + [partner(4 * k) for k in range(1, spans)]
            for device in others:
                pl.semaphore_signal(barrier, inc=1, device_id=device, device_id_type=pl.DeviceIdType.MESH)
            pl.semaphore_wait(barrier, len(others))

    def fetch(step):
        number = lax.rem(step + halves_of, 2 * halves_of)
        slot = lax.rem(step, ahead + 1)
        lanes = pl.ds(pl.multiple_of(number * part, LANES), part)
        return [
            pltpu.make_async_copy(ref.at[:, lanes], stream_ref.at[slot, at], stream_sem.at[slot, at])
            for at, ref in enumerate((normed_ref, cot_ref))
        ]

    @pl.when(turn == 1)
    def _():
        for step in range(ahead):
            for copy in fetch(step):
                copy.start()

    if inside:

        @pl.when((tile == tiles - 1) & (turn == 1))
        def _():
            dbc_core().start()

    backward_tile(
        sequence * length, z_ref, y_ref, dyn_ref, bc_ref, wide_ref, pick_ref, col_ref, row_ref, seg_ref,
        turned_ref, norm_ref, par_ref, rate_ref, state_ref, grad_ref, dbc_ref, dt_ref, head_ref, small_ref,
        turn_ref, halo_ref, carry_ref,
    )

    if inside:

        @pl.when((tile == tiles - 1) & (turn == 1))
        def _():
            dbc_core().wait()
            dbc_send_ref[...] = (dbc_ref[length:, :] + dbc_core_ref[...]).astype(BF16)
            dbc_x().start()

        @pl.when((turn == 1) & (tile >= 2) & (tile < done + 2))
        def _():
            finish(tile - 2)

        @pl.when((turn == 1) & (tile >= 1) & (tile <= inside))
        def _():
            pass_on(tile - 1)

        @pl.when((turn == 1) & (tile == inside))
        def _():
            for copy in z_out():
                copy.start()

    def out_copies():
        place = tile - inside
        return [
            pltpu.make_async_copy(far_ref, far_out_ref.at[place], out_sem.at[0]),
            pltpu.make_async_copy(near_ref, near_out_ref.at[place], out_sem.at[1]),
        ]

    @pl.when(turn == 1)
    def _():
        def one_part(step, carried):
            slot = lax.rem(step, ahead + 1)

            @pl.when(step + ahead < 2 * halves_of)
            def _():
                for copy in fetch(step + ahead):
                    copy.start()

            for copy in fetch(step):
                copy.wait()
            upper = dot(turn_ref[:OUT, :], stream_ref[slot, 0])
            lower = dot(turn_ref[OUT:, :], stream_ref[slot, 1])

            @pl.when(step < halves_of)
            def _():
                far_ref[step, :OUT, :] = upper.astype(BF16)
                far_ref[step, OUT:, :] = lower.astype(BF16)
                if inside:

                    @pl.when(tile < inside)
                    def _():
                        y_copy(tile, step).start()

            @pl.when(step >= halves_of)
            def _():
                near_ref[step - halves_of, :OUT, :] = upper
                near_ref[step - halves_of, OUT:, :] = lower

            return carried

        lax.fori_loop(0, 2 * halves_of, one_part, 0)

        @pl.when(tile >= inside)
        def _():
            for copy in out_copies():
                copy.start()
            for copy in out_copies():
                copy.wait()

    if inside:

        @pl.when((turn == 1) & (tile == tiles - 1))
        def _():
            for copy in z_out():
                copy.wait()
            for number in range(done):
                w_copy(number).wait()
            theirs_ref[...] = w_recv_ref[...]
            dbc_x().wait()
            dbc_x_ref[...] = dbc_recv_ref[...]


def by_sequence(rows, width):
    return pl.BlockSpec((rows, width), lambda i: (i, 0))


def by_columns(rows, length):
    return pl.BlockSpec((rows, length), lambda i: (0, i))


def whole(shape):
    return pl.BlockSpec(shape, lambda i: (0,) * len(shape))


def shaped(shape, kind=F32):
    return jax.ShapeDtypeStruct(shape, kind)


def cost(flops):
    return pl.CostEstimate(flops=int(flops), bytes_accessed=10**7, transcendentals=10**6)


def run_tables(normed, weight, ids, par, head, length):
    tokens, width = normed.shape
    cols = weight.shape[1]
    return pl.pallas_call(
        table_kernel,
        grid=(tokens // length,),
        in_specs=[
            by_sequence(length, width),
            whole((width, cols)),
            by_sequence(length, 1),
            by_columns(1, length),
            whole((8, 2 * LANES)),
            whole((8, LANES)),
        ],
        out_specs=[
            by_sequence(length, 2 * LANES),
            by_sequence(length, 2 * LANES),
            by_sequence(length, LANES),
            by_sequence(length, COLS),
            by_columns(2 * HEADS, length),
            by_sequence(length, BLOCK),
            by_sequence(length, BLOCK),
        ],
        out_shape=[
            shaped((tokens, 2 * LANES)),
            shaped((tokens, 2 * LANES)),
            shaped((tokens, LANES), BF16),
            shaped((tokens, COLS)),
            shaped((2 * HEADS, tokens)),
            shaped((tokens, BLOCK)),
            shaped((tokens, BLOCK)),
        ],
        compiler_params=pltpu.CompilerParams(vmem_limit_bytes=VMEM_LIMIT),
        cost_estimate=cost(1e10),
    )(normed, weight, ids[:, None], ids[None, :], par, head)


def pick_table(tile):
    row, lane = np.arange(LANES)[:, None], np.arange(2 * TILE)[None, :]
    head = tile * GROUP + (lane % TILE) // WIDTH
    return ((row % HEADS == head) & (row // (3 * HEADS) == lane // TILE)).astype(np.float32)


def run_forward(pieces, normed, cot, bc, wide, col, rows, score, par, tile, length):
    tokens, width = normed.shape
    number, blocks = tokens // length, length // BLOCK
    return pl.pallas_call(
        functools.partial(forward_kernel, pieces=len(pieces)),
        grid=(number,),
        in_specs=[whole(p.shape) for p in pieces]
        + [
            by_sequence(length, width),
            by_sequence(length, width),
            by_sequence(length, 2 * LANES),
            by_sequence(length, LANES),
            whole((LANES, 2 * TILE)),
            by_sequence(length, COLS),
            pl.BlockSpec((8, length), lambda i: (tile, i)),
            by_sequence(length, BLOCK),
            whole((8, TILE)),
        ],
        out_specs=[
            whole((width, 3 * TILE)),
            by_sequence(length, 2 * TILE),
            by_sequence(length, TILE),
            by_sequence(length, TILE),
            pl.BlockSpec((blocks, LANES, TILE), lambda i: (i, 0, 0)),
            by_columns(8, length),
        ],
        out_shape=[
            shaped((width, 3 * TILE), BF16),
            shaped((tokens, 2 * TILE)),
            shaped((tokens, TILE)),
            shaped((tokens, TILE)),
            shaped((number * blocks, LANES, TILE)),
            shaped((8, tokens)),
        ],
        scratch_shapes=[pltpu.VMEM((LANES, TILE), F32)],
        compiler_params=pltpu.CompilerParams(vmem_limit_bytes=VMEM_LIMIT),
        cost_estimate=cost(2e10),
    )(*pieces, normed, cot, bc, wide, jnp.asarray(pick_table(tile), BF16), col, rows, score, par)


def run_gather(normed, cot, own, other, small_own, ids, bc_par, head_par, pars, length, spans, inner_total):
    rows, width = normed.shape
    tiles, _, cols = own.shape
    small_cols = small_own.shape[1] + LANES
    tokens, blocks = 2 * length, length // BLOCK

    def by_tile(size, count):
        return pl.BlockSpec((None, size, count), lambda i: step_of(i) + (0,))

    def fixed(*shape):
        return pl.BlockSpec((None,) + shape, lambda i: (step_of(i)[0],) + (0,) * len(shape))

    def constant(*shape):
        return pl.BlockSpec(shape, lambda i: (0,) * len(shape))

    dma = pltpu.SemaphoreType.DMA
    table_shapes = [
        ((tokens, 2 * LANES), F32),
        ((tokens, 2 * LANES), F32),
        ((tokens, LANES), BF16),
        ((tokens, COLS), F32),
        ((2 * HEADS, tokens), F32),
        ((tokens, BLOCK), F32),
    ]
    return pl.pallas_call(
        functools.partial(gather_kernel, tiles=tiles, spans=spans, inner_total=inner_total),
        grid=(2 * tiles,),
        in_specs=[ANY] * 5
        + [
            constant(tokens, 1),
            constant(1, tokens),
            constant(8, 2 * LANES),
            constant(8, LANES),
            fixed(LANES, 2 * TILE),
            fixed(8, TILE),
        ],
        out_specs=[
            ANY,
            ANY,
            ANY,
            ANY,
            by_tile(length, 2 * TILE),
            by_tile(length, TILE),
            by_tile(length, TILE),
            pl.BlockSpec((None, blocks, LANES, TILE), lambda i: step_of(i) + (0, 0)),
        ]
        + [ANY] * 6
        + [constant(8, tokens)],
        out_shape=[
            shaped((tokens, width), BF16),
            shaped((tokens, width), BF16),
            shaped((tiles, width, cols), BF16),
            shaped((width, small_cols), BF16),
            shaped((tiles, tokens, 2 * TILE)),
            shaped((tiles, tokens, TILE)),
            shaped((tiles, tokens, TILE)),
            shaped((tiles, 2 * blocks, LANES, TILE)),
        ]
        + [shaped(*one) for one in table_shapes]
        + [shaped((8, tokens))],
        scratch_shapes=[
            pltpu.VMEM((tokens, width), BF16),
            pltpu.VMEM((tokens, width), BF16),
            pltpu.VMEM((tiles, width, cols), BF16),
            pltpu.VMEM((width, small_cols), BF16),
        ]
        + [pltpu.VMEM(*one) for one in table_shapes[:5]]
        + [
            pltpu.VMEM((tokens, BLOCK), F32),
            pltpu.VMEM((tokens, BLOCK), F32),
            pltpu.VMEM((8, tokens), F32),
            pltpu.VMEM((2, 8, tokens), F32),
            pltpu.VMEM((LANES, TILE), F32),
            pltpu.VMEM((2, width // 2, 2 * LANES), BF16),
            pltpu.VMEM((width, LANES), BF16),
            pltpu.VMEM((width, LANES), BF16),
            dma((3 + tiles,)),
            dma((9 + tiles,)),
            dma((2, 3)),
            dma((2, 3)),
            dma((1 + tiles,)),
            dma((1 + tiles,)),
            dma((1 + tiles, spans - 1)),
            dma((1 + tiles, spans - 1)),
            dma((1 + tiles, spans)),
            dma((1 + tiles, spans)),
            dma((3,)),
            dma((3,)),
        ],
        compiler_params=pltpu.CompilerParams(
            vmem_limit_bytes=VMEM_LIMIT, collective_id=2, has_side_effects=True
        ),
        cost_estimate=cost(2e11),
    )(
        normed, cot, own, other, small_own, ids[:, None], ids[None, :], bc_par, head_par,
        jnp.asarray(np.stack([pick_table(tile) for tile in range(tiles)]), BF16), pars,
    )


def run_backward(
    ties, normed, cot, zv, y, dyn, bc, wide, col, rows, ids, turned, norms, par, rate, state, length, spans
):
    tiles, tokens = zv.shape[:2]
    width = normed.shape[1]
    number, blocks = tokens // length, length // BLOCK
    part = 2 * LANES
    near = width // part // 2
    inside = tiles - 1 if near == spans else 0
    done = max(inside - 1, 1)
    hops = 3

    def by_tile(size, cols):
        return pl.BlockSpec((None, size, cols), lambda j, i: (j, 1 - i, 0))

    def shared(size, cols):
        return pl.BlockSpec((size, cols), lambda j, i: (1 - i, 0))

    def fixed(*shape):
        return pl.BlockSpec((None,) + shape, lambda j, i: (j,) + (0,) * len(shape))

    def constant(*shape):
        return pl.BlockSpec(shape, lambda j, i: (0,) * len(shape))

    dma = pltpu.SemaphoreType.DMA
    params = dict(vmem_limit_bytes=VMEM_LIMIT)
    if inside:
        params.update(collective_id=1, has_side_effects=True)
    return inside, pl.pallas_call(
        functools.partial(backward_kernel, ties=len(ties), inside=inside, tiles=tiles, spans=spans),
        grid=(tiles, number),
        in_specs=[ANY for _ in ties]
        + [
            ANY,
            ANY,
            by_tile(length, 2 * TILE),
            by_tile(length, TILE),
            by_tile(length, TILE),
            shared(length, 2 * LANES),
            shared(length, LANES),
            fixed(LANES, 2 * TILE),
            shared(length, COLS),
            pl.BlockSpec((8, length), lambda j, i: (j, 1 - i)),
            pl.BlockSpec((1, length), lambda j, i: (0, 1 - i)),
            shared(length, BLOCK),
            shared(length, 8),
            fixed(8, TILE),
            fixed(8, LANES),
            pl.BlockSpec((None, blocks, LANES, TILE), lambda j, i: (j, 1 - i, 0, 0)),
        ],
        out_specs=[
            by_tile(length, 3 * TILE),
            constant(tokens, 2 * LANES),
            pl.BlockSpec((16, length), lambda j, i: (j, 1 - i)),
            pl.BlockSpec((None, None, 8, LANES), lambda j, i: (j, 1 - i, 0, 0)),
            pl.BlockSpec((None, None, 8, TILE), lambda j, i: (j, 1 - i, 0, 0)),
            ANY,
            ANY,
            ANY,
            ANY,
            constant(done, SHARE, LANES),
            constant(done, SHARE, LANES),
            constant(length, part),
        ],
        out_shape=[
            shaped((tiles, tokens, 3 * TILE), BF16),
            shaped((tokens, 2 * LANES)),
            shaped((tiles * 16, tokens), BF16),
            shaped((tiles, number, 8, LANES)),
            shaped((tiles, number, 8, TILE)),
            shaped((tiles - inside, near, SHARE, part), BF16),
            shaped((tiles - inside, near, SHARE, part)),
            shaped((SHARE, part)),
            shaped((hops, SHARE, part), BF16),
            shaped((done, SHARE, LANES)),
            shaped((done, SHARE, LANES), BF16),
            shaped((length, part), BF16),
        ],
        scratch_shapes=[
            pltpu.VMEM((SHARE, tokens), BF16),
            pltpu.VMEM((8, TILE), F32),
            pltpu.VMEM((LANES, TILE), F32),
            pltpu.VMEM((4, 2, tokens, part), BF16),
            pltpu.VMEM((near, SHARE, part), BF16),
            pltpu.VMEM((near, SHARE, part), F32),
            pltpu.VMEM((2, near, SHARE, part), BF16),
            pltpu.VMEM((hops, SHARE, part), BF16),
            pltpu.VMEM((SHARE, part), F32),
            pltpu.VMEM((2, hops, SHARE, part), BF16),
            pltpu.VMEM((done, SHARE, LANES), BF16),
            pltpu.VMEM((done, SHARE, LANES), BF16),
            pltpu.VMEM((length, part), F32),
            pltpu.VMEM((length, part), BF16),
            pltpu.VMEM((length, part), BF16),
            dma((4, 2)),
            dma((4,)),
            dma((near,)),
            dma((2, near)),
            dma((hops,)),
            dma((2, hops)),
            dma((done,)),
            dma((done,)),
            dma((2,)),
            dma((2,)),
        ],
        compiler_params=pltpu.CompilerParams(**params),
        cost_estimate=cost(2e11),
    )(
        *ties, normed, cot, zv, y, dyn, bc, wide, jnp.asarray(np.stack([pick_table(tile) for tile in range(tiles)]), BF16), col,
        rows, ids[None, :], turned, norms, par, rate, state,
    )


def mixer_kernel(
    z_hbm, y_hbm, norm_ref, par_ref, w_ref, own_ref, give_ref,
    z_buf, y_buf, norm_buf, away, recv, z_sem, y_sem, send_sem, recv_sem, *, spans, length,
):
    tiles, rows = z_buf.shape[1:3]
    dp, mp = lax.axis_index("dp"), lax.axis_index("mp")
    part = 2 * LANES
    order = ((1, 1 - mp), (0, 1 - mp), (1, mp), (0, mp))

    def rows_of(step):
        sequence, half = order[step]
        return pl.ds(pl.multiple_of(sequence * length + half * rows, rows), rows)

    def fetch(step):
        slot = step % 2
        at = rows_of(step)
        return [
            pltpu.make_async_copy(z_hbm.at[:, at, pl.ds(0, TILE)], z_buf.at[slot], z_sem.at[slot]),
            pltpu.make_async_copy(y_hbm.at[:, at, :], y_buf.at[slot], y_sem.at[slot]),
        ]

    def core_copy(step):
        return pltpu.make_async_remote_copy(
            src_ref=away.at[step], dst_ref=recv.at[step], send_sem=send_sem.at[step], recv_sem=recv_sem.at[step],
            device_id=(dp, 1 - mp), device_id_type=pl.DeviceIdType.MESH,
        )

    for copy in fetch(0):
        copy.start()
    barrier = pltpu.get_barrier_semaphore()
    pl.semaphore_signal(barrier, inc=1, device_id=(dp, 1 - mp), device_id_type=pl.DeviceIdType.MESH)
    pl.semaphore_wait(barrier, 1)
    for step in range(4):
        if step < 3:
            for copy in fetch(step + 1):
                copy.start()
        for copy in fetch(step):
            copy.wait()
        norm_buf[...] = norm_ref[rows_of(step), :]
        parts = []
        for tile in range(tiles):
            z = z_buf[step % 2, tile]
            yg = y_buf[step % 2, tile] * (z * sigmoid(z))
            parts.append((yg * norm_buf[:, 0:1] * par_ref[tile, GAIN : GAIN + 1, :]).astype(BF16))
        if step >= 2:
            core_copy(step - 2).wait()

        def columns(number, carried, step=step, parts=parts):
            at = pl.ds(pl.multiple_of(number * part, part), part)
            total = dot(parts[0], w_ref[0, at, :], NT)
            for tile in range(1, tiles):
                total = total + dot(parts[tile], w_ref[tile, at, :], NT)
            lanes = pl.ds(pair_start(number, dp, spans), part)
            if step < 2:
                away[step, :, lanes] = total.astype(BF16)
            elif step == 2:
                give_ref[:, lanes] = (total + recv[0, :, lanes].astype(F32)).astype(BF16)
            else:
                own_ref[:, lanes] = (total + recv[1, :, lanes].astype(F32)).astype(BF16)
            return carried

        lax.fori_loop(0, 2 * spans, columns, 0)
        if step < 2:
            core_copy(step).start()


def pair_start(number, dp, spans):
    bits = number // spans * 2 + number % spans * 4
    return pl.multiple_of(jnp.bitwise_xor(dp - lax.rem(dp, 2), bits) * LANES, 2 * LANES)


def run_mixer(zvs, ys, norms, params, weights, rows, length, spans):
    tiles, tokens, _ = ys.shape
    width = weights.shape[1]
    dma = pltpu.SemaphoreType.DMA
    return pl.pallas_call(
        functools.partial(mixer_kernel, spans=spans, length=length),
        grid=(1,),
        in_specs=[
            ANY,
            ANY,
            pl.BlockSpec((tokens, 8), lambda i: (0, 0)),
            pl.BlockSpec((tiles, 8, TILE), lambda i: (0, 0, 0)),
            pl.BlockSpec((tiles, width, TILE), lambda i: (0, 0, 2)),
        ],
        out_specs=[
            pl.BlockSpec((rows, width), lambda i: (0, 0)),
            pl.BlockSpec((rows, width), lambda i: (0, 0)),
        ],
        out_shape=[shaped((rows, width), BF16), shaped((rows, width), BF16)],
        scratch_shapes=[
            pltpu.VMEM((2, tiles, rows, TILE), F32),
            pltpu.VMEM((2, tiles, rows, TILE), F32),
            pltpu.VMEM((rows, 8), F32),
            pltpu.VMEM((2, rows, width), BF16),
            pltpu.VMEM((2, rows, width), BF16),
            dma((2,)),
            dma((2,)),
            dma((2,)),
            dma((2,)),
        ],
        compiler_params=pltpu.CompilerParams(
            vmem_limit_bytes=VMEM_LIMIT, collective_id=4, has_side_effects=True
        ),
        cost_estimate=cost(1e10),
    )(zvs, ys, norms, params, weights)


def tail_kernel(
    hidden_hbm, cot_hbm, inv_ref, gain_ref, grads_hbm, weights_hbm, small_ref, dt_ref, far_hbm, near_hbm,
    z_own_ref, z_send_hbm, mine_ref, theirs_ref, dbc_ref, dbc_x_ref, proj_ref, col_ref, par_ref, normed_hbm,
    smalls_ref, heads_ref, rate_ref, usable_ref, mixer_own_hbm, mixer_x_hbm,
    grad_out, residual_out, zx_ref, out_ref, steps_ref, bc_out_ref, pack_out_ref, last_ref,
    grads_seq, wblk, acc_ref, give_ref, core_recv, own_ref, x_give, x_recv, y_recv, z_send, z_own, z_total, z_recv, w_send,
    w_recv, dbc_core, dbc_low, dt_cols, normed_blk, bc_grad, bc_xs, bc_own, bc_xr, bc_yr, bc_zr, bc_core,
    pack_recv, last_recv, hidden_ref, cot_ref, near_ref,
    load_sem, seq_sem, w_sem, blk_sem, out_sem, core_send, core_rsem, xs_sem, xr_sem, ys_sem, yr_sem, zs_sem, zr_sem, ws_sem, wr_sem,
    ds_sem, dr_sem, bs_sem, br_sem, ps_sem, pr_sem, ls_sem, lr_sem,
    *, spans, inside, extent,
):
    tiles = weights_hbm.shape[0]
    length = grads_seq.shape[0]
    rows, width = hidden_ref.shape
    loads = [
        pltpu.make_async_copy(src, dst, load_sem.at[at])
        for at, (src, dst) in enumerate(
            [(near_hbm.at[0], near_ref), (hidden_hbm, hidden_ref), (cot_hbm, cot_ref)]
        )
    ]
    part = 2 * LANES
    count = 2 * spans
    dp, mp = lax.axis_index("dp"), lax.axis_index("mp")
    side = lax.rem(dp, 2)
    ours = pl.ds(pl.multiple_of(side * LANES, LANES), LANES)
    others = pl.ds(pl.multiple_of((1 - side) * LANES, LANES), LANES)
    other_core = (dp, 1 - mp)

    def along(bits):
        return (jnp.bitwise_xor(dp, bits), mp)

    def remote(src, dst, send, recv, device):
        return pltpu.make_async_remote_copy(
            src_ref=src, dst_ref=dst, send_sem=send, recv_sem=recv, device_id=device,
            device_id_type=pl.DeviceIdType.MESH,
        )

    def lanes_of(number):
        return pl.ds(pair_start(number, dp, spans), part)

    def seq_fetch(sequence):
        return [
            pltpu.make_async_copy(
                grads_hbm.at[tile, pl.ds(sequence * length, length), pl.ds(0, 2 * TILE)],
                grads_seq.at[:, pl.ds(tile * 2 * TILE, 2 * TILE)],
                seq_sem.at[tile],
            )
            for tile in range(tiles)
        ]

    def w_fetch(number, slot):
        at = pl.ds(pl.multiple_of(number * part, part), part)
        return [
            pltpu.make_async_copy(
                weights_hbm.at[tile, at, pl.ds(0, 2 * TILE)],
                wblk.at[slot, :, pl.ds(tile * 2 * TILE, 2 * TILE)],
                w_sem.at[slot, tile],
            )
            for tile in range(tiles)
        ]

    def begin(copies):
        for copy in copies:
            copy.start()

    def end(copies):
        for copy in copies:
            copy.wait()

    def normed_fetch(number, slot):
        at = pl.ds(pl.multiple_of(number * part, part), part)
        return pltpu.make_async_copy(
            normed_hbm.at[pl.ds(0, length), at], normed_blk.at[slot], blk_sem.at[slot]
        )

    def core_copy(sequence, number):
        at = lanes_of(number)
        return remote(
            give_ref.at[:, at], core_recv.at[sequence, :, at], core_send.at[sequence, number],
            core_rsem.at[sequence, number], other_core,
        )

    def x_copy(number):
        at = lanes_of(number)
        return remote(x_give.at[:, at], x_recv.at[:, at], xs_sem.at[number], xr_sem.at[number], along(1))

    def y_copy(k):
        return remote(far_hbm.at[0, k], y_recv.at[k], ys_sem.at[k], yr_sem.at[k], along(2))

    def z_copy(number, k):
        src = z_send_hbm if number == 0 else z_send
        return remote(
            src.at[k - 1], z_recv.at[number, k - 1], zs_sem.at[number, k - 1], zr_sem.at[number, k - 1],
            along(4 * k),
        )

    def w_copy(number):
        return remote(w_send.at[number], w_recv.at[number], ws_sem.at[number], wr_sem.at[number], along(1))

    dbc_between = remote(dbc_ref, dbc_core, ds_sem.at[0], dr_sem.at[0], other_core)
    bc_x = remote(bc_xs, bc_xr, bs_sem.at[0], br_sem.at[0], along(1))
    bc_y = remote(bc_own.at[pl.ds(spans, spans)], bc_yr, bs_sem.at[1], br_sem.at[1], along(2))

    def bc_z(k):
        return remote(bc_own.at[k], bc_zr.at[k - 1], bs_sem.at[1 + k], br_sem.at[1 + k], along(4 * k))

    bc_between = remote(bc_own.at[0], bc_core, bs_sem.at[1 + spans], br_sem.at[1 + spans], other_core)
    bits = [1 << place for place in range(extent.bit_length() - 1)]

    def pack_copy(step):
        return remote(pack_out_ref, pack_recv.at[step], ps_sem.at[step], pr_sem.at[step], along(bits[step]))

    def pack_step(step):
        pack_copy(step).wait()
        pack_out_ref[...] += pack_recv[step]
        if step + 1 < len(bits):
            pack_copy(step + 1).start()

    def last_copy(step):
        device = along(bits[step - 1]) if step else other_core
        return remote(last_ref, last_recv.at[step], ls_sem.at[step], lr_sem.at[step], device)

    def emit(tile, share, owner):
        channels = (owner * tiles + tile) * TILE
        for plane in range(2):
            lanes = pl.ds(pl.multiple_of(plane * 2 * tiles * TILE + channels, TILE), TILE)
            zx_ref[:, lanes] = share[plane * TILE : (plane + 1) * TILE, :].astype(F32).T
        out_ref[pl.ds(pl.multiple_of(channels, TILE), TILE), :] = share[OUT:, :].astype(F32)
        steps_ref[tile, owner] = share[STEPS : STEPS + 16, :].astype(F32)[:8]

    def give_total(number, total_ref):
        w_send[number] = total_ref[:, others].astype(BF16)
        w_copy(number).start()
        emit(inside - 1 + number, total_ref[:, ours], side)

    def finish_z(number, own):
        total = own[...]
        for k in range(1, spans):
            z_copy(number, k).wait()
            total = total + z_recv[number, k - 1].astype(F32)
        z_total[...] = total
        give_total(number, z_total)

    def relay(number):
        core_copy(1, number).wait()
        lanes = lanes_of(number)
        x_give[:, lanes] = (own_ref[:, lanes] + core_recv[1, :, lanes].astype(F32)).astype(BF16)
        x_copy(number).start()

    def products(sequence):
        dt_rows = jnp.concatenate(
            [
                dt_ref[tile * 16 : tile * 16 + GROUP, sequence * length : (sequence + 1) * length].astype(F32)
                for tile in range(tiles)
            ],
            axis=0,
        )
        blank = jnp.zeros_like(dt_rows)
        dt_rows = jnp.concatenate(
            [
                jnp.where(side == 0, dt_rows, blank),
                jnp.where(side == 0, blank, dt_rows),
                jnp.zeros((LANES - 2 * tiles * GROUP, length), F32),
            ],
            axis=0,
        )
        dt_cols[...] = dt_rows.T.astype(BF16)
        end(seq_fetch(sequence))

        def one(number, carried):
            slot = lax.rem(number, 2)

            @pl.when(number + 1 < count)
            def _():
                begin(w_fetch(number + 1, 1 - slot))

            end(w_fetch(number, slot))
            at = pl.ds(pl.multiple_of(number * part, part), part)
            acc_ref[...] = dot(grads_seq[...], wblk[slot], NT) + dot(
                dt_cols[...], small_ref[at, 2 * LANES :], NT
            )
            lanes = lanes_of(number)
            away = pl.ds(pl.multiple_of((1 - mp) * rows, rows), rows)
            here = pl.ds(pl.multiple_of(mp * rows, rows), rows)
            give_ref[:, lanes] = acc_ref[away, :].astype(BF16)
            core_copy(sequence, number).start()
            own_ref[:, lanes] = acc_ref[here, :]
            if sequence == 1:

                @pl.when(number > 0)
                def _():
                    relay(number - 1)

            return carried

        lax.fori_loop(0, count, one, 0)

    begin(seq_fetch(1))
    begin(w_fetch(0, 0))
    barrier = pltpu.get_barrier_semaphore()
    partners = [along(1), along(2), other_core] + [along(4 * k) for k in range(1, spans)]
    for device in partners:
        pl.semaphore_signal(barrier, inc=1, device_id=device, device_id_type=pl.DeviceIdType.MESH)
    pl.semaphore_wait(barrier, len(partners))
    for k in range(spans - 1, -1, -1):
        y_copy(k).start()
    for k in range(spans - 1, 0, -1):
        z_copy(0, k).start()
    dbc_between.start()
    for load in loads:
        load.start()
    pack_out_ref[...] = jnp.zeros_like(pack_out_ref)
    head_row = jnp.zeros((1, LANES), F32)
    for tile in range(tiles):
        lanes = pl.ds(pl.multiple_of((side * tiles + tile) * TILE, TILE), TILE)
        pack_out_ref[: GAIN + 1, lanes] = (smalls_ref[tile, 0] + smalls_ref[tile, 1])[: GAIN + 1]
        heads = heads_ref[tile, 0] + heads_ref[tile, 1]
        heads = jnp.concatenate([heads[:GROUP], heads[GROUP:] * rate_ref[tile, :GROUP]], axis=0)
        row = iota((8, LANES), 0)
        target = (row // GROUP) * 2 * HEADS + side * HEADS + tile * GROUP + row % GROUP
        head_row = head_row + jnp.sum(
            jnp.where(iota((8, LANES), 1) == target, heads, 0.0), axis=0, keepdims=True
        )
    pack_out_ref[GAIN + 1 : GAIN + 2, :LANES] = head_row
    pack_copy(0).start()
    products(1)
    begin(seq_fetch(0))
    begin(w_fetch(0, 0))
    relay(count - 1)
    pack_step(0)

    def y_pass(k):
        y_copy(k).wait()
        total = near_ref[k] + y_recv[k].astype(F32)
        if k == 0:
            z_own[...] = total
        else:
            z_send[k - 1] = total.astype(BF16)
            z_copy(1, k).start()

    loads[0].wait()
    for k in range(spans - 1, spans // 2 - 1, -1):
        y_pass(k)
    normed_fetch(0, 0).start()
    dbc_between.wait()
    conv = conv_of(proj_ref[...], col_ref[...], par_ref)
    gate = sigmoid(conv)
    d_conv = (dbc_ref[...] + dbc_core[...] + dbc_x_ref[...].astype(F32)) * (gate * (1.0 + conv * (1.0 - gate)))
    d_proj = par_ref[TAPS + 3 : TAPS + 4, :] * d_conv
    small = [None] * 4
    small[3] = jnp.sum(d_conv * proj_ref[...], axis=0, keepdims=True)
    for offset in range(1, 4):
        place = TAPS + 3 - offset
        counted = d_conv * col_ref[:, VALID + offset - 1 : VALID + offset]
        small[place] = jnp.sum(counted * pltpu.roll(proj_ref[...], offset, 0), axis=0, keepdims=True)
        d_proj = d_proj + par_ref[place : place + 1, :] * pltpu.roll(counted, length - offset, 0)
    small.append(jnp.sum(d_conv, axis=0, keepdims=True))
    conv_grads = jnp.concatenate(small + [jnp.zeros((3, part), F32)], axis=0)
    dbc_low[...] = d_proj.astype(BF16)
    half = pl.ds(pl.multiple_of(mp * LANES, LANES), LANES)
    turned = dbc_low[:, half].T

    def bc_product(number, carried):
        slot = lax.rem(number, 2)

        @pl.when(number + 1 < count)
        def _():
            normed_fetch(number + 1, 1 - slot).start()

        normed_fetch(number, slot).wait()
        bc_grad[...] = dot(turned, normed_blk[slot])
        bc_own[number] = bc_grad[:, ours]
        bc_xs[number] = bc_grad[:, others].astype(BF16)
        return carried

    lax.fori_loop(0, count, bc_product, 0)
    bc_x.start()
    products(0)
    mixer_copies = [
        pltpu.make_async_copy(mixer_own_hbm, grads_seq.at[pl.ds(0, rows), :], seq_sem.at[0]),
        pltpu.make_async_copy(mixer_x_hbm, grads_seq.at[pl.ds(rows, rows), :], seq_sem.at[1]),
    ]
    begin(mixer_copies)
    pack_step(1)
    for k in range(spans // 2 - 1, -1, -1):
        y_pass(k)
    for tile in range(inside - 1):
        emit(tile, mine_ref[tile], side)
        emit(tile, theirs_ref[tile], 1 - side)
    here = pl.ds(pl.multiple_of(mp * rows, rows), rows)

    def add_core(number, carried):
        core_copy(0, number).wait_recv()
        lanes = lanes_of(number)
        at = pl.ds(pl.multiple_of(number * part, part), part)
        own_ref[:, lanes] += core_recv[0, :, lanes].astype(F32) + dot(
            dbc_low[here, :], small_ref[at, : 2 * LANES], NT
        )
        return carried

    lax.fori_loop(0, count, add_core, 0)
    step_rows = 64
    end(mixer_copies + loads[1:])

    def residual(number, carried):
        at = pl.ds(pl.multiple_of(number * step_rows, step_rows), step_rows)
        away = pl.ds(pl.multiple_of(rows + number * step_rows, step_rows), step_rows)
        u = hidden_ref[at, :].astype(F32)
        mixer = grads_seq[at, :].astype(F32) + grads_seq[away, :].astype(F32)
        slot = number // (part // step_rows)
        place = lax.rem(number, part // step_rows) * step_rows
        wblk[slot, pl.ds(pl.multiple_of(place, step_rows), step_rows), :] = (u + mixer).astype(BF16)
        usable = usable_ref[at, :]
        return (
            carried[0] + jnp.sum(usable * (u * u), axis=0, keepdims=True),
            carried[1] + jnp.sum(usable * (mixer * mixer), axis=0, keepdims=True),
        )

    zero_row = jnp.zeros((1, width), F32)
    squares = lax.fori_loop(0, rows // step_rows, residual, (zero_row, zero_row))
    residual_copies = [
        pltpu.make_async_copy(wblk.at[slot], residual_out.at[pl.ds(slot * part, part), :], seq_sem.at[2 + slot])
        for slot in range(2)
    ]
    begin(residual_copies)
    finish_z(0, z_own_ref)

    def add_x(number, carried):
        x_copy(number).wait_recv()
        lanes = lanes_of(number)
        own_ref[:, lanes] += x_recv[:, lanes].astype(F32)
        return carried

    lax.fori_loop(0, count, add_x, 0)
    last_ref[...] = jnp.zeros_like(last_ref)
    last_ref[:, part : 2 * part] = 0.5 * conv_grads
    for at, total in enumerate(
        [
            jnp.sum(squares[0], axis=1, keepdims=True),
            jnp.sum(squares[1], axis=1, keepdims=True),
            jnp.sum(usable_ref[...], axis=0, keepdims=True),
        ]
    ):
        last_ref[at : at + 1, 2 * part : 2 * part + LANES] = jnp.broadcast_to(total, (1, LANES))

    def finish(number, gain_sum):
        at = pl.ds(pl.multiple_of(number * step_rows, step_rows), step_rows)
        u, d_normed = hidden_ref[at, :].astype(F32), own_ref[at, :]
        inv = inv_ref[at, :]
        scaled = gain_ref[...] * d_normed
        mean = jnp.mean(u * scaled, axis=-1, keepdims=True)
        own_ref[at, :] = cot_ref[at, :].astype(F32) + inv * scaled - u * (inv * inv * inv * mean)
        return gain_sum + jnp.sum(d_normed * u * inv, axis=0, keepdims=True)

    gain_sum = lax.fori_loop(0, rows // step_rows, finish, jnp.zeros((1, width), F32))
    out = pltpu.make_async_copy(own_ref, grad_out, out_sem.at[0])
    out.start()
    for number in range(8):
        last_ref[number : number + 1, :part] = gain_sum[:, number * part : (number + 1) * part]

    def last_step(step):
        last_copy(step).wait()
        last_ref[...] += last_recv[step]
        if step < len(bits):
            last_copy(step + 1).start()

    last_copy(0).start()
    bc_x.wait()
    bc_own[...] += bc_xr[...].astype(F32)
    bc_y.start()
    last_step(0)
    last_step(1)
    bc_y.wait()
    bc_own[:spans] += bc_yr[...]
    for k in range(1, spans):
        bc_z(k).start()
    last_step(2)
    finish_z(1, z_own)
    for step in range(2, len(bits)):
        pack_step(step)
        last_step(step + 1)
    total = bc_own[0]
    for k in range(1, spans):
        bc_z(k).wait()
        total = total + bc_zr[k - 1]
    bc_own[0] = total
    bc_between.start()
    bc_between.wait()
    first = jnp.where(mp == 0, 1.0, 0.0)
    bc_out_ref[:LANES, :] = first * bc_own[0] + (1.0 - first) * bc_core[...]
    bc_out_ref[LANES:, :] = (1.0 - first) * bc_own[0] + first * bc_core[...]
    for number in range(2):
        w_copy(number).wait()
        emit(inside - 1 + number, w_recv[number], 1 - side)
    for number in range(count):
        core_copy(0, number).wait_send()
        x_copy(number).wait_send()
    out.wait()
    end(residual_copies)


def run_tail(
    hidden, cot, inv, gain, grads, weights, small, dts, far_share, near_share, z_own, z_send, mine, theirs, dbc,
    dbc_x, proj, col, bc_par, normed, smalls, heads, rate, usable, mixer_own, mixer_x, length, spans, extent,
):
    rows, width = hidden.shape
    tiles, tokens = grads.shape[:2]
    part, inside = 2 * LANES, tiles - 1
    hops = extent.bit_length() - 1
    channels = 2 * tiles * TILE
    dma = pltpu.SemaphoreType.DMA

    def full(*shape):
        return pl.BlockSpec(shape, lambda i: (0,) * len(shape))

    return pl.pallas_call(
        functools.partial(tail_kernel, spans=spans, inside=inside, extent=extent),
        grid=(1,),
        in_specs=[
            ANY,
            ANY,
            full(rows, 1),
            full(1, width),
            ANY,
            ANY,
            full(*small.shape),
            full(*dts.shape),
            ANY,
            ANY,
            full(*z_own.shape),
            ANY,
            full(*mine.shape),
            full(*theirs.shape),
            full(length, part),
            full(length, part),
            full(length, part),
            full(length, COLS),
            full(8, part),
            ANY,
            full(*smalls.shape),
            full(*heads.shape),
            full(*rate.shape),
            full(rows, 1),
            ANY,
            ANY,
        ],
        out_specs=[
            ANY,
            ANY,
            full(LANES, 2 * channels),
            full(channels, LANES),
            full(tiles, 2, 8, LANES),
            full(part, LANES),
            full(8, channels),
            full(8, 3 * part),
        ],
        out_shape=[
            shaped((rows, width)),
            shaped((rows, width), BF16),
            shaped((LANES, 2 * channels)),
            shaped((channels, LANES)),
            shaped((tiles, 2, 8, LANES)),
            shaped((part, LANES)),
            shaped((8, channels)),
            shaped((8, 3 * part)),
        ],
        scratch_shapes=[
            pltpu.VMEM((length, tiles * 2 * TILE), BF16),
            pltpu.VMEM((2, part, tiles * 2 * TILE), BF16),
            pltpu.VMEM((length, part), F32),
            pltpu.VMEM((rows, width), BF16),
            pltpu.VMEM((2, rows, width), BF16),
            pltpu.VMEM((rows, width), F32),
            pltpu.VMEM((rows, width), BF16),
            pltpu.VMEM((rows, width), BF16),
            pltpu.VMEM((spans, SHARE, part), BF16),
            pltpu.VMEM((spans - 1, SHARE, part), BF16),
            pltpu.VMEM((SHARE, part), F32),
            pltpu.VMEM((SHARE, part), F32),
            pltpu.VMEM((2, spans - 1, SHARE, part), BF16),
            pltpu.VMEM((2, SHARE, LANES), BF16),
            pltpu.VMEM((2, SHARE, LANES), BF16),
            pltpu.VMEM((length, part), F32),
            pltpu.VMEM((length, part), BF16),
            pltpu.VMEM((length, LANES), BF16),
            pltpu.VMEM((2, length, part), BF16),
            pltpu.VMEM((LANES, part), F32),
            pltpu.VMEM((2 * spans, LANES, LANES), BF16),
            pltpu.VMEM((2 * spans, LANES, LANES), F32),
            pltpu.VMEM((2 * spans, LANES, LANES), BF16),
            pltpu.VMEM((spans, LANES, LANES), F32),
            pltpu.VMEM((spans - 1, LANES, LANES), F32),
            pltpu.VMEM((LANES, LANES), F32),
            pltpu.VMEM((hops, 8, channels), F32),
            pltpu.VMEM((hops + 1, 8, 3 * part), F32),
            pltpu.VMEM((rows, width), BF16),
            pltpu.VMEM((rows, width), BF16),
            pltpu.VMEM((spans, SHARE, part), F32),
            dma((3,)),
            dma((tiles,)),
            dma((2, tiles)),
            dma((2,)),
            dma((1,)),
            dma((2, 2 * spans)),
            dma((2, 2 * spans)),
            dma((2 * spans,)),
            dma((2 * spans,)),
            dma((spans,)),
            dma((spans,)),
            dma((2, spans - 1)),
            dma((2, spans - 1)),
            dma((2,)),
            dma((2,)),
            dma((1,)),
            dma((1,)),
            dma((2 + spans,)),
            dma((2 + spans,)),
            dma((hops,)),
            dma((hops,)),
            dma((hops + 1,)),
            dma((hops + 1,)),
        ],
        compiler_params=pltpu.CompilerParams(
            vmem_limit_bytes=VMEM_LIMIT, collective_id=3, has_side_effects=True
        ),
        cost_estimate=cost(1e11),
    )(
        hidden, cot, inv, gain, grads, weights, small, dts, far_share, near_share, z_own, z_send, mine, theirs, dbc,
        dbc_x, proj, col, bc_par, normed, smalls, heads, rate, usable, mixer_own, mixer_x,
    )


def segment_conv(inputs, taps, bias, masks):
    reach = taps.shape[0]
    result = bias[None, :] + taps[reach - 1][None, :] * inputs
    for offset in range(1, reach):
        moved = jnp.concatenate(
            [jnp.zeros((offset, inputs.shape[1]), inputs.dtype), inputs[:-offset]], axis=0
        )
        result = result + taps[reach - 1 - offset][None, :] * (
            moved * masks[:, offset - 1 : offset]
        )
    return result


def local(
    hidden_in,
    segments,
    norm_gain,
    w_zx,
    w_dt,
    w_bc,
    conv_x,
    conv_x_bias,
    conv_bc,
    conv_bc_bias,
    dt_bias,
    a_log,
    d_skip,
    gated_gain,
    w_out,
    cotangent,
):
    dp, mp = lax.axis_index("dp"), lax.axis_index("mp")
    extent = lax.axis_size("dp")
    far = extent // 4
    x_side = lax.rem(dp, 2)
    rows, width = hidden_in.shape
    length = segments.shape[0]
    inner = conv_x.shape[1]
    inner_total = inner * lax.axis_size("mp")
    heads = dt_bias.shape[0]
    quarter, own_heads = inner // 2, heads // 2
    tiles = quarter // TILE
    depth = w_zx.shape[0]

    def by_side(own, other, axis):
        return jnp.where(
            x_side == 0,
            jnp.concatenate([own, other], axis=axis),
            jnp.concatenate([other, own], axis=axis),
        )

    def by_core(own, other, axis):
        return jnp.where(
            mp == 0,
            jnp.concatenate([own, other], axis=axis),
            jnp.concatenate([other, own], axis=axis),
        )

    def of_side(a, side, axis):
        size = a.shape[axis] // 2
        return lax.dynamic_slice_in_dim(a, side * size, size, axis)

    def of_core(a):
        return lax.dynamic_slice_in_dim(a, mp * LANES, LANES, 1)

    packed = jnp.concatenate([w_zx[:, 0], w_zx[:, 1], w_out.T], axis=1)
    packed = packed.reshape(depth, 3, 2, tiles, TILE).transpose(2, 3, 0, 1, 4)
    packed = packed.reshape(2, tiles, depth, 3 * TILE)

    filler = jnp.zeros((depth, LANES - heads), BF16)
    packed_own = lax.dynamic_index_in_dim(packed, x_side, 0, False)
    packed_other = lax.dynamic_index_in_dim(packed, 1 - x_side, 0, False)

    def gathered(piece):
        near = [piece] + [flip(piece, "dp", 4 * k) for k in range(1, far)]
        return near + [flip(p, "dp", 2) for p in near]

    normed, cot, inverse_rows = input_norm(hidden_in, cotangent, norm_gain, dp, extent)

    ids = (segments, flip(segments, "dp", 1))
    ids_all = jnp.concatenate(ids, axis=0).astype(F32)
    side_bias = of_side(dt_bias, x_side, 0)
    rate = -jnp.exp(of_side(a_log, x_side, 0))
    bc_par = jnp.concatenate([conv_bc, conv_bc_bias[None], jnp.zeros((3, 2 * LANES), F32)], axis=0)
    head_par = jnp.stack([side_bias, rate, jnp.full_like(rate, x_side)])
    head_par = jnp.pad(head_par, ((0, 5), (0, LANES - own_heads)))
    params = jnp.concatenate(
        [
            of_side(conv_x, x_side, 1),
            of_side(conv_x_bias, x_side, 0)[None],
            of_side(jnp.repeat(d_skip, WIDTH), x_side, 0)[None],
            of_side(gated_gain, x_side, 0)[None],
            jnp.zeros((1, quarter), F32),
        ],
        axis=0,
    )
    params = params.reshape(8, tiles, TILE).transpose(1, 0, 2)
    tokens = 2 * length
    if depth == LANES:
        (
            normed_all, cot_all, weights, bc_weight, zvs, dyns, ys, states, proj_bc, bc, wide, col, rows_all, turned, norms,
        ) = run_gather(
            normed, cot, packed_own, packed_other, jnp.concatenate([of_core(w_bc), w_dt, filler], axis=1),
            ids_all, bc_par, head_par, params, length, far, inner_total,
        )
    else:

        def both_sequences(a):
            near = flip(a, "dp", 1)
            return jnp.concatenate(
                [by_core(a, flip(a, "mp", 1), 0), by_core(near, flip(near, "mp", 1), 0)], axis=0
            )

        normed_all, cot_all = both_sequences(normed), both_sequences(cot)
        packed_other = flip(packed_other, "dp", 1)
        small_weights = jnp.concatenate([w_bc, w_dt, filler], axis=1)
        bc_weight = jnp.concatenate(
            gathered(by_side(small_weights, flip(small_weights, "dp", 1), 0)), axis=0
        )
        proj_bc, bc, wide, col, rows_all, score, turned = run_tables(
            normed_all, bc_weight, ids_all, bc_par, head_par, length
        )
        results = []
        for tile in range(tiles):
            pieces = gathered(by_side(packed_own[tile], packed_other[tile], 0))
            results.append(
                run_forward(
                    pieces, normed_all, cot_all, bc, wide, col, rows_all, score, params[tile], tile, length
                )
            )
        weights, zvs, dyns, ys, states, sums = [jnp.stack(part) for part in zip(*results)]
        sums = jnp.sum(sums, axis=0)
        sums = sums + flip(sums, "mp", 1)
        near = flip(sums, "dp", 1)
        sums = sums + jnp.concatenate([near[:, length:], near[:, :length]], axis=1)
        norms = norm_rows(sums, inner_total)

    inputs = hidden_in.astype(F32)
    usable = (lax.dynamic_slice_in_dim(segments, mp * rows, rows, 0) >= 0).astype(F32)[:, None]
    native = depth == LANES
    norm_cols = norms.T
    ties = []
    if native:
        mixer_own, mixer_give = run_mixer(zvs, ys, norm_cols, params, weights, rows, length, far)
        ties = [mixer_own]
        mixer_x = flip(mixer_give, "dp", 1)

    rate_rows = jnp.pad(rate.reshape(tiles, GROUP, 1), ((0, 0), (0, 8 - GROUP), (0, 0)))
    rate_rows = jnp.broadcast_to(rate_rows, (tiles, 8, LANES))
    inside, results = run_backward(
        ties, normed_all, cot_all, zvs, ys, dyns, bc, wide, col, rows_all, ids_all, turned, norm_cols, params,
        rate_rows, states, length, far,
    )
    (
        grads, dbc, dts, head_sums, smalls, far_share, near_share, z_own, z_send, mine, theirs, dbc_x,
    ) = results

    def placed(a):
        return by_side(a, jnp.zeros_like(a), a.ndim - 1)

    def summed(a, axes):
        for axis in axes:
            bit = 1
            while bit < lax.axis_size(axis):
                a = a + flip(a, axis, bit)
                bit *= 2
        return a

    def mixer_sums(mixer_out):
        return jnp.stack(
            [
                jnp.sum(usable * inputs * inputs),
                jnp.sum(usable * mixer_out * mixer_out),
                jnp.sum(usable),
            ]
        )

    if native:
        input_grad, residual_out, grad_zx, grad_out_weight, grad_steps, grad_bc, pack, last = run_tail(
            hidden_in, cotangent, inverse_rows, norm_gain[None], grads, weights, bc_weight, dts, far_share,
            near_share, z_own, z_send, mine, theirs, dbc, dbc_x, proj_bc, col, bc_par, normed_all, smalls,
            head_sums, rate_rows, usable, mixer_own, mixer_x, length, far, extent,
        )
        grad_zx_weight = grad_zx.reshape(depth, 2, inner)
        grad_dt_weight = grad_steps[:, :, :GROUP].transpose(1, 0, 2, 3).reshape(heads, depth).T
        grad_bc_weight = grad_bc.T
        part = 2 * LANES
        grad_norm_gain = last[:, :part].reshape(width)
        grad_conv_bc, grad_conv_bc_bias = last[:4, part : 2 * part], last[4, part : 2 * part]
        totals = last[:3, 2 * part]
    else:

        def spread_sum(far_part, near_part):
            def arranged(a):
                return a.transpose(1, 0, 2).reshape(SHARE, far, 2 * depth).transpose(1, 0, 2)

            total = arranged(near_part) + arranged(flip(far_part, "dp", 2)).astype(F32)
            out = total.astype(BF16)
            total = total[0]
            for k in range(1, far):
                total = total + flip(out[k], "dp", 4 * k).astype(F32)
            return total

        stacked = jnp.stack([spread_sum(far_share[at], near_share[at]) for at in range(tiles)])
        mine = of_side(stacked, x_side, 2)
        theirs = flip(of_side(stacked, 1 - x_side, 2).astype(BF16), "dp", 1).astype(F32)

        dbc = dbc + flip(dbc, "mp", 1)
        dbc = dbc[:length] + flip(dbc[length:], "dp", 1)
        own_masks = col[:length, VALID : VALID + 3]
        _, state_back = jax.vjp(
            lambda values, taps, bias: jax.nn.silu(segment_conv(values, taps, bias, own_masks)),
            proj_bc[:length],
            conv_bc,
            conv_bc_bias,
        )
        d_bc, grad_conv_bc, grad_conv_bc_bias = state_back(dbc)
        bc_grad = d_bc.astype(BF16)
        small_grad = dot(normed_all[:length], lax.dynamic_slice_in_dim(bc_grad, mp * LANES, LANES, 1), TN)
        small_grad = small_grad.reshape(2 * far, 2, depth, -1)
        small_grad = of_side(small_grad, x_side, 1) + flip(of_side(small_grad, 1 - x_side, 1), "dp", 1)
        small_grad = small_grad.reshape(2, far, depth, -1)
        small_grad = small_grad[0] + flip(small_grad[1], "dp", 2)
        own_bc = small_grad[0]
        for k in range(1, far):
            own_bc = own_bc + flip(small_grad[k], "dp", 4 * k)
        grad_bc_weight = by_core(own_bc, flip(own_bc, "mp", 1), 1)

        def token_sum(products):
            def part(core):
                return products(
                    lambda a: of_side(a.reshape(2, 2, rows, -1), core, 1).reshape(2 * rows, -1)
                )

            total = part(mp) + flip(part(1 - mp).astype(BF16), "mp", 1).astype(F32)
            return total[:rows] + flip(total[rows:].astype(BF16), "dp", 1).astype(F32)

        out_all = jnp.concatenate([w[:, 2 * TILE :] for w in weights], axis=1)
        yn_all = jnp.concatenate([g[:, 2 * TILE :] for g in grads], axis=1)
        mixer_out = restore_order(token_sum(lambda pick: dot(pick(yn_all), out_all, NT)), dp, extent)
        zv_all = jnp.concatenate([w[:, : 2 * TILE] for w in weights], axis=1)
        dt_weight = of_side(bc_weight[:, 2 * LANES : 2 * LANES + heads], x_side, 1)
        dzx_all = jnp.concatenate([g[:, : 2 * TILE] for g in grads], axis=1)
        dt_grad = dts.reshape(tiles, 16, tokens)[:, :GROUP].reshape(own_heads, tokens).T
        d_normed = token_sum(
            lambda pick: dot(pick(dzx_all), zv_all, NT) + dot(pick(dt_grad), dt_weight, NT)
        )
        d_normed = d_normed + dot(
            lax.dynamic_slice_in_dim(bc_grad, mp * rows, rows, 0), bc_weight[:, : 2 * LANES], NT
        )
        d_normed = restore_order(d_normed, dp, extent)
        grad_norm_gain = jnp.sum(d_normed * inputs * inverse_rows, axis=0)
        inverse_cube_rows = inverse_rows * inverse_rows * inverse_rows
        input_grad = (
            cotangent.astype(F32)
            + inverse_rows * norm_gain * d_normed
            - inputs
            * inverse_cube_rows
            * jnp.mean(inputs * norm_gain * d_normed, axis=-1, keepdims=True)
        )
        small = jnp.sum(smalls, axis=1).transpose(1, 0, 2).reshape(8, quarter)
        head_sums = jnp.sum(head_sums[..., 0], axis=1)
        grad_dt_bias = placed(head_sums[:, :GROUP].reshape(own_heads))
        grad_a_log = placed(head_sums[:, GROUP:].reshape(own_heads) * rate)
        head_row = jnp.pad(jnp.concatenate([grad_dt_bias, grad_a_log]), (0, inner - 2 * heads))
        pack = jnp.concatenate([placed(small[: GAIN + 1]), head_row[None]], axis=0)
        pack = summed(pack, ("dp",))
        conv_sums = jnp.concatenate([grad_conv_bc, grad_conv_bc_bias[None]], axis=0)
        conv_sums = summed(conv_sums, ("dp",))
        grad_conv_bc, grad_conv_bc_bias = conv_sums[:4], conv_sums[4]
        last = summed(jnp.concatenate([grad_norm_gain, mixer_sums(mixer_out)]), ("mp", "dp"))
        grad_norm_gain, totals = last[:width], last[width:]

        def assembled(first, last_row):
            def columns(a):
                return a[:, first:last_row].reshape(-1, depth)

            return by_side(columns(mine), columns(theirs), 0)

        grad_zx_weight = jnp.stack([assembled(0, TILE).T, assembled(TILE, STEPS).T], axis=1)
        grad_dt_weight = assembled(STEPS, STEPS + GROUP).T
        grad_out_weight = assembled(OUT, SHARE)
        residual_out = (inputs + mixer_out).astype(BF16)

    skip_grad = jnp.sum(pack[SKIP].reshape(heads, WIDTH), axis=1)
    sum_inputs, sum_mixer, usable_count = totals[0], totals[1], totals[2]
    rms_residual = jnp.sqrt(sum_inputs / (usable_count * width))
    rms_mixer = jnp.sqrt(sum_mixer / (usable_count * width))
    return (
        residual_out,
        input_grad,
        grad_norm_gain,
        grad_zx_weight,
        grad_dt_weight,
        grad_bc_weight,
        pack[TAPS:BIAS],
        pack[BIAS],
        grad_conv_bc,
        grad_conv_bc_bias,
        pack[GAIN + 1, :heads],
        pack[GAIN + 1, heads : 2 * heads],
        skip_grad,
        pack[GAIN],
        grad_out_weight,
        rms_residual,
        rms_mixer,
    )


def solution(mesh):
    in_specs = (
        P(("dp", "mp"), None),
        P("dp"),
        P(),
        P("dp", None, "mp"),
        P("dp", "mp"),
        P("dp", None),
        P(None, "mp"),
        P("mp"),
        P(),
        P(),
        P("mp"),
        P("mp"),
        P("mp"),
        P("mp"),
        P("mp", "dp"),
        P(("dp", "mp"), None),
    )
    out_specs = (
        P(("dp", "mp"), None),
        P(("dp", "mp"), None),
        P(),
        P("dp", None, "mp"),
        P("dp", "mp"),
        P("dp", None),
        P(None, "mp"),
        P("mp"),
        P(),
        P(),
        P("mp"),
        P("mp"),
        P("mp"),
        P("mp"),
        P("mp", "dp"),
        P(),
        P(),
    )
    return jax.shard_map(local, mesh=mesh, in_specs=in_specs, out_specs=out_specs, check_vma=False)
```
